128 devices in a mesh: grp: 4 (over y), sub: 32 (over x, z, core).
Axes of the slice: x: 4, y: 4, z: 4, core: 2. Of those that a mesh axis runs over, the one named last changes fastest.
Arguments:
- modes: bfloat16 [48, 64, 512, 256], P(None, 'grp', 'sub'), as said below
- counts: int32 [128], P(('grp', 'sub')), may hold values from 8 to 40, as said below
- kappa: bfloat16 [64, 512, 256], P('grp', 'sub'), may hold values from 0.29882812 to 3
- react: bfloat16 [64, 512, 256], P('grp', 'sub'), may hold values from 0.19921875 to 2
Outputs:
- factored: float32 [6144, 6144], P(('grp', 'sub'))
The draws below stay inside these ranges and needn't reach their ends.
Inputs may be any that keep to these rules, and one draw needn't show every extreme that they name: A subdomain's live slots are its first counts of 48; at least one subdomain has 40 and one has 8. `modes`: entries of slots at or beyond a subdomain's count are not used.
All inputs are finite; a program needn't handle non-finite values.
Results may differ from the reference program's by a relative error of at most 0.00065.
Values may be sent and summed in bfloat16 or wider, within the bound.
A program may use at most 256 MiB of HBM per device.

```python
import math
import jax
import jax.numpy as jnp
from jax import lax

CX = 16
CY = 16
NZ = 256
KSLOT = 48
KMIN = 8
KMAX = 40
PANEL = 512
PANELS = 2
NX = 64
NY = 512
N_GRP = 4
N_SUB = 32


def draw_modes(key, part):
    key = jax.random.fold_in(key, 11)
    key_level, key_rough = jax.random.split(key)
    level = jax.random.uniform(key_level, (KSLOT, N_GRP, N_SUB), jnp.float32, -1.0, 1.0)
    rough = jax.random.normal(key_rough, (KSLOT, NX, NY, NZ), jnp.float32)
    spread = jnp.repeat(jnp.repeat(level, CX, axis=1), CY, axis=2)[..., None]
    scale = 1.0 / jnp.sqrt(jnp.float32(CX * CY * NZ))
    return ((spread + 0.3 * rough) * scale).astype(jnp.bfloat16)


def draw_counts(key, part):
    key = jax.random.fold_in(key, 23)
    key_a, key_b, key_c = jax.random.split(key, 3)
    total = N_GRP * N_SUB
    values = jax.random.randint(key_a, (total,), KMIN, KMAX + 1, jnp.int32)
    first = jax.random.randint(key_b, (), 0, total, jnp.int32)
    second = (first + 1 + jax.random.randint(key_c, (), 0, total - 1, jnp.int32)) % total
    return values.at[first].set(KMAX).at[second].set(KMIN)


def block_scale(stream_key, dims, cuts, low, high):
    def one(position, blocks):
        steps = jax.random.uniform(jax.random.fold_in(jax.random.fold_in(stream_key, 6), position), (blocks,), jnp.float32, low / len(cuts), high / len(cuts))
        return jnp.repeat(jnp.exp(steps), dims[position] // blocks).reshape((-1,) + (1,) * (len(dims) - position - 1))

    level = one(*cuts[0])
    for cut in cuts[1:]:
        level = level * one(*cut)
    return level


def setup_inputs(seed: int = 0) -> dict:
    key_list = jax.random.split(jax.random.key(seed), 5)
    return {
        "modes": draw_modes(jax.random.fold_in(key_list[4], 71), 0),
        "counts": draw_counts(jax.random.fold_in(key_list[4], 71), 0),
        "kappa": jnp.clip(jnp.exp(math.log(3.0) - 2.306499 * jax.random.uniform(key_list[2], (NX, NY, NZ), jnp.float32) ** block_scale(key_list[2], (NX, NY, NZ), ((0, 4), (1, 32)), -0.2, 0.2)), 0.29882812, 3.0).astype(jnp.bfloat16),
        "react": jnp.clip(jnp.exp(math.log(2.0) - 2.306499 * jax.random.uniform(key_list[3], (NX, NY, NZ), jnp.float32) ** block_scale(key_list[3], (NX, NY, NZ), ((0, 4), (1, 32)), -0.2, 0.2)), 0.19921875, 2.0).astype(jnp.bfloat16),
    }


def right_solve(lower, matrix):
    return lax.linalg.triangular_solve(lower, matrix, left_side=False, lower=True, transpose_a=True)

def block_row(zmask, kext, react, faces, sidx, n_sub, nc, unused):
    kb = kext[1:-1, 1:-1]
    wx = 0.5 * (kb[:-1] + kb[1:])
    wy = 0.5 * (kb[:, :-1] + kb[:, 1:])
    wz = 0.5 * (kb[:, :, :-1] + kb[:, :, 1:])
    wxm = 0.5 * (kb[0] + kext[0, 1:-1])
    wxp = 0.5 * (kb[-1] + kext[-1, 1:-1])
    wym = 0.5 * (kb[:, 0] + kext[1:-1, 0])
    wyp = 0.5 * (kb[:, -1] + kext[1:-1, -1])
    dx = jnp.concatenate([wxm[None], wx], 0) + jnp.concatenate([wx, wxp[None]], 0)
    dy = jnp.concatenate([wym[:, None], wy], 1) + jnp.concatenate([wy, wyp[:, None]], 1)
    dz = jnp.concatenate([0.5 * kb[:, :, :1], wz], 2) + jnp.concatenate([wz, 0.5 * kb[:, :, -1:]], 2)
    diag = react + dx + dy + dz
    field = zmask.astype(jnp.float32)
    sx = jnp.pad(wx * field[:, 1:], ((0, 0), (0, 1), (0, 0), (0, 0))) + jnp.pad(wx * field[:, :-1], ((0, 0), (1, 0), (0, 0), (0, 0)))
    sy = jnp.pad(wy * field[:, :, 1:], ((0, 0), (0, 0), (0, 1), (0, 0))) + jnp.pad(wy * field[:, :, :-1], ((0, 0), (0, 0), (1, 0), (0, 0)))
    sz = jnp.pad(wz * field[:, :, :, 1:], ((0, 0), (0, 0), (0, 0), (0, 1))) + jnp.pad(wz * field[:, :, :, :-1], ((0, 0), (0, 0), (0, 0), (1, 0)))
    applied = (diag * field - sx - sy - sz).astype(jnp.bfloat16)
    slots = field.shape[0]
    self_block = jnp.dot(field.reshape(slots, -1), applied.astype(jnp.float32).reshape(slots, -1).T, precision=lax.Precision.HIGHEST) + jnp.diag(unused)

    def couple(own_face, weight, other):
        left = (own_face * weight).reshape(slots, -1)
        right = other.astype(jnp.float32).reshape(slots, -1)
        return -jnp.dot(left, right.T, precision=lax.Precision.HIGHEST)
    blocks = [self_block, couple(field[:, 0], wxm, faces[0]), couple(field[:, -1], wxp, faces[1]), couple(field[:, :, 0], wym, faces[2]), couple(field[:, :, -1], wyp, faces[3])]
    targets = [sidx, sidx - n_sub, sidx + n_sub, sidx - 1, sidx + 1]
    owners = jnp.arange(nc // slots, dtype=jnp.int32)
    row = jnp.zeros((slots, nc // slots, slots), jnp.float32)
    for block, target in zip(blocks, targets):
        row = row + jnp.where((owners == target)[None, :, None], block[:, None, :], jnp.float32(0.0))
    return row.reshape(slots, nc)

def reference(modes, counts, kappa, react):
    slots = modes.shape[0]
    n_sub = N_SUB
    n_grp = N_GRP
    nc = slots * n_grp * n_sub
    kpad = jnp.pad(kappa.astype(jnp.float32), ((1, 1), (1, 1), (0, 0)))
    slot = jnp.arange(slots, dtype=jnp.int32)
    zero_b = jnp.bfloat16(0.0)

    def neighbour_face(start, size, valid, other):
        face = lax.dynamic_slice(modes, start, size)
        live = (slot < counts[jnp.clip(other, 0, n_grp * n_sub - 1)]) & valid
        return jnp.where(live[:, None, None, None], face, zero_b)

    def one(sidx):
        g = sidx // n_sub
        u = sidx % n_sub
        x0 = (g * CX).astype(jnp.int32)
        y0 = (u * CY).astype(jnp.int32)
        zero = jnp.int32(0)
        block = lax.dynamic_slice(modes, (zero, x0, y0, zero), (slots, CX, CY, NZ))
        live = slot < counts[sidx]
        zmask = jnp.where(live[:, None, None, None], block, zero_b)
        kext = lax.dynamic_slice(kpad, (x0, y0, zero), (CX + 2, CY + 2, NZ))
        cb = lax.dynamic_slice(react, (x0, y0, zero), (CX, CY, NZ)).astype(jnp.float32)
        xm = neighbour_face((zero, jnp.maximum(x0 - 1, 0), y0, zero), (slots, 1, CY, NZ), g > 0, sidx - n_sub)[:, 0]
        xp = neighbour_face((zero, jnp.minimum(x0 + CX, CX * n_grp - 1), y0, zero), (slots, 1, CY, NZ), g < n_grp - 1, sidx + n_sub)[:, 0]
        ym = neighbour_face((zero, x0, jnp.maximum(y0 - 1, 0), zero), (slots, CX, 1, NZ), u > 0, sidx - 1)[:, :, 0]
        yp = neighbour_face((zero, x0, jnp.minimum(y0 + CY, CY * n_sub - 1), zero), (slots, CX, 1, NZ), u < n_sub - 1, sidx + 1)[:, :, 0]
        unused = 1.0 - live.astype(jnp.float32)
        return block_row(zmask, kext, cb, (xm, xp, ym, yp), sidx, n_sub, nc, unused)
    coarse = lax.map(one, jnp.arange(n_grp * n_sub, dtype=jnp.int32)).reshape(nc, nc)
    for step in range(PANELS):
        c0 = step * PANEL
        c1 = c0 + PANEL
        whole = coarse[:, c0:c1]
        lower = jnp.linalg.cholesky(whole[c0:c1])
        solved = right_solve(lower, whole)
        solved = solved.at[c0:c1].set(lower).at[:c0].set(0.0)
        update = jnp.dot(solved, solved[c1:].T, precision=lax.Precision.HIGHEST)
        coarse = jnp.concatenate([coarse[:, :c0], solved, coarse[:, c1:] - update], 1)
    done = PANELS * PANEL
    rows = jnp.arange(nc)[:, None]
    cols = jnp.arange(nc)[None, :]
    return jnp.where((rows < done) & (cols >= done), jnp.float32(0.0), coarse)
```

```python
import jax
import jax.numpy as jnp
from jax import lax
from jax.experimental import pallas as pl
from jax.experimental.pallas import tpu as pltpu
from jax.sharding import PartitionSpec as P

F32 = jnp.float32
BF16 = jnp.bfloat16
MESH = pl.DeviceIdType.MESH
NG, NU = 4, 32
CX, CY, NZ = 16, 16, 256
SLOTS, LIVE = 48, 40
NB = 22
DONE = 1024
NC = SLOTS * NG * NU
XR = 1280
XC = 1152
HI = lax.Precision.HIGHEST


def nt(a, b, precision=None):
    return lax.dot_general(
        a, b, (((1,), (1,)), ((), ())), preferred_element_type=F32, precision=precision
    )


def lanes_of(shape):
    return lax.broadcasted_iota(jnp.int32, shape, len(shape) - 1)


def rows_of(shape):
    return lax.broadcasted_iota(jnp.int32, shape, len(shape) - 2)


def split(x):
    hi = x.astype(BF16)
    return hi, (x - hi.astype(F32)).astype(BF16)


def pad_rows(x, rows):
    return jnp.concatenate([x, jnp.zeros((rows - x.shape[0], x.shape[1]), x.dtype)], 0)


def pad_lanes(x, lanes):
    return jnp.concatenate([x, jnp.zeros((x.shape[0], lanes - x.shape[1]), x.dtype)], 1)


def transposed(x):
    return jnp.transpose(pad_rows(x, 128))


def assemble_kernel(
    count_ref, modes_ref, kappa_ref, react_ref, blocks_ref, payload_ref,
    raw, field, masked, wx, wy, wz, diag, edge, halo, face,
    raw_sem, halo_send, halo_recv, face_send, face_recv,
):
    g, u = lax.axis_index("grp"), lax.axis_index("sub")
    partners = [
        (lax.rem(g + NG - 1, NG), u),
        (lax.rem(g + 1, NG), u),
        (g, lax.rem(u + NU - 1, NU)),
        (g, lax.rem(u + 1, NU)),
    ]
    inside = [g > 0, g < NG - 1, u > 0, u < NU - 1]
    mirror = [1, 0, 3, 2]

    def fetch(x):
        return pltpu.make_async_copy(
            modes_ref.at[pl.ds(0, LIVE), x], raw.at[x], raw_sem.at[x]
        )

    for x in range(CX):
        fetch(x).start()

    barrier = pltpu.get_barrier_semaphore()
    for partner in partners:
        pl.semaphore_signal(barrier, inc=1, device_id=partner, device_id_type=MESH)

    count = count_ref[0]
    kap = kappa_ref[...].astype(F32)
    edge[0] = kap[0]
    edge[1] = kap[CX - 1]
    for x in range(CX):
        edge[2, x : x + 1] = kap[x, 0:1]
        edge[3, x : x + 1] = kap[x, CY - 1 : CY]
    pl.semaphore_wait(barrier, 4)

    def halo_copy(k):
        return pltpu.make_async_remote_copy(
            src_ref=edge.at[k], dst_ref=halo.at[mirror[k]],
            send_sem=halo_send.at[k], recv_sem=halo_recv.at[mirror[k]],
            device_id=partners[k], device_id_type=MESH,
        )

    for k in range(4):
        halo_copy(k).start()

    live = rows_of((CY, LIVE, NZ)) < count

    def turn(x, carry):
        pltpu.make_async_copy(
            modes_ref.at[pl.ds(0, LIVE), x], raw.at[x], raw_sem.at[x]
        ).wait()
        plane = jnp.swapaxes(raw[x].astype(F32), 0, 1)
        plane = jnp.where(live, plane, 0.0)
        field[x] = plane
        masked[x] = jnp.concatenate(
            [plane, jnp.zeros((CY, SLOTS - LIVE, NZ), F32)], 1
        ).astype(BF16)
        return carry

    lax.fori_loop(0, CX, turn, 0)

    sources = [masked.at[0], masked.at[CX - 1], masked.at[:, 0], masked.at[:, CY - 1]]

    def face_copy(k):
        return pltpu.make_async_remote_copy(
            src_ref=sources[k], dst_ref=face.at[mirror[k]],
            send_sem=face_send.at[k], recv_sem=face_recv.at[mirror[k]],
            device_id=partners[k], device_id_type=MESH,
        )

    for k in range(4):
        face_copy(k).start()

    plane0 = jnp.zeros((CY, NZ), F32)
    row0 = jnp.zeros((1, NZ), F32)
    last = lanes_of((CY, NZ)) == NZ - 1
    first = lanes_of((CY, NZ)) == 0
    wx[0] = plane0
    wx[CX] = plane0
    for x in range(CX - 1):
        wx[x + 1] = 0.5 * (kap[x] + kap[x + 1])
    for x in range(CX):
        k = kap[x]
        wy[x, 0:1] = row0
        wy[x, 1:CY] = 0.5 * (k[: CY - 1] + k[1:])
        wy[x, CY : CY + 1] = row0
        wz[x] = jnp.where(last, 0.0, 0.5 * (k + pltpu.roll(k, NZ - 1, 1)))
    for k in range(4):
        halo_copy(k).wait_recv()
    ext = [jnp.where(inside[k], halo[k], 0.0) for k in range(4)]
    bound = [0.5 * (edge[k] + ext[k]) for k in range(4)]
    for x in range(CX):
        k = kap[x]
        w = wz[x]
        below = jnp.where(first, 0.5 * k, pltpu.roll(w, 1, 1))
        above = jnp.where(last, 0.5 * k, w)
        dx = (bound[0] if x == 0 else wx[x]) + (bound[1] if x == CX - 1 else wx[x + 1])
        dy = wy[x, 0:CY] + wy[x, 1 : CY + 1]
        dy = dy + jnp.concatenate(
            [bound[2][x : x + 1], jnp.zeros((CY - 2, NZ), F32), bound[3][x : x + 1]], 0
        )
        diag[x] = react_ref[x].astype(F32) + dx + dy + (below + above)

    def apply(x, total):
        before, after = jnp.maximum(x - 1, 0), jnp.minimum(x + 1, CX - 1)
        for y in range(CY):
            v = field[x, y]
            out = diag[x, y : y + 1] * v
            out = out - wx[x, y : y + 1] * field[before, y]
            out = out - wx[x + 1, y : y + 1] * field[after, y]
            if y > 0:
                out = out - wy[x, y : y + 1] * field[x, y - 1]
            if y < CY - 1:
                out = out - wy[x, y + 1 : y + 2] * field[x, y + 1]
            w = wz[x, y : y + 1]
            out = out - w * pltpu.roll(v, NZ - 1, 1)
            out = out - pltpu.roll(w * v, 1, 1)
            local = pad_rows(out, SLOTS).astype(BF16)
            total = total + nt(masked[x, y], local)
        return total

    own = lax.fori_loop(0, CX, apply, jnp.zeros((SLOTS, SLOTS), F32))
    spot, slot = lanes_of((SLOTS, SLOTS)), rows_of((SLOTS, SLOTS))
    own = own + jnp.where((spot == slot) & (slot >= count), 1.0, 0.0)

    found = []
    for k in range(4):
        face_copy(mirror[k]).wait_recv()

        def couple(i, total, k=k):
            if k < 2:
                mine = field[0 if k == 0 else CX - 1, i]
                other = pl.ds(i, 1)
                weight = 0.5 * (edge[k, other] + jnp.where(inside[k], halo[k, other], 0.0))
            else:
                mine = field[i, 0 if k == 2 else CY - 1]
                other = pl.ds(i, 1)
                weight = 0.5 * (edge[k, other] + jnp.where(inside[k], halo[k, other], 0.0))
            hi, lo = split(pad_rows(mine * weight, SLOTS))
            other = face[k, i]
            return total - (nt(hi, other) + nt(lo, other))

        block = lax.fori_loop(0, CX, couple, jnp.zeros((SLOTS, SLOTS), F32))
        found.append(jnp.where(inside[k], block, 0.0))

    blocks = [pad_lanes(b, 128) for b in [own] + found]
    for k in range(5):
        blocks_ref[k] = blocks[k]
    sym = 0.5 * (blocks[0] + transposed(blocks[0])[:SLOTS])
    up = transposed(blocks[2])[:SLOTS]
    lane = lanes_of((SLOTS, 128))
    sym = jnp.where(lane < LIVE, sym, 0.0)
    payload = sym + pltpu.roll(blocks[4], LIVE, 1) + pltpu.roll(up, 2 * LIVE, 1)
    payload_ref[...] = payload[:LIVE]

    for k in range(4):
        halo_copy(k).wait_send()
        face_copy(k).wait_send()


def assemble(count, modes, kappa, react):
    vmem = pl.BlockSpec(memory_space=pltpu.VMEM)
    return pl.pallas_call(
        assemble_kernel,
        out_shape=(
            jax.ShapeDtypeStruct((5, SLOTS, 128), F32),
            jax.ShapeDtypeStruct((LIVE, 128), F32),
        ),
        in_specs=[
            pl.BlockSpec(memory_space=pltpu.SMEM),
            pl.BlockSpec(memory_space=pl.ANY),
            vmem,
            vmem,
        ],
        out_specs=(vmem, vmem),
        scratch_shapes=[
            pltpu.VMEM((CX, LIVE, CY, NZ), BF16),
            pltpu.VMEM((CX, CY, LIVE, NZ), F32),
            pltpu.VMEM((CX, CY, SLOTS, NZ), BF16),
            pltpu.VMEM((CX + 1, CY, NZ), F32),
            pltpu.VMEM((CX, 24, NZ), F32),
            pltpu.VMEM((CX, CY, NZ), F32),
            pltpu.VMEM((CX, CY, NZ), F32),
            pltpu.VMEM((4, 16, NZ), F32),
            pltpu.VMEM((4, 16, NZ), F32),
            pltpu.VMEM((4, 16, SLOTS, NZ), BF16),
            pltpu.SemaphoreType.DMA((CX,)),
            pltpu.SemaphoreType.DMA((4,)),
            pltpu.SemaphoreType.DMA((4,)),
            pltpu.SemaphoreType.DMA((4,)),
            pltpu.SemaphoreType.DMA((4,)),
        ],
        compiler_params=pltpu.CompilerParams(
            collective_id=0, has_side_effects=True, vmem_limit_bytes=50 * 2**20
        ),
        name="assemble",
    )(count, modes, kappa, react)


def spread_kernel(payload_ref, all_ref, slots, send_sem, recv_sem):
    g, u = lax.axis_index("grp"), lax.axis_index("sub")
    source = (g == 0) & (u < NB)
    target = ((g == 0) & (u < NB + 1)) | ((g == 1) & (u < NB))
    barrier = pltpu.get_barrier_semaphore()

    @pl.when(target)
    def _():
        def greet(v, carry):
            @pl.when((g == 1) | (v != u))
            def _():
                pl.semaphore_signal(barrier, inc=1, device_id=(0, v), device_id_type=MESH)
            return carry

        lax.fori_loop(0, NB, greet, 0)

    def copy(to_g, to_u, slot, sem):
        return pltpu.make_async_remote_copy(
            src_ref=payload_ref, dst_ref=slots.at[slot],
            send_sem=send_sem.at[sem], recv_sem=recv_sem.at[slot],
            device_id=(to_g, to_u), device_id_type=MESH,
        )

    @pl.when(source)
    def _():
        pl.semaphore_wait(barrier, 2 * NB)

        def send(v, carry):
            @pl.when(v < NB)
            def _():
                copy(1, v, u, v).start()

            @pl.when(v != u)
            def _():
                copy(0, v, u, NB + v).start()
            return carry

        lax.fori_loop(0, NB + 1, send, 0)

    @pl.when(target)
    def _():
        def receive(v, carry):
            @pl.when((g == 1) | (v != u))
            def _():
                copy(0, v, v, 0).wait_recv()
                all_ref[v] = slots[v]
            return carry

        lax.fori_loop(0, NB, receive, 0)

    @pl.when(source)
    def _():
        all_ref[u] = payload_ref[...]

        def sent(v, carry):
            @pl.when(v < NB)
            def _():
                copy(1, v, u, v).wait_send()

            @pl.when(v != u)
            def _():
                copy(0, v, u, NB + v).wait_send()
            return carry

        lax.fori_loop(0, NB + 1, sent, 0)


def spread(payload):
    vmem = pl.BlockSpec(memory_space=pltpu.VMEM)
    return pl.pallas_call(
        spread_kernel,
        out_shape=jax.ShapeDtypeStruct((NB, LIVE, 128), F32),
        in_specs=[vmem],
        out_specs=vmem,
        scratch_shapes=[
            pltpu.VMEM((NB, LIVE, 128), F32),
            pltpu.SemaphoreType.DMA((2 * NB + 1,)),
            pltpu.SemaphoreType.DMA((NB,)),
        ],
        compiler_params=pltpu.CompilerParams(collective_id=1, has_side_effects=True),
        name="spread",
    )(payload)


def eliminate(a, panels):
    tiles = [a[8 * v : 8 * v + 8] for v in range(LIVE // 8)]
    sub = rows_of((8, 128))
    wide = lambda x: jnp.broadcast_to(x, (8, 128))
    for p in range(panels):
        below = range(p, LIVE // 8)
        cols = [
            {v: wide(tiles[v][:, 8 * p + c : 8 * p + c + 1]) for v in below} for c in range(8)
        ]
        for c in range(8):
            rinv = lax.rsqrt(wide(cols[c][p][c : c + 1]))
            low = {v: cols[c][v] * rinv for v in below}
            row = wide(tiles[p][c : c + 1]) * rinv
            for d in range(c + 1, 8):
                coef = wide(low[p][d : d + 1])
                cols[d] = {v: cols[d][v] - low[v] * coef for v in below}
            for v in below:
                if v == p:
                    reduced = tiles[v] - low[v] * row
                    tiles[v] = jnp.where(sub > c, reduced, jnp.where(sub == c, row, tiles[v]))
                else:
                    tiles[v] = tiles[v] - low[v] * row
    return jnp.concatenate(tiles, 0)


def place(out_ref, block, pos, keep):
    base = jnp.minimum((pos // 128) * 128, NC - 256)
    base = pl.multiple_of(base, 128)
    shifted = pltpu.roll(pad_lanes(block, 256), pos - base, 1)
    cols = lanes_of((SLOTS, 256)) + base
    out_ref[:, pl.ds(base, 256)] += jnp.where(keep(cols), shifted, 0.0)


def factor_kernel(all_ref, blocks_ref, out_ref, done, xh, xl, hh, hl):
    g, u = lax.axis_index("grp"), lax.axis_index("sub")
    s = g * NU + u
    upper = s <= 21
    member = (s == 21) | (s == 22) | ((s >= NU) & (s < NU + NB))
    lane = lanes_of((LIVE, 128))
    row = rows_of((LIVE, 128))
    out_ref[...] = jnp.zeros_like(out_ref)

    def spot(t):
        pos = SLOTS * t
        base = pl.multiple_of((pos // 128) * 128, 128)
        return base, pos - base

    def left(x, by):
        return jnp.where(lane < LIVE, pltpu.roll(x, 128 - by, 1), 0.0)

    def step(t, panels):
        prev = left(done[t], LIVE)
        gram = lax.dot_general(
            prev, prev, (((0,), (0,)), ((), ())), preferred_element_type=F32, precision=HI
        )[:LIVE]
        given = all_ref[t]
        a = jnp.where(lane < 2 * LIVE, given, jnp.where(lane == row + 2 * LIVE, 1.0, 0.0))
        a = eliminate(a - gram, panels)
        a = jnp.where((lane >= row) & (row < 8 * panels), a, 0.0)
        done[t + 1] = a
        linv = left(a, 2 * LIVE)
        rising = left(given, 2 * LIVE)
        mixed = nt(jnp.concatenate([-prev, rising], 0), pad_rows(linv, 128), HI)
        base, off = spot(t)
        last_base, last_off = spot(jnp.maximum(t - 1, 0))
        mixed = pltpu.roll(pad_lanes(mixed, 256), off, 1)
        zero = jnp.zeros((256, 256), BF16)
        hh[...] = zero
        hl[...] = zero
        hi, lo = split(pad_rows(mixed[:LIVE], SLOTS))
        last_off = pl.multiple_of(last_off, 16)
        hh[pl.ds(last_off, SLOTS), :] = hi
        hl[pl.ds(last_off, SLOTS), :] = lo
        tall = 4 * SLOTS
        span = lanes_of((tall, 256))
        fresh = (span >= off) & (span < off + SLOTS)

        def fill(c, carry):
            r = pl.multiple_of(128 + c * tall, 16)
            xhi = xh[pl.ds(r, tall), pl.ds(last_base, 256)]
            xlo = xl[pl.ds(r, tall), pl.ds(last_base, 256)]
            dot = lambda p, q: jnp.dot(p, q[...], preferred_element_type=F32)
            new = dot(xhi, hh) + dot(xhi, hl) + dot(xlo, hh)
            hi, lo = split(new)
            cols = pl.ds(base, 256)
            rows = pl.ds(r, tall)
            xh[rows, cols] = jnp.where(fresh, hi, xh[rows, cols])
            xl[rows, cols] = jnp.where(fresh, lo, xl[rows, cols])
            return carry

        lax.fori_loop(0, (t + 3) // 4, fill, 0)
        hi, lo = split(pad_rows(mixed[LIVE:], SLOTS))
        r = pl.multiple_of(128 + SLOTS * t, 16)
        xh[pl.ds(r, SLOTS), pl.ds(base, 256)] = hi
        xl[pl.ds(r, SLOTS), pl.ds(base, 256)] = lo

    @pl.when(upper | member)
    def _():
        done[0] = jnp.zeros((LIVE, 128), F32)

        def clear(c, carry):
            xh[pl.ds(pl.multiple_of(c * 128, 128), 128), :] = jnp.zeros((128, XC), BF16)
            xl[pl.ds(pl.multiple_of(c * 128, 128), 128), :] = jnp.zeros((128, XC), BF16)
            return carry

        lax.fori_loop(0, XR // 128, clear, 0)

        def loop(t, carry):
            step(t, LIVE // 8)
            return carry

        lax.fori_loop(0, NB - 1, loop, 0)
        step(NB - 1, 2)

        w20 = transposed(left(done[NB - 1], LIVE))
        w21 = transposed(left(done[NB], LIVE))
        r21 = transposed(jnp.where(lane < LIVE, done[NB], 0.0))
        put = lambda x, by: pltpu.roll(pad_lanes(x, 256), by, 1)
        part = put(w20[16:LIVE], 64) + put(r21[16:LIVE], 112)
        region = jnp.concatenate(
            [part, jnp.zeros((8, 256), F32), put(w21[:LIVE], 112), jnp.zeros((56, 256), F32)], 0
        )
        hi, lo = split(region)
        xh[0:128, 896:1152] = hi
        xl[0:128, 896:1152] = lo

    @pl.when(upper)
    def _():
        ahead = transposed(left(done[jnp.minimum(s, NB)], LIVE))[:SLOTS]
        own = transposed(jnp.where(lane < LIVE, done[jnp.minimum(s, NB - 1) + 1], 0.0))[:SLOTS]
        r, c = rows_of((SLOTS, 128)), lanes_of((SLOTS, 128))
        own = own + jnp.where((r == c) & (r >= LIVE), 1.0, 0.0)
        keep = lambda cols: cols < DONE
        place(out_ref, ahead, SLOTS * jnp.maximum(s - 1, 0), keep)
        place(out_ref, own, SLOTS * s, keep)

    @pl.when(member)
    def _():
        r0 = jnp.where(s >= NU, 128 + SLOTS * (s - NU), jnp.where(s == 22, 32, 0))
        r0 = pl.multiple_of(r0, 16)
        hi = xh[pl.ds(r0, SLOTS), 0:DONE]
        lo = xl[pl.ds(r0, SLOTS), 0:DONE]
        late = jnp.concatenate([jnp.zeros((16, DONE), BF16), hi[:32]], 0)
        hi = jnp.where(s == 21, late, hi)
        late = jnp.concatenate([jnp.zeros((16, DONE), BF16), lo[:32]], 0)
        lo = jnp.where(s == 21, late, lo)

        @pl.when(s != 21)
        def _():
            out_ref[:, 0:DONE] = hi.astype(F32) + lo.astype(F32)

        for c in range(XR // 128):
            rows = pl.ds(c * 128, 128)
            th, tl = xh[rows, 0:DONE], xl[rows, 0:DONE]
            col = DONE if c == 0 else 1408 + 128 * c
            out_ref[:, col : col + 128] = -(nt(hi, th) + nt(hi, tl) + nt(lo, th))

    @pl.when(s >= 21)
    def _():
        targets = [s, s - NU, s + NU, s - 1, s + 1]
        valid = [True, g > 0, g < NG - 1, u > 0, u < NU - 1]
        for k in range(5):
            block = blocks_ref[k]
            block = jnp.where((s > 21) | (rows_of((SLOTS, 128)) >= 16), block, 0.0)
            pos = SLOTS * jnp.clip(targets[k], 0, NG * NU - 1)
            place(out_ref, jnp.where(valid[k], block, 0.0), pos, lambda cols: cols >= DONE)


def factor(everyone, blocks):
    vmem = pl.BlockSpec(memory_space=pltpu.VMEM)
    return pl.pallas_call(
        factor_kernel,
        out_shape=jax.ShapeDtypeStruct((SLOTS, NC), F32),
        in_specs=[vmem, vmem],
        out_specs=vmem,
        scratch_shapes=[
            pltpu.VMEM((NB + 1, LIVE, 128), F32),
            pltpu.VMEM((XR, XC), BF16),
            pltpu.VMEM((XR, XC), BF16),
            pltpu.VMEM((256, 256), BF16),
            pltpu.VMEM((256, 256), BF16),
        ],
        compiler_params=pltpu.CompilerParams(vmem_limit_bytes=40 * 2**20),
        name="factor",
    )(everyone, blocks)


def per_device(modes, counts, kappa, react):
    blocks, payload = assemble(counts, modes, kappa, react)
    everyone = spread(payload)
    return factor(everyone, blocks)


def solution(mesh):
    in_specs = (
        P(None, "grp", "sub", None),
        P(("grp", "sub")),
        P("grp", "sub", None),
        P("grp", "sub", None),
    )
    out_specs = P(("grp", "sub"), None)
    return jax.shard_map(
        per_device, mesh=mesh, in_specs=in_specs, out_specs=out_specs, check_vma=False
    )
```

```python
import jax
import jax.numpy as jnp
from jax import lax
from jax.experimental import pallas as pl
from jax.experimental.pallas import tpu as pltpu
from jax.sharding import PartitionSpec as P

F32 = jnp.float32
BF16 = jnp.bfloat16
MESH = pl.DeviceIdType.MESH
NG, NU = 4, 32
CX, CY, NZ = 16, 16, 256
SLOTS, LIVE = 48, 40
NB = 22
DONE = 1024
NC = SLOTS * NG * NU


def nt(a, b, precision=None):
    return lax.dot_general(
        a, b, (((1,), (1,)), ((), ())), preferred_element_type=F32, precision=precision
    )


def lanes_of(shape):
    return lax.broadcasted_iota(jnp.int32, shape, len(shape) - 1)


def rows_of(shape):
    return lax.broadcasted_iota(jnp.int32, shape, len(shape) - 2)


def split(x):
    hi = x.astype(BF16)
    return hi, (x - hi.astype(F32)).astype(BF16)


def pad_rows(x, rows):
    return jnp.concatenate([x, jnp.zeros((rows - x.shape[0], x.shape[1]), x.dtype)], 0)


def pad_lanes(x, lanes):
    return jnp.concatenate([x, jnp.zeros((x.shape[0], lanes - x.shape[1]), x.dtype)], 1)


def transposed(x):
    return jnp.transpose(pad_rows(x, 128))


def assemble_kernel(
    count_ref, modes_ref, kappa_ref, react_ref, blocks_ref, payload_ref,
    raw, field, masked, wx, wy, wz, diag, edge, halo, face,
    raw_sem, halo_send, halo_recv, face_send, face_recv,
):
    g, u = lax.axis_index("grp"), lax.axis_index("sub")
    partners = [
        (lax.rem(g + NG - 1, NG), u),
        (lax.rem(g + 1, NG), u),
        (g, lax.rem(u + NU - 1, NU)),
        (g, lax.rem(u + 1, NU)),
    ]
    inside = [g > 0, g < NG - 1, u > 0, u < NU - 1]
    mirror = [1, 0, 3, 2]

    def fetch(x):
        return pltpu.make_async_copy(
            modes_ref.at[pl.ds(0, LIVE), x], raw.at[x], raw_sem.at[x]
        )

    for x in range(CX):
        fetch(x).start()

    barrier = pltpu.get_barrier_semaphore()
    for partner in partners:
        pl.semaphore_signal(barrier, inc=1, device_id=partner, device_id_type=MESH)

    count = count_ref[0]
    kap = kappa_ref[...].astype(F32)
    edge[0] = kap[0]
    edge[1] = kap[CX - 1]
    for x in range(CX):
        edge[2, x : x + 1] = kap[x, 0:1]
        edge[3, x : x + 1] = kap[x, CY - 1 : CY]
    pl.semaphore_wait(barrier, 4)

    def halo_copy(k):
        return pltpu.make_async_remote_copy(
            src_ref=edge.at[k], dst_ref=halo.at[mirror[k]],
            send_sem=halo_send.at[k], recv_sem=halo_recv.at[mirror[k]],
            device_id=partners[k], device_id_type=MESH,
        )

    for k in range(4):
        halo_copy(k).start()

    live = rows_of((CY, LIVE, NZ)) < count

    def turn(x, carry):
        pltpu.make_async_copy(
            modes_ref.at[pl.ds(0, LIVE), x], raw.at[x], raw_sem.at[x]
        ).wait()
        plane = jnp.swapaxes(raw[x].astype(F32), 0, 1)
        plane = jnp.where(live, plane, 0.0)
        field[x] = plane
        masked[x] = jnp.concatenate(
            [plane, jnp.zeros((CY, SLOTS - LIVE, NZ), F32)], 1
        ).astype(BF16)
        return carry

    lax.fori_loop(0, CX, turn, 0)

    sources = [masked.at[0], masked.at[CX - 1], masked.at[:, 0], masked.at[:, CY - 1]]

    def face_copy(k):
        return pltpu.make_async_remote_copy(
            src_ref=sources[k], dst_ref=face.at[mirror[k]],
            send_sem=face_send.at[k], recv_sem=face_recv.at[mirror[k]],
            device_id=partners[k], device_id_type=MESH,
        )

    for k in range(4):
        face_copy(k).start()

    plane0 = jnp.zeros((CY, NZ), F32)
    row0 = jnp.zeros((1, NZ), F32)
    last = lanes_of((CY, NZ)) == NZ - 1
    first = lanes_of((CY, NZ)) == 0
    wx[0] = plane0
    wx[CX] = plane0
    for x in range(CX - 1):
        wx[x + 1] = 0.5 * (kap[x] + kap[x + 1])
    for x in range(CX):
        k = kap[x]
        wy[x, 0:1] = row0
        wy[x, 1:CY] = 0.5 * (k[: CY - 1] + k[1:])
        wy[x, CY : CY + 1] = row0
        wz[x] = jnp.where(last, 0.0, 0.5 * (k + pltpu.roll(k, NZ - 1, 1)))
    for k in range(4):
        halo_copy(k).wait_recv()
    ext = [jnp.where(inside[k], halo[k], 0.0) for k in range(4)]
    bound = [0.5 * (edge[k] + ext[k]) for k in range(4)]
    for x in range(CX):
        k = kap[x]
        w = wz[x]
        below = jnp.where(first, 0.5 * k, pltpu.roll(w, 1, 1))
        above = jnp.where(last, 0.5 * k, w)
        dx = (bound[0] if x == 0 else wx[x]) + (bound[1] if x == CX - 1 else wx[x + 1])
        dy = wy[x, 0:CY] + wy[x, 1 : CY + 1]
        dy = dy + jnp.concatenate(
            [bound[2][x : x + 1], jnp.zeros((CY - 2, NZ), F32), bound[3][x : x + 1]], 0
        )
        diag[x] = react_ref[x].astype(F32) + dx + dy + (below + above)

    def apply(x, total):
        before, after = jnp.maximum(x - 1, 0), jnp.minimum(x + 1, CX - 1)
        for y in range(CY):
            v = field[x, y]
            out = diag[x, y : y + 1] * v
            out = out - wx[x, y : y + 1] * field[before, y]
            out = out - wx[x + 1, y : y + 1] * field[after, y]
            if y > 0:
                out = out - wy[x, y : y + 1] * field[x, y - 1]
            if y < CY - 1:
                out = out - wy[x, y + 1 : y + 2] * field[x, y + 1]
            w = wz[x, y : y + 1]
            out = out - w * pltpu.roll(v, NZ - 1, 1)
            out = out - pltpu.roll(w * v, 1, 1)
            local = pad_rows(out, SLOTS).astype(BF16)
            total = total + nt(masked[x, y], local)
        return total

    own = lax.fori_loop(0, CX, apply, jnp.zeros((SLOTS, SLOTS), F32))
    spot, slot = lanes_of((SLOTS, SLOTS)), rows_of((SLOTS, SLOTS))
    own = own + jnp.where((spot == slot) & (slot >= count), 1.0, 0.0)

    found = []
    for k in range(4):
        face_copy(mirror[k]).wait_recv()

        def couple(i, total, k=k):
            if k < 2:
                mine = field[0 if k == 0 else CX - 1, i]
                other = pl.ds(i, 1)
                weight = 0.5 * (edge[k, other] + jnp.where(inside[k], halo[k, other], 0.0))
            else:
                mine = field[i, 0 if k == 2 else CY - 1]
                other = pl.ds(i, 1)
                weight = 0.5 * (edge[k, other] + jnp.where(inside[k], halo[k, other], 0.0))
            hi, lo = split(pad_rows(mine * weight, SLOTS))
            other = face[k, i]
            return total - (nt(hi, other) + nt(lo, other))

        block = lax.fori_loop(0, CX, couple, jnp.zeros((SLOTS, SLOTS), F32))
        found.append(jnp.where(inside[k], block, 0.0))

    blocks = [pad_lanes(b, 128) for b in [own] + found]
    for k in range(5):
        blocks_ref[k] = blocks[k]
    sym = 0.5 * (blocks[0] + transposed(blocks[0])[:SLOTS])
    up = transposed(blocks[2])[:SLOTS]
    lane = lanes_of((SLOTS, 128))
    sym = jnp.where(lane < LIVE, sym, 0.0)
    blocks_ref[5] = sym
    odd = lax.rem(u, 2) == 1
    ahead = blocks[4]
    payload = jnp.where(odd, ahead, sym) + pltpu.roll(jnp.where(odd, sym, ahead), LIVE, 1)
    payload = payload + pltpu.roll(up, 2 * LIVE, 1)
    payload = jnp.where(lane >= 3 * LIVE, count.astype(F32), payload)
    payload_ref[...] = payload[:LIVE]

    for k in range(4):
        halo_copy(k).wait_send()
        face_copy(k).wait_send()


def assemble(count, modes, kappa, react):
    vmem = pl.BlockSpec(memory_space=pltpu.VMEM)
    return pl.pallas_call(
        assemble_kernel,
        out_shape=(
            jax.ShapeDtypeStruct((6, SLOTS, 128), F32),
            jax.ShapeDtypeStruct((LIVE, 128), F32),
        ),
        in_specs=[
            pl.BlockSpec(memory_space=pltpu.SMEM),
            pl.BlockSpec(memory_space=pl.ANY),
            vmem,
            vmem,
        ],
        out_specs=(vmem, vmem),
        scratch_shapes=[
            pltpu.VMEM((CX, LIVE, CY, NZ), BF16),
            pltpu.VMEM((CX, CY, LIVE, NZ), F32),
            pltpu.VMEM((CX, CY, SLOTS, NZ), BF16),
            pltpu.VMEM((CX + 1, CY, NZ), F32),
            pltpu.VMEM((CX, 24, NZ), F32),
            pltpu.VMEM((CX, CY, NZ), F32),
            pltpu.VMEM((CX, CY, NZ), F32),
            pltpu.VMEM((4, 16, NZ), F32),
            pltpu.VMEM((4, 16, NZ), F32),
            pltpu.VMEM((4, 16, SLOTS, NZ), BF16),
            pltpu.SemaphoreType.DMA((CX,)),
            pltpu.SemaphoreType.DMA((4,)),
            pltpu.SemaphoreType.DMA((4,)),
            pltpu.SemaphoreType.DMA((4,)),
            pltpu.SemaphoreType.DMA((4,)),
        ],
        compiler_params=pltpu.CompilerParams(
            collective_id=0, has_side_effects=True, vmem_limit_bytes=50 * 2**20
        ),
        name="assemble",
    )(count, modes, kappa, react)


def spread_kernel(payload_ref, all_ref, slots, send_sem, recv_sem):
    g, u = lax.axis_index("grp"), lax.axis_index("sub")
    source = (g == 0) & (u < NB)
    target = ((g == 0) & (u < NB + 1)) | ((g == 1) & (u < NB))
    barrier = pltpu.get_barrier_semaphore()

    @pl.when(target)
    def _():
        def greet(v, carry):
            @pl.when((g == 1) | (v != u))
            def _():
                pl.semaphore_signal(barrier, inc=1, device_id=(0, v), device_id_type=MESH)
            return carry

        lax.fori_loop(0, NB, greet, 0)

    def copy(to_g, to_u, slot, sem):
        return pltpu.make_async_remote_copy(
            src_ref=payload_ref, dst_ref=slots.at[slot],
            send_sem=send_sem.at[sem], recv_sem=recv_sem.at[slot],
            device_id=(to_g, to_u), device_id_type=MESH,
        )

    @pl.when(source)
    def _():
        pl.semaphore_wait(barrier, 2 * NB)

        def send(v, carry):
            @pl.when(v < NB)
            def _():
                copy(1, v, u, v).start()

            @pl.when(v != u)
            def _():
                copy(0, v, u, NB + v).start()
            return carry

        lax.fori_loop(0, NB + 1, send, 0)

    @pl.when(target)
    def _():
        def receive(v, carry):
            @pl.when((g == 1) | (v != u))
            def _():
                copy(0, v, v, 0).wait_recv()
                all_ref[v] = slots[v]
            return carry

        lax.fori_loop(0, NB, receive, 0)

    @pl.when(source)
    def _():
        all_ref[u] = payload_ref[...]

        def sent(v, carry):
            @pl.when(v < NB)
            def _():
                copy(1, v, u, v).wait_send()

            @pl.when(v != u)
            def _():
                copy(0, v, u, NB + v).wait_send()
            return carry

        lax.fori_loop(0, NB + 1, sent, 0)


def spread(payload):
    vmem = pl.BlockSpec(memory_space=pltpu.VMEM)
    return pl.pallas_call(
        spread_kernel,
        out_shape=jax.ShapeDtypeStruct((NB, LIVE, 128), F32),
        in_specs=[vmem],
        out_specs=vmem,
        scratch_shapes=[
            pltpu.VMEM((NB, LIVE, 128), F32),
            pltpu.SemaphoreType.DMA((2 * NB + 1,)),
            pltpu.SemaphoreType.DMA((NB,)),
        ],
        compiler_params=pltpu.CompilerParams(collective_id=1, has_side_effects=True),
        name="spread",
    )(payload)


def dot3(a, b, dims):
    ah, al = split(a)
    bh, bl = split(b)
    dot = lambda p, q: lax.dot_general(p, q, (dims, ((), ())), preferred_element_type=F32)
    return dot(ah, bh) + (dot(ah, bl) + dot(al, bh))


def nn3(a, b):
    return dot3(a, b, ((1,), (0,)))


def nt3(a, b):
    return dot3(a, b, ((1,), (1,)))


def wide(x):
    return jnp.broadcast_to(x, (8, 128))


def pivots(p, soff, state):
    tiles, saved, invs = (list(part) for part in state)
    sub = rows_of((8, 128))
    count = range(LIVE // 8)
    at = soff + 8 * p
    cols = [[wide(tiles[v][:, at + c : at + c + 1]) for v in count] for c in range(8)]
    for c in range(8):
        here = sub == c
        rinv = lax.rsqrt(wide(cols[c][p][c : c + 1]))
        inv = rinv * rinv
        row = wide(tiles[p][c : c + 1])
        saved[p] = jnp.where(here, row * rinv, saved[p])
        invs[p] = jnp.where(here, inv, invs[p])
        mult = [jnp.where(here, 0.0, cols[c][v]) if v == p else cols[c][v] for v in count]
        for d in range(c + 1, 8):
            coef = wide(cols[c][p][d : d + 1]) * inv
            cols[d] = [cols[d][v] - mult[v] * coef for v in count]
        row = row * inv
        tiles = [tiles[v] - mult[v] * row for v in count]
    return tuple(tiles), tuple(saved), tuple(invs)


def place(out_ref, block, pos, keep):
    base = jnp.minimum((pos // 128) * 128, NC - 256)
    base = pl.multiple_of(base, 128)
    shifted = pltpu.roll(pad_lanes(block, 256), pos - base, 1)
    cols = lanes_of((SLOTS, 256)) + base
    out_ref[:, pl.ds(base, 256)] += jnp.where(keep(cols), shifted, 0.0)


def factor_kernel(all_ref, blocks_ref, out_ref, linv_ref, k_ref, g_ref, f_ref):
    g, u = lax.axis_index("grp"), lax.axis_index("sub")
    s = g * NU + u
    upper = s <= 21
    member = (s == 21) | (s == 22) | ((s >= NU) & (s < NU + NB))
    lane = lanes_of((LIVE, 128))
    row = rows_of((LIVE, 128))
    lane48 = lanes_of((SLOTS, 128))
    row48 = rows_of((SLOTS, 128))
    out_ref[...] = jnp.zeros_like(out_ref)
    before = lambda cols: cols < DONE
    after = lambda cols: cols >= DONE

    def left(x, by):
        x = pltpu.roll(x, 128 - by, 1) if by else x
        return jnp.where(lanes_of(x.shape) < LIVE, x, 0.0)

    def own_row(q):
        mine = jnp.where(q == s, blocks_ref[5], 0.0)
        mine = jnp.where(q == s - 1, blocks_ref[3], mine)
        mine = jnp.where(q == s - NU, blocks_ref[1], mine)
        mine = jnp.where(lane48 < jnp.where(q == NB - 1, 16, LIVE), mine, 0.0)
        carried = nn3(f_ref[...], pad_rows(k_ref[q], 128))
        carried = jnp.where(lane48 < jnp.where(q == NB - 1, 16, LIVE), carried, 0.0)
        f = jnp.where(q <= s, mine - carried, 0.0)
        f_ref[...] = f
        linv = pad_rows(linv_ref[q], 128)
        x = nt3(f, linv)
        x = jnp.where((q == s) & (lane48 > row48), 0.0, x)
        place(out_ref, x, SLOTS * q, before)
        g_ref[q] = nn3(x, linv)

    def step(t, odd, scur, n):
        soff, uoff = (LIVE, 0) if odd else (0, LIVE)
        given = all_ref[t]
        limit = jnp.where(t == NB - 1, 16, LIVE)
        in_s = (lane >= soff) & (lane < soff + LIVE)
        eye = jnp.where(lane == row + soff, 1.0, 0.0)
        a = jnp.where((row < limit) & (lane < soff + limit), scur, eye)
        rest = jnp.where(lane < 2 * LIVE, jnp.where(row < limit, given, 0.0),
                         jnp.where(lane == row + 2 * LIVE, 1.0, 0.0))
        a = jnp.where(in_s, a, rest)
        ut = transposed(given)[uoff : uoff + LIVE]
        tiles = tuple(a[8 * v : 8 * v + 8] for v in range(LIVE // 8))
        ones = tuple(jnp.ones((8, 128), F32) for _ in tiles)
        state = pivots(0, soff, (tiles, tiles, ones))

        @pl.when(t > 0)
        def _():
            own_row(t - 1)

        coming = all_ref[jnp.minimum(t + 1, NB - 1)]
        coming_n = jnp.max(jnp.where(lanes_of((8, 128)) >= 3 * LIVE, coming[0:8], 0.0))
        n = jnp.where(t == NB - 1, jnp.minimum(n, 16.0), n)
        for p in range(1, LIVE // 8):
            state = lax.cond(
                n > 8.0 * p, lambda st, p=p: pivots(p, soff, st), lambda st: st, state
            )
        tiles, saved, invs = state
        k = jnp.concatenate([tiles[v] * invs[v] for v in range(LIVE // 8)], 0)
        snext = coming - nn3(ut, pad_rows(k, 128))
        linv_ref[t] = left(jnp.concatenate(saved, 0), 2 * LIVE)
        k_ref[t + 1] = left(k, uoff)
        return snext, coming_n

    @pl.when(upper | member)
    def _():
        k_ref[0] = jnp.zeros((LIVE, 128), F32)
        f_ref[...] = jnp.zeros((SLOTS, 128), F32)
        first = all_ref[0]
        n = jnp.max(jnp.where(lanes_of((8, 128)) >= 3 * LIVE, first[0:8], 0.0))

        def pair(i, carry):
            carry = step(2 * i, False, *carry)
            return step(2 * i + 1, True, *carry)

        lax.fori_loop(0, NB // 2, pair, (first, n))
        own_row(NB - 1)

    @pl.when(upper)
    def _():
        dead = jnp.where((row48 == lane48) & (row48 >= LIVE), 1.0, 0.0)
        place(out_ref, dead, SLOTS * s, before)

    @pl.when(member)
    def _():
        def schur(y, t):
            rising = pad_rows(left(all_ref[t], 2 * LIVE), 128)
            place(out_ref, -nt3(y, rising), SLOTS * (t + NU), after)

        late = lane >= 16
        y = g_ref[NB - 1]
        schur(y, NB - 1)
        last = jnp.where(row < 16, all_ref[NB - 1], 0.0)
        place(out_ref, -nn3(y, pad_rows(left(last, 0), 128)), SLOTS * NB, after)
        own = jnp.where(late, left(last, LIVE), 0.0)
        place(out_ref, -nn3(y, pad_rows(own, 128)), SLOTS * (NB - 1), after)
        y = g_ref[NB - 2] - nt3(y, pad_rows(k_ref[NB - 1], 128))
        schur(y, NB - 2)
        over = jnp.where(late, left(all_ref[NB - 2], LIVE), 0.0)
        place(out_ref, -nn3(y, pad_rows(over, 128)), SLOTS * (NB - 1), after)

        def back(i, y):
            t = NB - 3 - i
            y = g_ref[t] - nt3(y, pad_rows(k_ref[t + 1], 128))
            schur(y, t)
            return y

        lax.fori_loop(0, NB - 2, back, y)

    @pl.when(s >= 21)
    def _():
        targets = [s, s - NU, s + NU, s - 1, s + 1]
        valid = [True, g > 0, g < NG - 1, u > 0, u < NU - 1]
        for k in range(5):
            pos = SLOTS * jnp.clip(targets[k], 0, NG * NU - 1)
            place(out_ref, jnp.where(valid[k], blocks_ref[k], 0.0), pos, after)

    @pl.when(s == 21)
    def _():
        out_ref[0:16, DONE:] = jnp.zeros((16, NC - DONE), F32)


def factor(everyone, blocks):
    vmem = pl.BlockSpec(memory_space=pltpu.VMEM)
    return pl.pallas_call(
        factor_kernel,
        out_shape=jax.ShapeDtypeStruct((SLOTS, NC), F32),
        in_specs=[vmem, vmem],
        out_specs=vmem,
        scratch_shapes=[
            pltpu.VMEM((NB, LIVE, 128), F32),
            pltpu.VMEM((NB + 1, LIVE, 128), F32),
            pltpu.VMEM((NB, SLOTS, 128), F32),
            pltpu.VMEM((SLOTS, 128), F32),
        ],
        compiler_params=pltpu.CompilerParams(vmem_limit_bytes=40 * 2**20),
        name="factor",
    )(everyone, blocks)


def per_device(modes, counts, kappa, react):
    blocks, payload = assemble(counts, modes, kappa, react)
    everyone = spread(payload)
    return factor(everyone, blocks)


def solution(mesh):
    in_specs = (
        P(None, "grp", "sub", None),
        P(("grp", "sub")),
        P("grp", "sub", None),
        P("grp", "sub", None),
    )
    out_specs = P(("grp", "sub"), None)
    return jax.shard_map(
        per_device, mesh=mesh, in_specs=in_specs, out_specs=out_specs, check_vma=False
    )
```

```python
import jax
import jax.numpy as jnp
from jax import lax
from jax.experimental import pallas as pl
from jax.experimental.pallas import tpu as pltpu
from jax.sharding import PartitionSpec as P

F32 = jnp.float32
BF16 = jnp.bfloat16
MESH = pl.DeviceIdType.MESH
NG, NU = 4, 32
CX, CY, NZ = 16, 16, 256
SLOTS, LIVE = 48, 40
NB = 22
DONE = 1024
NC = SLOTS * NG * NU


def nt(a, b, precision=None):
    return lax.dot_general(
        a, b, (((1,), (1,)), ((), ())), preferred_element_type=F32, precision=precision
    )


def lanes_of(shape):
    return lax.broadcasted_iota(jnp.int32, shape, len(shape) - 1)


def rows_of(shape):
    return lax.broadcasted_iota(jnp.int32, shape, len(shape) - 2)


def split(x):
    hi = x.astype(BF16)
    return hi, (x - hi.astype(F32)).astype(BF16)


def pad_rows(x, rows):
    return jnp.concatenate([x, jnp.zeros((rows - x.shape[0], x.shape[1]), x.dtype)], 0)


def pad_lanes(x, lanes):
    return jnp.concatenate([x, jnp.zeros((x.shape[0], lanes - x.shape[1]), x.dtype)], 1)


def transposed(x):
    return jnp.transpose(pad_rows(x, 128))


def assemble_kernel(
    count_ref, modes_ref, kappa_ref, react_ref, blocks_ref, all_ref,
    raw, kappa, react, field, masked, wx, wy, wz, diag, edge, halo, face_x, face_y,
    local0, local1, gram, side, slots,
    raw_sem, cell_sem, halo_send, halo_recv, face_send, face_recv,
    y_sem, x_send, x_recv, z_send, z_recv, core_send, core_recv,
):
    g, u = lax.axis_index("grp"), lax.axis_index("sub")
    partners = [
        (lax.rem(g + NG - 1, NG), u),
        (lax.rem(g + 1, NG), u),
        (g, lax.rem(u + NU - 1, NU)),
        (g, lax.rem(u + 1, NU)),
    ]
    inside = [g > 0, g < NG - 1, u > 0, u < NU - 1]
    mirror = [1, 0, 3, 2]
    px, pz, pc = u // 8, lax.rem(u // 2, 4), lax.rem(u, 2)
    joined = (g < 2) & (u < 24)

    def at(x, z, c):
        return (g, x * 8 + z * 2 + c)

    x_partner = [lax.rem(px + i, 3) for i in (1, 2)]
    z_partner = [lax.rem(pz + i, 4) for i in (1, 2, 3)]

    def fetch(x):
        return pltpu.make_async_copy(
            modes_ref.at[pl.ds(0, LIVE), x], raw.at[x], raw_sem.at[x]
        )

    cells = [
        pltpu.make_async_copy(kappa_ref, kappa, cell_sem.at[0]),
        pltpu.make_async_copy(react_ref, react, cell_sem.at[1]),
    ]
    cells[0].start()
    for x in range(CX):
        fetch(x).start()
    cells[1].start()

    barrier = pltpu.get_barrier_semaphore()

    def greet(device):
        pl.semaphore_signal(barrier, inc=1, device_id=device, device_id_type=MESH)

    for partner in partners:
        greet(partner)

    @pl.when(joined)
    def _():
        for x in x_partner:
            greet(at(x, pz, pc))
        for z in z_partner:
            greet(at(px, z, pc))
        greet(at(px, pz, 1 - pc))

    count = count_ref[0]
    cells[0].wait()
    kap = kappa[...].astype(F32)
    edge[0] = kap[0]
    edge[1] = kap[CX - 1]
    for x in range(CX):
        edge[2, x : x + 1] = kap[x, 0:1]
        edge[3, x : x + 1] = kap[x, CY - 1 : CY]
    pl.semaphore_wait(barrier, jnp.where(joined, 10, 4))

    def halo_copy(k):
        return pltpu.make_async_remote_copy(
            src_ref=edge.at[k], dst_ref=halo.at[mirror[k]],
            send_sem=halo_send.at[k], recv_sem=halo_recv.at[mirror[k]],
            device_id=partners[k], device_id_type=MESH,
        )

    for k in range(4):
        halo_copy(k).start()

    live = rows_of((CY, LIVE, NZ)) < count

    def turn(x, carry):
        fetch(x).wait()
        plane = jnp.swapaxes(raw[x].astype(F32), 0, 1)
        plane = jnp.where(live, plane, 0.0)
        field[x] = plane
        for y in range(CY):
            r, c = SLOTS * (y % 4), NZ * (y // 4)
            masked[x, r : r + SLOTS, c : c + NZ] = pad_rows(plane[y], SLOTS).astype(BF16)
        return carry

    lax.fori_loop(0, CX, turn, 0)

    sources = [
        masked.at[0],
        masked.at[CX - 1],
        masked.at[:, pl.ds(0, SLOTS), pl.ds(0, NZ)],
        masked.at[:, pl.ds(3 * SLOTS, SLOTS), pl.ds(3 * NZ, NZ)],
    ]
    landings = [face_x.at[0], face_x.at[1], face_y.at[0], face_y.at[1]]

    def face_copy(k):
        return pltpu.make_async_remote_copy(
            src_ref=sources[k], dst_ref=landings[mirror[k]],
            send_sem=face_send.at[k], recv_sem=face_recv.at[mirror[k]],
            device_id=partners[k], device_id_type=MESH,
        )

    for k in range(4):
        face_copy(k).start()

    plane0 = jnp.zeros((CY, NZ), F32)
    row0 = jnp.zeros((1, NZ), F32)
    last = lanes_of((CY, NZ)) == NZ - 1
    first = lanes_of((CY, NZ)) == 0
    wx[0] = plane0
    wx[CX] = plane0
    for x in range(CX - 1):
        wx[x + 1] = 0.5 * (kap[x] + kap[x + 1])
    for x in range(CX):
        k = kap[x]
        wy[x, 0:1] = row0
        wy[x, 1:CY] = 0.5 * (k[: CY - 1] + k[1:])
        wy[x, CY : CY + 1] = row0
        wz[x] = jnp.where(last, 0.0, 0.5 * (k + pltpu.roll(k, NZ - 1, 1)))
    cells[1].wait()
    for k in range(4):
        halo_copy(k).wait_recv()
    ext = [jnp.where(inside[k], halo[k], 0.0) for k in range(4)]
    bound = [0.5 * (edge[k] + ext[k]) for k in range(4)]
    for x in range(CX):
        k = kap[x]
        w = wz[x]
        below = jnp.where(first, 0.5 * k, pltpu.roll(w, 1, 1))
        above = jnp.where(last, 0.5 * k, w)
        dx = (bound[0] if x == 0 else wx[x]) + (bound[1] if x == CX - 1 else wx[x + 1])
        dy = wy[x, 0:CY] + wy[x, 1 : CY + 1]
        dy = dy + jnp.concatenate(
            [bound[2][x : x + 1], jnp.zeros((CY - 2, NZ), F32), bound[3][x : x + 1]], 0
        )
        diag[x] = react[x].astype(F32) + dx + dy + (below + above)

    def apply(x, local):
        before, after = jnp.maximum(x - 1, 0), jnp.minimum(x + 1, CX - 1)
        for y in range(CY):
            v = field[x, y]
            out = diag[x, y : y + 1] * v
            out = out - wx[x, y : y + 1] * field[before, y]
            out = out - wx[x + 1, y : y + 1] * field[after, y]
            if y > 0:
                out = out - wy[x, y : y + 1] * field[x, y - 1]
            if y < CY - 1:
                out = out - wy[x, y + 1 : y + 2] * field[x, y + 1]
            w = wz[x, y : y + 1]
            out = out - w * pltpu.roll(v, NZ - 1, 1)
            out = out - pltpu.roll(w * v, 1, 1)
            r, c = SLOTS * (y % 4), NZ * (y // 4)
            local[r : r + SLOTS, c : c + NZ] = pad_rows(out, SLOTS).astype(BF16)

    def collect(total):
        total_lanes = lanes_of((SLOTS, 128))
        out = jnp.zeros((SLOTS, 128), F32)
        for i in range(4):
            part = total[SLOTS * i : SLOTS * (i + 1), :]
            part = pltpu.roll(part, 256 - SLOTS * i, 1) if i else part
            out = out + part[:, :128]
        return jnp.where(total_lanes < SLOTS, out, 0.0)

    gram[...] = jnp.zeros_like(gram)
    local1[...] = jnp.zeros_like(local1)

    def pair(i, carry):
        x = 2 * i
        gram[:, 0:192] += nt(masked[jnp.maximum(x - 1, 0)], local1[...])
        apply(x, local0)
        gram[:, 0:192] += nt(masked[x], local0[...])
        apply(x + 1, local1)
        return carry

    lax.fori_loop(0, CX // 2, pair, 0)
    gram[:, 0:192] += nt(masked[CX - 1], local1[...])
    own = collect(gram)
    spot, slot = lanes_of((SLOTS, 128)), rows_of((SLOTS, 128))
    own = own + jnp.where((spot == slot) & (slot >= count), 1.0, 0.0)

    found = []
    for k in range(4):
        weight = bound[k]
        for i in range(16):
            mine = field[0 if k == 0 else CX - 1, i] if k < 2 else field[i, 0 if k == 2 else CY - 1]
            hi, lo = split(pad_rows(mine * weight[i : i + 1], SLOTS))
            r, c = SLOTS * (i % 4), NZ * (i // 4)
            local0[r : r + SLOTS, c : c + NZ] = hi
            local1[r : r + SLOTS, c : c + NZ] = lo
        face_copy(mirror[k]).wait_recv()
        if k < 2:
            other = face_x[k]
            total = nt(local0[...], other) + nt(local1[...], other)
        else:
            total = jnp.zeros((192, 192), F32)
            for q in range(4):
                other = face_y[k - 2, 4 * q : 4 * q + 4].reshape(192, NZ)
                cols = slice(NZ * q, NZ * (q + 1))
                total = total + nt(local0[:, cols], other) + nt(local1[:, cols], other)
        side[:, 0:192] = -total
        found.append(jnp.where(inside[k], collect(side), 0.0))

    blocks = [own] + found
    for k in range(5):
        blocks_ref[k] = blocks[k]
    sym = 0.5 * (blocks[0] + transposed(blocks[0])[:SLOTS])
    up = transposed(blocks[2])[:SLOTS]
    lane = lanes_of((SLOTS, 128))
    sym = jnp.where(lane < LIVE, sym, 0.0)
    blocks_ref[5] = sym
    ahead = blocks[4]
    odd = pc == 1
    payload = jnp.where(odd, ahead, sym) + pltpu.roll(jnp.where(odd, sym, ahead), LIVE, 1)
    payload = payload + pltpu.roll(up, 2 * LIVE, 1)
    payload = jnp.where(lane >= 3 * LIVE, count.astype(F32), payload)

    def y_copy():
        return pltpu.make_async_remote_copy(
            src_ref=slots.at[px, pz, pc], dst_ref=slots.at[px, pz, pc],
            send_sem=y_sem.at[0], recv_sem=y_sem.at[1],
            device_id=(1, u), device_id_type=MESH,
        )

    def x_copy(i, x):
        return pltpu.make_async_remote_copy(
            src_ref=slots.at[px, pz, pc], dst_ref=slots.at[px, pz, pc],
            send_sem=x_send.at[i], recv_sem=x_recv.at[px],
            device_id=at(x, pz, pc), device_id_type=MESH,
        )

    def x_land(x):
        return pltpu.make_async_remote_copy(
            src_ref=slots.at[x, pz, pc], dst_ref=slots.at[x, pz, pc],
            send_sem=x_send.at[0], recv_sem=x_recv.at[x],
            device_id=at(x, pz, pc), device_id_type=MESH,
        )

    def z_copy(i, z):
        return pltpu.make_async_remote_copy(
            src_ref=slots.at[:, pz, pc], dst_ref=slots.at[:, pz, pc],
            send_sem=z_send.at[i], recv_sem=z_recv.at[pz],
            device_id=at(px, z, pc), device_id_type=MESH,
        )

    def z_land(z):
        return pltpu.make_async_remote_copy(
            src_ref=slots.at[:, z, pc], dst_ref=slots.at[:, z, pc],
            send_sem=z_send.at[0], recv_sem=z_recv.at[z],
            device_id=at(px, z, pc), device_id_type=MESH,
        )

    def core_copy(z):
        return pltpu.make_async_remote_copy(
            src_ref=slots.at[:, z, pc], dst_ref=slots.at[:, z, pc],
            send_sem=core_send.at[z], recv_sem=core_recv.at[z],
            device_id=at(px, pz, 1 - pc), device_id_type=MESH,
        )

    def core_land(z):
        return pltpu.make_async_remote_copy(
            src_ref=slots.at[:, z, 1 - pc], dst_ref=slots.at[:, z, 1 - pc],
            send_sem=core_send.at[z], recv_sem=core_recv.at[z],
            device_id=at(px, pz, 1 - pc), device_id_type=MESH,
        )

    @pl.when(joined)
    def _():
        @pl.when(g == 0)
        def _():
            slots[px, pz, pc] = payload[:LIVE]
            y_copy().start()

        @pl.when(g == 1)
        def _():
            y_copy().wait_recv()

        for i, x in enumerate(x_partner):
            x_copy(i, x).start()
        for x in x_partner:
            x_land(x).wait_recv()
        for i, z in enumerate(z_partner):
            z_copy(i, z).start()
        core_copy(pz).start()
        for z in z_partner:
            z_land(z).wait_recv()
            core_copy(z).start()
        for z in [pz] + z_partner:
            core_land(z).wait_recv()
        for x in range(3):
            for z in range(4):
                for c in range(2):
                    all_ref[x * 8 + z * 2 + c] = slots[x, z, c]

        @pl.when(g == 0)
        def _():
            y_copy().wait_send()

        for i, x in enumerate(x_partner):
            x_copy(i, x).wait_send()
        for i, z in enumerate(z_partner):
            z_copy(i, z).wait_send()
        for z in [pz] + z_partner:
            core_copy(z).wait_send()

    for k in range(4):
        halo_copy(k).wait_send()
        face_copy(k).wait_send()


def assemble(count, modes, kappa, react):
    vmem = pl.BlockSpec(memory_space=pltpu.VMEM)
    hbm = pl.BlockSpec(memory_space=pltpu.HBM)
    dma = pltpu.SemaphoreType.DMA
    return pl.pallas_call(
        assemble_kernel,
        out_shape=(
            jax.ShapeDtypeStruct((6, SLOTS, 128), F32),
            jax.ShapeDtypeStruct((24, LIVE, 128), F32),
        ),
        in_specs=[pl.BlockSpec(memory_space=pltpu.SMEM), hbm, hbm, hbm],
        out_specs=(vmem, vmem),
        scratch_shapes=[
            pltpu.VMEM((CX, LIVE, CY, NZ), BF16),
            pltpu.VMEM((CX, CY, NZ), BF16),
            pltpu.VMEM((CX, CY, NZ), BF16),
            pltpu.VMEM((CX, CY, LIVE, NZ), F32),
            pltpu.VMEM((CX, 4 * SLOTS, 4 * NZ), BF16),
            pltpu.VMEM((CX + 1, CY, NZ), F32),
            pltpu.VMEM((CX, 24, NZ), F32),
            pltpu.VMEM((CX, CY, NZ), F32),
            pltpu.VMEM((CX, CY, NZ), F32),
            pltpu.VMEM((4, 16, NZ), F32),
            pltpu.VMEM((4, 16, NZ), F32),
            pltpu.VMEM((2, 4 * SLOTS, 4 * NZ), BF16),
            pltpu.VMEM((2, 16, SLOTS, NZ), BF16),
            pltpu.VMEM((4 * SLOTS, 4 * NZ), BF16),
            pltpu.VMEM((4 * SLOTS, 4 * NZ), BF16),
            pltpu.VMEM((4 * SLOTS, 256), F32),
            pltpu.VMEM((4 * SLOTS, 256), F32),
            pltpu.VMEM((3, 4, 2, LIVE, 128), F32),
            dma((CX,)),
            dma((2,)),
            dma((4,)),
            dma((4,)),
            dma((4,)),
            dma((4,)),
            dma((2,)),
            dma((2,)),
            dma((3,)),
            dma((3,)),
            dma((4,)),
            dma((4,)),
            dma((4,)),
        ],
        compiler_params=pltpu.CompilerParams(
            collective_id=0, has_side_effects=True, vmem_limit_bytes=50 * 2**20
        ),
        name="assemble",
    )(count, modes, kappa, react)


def dot3(a, b, dims):
    ah, al = split(a)
    bh, bl = split(b)
    dot = lambda p, q: lax.dot_general(p, q, (dims, ((), ())), preferred_element_type=F32)
    return dot(ah, bh) + (dot(ah, bl) + dot(al, bh))


def nn3(a, b):
    return dot3(a, b, ((1,), (0,)))


def nt3(a, b):
    return dot3(a, b, ((1,), (1,)))


def wide(x):
    return jnp.broadcast_to(x, (8, 128))


def pivots(p, soff, state):
    tiles, saved, invs = (list(part) for part in state)
    sub = rows_of((8, 128))
    count = range(LIVE // 8)
    at = soff + 8 * p
    cols = [[wide(tiles[v][:, at + c : at + c + 1]) for v in count] for c in range(8)]
    for c in range(8):
        here = sub == c
        rinv = lax.rsqrt(wide(cols[c][p][c : c + 1]))
        inv = rinv * rinv
        row = wide(tiles[p][c : c + 1])
        saved[p] = jnp.where(here, row * rinv, saved[p])
        invs[p] = jnp.where(here, inv, invs[p])
        mult = [jnp.where(here, 0.0, cols[c][v]) if v == p else cols[c][v] for v in count]
        for d in range(c + 1, 8):
            coef = wide(cols[c][p][d : d + 1]) * inv
            cols[d] = [cols[d][v] - mult[v] * coef for v in count]
        row = row * inv
        tiles = [tiles[v] - mult[v] * row for v in count]
    return tuple(tiles), tuple(saved), tuple(invs)


def place(out_ref, block, pos, keep):
    base = jnp.minimum((pos // 128) * 128, NC - 256)
    base = pl.multiple_of(base, 128)
    shifted = pltpu.roll(pad_lanes(block, 256), pos - base, 1)
    cols = lanes_of((SLOTS, 256)) + base
    out_ref[:, pl.ds(base, 256)] += jnp.where(keep(cols), shifted, 0.0)


def factor_kernel(all_ref, blocks_ref, out_ref, linv_ref, k_ref, g_ref, f_ref, x_ref):
    g, u = lax.axis_index("grp"), lax.axis_index("sub")
    s = g * NU + u
    upper = s <= 21
    member = (s == 21) | (s == 22) | ((s >= NU) & (s < NU + NB))
    lane = lanes_of((LIVE, 128))
    row = rows_of((LIVE, 128))
    lane48 = lanes_of((SLOTS, 128))
    row48 = rows_of((SLOTS, 128))
    out_ref[...] = jnp.zeros_like(out_ref)
    before = lambda cols: cols < DONE
    after = lambda cols: cols >= DONE

    def left(x, by):
        x = pltpu.roll(x, 128 - by, 1) if by else x
        return jnp.where(lanes_of(x.shape) < LIVE, x, 0.0)

    def reduce_row(q):
        at, wide_enough = jnp.maximum(q, 0), jnp.where(q == NB - 1, 16, LIVE)
        mine = jnp.where(q == s, blocks_ref[5], 0.0)
        mine = jnp.where(q == s - 1, blocks_ref[3], mine)
        mine = jnp.where(q == s - NU, blocks_ref[1], mine)
        held = jnp.where(q > 0, f_ref[jnp.maximum(q - 1, 0)], 0.0)
        f = mine - nn3(held, pad_rows(k_ref[at], 128))
        f_ref[at] = jnp.where((q <= s) & (lane48 < wide_enough), f, 0.0)

    def solve_row(q):
        at = jnp.maximum(q, 0)
        x = nt3(f_ref[at], pad_rows(linv_ref[at], 128))
        x_ref[at] = jnp.where((q == s) & (lane48 > row48), 0.0, x)

    def store_row(q):
        at = jnp.maximum(q, 0)
        x = jnp.where(q >= 0, x_ref[at], 0.0)
        place(out_ref, x, SLOTS * at, before)
        g_ref[at] = nn3(x, pad_rows(linv_ref[at], 128))

    def step(t, odd, scur, n):
        soff, uoff = (LIVE, 0) if odd else (0, LIVE)
        given = all_ref[t]
        limit = jnp.where(t == NB - 1, 16, LIVE)
        in_s = (lane >= soff) & (lane < soff + LIVE)
        eye = jnp.where(lane == row + soff, 1.0, 0.0)
        a = jnp.where((row < limit) & (lane < soff + limit), scur, eye)
        rest = jnp.where(lane < 2 * LIVE, jnp.where(row < limit, given, 0.0),
                         jnp.where(lane == row + 2 * LIVE, 1.0, 0.0))
        a = jnp.where(in_s, a, rest)
        ut = transposed(given)[uoff : uoff + LIVE]
        tiles = tuple(a[8 * v : 8 * v + 8] for v in range(LIVE // 8))
        ones = tuple(jnp.ones((8, 128), F32) for _ in tiles)
        state = pivots(0, soff, (tiles, tiles, ones))

        store_row(t - 3)
        solve_row(t - 2)
        reduce_row(t - 1)
        coming = all_ref[jnp.minimum(t + 1, NB - 1)]
        coming_n = jnp.max(jnp.where(lanes_of((8, 128)) >= 3 * LIVE, coming[0:8], 0.0))
        n = jnp.where(t == NB - 1, jnp.minimum(n, 16.0), n)
        for p in range(1, LIVE // 8):
            state = lax.cond(
                n > 8.0 * p, lambda st, p=p: pivots(p, soff, st), lambda st: st, state
            )
        tiles, saved, invs = state
        k = jnp.concatenate([tiles[v] * invs[v] for v in range(LIVE // 8)], 0)
        snext = coming - nn3(ut, pad_rows(k, 128))
        linv_ref[t] = left(jnp.concatenate(saved, 0), 2 * LIVE)
        k_ref[t + 1] = left(k, uoff)
        return snext, coming_n

    @pl.when(upper | member)
    def _():
        k_ref[0] = jnp.zeros((LIVE, 128), F32)
        linv_ref[0] = jnp.zeros((LIVE, 128), F32)
        f_ref[0] = jnp.zeros((SLOTS, 128), F32)
        x_ref[0] = jnp.zeros((SLOTS, 128), F32)
        first = all_ref[0]
        n = jnp.max(jnp.where(lanes_of((8, 128)) >= 3 * LIVE, first[0:8], 0.0))

        def pair(i, carry):
            carry = step(2 * i, False, *carry)
            return step(2 * i + 1, True, *carry)

        lax.fori_loop(0, NB // 2, pair, (first, n))
        store_row(NB - 3)
        solve_row(NB - 2)
        reduce_row(NB - 1)
        store_row(NB - 2)
        solve_row(NB - 1)
        store_row(NB - 1)

    @pl.when(upper)
    def _():
        dead = jnp.where((row48 == lane48) & (row48 >= LIVE), 1.0, 0.0)
        place(out_ref, dead, SLOTS * s, before)

    @pl.when(member)
    def _():
        def schur(y, t):
            rising = pad_rows(left(all_ref[t], 2 * LIVE), 128)
            place(out_ref, -nt3(y, rising), SLOTS * (t + NU), after)

        late = lane >= 16
        y = g_ref[NB - 1]
        schur(y, NB - 1)
        last = jnp.where(row < 16, all_ref[NB - 1], 0.0)
        place(out_ref, -nn3(y, pad_rows(left(last, 0), 128)), SLOTS * NB, after)
        own = jnp.where(late, left(last, LIVE), 0.0)
        place(out_ref, -nn3(y, pad_rows(own, 128)), SLOTS * (NB - 1), after)
        y = g_ref[NB - 2] - nt3(y, pad_rows(k_ref[NB - 1], 128))
        over = jnp.where(late, left(all_ref[NB - 2], LIVE), 0.0)
        place(out_ref, -nn3(y, pad_rows(over, 128)), SLOTS * (NB - 1), after)

        def back(i, y):
            t = NB - 3 - i
            schur(y, t + 1)
            return g_ref[t] - nt3(y, pad_rows(k_ref[t + 1], 128))

        schur(lax.fori_loop(0, NB - 2, back, y), 0)

    @pl.when(s >= 21)
    def _():
        targets = [s, s - NU, s + NU, s - 1, s + 1]
        valid = [True, g > 0, g < NG - 1, u > 0, u < NU - 1]
        for k in range(5):
            pos = SLOTS * jnp.clip(targets[k], 0, NG * NU - 1)
            place(out_ref, jnp.where(valid[k], blocks_ref[k], 0.0), pos, after)

    @pl.when(s == 21)
    def _():
        out_ref[0:16, DONE:] = jnp.zeros((16, NC - DONE), F32)


def factor(everyone, blocks):
    vmem = pl.BlockSpec(memory_space=pltpu.VMEM)
    return pl.pallas_call(
        factor_kernel,
        out_shape=jax.ShapeDtypeStruct((SLOTS, NC), F32),
        in_specs=[vmem, vmem],
        out_specs=vmem,
        scratch_shapes=[
            pltpu.VMEM((NB, LIVE, 128), F32),
            pltpu.VMEM((NB + 1, LIVE, 128), F32),
            pltpu.VMEM((NB, SLOTS, 128), F32),
            pltpu.VMEM((NB, SLOTS, 128), F32),
            pltpu.VMEM((NB, SLOTS, 128), F32),
        ],
        compiler_params=pltpu.CompilerParams(vmem_limit_bytes=40 * 2**20),
        name="factor",
    )(everyone, blocks)


def per_device(modes, counts, kappa, react):
    blocks, everyone = assemble(counts, modes, kappa, react)
    return factor(everyone, blocks)


def solution(mesh):
    in_specs = (
        P(None, "grp", "sub", None),
        P(("grp", "sub")),
        P("grp", "sub", None),
        P("grp", "sub", None),
    )
    out_specs = P(("grp", "sub"), None)
    return jax.shard_map(
        per_device, mesh=mesh, in_specs=in_specs, out_specs=out_specs, check_vma=False
    )
```

```python
import jax
import jax.numpy as jnp
from jax import lax
from jax.experimental import pallas as pl
from jax.experimental.pallas import tpu as pltpu
from jax.sharding import PartitionSpec as P

F32 = jnp.float32
BF16 = jnp.bfloat16
MESH = pl.DeviceIdType.MESH
NG, NU = 4, 32
CX, CY, NZ = 16, 16, 256
SLOTS, LIVE = 48, 40
NB = 22
DONE = 1024
NC = SLOTS * NG * NU


def nt(a, b, precision=None):
    return lax.dot_general(
        a, b, (((1,), (1,)), ((), ())), preferred_element_type=F32, precision=precision
    )


def lanes_of(shape):
    return lax.broadcasted_iota(jnp.int32, shape, len(shape) - 1)


def rows_of(shape):
    return lax.broadcasted_iota(jnp.int32, shape, len(shape) - 2)


def split(x):
    hi = x.astype(BF16)
    return hi, (x - hi.astype(F32)).astype(BF16)


def pad_rows(x, rows):
    return jnp.concatenate([x, jnp.zeros((rows - x.shape[0], x.shape[1]), x.dtype)], 0)


def pad_lanes(x, lanes):
    return jnp.concatenate([x, jnp.zeros((x.shape[0], lanes - x.shape[1]), x.dtype)], 1)


def transposed(x):
    return jnp.transpose(pad_rows(x, 128))


def assemble_kernel(
    count_ref, modes_ref, kappa_ref, react_ref, blocks_ref, all_ref,
    raw, kappa, react, field, masked, wx, wy, wz, diag, edge, halo, face_x, face_y,
    local0, local1, gram, side, slots,
    raw_sem, cell_sem, halo_send, halo_recv, face_send, face_recv,
    y_sem, x_send, x_recv, z_send, z_recv, core_send, core_recv,
):
    g, u = lax.axis_index("grp"), lax.axis_index("sub")
    partners = [
        (lax.rem(g + NG - 1, NG), u),
        (lax.rem(g + 1, NG), u),
        (g, lax.rem(u + NU - 1, NU)),
        (g, lax.rem(u + 1, NU)),
    ]
    inside = [g > 0, g < NG - 1, u > 0, u < NU - 1]
    mirror = [1, 0, 3, 2]
    px, pz, pc = u // 8, lax.rem(u // 2, 4), lax.rem(u, 2)
    joined = (g < 2) & (u < 24)

    def at(x, z, c):
        return (g, x * 8 + z * 2 + c)

    x_partner = [lax.rem(px + i, 3) for i in (1, 2)]
    z_partner = [lax.rem(pz + i, 4) for i in (1, 2, 3)]

    def fetch(x):
        return pltpu.make_async_copy(
            modes_ref.at[pl.ds(0, LIVE), x], raw.at[x], raw_sem.at[x]
        )

    cells = [
        pltpu.make_async_copy(kappa_ref, kappa, cell_sem.at[0]),
        pltpu.make_async_copy(react_ref, react, cell_sem.at[1]),
    ]
    cells[0].start()
    for x in range(CX):
        fetch(x).start()
    cells[1].start()

    barrier = pltpu.get_barrier_semaphore()

    def greet(device):
        pl.semaphore_signal(barrier, inc=1, device_id=device, device_id_type=MESH)

    for partner in partners:
        greet(partner)

    @pl.when(joined)
    def _():
        for x in x_partner:
            greet(at(x, pz, pc))
        for z in z_partner:
            greet(at(px, z, pc))
        greet(at(px, pz, 1 - pc))

    count = count_ref[0]
    cells[0].wait()
    kap = kappa[...].astype(F32)
    edge[0] = kap[0]
    edge[1] = kap[CX - 1]
    for x in range(CX):
        edge[2, x : x + 1] = kap[x, 0:1]
        edge[3, x : x + 1] = kap[x, CY - 1 : CY]
    pl.semaphore_wait(barrier, jnp.where(joined, 10, 4))

    def halo_copy(k):
        return pltpu.make_async_remote_copy(
            src_ref=edge.at[k], dst_ref=halo.at[mirror[k]],
            send_sem=halo_send.at[k], recv_sem=halo_recv.at[mirror[k]],
            device_id=partners[k], device_id_type=MESH,
        )

    for k in range(4):
        halo_copy(k).start()

    live = rows_of((CY, LIVE, NZ)) < count

    def turn(x, carry):
        fetch(x).wait()
        plane = jnp.swapaxes(raw[x].astype(F32), 0, 1)
        plane = jnp.where(live, plane, 0.0)
        field[x] = plane
        for y in range(CY):
            r, c = SLOTS * (y % 4), NZ * (y // 4)
            masked[x, r : r + SLOTS, c : c + NZ] = pad_rows(plane[y], SLOTS).astype(BF16)
        return carry

    lax.fori_loop(0, CX, turn, 0)

    sources = [
        masked.at[0],
        masked.at[CX - 1],
        masked.at[:, pl.ds(0, SLOTS), pl.ds(0, NZ)],
        masked.at[:, pl.ds(3 * SLOTS, SLOTS), pl.ds(3 * NZ, NZ)],
    ]
    landings = [face_x.at[0], face_x.at[1], face_y.at[0], face_y.at[1]]

    def face_copy(k):
        return pltpu.make_async_remote_copy(
            src_ref=sources[k], dst_ref=landings[mirror[k]],
            send_sem=face_send.at[k], recv_sem=face_recv.at[mirror[k]],
            device_id=partners[k], device_id_type=MESH,
        )

    for k in range(4):
        face_copy(k).start()

    plane0 = jnp.zeros((CY, NZ), F32)
    row0 = jnp.zeros((1, NZ), F32)
    last = lanes_of((CY, NZ)) == NZ - 1
    first = lanes_of((CY, NZ)) == 0
    wx[0] = plane0
    wx[CX] = plane0
    for x in range(CX - 1):
        wx[x + 1] = 0.5 * (kap[x] + kap[x + 1])
    for x in range(CX):
        k = kap[x]
        wy[x, 0:1] = row0
        wy[x, 1:CY] = 0.5 * (k[: CY - 1] + k[1:])
        wy[x, CY : CY + 1] = row0
        wz[x] = jnp.where(last, 0.0, 0.5 * (k + pltpu.roll(k, NZ - 1, 1)))
    cells[1].wait()
    for k in range(4):
        halo_copy(k).wait_recv()
    ext = [jnp.where(inside[k], halo[k], 0.0) for k in range(4)]
    bound = [0.5 * (edge[k] + ext[k]) for k in range(4)]
    for x in range(CX):
        k = kap[x]
        w = wz[x]
        below = jnp.where(first, 0.5 * k, pltpu.roll(w, 1, 1))
        above = jnp.where(last, 0.5 * k, w)
        dx = (bound[0] if x == 0 else wx[x]) + (bound[1] if x == CX - 1 else wx[x + 1])
        dy = wy[x, 0:CY] + wy[x, 1 : CY + 1]
        dy = dy + jnp.concatenate(
            [bound[2][x : x + 1], jnp.zeros((CY - 2, NZ), F32), bound[3][x : x + 1]], 0
        )
        diag[x] = react[x].astype(F32) + dx + dy + (below + above)

    def apply(x, local):
        before, after = jnp.maximum(x - 1, 0), jnp.minimum(x + 1, CX - 1)
        behind, v = None, field[x, 0]
        for y in range(CY):
            ahead = field[x, y + 1] if y < CY - 1 else None
            out = diag[x, y : y + 1] * v
            out = out - wx[x, y : y + 1] * field[before, y]
            out = out - wx[x + 1, y : y + 1] * field[after, y]
            if y > 0:
                out = out - wy[x, y : y + 1] * behind
            if y < CY - 1:
                out = out - wy[x, y + 1 : y + 2] * ahead
            w = wz[x, y : y + 1]
            out = out - w * pltpu.roll(v, NZ - 1, 1)
            out = out - pltpu.roll(w * v, 1, 1)
            r, c = SLOTS * (y % 4), NZ * (y // 4)
            local[r : r + SLOTS, c : c + NZ] = pad_rows(out, SLOTS).astype(BF16)
            behind, v = v, ahead

    def collect(total):
        total_lanes = lanes_of((SLOTS, 128))
        out = jnp.zeros((SLOTS, 128), F32)
        for i in range(4):
            part = total[SLOTS * i : SLOTS * (i + 1), :]
            part = pltpu.roll(part, 256 - SLOTS * i, 1) if i else part
            out = out + part[:, :128]
        return jnp.where(total_lanes < SLOTS, out, 0.0)

    gram[...] = jnp.zeros_like(gram)
    local1[...] = jnp.zeros_like(local1)

    def pair(i, carry):
        x = 2 * i
        gram[:, 0:192] += nt(masked[jnp.maximum(x - 1, 0)], local1[...])
        apply(x, local0)
        gram[:, 0:192] += nt(masked[x], local0[...])
        apply(x + 1, local1)
        return carry

    lax.fori_loop(0, CX // 2, pair, 0)
    gram[:, 0:192] += nt(masked[CX - 1], local1[...])
    own = collect(gram)
    spot, slot = lanes_of((SLOTS, 128)), rows_of((SLOTS, 128))
    own = own + jnp.where((spot == slot) & (slot >= count), 1.0, 0.0)

    found = []
    for k in range(4):
        weight = bound[k]
        for i in range(16):
            mine = field[0 if k == 0 else CX - 1, i] if k < 2 else field[i, 0 if k == 2 else CY - 1]
            hi, lo = split(pad_rows(mine * weight[i : i + 1], SLOTS))
            r, c = SLOTS * (i % 4), NZ * (i // 4)
            local0[r : r + SLOTS, c : c + NZ] = hi
            local1[r : r + SLOTS, c : c + NZ] = lo
        face_copy(mirror[k]).wait_recv()
        if k < 2:
            other = face_x[k]
            total = nt(local0[...], other) + nt(local1[...], other)
        else:
            total = jnp.zeros((192, 192), F32)
            for q in range(4):
                other = face_y[k - 2, 4 * q : 4 * q + 4].reshape(192, NZ)
                cols = slice(NZ * q, NZ * (q + 1))
                total = total + nt(local0[:, cols], other) + nt(local1[:, cols], other)
        side[:, 0:192] = -total
        found.append(jnp.where(inside[k], collect(side), 0.0))

    blocks = [own] + found
    for k in range(5):
        blocks_ref[k] = blocks[k]
    sym = 0.5 * (blocks[0] + transposed(blocks[0])[:SLOTS])
    up = transposed(blocks[2])[:SLOTS]
    lane = lanes_of((SLOTS, 128))
    sym = jnp.where(lane < LIVE, sym, 0.0)
    blocks_ref[5] = sym
    ahead = blocks[4]
    odd = pc == 1
    payload = jnp.where(odd, ahead, sym) + pltpu.roll(jnp.where(odd, sym, ahead), LIVE, 1)
    payload = payload + pltpu.roll(up, 2 * LIVE, 1)
    payload = jnp.where(lane >= 3 * LIVE, count.astype(F32), payload)

    def y_copy():
        return pltpu.make_async_remote_copy(
            src_ref=slots.at[px, pz, pc], dst_ref=slots.at[px, pz, pc],
            send_sem=y_sem.at[0], recv_sem=y_sem.at[1],
            device_id=(1, u), device_id_type=MESH,
        )

    def x_copy(i, x):
        return pltpu.make_async_remote_copy(
            src_ref=slots.at[px, pz, pc], dst_ref=slots.at[px, pz, pc],
            send_sem=x_send.at[i], recv_sem=x_recv.at[px],
            device_id=at(x, pz, pc), device_id_type=MESH,
        )

    def x_land(x):
        return pltpu.make_async_remote_copy(
            src_ref=slots.at[x, pz, pc], dst_ref=slots.at[x, pz, pc],
            send_sem=x_send.at[0], recv_sem=x_recv.at[x],
            device_id=at(x, pz, pc), device_id_type=MESH,
        )

    def z_copy(i, z):
        return pltpu.make_async_remote_copy(
            src_ref=slots.at[:, pz, pc], dst_ref=slots.at[:, pz, pc],
            send_sem=z_send.at[i], recv_sem=z_recv.at[pz],
            device_id=at(px, z, pc), device_id_type=MESH,
        )

    def z_land(z):
        return pltpu.make_async_remote_copy(
            src_ref=slots.at[:, z, pc], dst_ref=slots.at[:, z, pc],
            send_sem=z_send.at[0], recv_sem=z_recv.at[z],
            device_id=at(px, z, pc), device_id_type=MESH,
        )

    def core_copy(z):
        return pltpu.make_async_remote_copy(
            src_ref=slots.at[:, z, pc], dst_ref=slots.at[:, z, pc],
            send_sem=core_send.at[z], recv_sem=core_recv.at[z],
            device_id=at(px, pz, 1 - pc), device_id_type=MESH,
        )

    def core_land(z):
        return pltpu.make_async_remote_copy(
            src_ref=slots.at[:, z, 1 - pc], dst_ref=slots.at[:, z, 1 - pc],
            send_sem=core_send.at[z], recv_sem=core_recv.at[z],
            device_id=at(px, pz, 1 - pc), device_id_type=MESH,
        )

    @pl.when(joined)
    def _():
        @pl.when(g == 0)
        def _():
            slots[px, pz, pc] = payload[:LIVE]
            y_copy().start()

        @pl.when(g == 1)
        def _():
            y_copy().wait_recv()

        for i, x in enumerate(x_partner):
            x_copy(i, x).start()
        for x in x_partner:
            x_land(x).wait_recv()
        for i, z in enumerate(z_partner):
            z_copy(i, z).start()
        core_copy(pz).start()
        for z in z_partner:
            z_land(z).wait_recv()
            core_copy(z).start()
        for z in [pz] + z_partner:
            core_land(z).wait_recv()
        for x in range(3):
            for z in range(4):
                for c in range(2):
                    all_ref[x * 8 + z * 2 + c] = slots[x, z, c]

        @pl.when(g == 0)
        def _():
            y_copy().wait_send()

        for i, x in enumerate(x_partner):
            x_copy(i, x).wait_send()
        for i, z in enumerate(z_partner):
            z_copy(i, z).wait_send()
        for z in [pz] + z_partner:
            core_copy(z).wait_send()

    for k in range(4):
        halo_copy(k).wait_send()
        face_copy(k).wait_send()


def assemble(count, modes, kappa, react):
    vmem = pl.BlockSpec(memory_space=pltpu.VMEM)
    hbm = pl.BlockSpec(memory_space=pltpu.HBM)
    dma = pltpu.SemaphoreType.DMA
    return pl.pallas_call(
        assemble_kernel,
        out_shape=(
            jax.ShapeDtypeStruct((6, SLOTS, 128), F32),
            jax.ShapeDtypeStruct((24, LIVE, 128), F32),
        ),
        in_specs=[pl.BlockSpec(memory_space=pltpu.SMEM), hbm, hbm, hbm],
        out_specs=(vmem, vmem),
        scratch_shapes=[
            pltpu.VMEM((CX, LIVE, CY, NZ), BF16),
            pltpu.VMEM((CX, CY, NZ), BF16),
            pltpu.VMEM((CX, CY, NZ), BF16),
            pltpu.VMEM((CX, CY, LIVE, NZ), F32),
            pltpu.VMEM((CX, 4 * SLOTS, 4 * NZ), BF16),
            pltpu.VMEM((CX + 1, CY, NZ), F32),
            pltpu.VMEM((CX, 24, NZ), F32),
            pltpu.VMEM((CX, CY, NZ), F32),
            pltpu.VMEM((CX, CY, NZ), F32),
            pltpu.VMEM((4, 16, NZ), F32),
            pltpu.VMEM((4, 16, NZ), F32),
            pltpu.VMEM((2, 4 * SLOTS, 4 * NZ), BF16),
            pltpu.VMEM((2, 16, SLOTS, NZ), BF16),
            pltpu.VMEM((4 * SLOTS, 4 * NZ), BF16),
            pltpu.VMEM((4 * SLOTS, 4 * NZ), BF16),
            pltpu.VMEM((4 * SLOTS, 256), F32),
            pltpu.VMEM((4 * SLOTS, 256), F32),
            pltpu.VMEM((3, 4, 2, LIVE, 128), F32),
            dma((CX,)),
            dma((2,)),
            dma((4,)),
            dma((4,)),
            dma((4,)),
            dma((4,)),
            dma((2,)),
            dma((2,)),
            dma((3,)),
            dma((3,)),
            dma((4,)),
            dma((4,)),
            dma((4,)),
        ],
        compiler_params=pltpu.CompilerParams(
            collective_id=0, has_side_effects=True, vmem_limit_bytes=50 * 2**20
        ),
        name="assemble",
    )(count, modes, kappa, react)


def dot3(a, b, dims):
    ah, al = split(a)
    bh, bl = split(b)
    dot = lambda p, q: lax.dot_general(p, q, (dims, ((), ())), preferred_element_type=F32)
    return dot(ah, bh) + (dot(ah, bl) + dot(al, bh))


def nn3(a, b):
    return dot3(a, b, ((1,), (0,)))


def nt3(a, b):
    return dot3(a, b, ((1,), (1,)))


def wide(x):
    return jnp.broadcast_to(x, (8, 128))


def pivots(p, soff, state):
    tiles, saved = (list(part) for part in state)
    sub = rows_of((8, 128))
    at = soff + 8 * p
    column = lambda v, c: wide(tiles[v][:, at + c : at + c + 1])
    here = [column(p, c) for c in range(8)]
    d = {(i, j): wide(here[j][i : i + 1]) for i in range(8) for j in range(i, 8)}
    rows = [wide(tiles[p][c : c + 1]) for c in range(8)]
    m, inv = {}, []
    for c in range(8):
        rinv = lax.rsqrt(d[c, c])
        inv.append(rinv * rinv)
        saved[p] = jnp.where(sub == c, rows[c] * rinv, saved[p])
        if c < 7:
            square = d[c, c + 1] * d[c, c + 1]
        for i in range(c + 1, 8):
            m[c, i] = d[c, i] * inv[c]
            for j in range(i, 8):
                if (i, j) == (c + 1, c + 1):
                    d[i, j] = d[i, j] - square * inv[c]
                else:
                    d[i, j] = d[i, j] - m[c, i] * d[c, j]
            rows[i] = rows[i] - m[c, i] * rows[c]
    z = [rows[c] * inv[c] for c in range(8)]
    for c in range(7, 0, -1):
        for i in range(c):
            z[i] = z[i] - m[i, c] * z[c]
    for v in range(LIVE // 8):
        if v != p:
            terms = [column(v, c) * z[c] for c in range(8)]
            while len(terms) > 1:
                terms = [terms[i] + terms[i + 1] for i in range(0, len(terms), 2)]
            tiles[v] = tiles[v] - terms[0]
    for c in range(8):
        tiles[p] = jnp.where(sub == c, z[c], tiles[p])
    return tuple(tiles), tuple(saved)


def place(out_ref, block, pos, keep):
    base = jnp.minimum((pos // 128) * 128, NC - 256)
    base = pl.multiple_of(base, 128)
    shifted = pltpu.roll(pad_lanes(block, 256), pos - base, 1)
    cols = lanes_of((SLOTS, 256)) + base
    out_ref[:, pl.ds(base, 256)] += jnp.where(keep(cols), shifted, 0.0)


def factor_kernel(all_ref, blocks_ref, out_ref, linv_ref, k_ref, g_ref, f_ref, x_ref):
    g, u = lax.axis_index("grp"), lax.axis_index("sub")
    s = g * NU + u
    upper = s <= 21
    member = (s == 21) | (s == 22) | ((s >= NU) & (s < NU + NB))
    lane = lanes_of((LIVE, 128))
    row = rows_of((LIVE, 128))
    lane48 = lanes_of((SLOTS, 128))
    row48 = rows_of((SLOTS, 128))
    out_ref[...] = jnp.zeros_like(out_ref)
    before = lambda cols: cols < DONE
    after = lambda cols: cols >= DONE

    def left(x, by):
        x = pltpu.roll(x, 128 - by, 1) if by else x
        return jnp.where(lanes_of(x.shape) < LIVE, x, 0.0)

    def reduce_row(q):
        at, wide_enough = jnp.maximum(q, 0), jnp.where(q == NB - 1, 16, LIVE)
        mine = jnp.where(q == s, blocks_ref[5], 0.0)
        mine = jnp.where(q == s - 1, blocks_ref[3], mine)
        mine = jnp.where(q == s - NU, blocks_ref[1], mine)
        held = jnp.where(q > 0, f_ref[jnp.maximum(q - 1, 0)], 0.0)
        f = mine - nn3(held, pad_rows(k_ref[at], 128))
        f_ref[at] = jnp.where((q <= s) & (lane48 < wide_enough), f, 0.0)

    def solve_row(q):
        at = jnp.maximum(q, 0)
        x = nt3(f_ref[at], pad_rows(linv_ref[at], 128))
        x_ref[at] = jnp.where((q == s) & (lane48 > row48), 0.0, x)

    def store_row(q):
        at = jnp.maximum(q, 0)
        x = jnp.where(q >= 0, x_ref[at], 0.0)
        place(out_ref, x, SLOTS * at, before)
        g_ref[at] = nn3(x, pad_rows(linv_ref[at], 128))

    def step(t, odd, scur, n):
        soff, uoff = (LIVE, 0) if odd else (0, LIVE)
        given = all_ref[t]
        limit = jnp.where(t == NB - 1, 16, LIVE)
        in_s = (lane >= soff) & (lane < soff + LIVE)
        eye = jnp.where(lane == row + soff, 1.0, 0.0)
        a = jnp.where((row < limit) & (lane < soff + limit), scur, eye)
        rest = jnp.where(lane < 2 * LIVE, jnp.where(row < limit, given, 0.0),
                         jnp.where(lane == row + 2 * LIVE, 1.0, 0.0))
        a = jnp.where(in_s, a, rest)
        ut = transposed(given)[uoff : uoff + LIVE]
        tiles = tuple(a[8 * v : 8 * v + 8] for v in range(LIVE // 8))
        state = pivots(0, soff, (tiles, tiles))

        store_row(t - 3)
        solve_row(t - 2)
        reduce_row(t - 1)
        coming = all_ref[jnp.minimum(t + 1, NB - 1)]
        coming_n = jnp.max(jnp.where(lanes_of((8, 128)) >= 3 * LIVE, coming[0:8], 0.0))
        n = jnp.where(t == NB - 1, jnp.minimum(n, 16.0), n)
        for p in range(1, LIVE // 8):
            state = lax.cond(
                n > 8.0 * p, lambda st, p=p: pivots(p, soff, st), lambda st: st, state
            )
        tiles, saved = state
        k = jnp.concatenate(tiles, 0)
        snext = coming - nn3(ut, pad_rows(k, 128))
        linv_ref[t] = left(jnp.concatenate(saved, 0), 2 * LIVE)
        k_ref[t + 1] = left(k, uoff)
        return snext, coming_n

    @pl.when(upper | member)
    def _():
        k_ref[0] = jnp.zeros((LIVE, 128), F32)
        linv_ref[0] = jnp.zeros((LIVE, 128), F32)
        f_ref[0] = jnp.zeros((SLOTS, 128), F32)
        x_ref[0] = jnp.zeros((SLOTS, 128), F32)
        first = all_ref[0]
        n = jnp.max(jnp.where(lanes_of((8, 128)) >= 3 * LIVE, first[0:8], 0.0))

        def pair(i, carry):
            carry = step(2 * i, False, *carry)
            return step(2 * i + 1, True, *carry)

        lax.fori_loop(0, NB // 2, pair, (first, n))
        store_row(NB - 3)
        solve_row(NB - 2)
        reduce_row(NB - 1)
        store_row(NB - 2)
        solve_row(NB - 1)
        store_row(NB - 1)

    @pl.when(upper)
    def _():
        dead = jnp.where((row48 == lane48) & (row48 >= LIVE), 1.0, 0.0)
        place(out_ref, dead, SLOTS * s, before)

    @pl.when(member)
    def _():
        def put(block, pos):
            base = pos // 128 * 128
            shifted = pltpu.roll(pad_lanes(block, 256), pos - base, 1)
            if pos < DONE:
                shifted = jnp.where(lanes_of((SLOTS, 256)) + base >= DONE, shifted, 0.0)
            out_ref[:, base : base + 256] -= shifted

        late = lane >= 16
        last = jnp.where(row < 16, all_ref[NB - 1], 0.0)
        own = jnp.where(late, left(last, LIVE), 0.0)
        over = jnp.where(late, left(all_ref[NB - 2], LIVE), 0.0)
        y = None
        for t in range(NB - 1, -1, -1):
            if y is None:
                y = g_ref[t]
                put(nn3(y, pad_rows(left(last, 0), 128)), SLOTS * NB)
                put(nn3(y, pad_rows(own, 128)), SLOTS * (NB - 1))
            else:
                y = g_ref[t] - nt3(y, pad_rows(k_ref[t + 1], 128))
            if t == NB - 2:
                put(nn3(y, pad_rows(over, 128)), SLOTS * (NB - 1))
            rising = pad_rows(left(all_ref[t], 2 * LIVE), 128)
            put(nt3(y, rising), SLOTS * (t + NU))

    @pl.when(s >= 21)
    def _():
        targets = [s, s - NU, s + NU, s - 1, s + 1]
        valid = [True, g > 0, g < NG - 1, u > 0, u < NU - 1]
        for k in range(5):
            pos = SLOTS * jnp.clip(targets[k], 0, NG * NU - 1)
            place(out_ref, jnp.where(valid[k], blocks_ref[k], 0.0), pos, after)

    @pl.when(s == 21)
    def _():
        out_ref[0:16, DONE:] = jnp.zeros((16, NC - DONE), F32)


def factor(everyone, blocks):
    vmem = pl.BlockSpec(memory_space=pltpu.VMEM)
    return pl.pallas_call(
        factor_kernel,
        out_shape=jax.ShapeDtypeStruct((SLOTS, NC), F32),
        in_specs=[vmem, vmem],
        out_specs=vmem,
        scratch_shapes=[
            pltpu.VMEM((NB, LIVE, 128), F32),
            pltpu.VMEM((NB + 1, LIVE, 128), F32),
            pltpu.VMEM((NB, SLOTS, 128), F32),
            pltpu.VMEM((NB, SLOTS, 128), F32),
            pltpu.VMEM((NB, SLOTS, 128), F32),
        ],
        compiler_params=pltpu.CompilerParams(vmem_limit_bytes=40 * 2**20),
        name="factor",
    )(everyone, blocks)


def per_device(modes, counts, kappa, react):
    blocks, everyone = assemble(counts, modes, kappa, react)
    return factor(everyone, blocks)


def solution(mesh):
    in_specs = (
        P(None, "grp", "sub", None),
        P(("grp", "sub")),
        P("grp", "sub", None),
        P("grp", "sub", None),
    )
    out_specs = P(("grp", "sub"), None)
    return jax.shard_map(
        per_device, mesh=mesh, in_specs=in_specs, out_specs=out_specs, check_vma=False
    )
```

```python
import jax
import jax.numpy as jnp
from jax import lax
from jax.experimental import pallas as pl
from jax.experimental.pallas import tpu as pltpu
from jax.sharding import PartitionSpec as P

F32 = jnp.float32
BF16 = jnp.bfloat16
MESH = pl.DeviceIdType.MESH
NG, NU = 4, 32
CX, CY, NZ = 16, 16, 256
SLOTS, LIVE = 48, 40
NB = 22
DONE = 1024
NC = SLOTS * NG * NU


def nt(a, b, precision=None):
    return lax.dot_general(
        a, b, (((1,), (1,)), ((), ())), preferred_element_type=F32, precision=precision
    )


def lanes_of(shape):
    return lax.broadcasted_iota(jnp.int32, shape, len(shape) - 1)


def rows_of(shape):
    return lax.broadcasted_iota(jnp.int32, shape, len(shape) - 2)


def split(x):
    hi = x.astype(BF16)
    return hi, (x - hi.astype(F32)).astype(BF16)


def pad_rows(x, rows):
    return jnp.concatenate([x, jnp.zeros((rows - x.shape[0], x.shape[1]), x.dtype)], 0)


def pad_lanes(x, lanes):
    return jnp.concatenate([x, jnp.zeros((x.shape[0], lanes - x.shape[1]), x.dtype)], 1)


def transposed(x):
    return jnp.transpose(pad_rows(x, 128))


def assemble_kernel(
    count_ref, modes_ref, kappa_ref, react_ref, blocks_ref, all_ref,
    raw, kappa, react, field, masked, wx, wy, wz, diag, edge, halo, face_x, face_y,
    local0, local1, gram, side, slots,
    raw_sem, cell_sem, halo_send, halo_recv, face_send, face_recv,
    y_sem, x_send, x_recv, z_send, z_recv, core_send, core_recv,
):
    g, u = lax.axis_index("grp"), lax.axis_index("sub")
    partners = [
        (lax.rem(g + NG - 1, NG), u),
        (lax.rem(g + 1, NG), u),
        (g, lax.rem(u + NU - 1, NU)),
        (g, lax.rem(u + 1, NU)),
    ]
    inside = [g > 0, g < NG - 1, u > 0, u < NU - 1]
    mirror = [1, 0, 3, 2]
    px, pz, pc = u // 8, lax.rem(u // 2, 4), lax.rem(u, 2)
    joined = (g < 2) & (u < 24)

    def at(x, z, c):
        return (g, x * 8 + z * 2 + c)

    x_partner = [lax.rem(px + i, 3) for i in (1, 2)]
    z_partner = [lax.rem(pz + i, 4) for i in (1, 2, 3)]

    def fetch(x):
        return pltpu.make_async_copy(
            modes_ref.at[pl.ds(0, LIVE), x], raw.at[x], raw_sem.at[x]
        )

    cells = [
        pltpu.make_async_copy(kappa_ref, kappa, cell_sem.at[0]),
        pltpu.make_async_copy(react_ref, react, cell_sem.at[1]),
    ]
    cells[0].start()
    for x in range(CX):
        fetch(x).start()
    cells[1].start()

    barrier = pltpu.get_barrier_semaphore()

    def greet(device):
        pl.semaphore_signal(barrier, inc=1, device_id=device, device_id_type=MESH)

    for partner in partners:
        greet(partner)

    @pl.when(joined)
    def _():
        for x in x_partner:
            greet(at(x, pz, pc))
        for z in z_partner:
            greet(at(px, z, pc))
        greet(at(px, pz, 1 - pc))

    count = count_ref[0]
    cells[0].wait()
    kap = kappa[...].astype(F32)
    edge[0] = kap[0]
    edge[1] = kap[CX - 1]
    for x in range(CX):
        edge[2, x : x + 1] = kap[x, 0:1]
        edge[3, x : x + 1] = kap[x, CY - 1 : CY]
    pl.semaphore_wait(barrier, jnp.where(joined, 10, 4))

    def halo_copy(k):
        return pltpu.make_async_remote_copy(
            src_ref=edge.at[k], dst_ref=halo.at[mirror[k]],
            send_sem=halo_send.at[k], recv_sem=halo_recv.at[mirror[k]],
            device_id=partners[k], device_id_type=MESH,
        )

    for k in range(4):
        halo_copy(k).start()

    live = rows_of((CY, LIVE, NZ)) < count

    def turn(x, carry):
        fetch(x).wait()
        plane = jnp.swapaxes(raw[x].astype(F32), 0, 1)
        plane = jnp.where(live, plane, 0.0)
        field[x] = plane
        for y in range(CY):
            r, c = SLOTS * (y % 4), NZ * (y // 4)
            masked[x, r : r + SLOTS, c : c + NZ] = pad_rows(plane[y], SLOTS).astype(BF16)
        return carry

    lax.fori_loop(0, CX, turn, 0)

    sources = [
        masked.at[0],
        masked.at[CX - 1],
        masked.at[:, pl.ds(0, SLOTS), pl.ds(0, NZ)],
        masked.at[:, pl.ds(3 * SLOTS, SLOTS), pl.ds(3 * NZ, NZ)],
    ]
    landings = [face_x.at[0], face_x.at[1], face_y.at[0], face_y.at[1]]

    def face_copy(k):
        return pltpu.make_async_remote_copy(
            src_ref=sources[k], dst_ref=landings[mirror[k]],
            send_sem=face_send.at[k], recv_sem=face_recv.at[mirror[k]],
            device_id=partners[k], device_id_type=MESH,
        )

    for k in range(4):
        face_copy(k).start()

    plane0 = jnp.zeros((CY, NZ), F32)
    row0 = jnp.zeros((1, NZ), F32)
    last = lanes_of((CY, NZ)) == NZ - 1
    first = lanes_of((CY, NZ)) == 0
    wx[0] = plane0
    wx[CX] = plane0
    for x in range(CX - 1):
        wx[x + 1] = 0.5 * (kap[x] + kap[x + 1])
    for x in range(CX):
        k = kap[x]
        wy[x, 0:1] = row0
        wy[x, 1:CY] = 0.5 * (k[: CY - 1] + k[1:])
        wy[x, CY : CY + 1] = row0
        wz[x] = jnp.where(last, 0.0, 0.5 * (k + pltpu.roll(k, NZ - 1, 1)))
    cells[1].wait()
    for k in range(4):
        halo_copy(k).wait_recv()
    ext = [jnp.where(inside[k], halo[k], 0.0) for k in range(4)]
    bound = [0.5 * (edge[k] + ext[k]) for k in range(4)]
    for x in range(CX):
        k = kap[x]
        w = wz[x]
        below = jnp.where(first, 0.5 * k, pltpu.roll(w, 1, 1))
        above = jnp.where(last, 0.5 * k, w)
        dx = (bound[0] if x == 0 else wx[x]) + (bound[1] if x == CX - 1 else wx[x + 1])
        dy = wy[x, 0:CY] + wy[x, 1 : CY + 1]
        dy = dy + jnp.concatenate(
            [bound[2][x : x + 1], jnp.zeros((CY - 2, NZ), F32), bound[3][x : x + 1]], 0
        )
        diag[x] = react[x].astype(F32) + dx + dy + (below + above)

    def apply(x, local):
        before, after = jnp.maximum(x - 1, 0), jnp.minimum(x + 1, CX - 1)
        behind, v = None, field[x, 0]
        for y in range(CY):
            ahead = field[x, y + 1] if y < CY - 1 else None
            out = diag[x, y : y + 1] * v
            out = out - wx[x, y : y + 1] * field[before, y]
            out = out - wx[x + 1, y : y + 1] * field[after, y]
            if y > 0:
                out = out - wy[x, y : y + 1] * behind
            if y < CY - 1:
                out = out - wy[x, y + 1 : y + 2] * ahead
            w = wz[x, y : y + 1]
            out = out - w * pltpu.roll(v, NZ - 1, 1)
            out = out - pltpu.roll(w * v, 1, 1)
            r, c = SLOTS * (y % 4), NZ * (y // 4)
            local[r : r + SLOTS, c : c + NZ] = pad_rows(out, SLOTS).astype(BF16)
            behind, v = v, ahead

    def collect(total):
        total_lanes = lanes_of((SLOTS, 128))
        out = jnp.zeros((SLOTS, 128), F32)
        for i in range(4):
            part = total[SLOTS * i : SLOTS * (i + 1), :]
            part = pltpu.roll(part, 256 - SLOTS * i, 1) if i else part
            out = out + part[:, :128]
        return jnp.where(total_lanes < SLOTS, out, 0.0)

    gram[...] = jnp.zeros_like(gram)
    local1[...] = jnp.zeros_like(local1)

    def pair(i, carry):
        x = 2 * i
        gram[:, 0:192] += nt(masked[jnp.maximum(x - 1, 0)], local1[...])
        apply(x, local0)
        gram[:, 0:192] += nt(masked[x], local0[...])
        apply(x + 1, local1)
        return carry

    lax.fori_loop(0, CX // 2, pair, 0)
    gram[:, 0:192] += nt(masked[CX - 1], local1[...])
    own = collect(gram)
    spot, slot = lanes_of((SLOTS, 128)), rows_of((SLOTS, 128))
    own = own + jnp.where((spot == slot) & (slot >= count), 1.0, 0.0)

    found = []
    for k in range(4):
        weight = bound[k]
        for i in range(16):
            mine = field[0 if k == 0 else CX - 1, i] if k < 2 else field[i, 0 if k == 2 else CY - 1]
            hi, lo = split(pad_rows(mine * weight[i : i + 1], SLOTS))
            r, c = SLOTS * (i % 4), NZ * (i // 4)
            local0[r : r + SLOTS, c : c + NZ] = hi
            local1[r : r + SLOTS, c : c + NZ] = lo
        face_copy(mirror[k]).wait_recv()
        if k < 2:
            other = face_x[k]
            total = nt(local0[...], other) + nt(local1[...], other)
        else:
            total = jnp.zeros((192, 192), F32)
            for q in range(4):
                other = face_y[k - 2, 4 * q : 4 * q + 4].reshape(192, NZ)
                cols = slice(NZ * q, NZ * (q + 1))
                total = total + nt(local0[:, cols], other) + nt(local1[:, cols], other)
        side[:, 0:192] = -total
        found.append(jnp.where(inside[k], collect(side), 0.0))

    blocks = [own] + found
    for k in range(5):
        blocks_ref[k] = blocks[k]
    sym = 0.5 * (blocks[0] + transposed(blocks[0])[:SLOTS])
    up = transposed(blocks[2])[:SLOTS]
    lane = lanes_of((SLOTS, 128))
    sym = jnp.where(lane < LIVE, sym, 0.0)
    blocks_ref[5] = sym
    ahead = blocks[4]
    odd = pc == 1
    payload = jnp.where(odd, ahead, sym) + pltpu.roll(jnp.where(odd, sym, ahead), LIVE, 1)
    payload = payload + pltpu.roll(up, 2 * LIVE, 1)
    payload = jnp.where(lane >= 3 * LIVE, count.astype(F32), payload)

    def y_copy():
        return pltpu.make_async_remote_copy(
            src_ref=slots.at[px, pz, pc], dst_ref=slots.at[px, pz, pc],
            send_sem=y_sem.at[0], recv_sem=y_sem.at[1],
            device_id=(1, u), device_id_type=MESH,
        )

    def x_copy(i, x):
        return pltpu.make_async_remote_copy(
            src_ref=slots.at[px, pz, pc], dst_ref=slots.at[px, pz, pc],
            send_sem=x_send.at[i], recv_sem=x_recv.at[px],
            device_id=at(x, pz, pc), device_id_type=MESH,
        )

    def x_land(x):
        return pltpu.make_async_remote_copy(
            src_ref=slots.at[x, pz, pc], dst_ref=slots.at[x, pz, pc],
            send_sem=x_send.at[0], recv_sem=x_recv.at[x],
            device_id=at(x, pz, pc), device_id_type=MESH,
        )

    def z_copy(i, z):
        return pltpu.make_async_remote_copy(
            src_ref=slots.at[:, pz, pc], dst_ref=slots.at[:, pz, pc],
            send_sem=z_send.at[i], recv_sem=z_recv.at[pz],
            device_id=at(px, z, pc), device_id_type=MESH,
        )

    def z_land(z):
        return pltpu.make_async_remote_copy(
            src_ref=slots.at[:, z, pc], dst_ref=slots.at[:, z, pc],
            send_sem=z_send.at[0], recv_sem=z_recv.at[z],
            device_id=at(px, z, pc), device_id_type=MESH,
        )

    def core_copy(z):
        return pltpu.make_async_remote_copy(
            src_ref=slots.at[:, z, pc], dst_ref=slots.at[:, z, pc],
            send_sem=core_send.at[z], recv_sem=core_recv.at[z],
            device_id=at(px, pz, 1 - pc), device_id_type=MESH,
        )

    def core_land(z):
        return pltpu.make_async_remote_copy(
            src_ref=slots.at[:, z, 1 - pc], dst_ref=slots.at[:, z, 1 - pc],
            send_sem=core_send.at[z], recv_sem=core_recv.at[z],
            device_id=at(px, pz, 1 - pc), device_id_type=MESH,
        )

    @pl.when(joined)
    def _():
        @pl.when(g == 0)
        def _():
            slots[px, pz, pc] = payload[:LIVE]
            y_copy().start()

        @pl.when(g == 1)
        def _():
            y_copy().wait_recv()

        for i, x in enumerate(x_partner):
            x_copy(i, x).start()
        for x in x_partner:
            x_land(x).wait_recv()
        for i, z in enumerate(z_partner):
            z_copy(i, z).start()
        core_copy(pz).start()
        for z in z_partner:
            z_land(z).wait_recv()
            core_copy(z).start()
        for z in [pz] + z_partner:
            core_land(z).wait_recv()
        for x in range(3):
            for z in range(4):
                for c in range(2):
                    all_ref[x * 8 + z * 2 + c] = slots[x, z, c]

        @pl.when(g == 0)
        def _():
            y_copy().wait_send()

        for i, x in enumerate(x_partner):
            x_copy(i, x).wait_send()
        for i, z in enumerate(z_partner):
            z_copy(i, z).wait_send()
        for z in [pz] + z_partner:
            core_copy(z).wait_send()

    for k in range(4):
        halo_copy(k).wait_send()
        face_copy(k).wait_send()


def assemble(count, modes, kappa, react):
    vmem = pl.BlockSpec(memory_space=pltpu.VMEM)
    hbm = pl.BlockSpec(memory_space=pltpu.HBM)
    dma = pltpu.SemaphoreType.DMA
    return pl.pallas_call(
        assemble_kernel,
        out_shape=(
            jax.ShapeDtypeStruct((6, SLOTS, 128), F32),
            jax.ShapeDtypeStruct((24, LIVE, 128), F32),
        ),
        in_specs=[pl.BlockSpec(memory_space=pltpu.SMEM), hbm, hbm, hbm],
        out_specs=(vmem, vmem),
        scratch_shapes=[
            pltpu.VMEM((CX, LIVE, CY, NZ), BF16),
            pltpu.VMEM((CX, CY, NZ), BF16),
            pltpu.VMEM((CX, CY, NZ), BF16),
            pltpu.VMEM((CX, CY, LIVE, NZ), F32),
            pltpu.VMEM((CX, 4 * SLOTS, 4 * NZ), BF16),
            pltpu.VMEM((CX + 1, CY, NZ), F32),
            pltpu.VMEM((CX, 24, NZ), F32),
            pltpu.VMEM((CX, CY, NZ), F32),
            pltpu.VMEM((CX, CY, NZ), F32),
            pltpu.VMEM((4, 16, NZ), F32),
            pltpu.VMEM((4, 16, NZ), F32),
            pltpu.VMEM((2, 4 * SLOTS, 4 * NZ), BF16),
            pltpu.VMEM((2, 16, SLOTS, NZ), BF16),
            pltpu.VMEM((4 * SLOTS, 4 * NZ), BF16),
            pltpu.VMEM((4 * SLOTS, 4 * NZ), BF16),
            pltpu.VMEM((4 * SLOTS, 256), F32),
            pltpu.VMEM((4 * SLOTS, 256), F32),
            pltpu.VMEM((3, 4, 2, LIVE, 128), F32),
            dma((CX,)),
            dma((2,)),
            dma((4,)),
            dma((4,)),
            dma((4,)),
            dma((4,)),
            dma((2,)),
            dma((2,)),
            dma((3,)),
            dma((3,)),
            dma((4,)),
            dma((4,)),
            dma((4,)),
        ],
        compiler_params=pltpu.CompilerParams(
            collective_id=0, has_side_effects=True, vmem_limit_bytes=50 * 2**20
        ),
        name="assemble",
    )(count, modes, kappa, react)


def dot3(a, b, dims):
    ah, al = split(a)
    bh, bl = split(b)
    dot = lambda p, q: lax.dot_general(p, q, (dims, ((), ())), preferred_element_type=F32)
    return dot(ah, bh) + (dot(ah, bl) + dot(al, bh))


def nn3(a, b):
    return dot3(a, b, ((1,), (0,)))


def nt3(a, b):
    return dot3(a, b, ((1,), (1,)))


def wide(x):
    return jnp.broadcast_to(x, (8, 128))


def pivots(p, soff, state, spread_ref, rows_ref):
    tiles, saved = (list(part) for part in state)
    sub = rows_of((8, 128))
    at = soff + 8 * p
    column = lambda v, c: wide(tiles[v][:, at + c : at + c + 1])
    for c in range(8):
        spread_ref[p, c] = column(p, c)
    rows_ref[p] = tiles[p]
    d = {(i, j): wide(spread_ref[p, j, i : i + 1]) for i in range(8) for j in range(i, 8)}
    rows = [wide(rows_ref[p, c : c + 1]) for c in range(8)]
    m, inv = {}, []
    for c in range(8):
        rinv = lax.rsqrt(d[c, c])
        inv.append(rinv * rinv)
        saved[p] = jnp.where(sub == c, rows[c] * rinv, saved[p])
        if c < 7:
            square = d[c, c + 1] * d[c, c + 1]
        for i in range(c + 1, 8):
            m[c, i] = d[c, i] * inv[c]
            for j in range(i, 8):
                if (i, j) == (c + 1, c + 1):
                    d[i, j] = d[i, j] - square * inv[c]
                else:
                    d[i, j] = d[i, j] - m[c, i] * d[c, j]
            rows[i] = rows[i] - m[c, i] * rows[c]
    z = [rows[c] * inv[c] for c in range(8)]
    for c in range(7, 0, -1):
        for i in range(c):
            z[i] = z[i] - m[i, c] * z[c]
    for v in range(LIVE // 8):
        if v != p:
            terms = [column(v, c) * z[c] for c in range(8)]
            while len(terms) > 1:
                terms = [terms[i] + terms[i + 1] for i in range(0, len(terms), 2)]
            tiles[v] = tiles[v] - terms[0]
    for c in range(8):
        tiles[p] = jnp.where(sub == c, z[c], tiles[p])
    return tuple(tiles), tuple(saved)


def place(out_ref, block, pos, keep):
    base = jnp.minimum((pos // 128) * 128, NC - 256)
    base = pl.multiple_of(base, 128)
    shifted = pltpu.roll(pad_lanes(block, 256), pos - base, 1)
    cols = lanes_of((SLOTS, 256)) + base
    out_ref[:, pl.ds(base, 256)] += jnp.where(keep(cols), shifted, 0.0)


def factor_kernel(all_ref, blocks_ref, out_ref, linv_ref, k_ref, g_ref, f_ref, x_ref, spread_ref, rows_ref):
    g, u = lax.axis_index("grp"), lax.axis_index("sub")
    s = g * NU + u
    upper = s <= 21
    member = (s == 21) | (s == 22) | ((s >= NU) & (s < NU + NB))
    lane = lanes_of((LIVE, 128))
    row = rows_of((LIVE, 128))
    lane48 = lanes_of((SLOTS, 128))
    row48 = rows_of((SLOTS, 128))
    out_ref[...] = jnp.zeros_like(out_ref)
    before = lambda cols: cols < DONE
    after = lambda cols: cols >= DONE

    def left(x, by):
        x = pltpu.roll(x, 128 - by, 1) if by else x
        return jnp.where(lanes_of(x.shape) < LIVE, x, 0.0)

    def reduce_row(q):
        at, wide_enough = jnp.maximum(q, 0), jnp.where(q == NB - 1, 16, LIVE)
        mine = jnp.where(q == s, blocks_ref[5], 0.0)
        mine = jnp.where(q == s - 1, blocks_ref[3], mine)
        mine = jnp.where(q == s - NU, blocks_ref[1], mine)
        held = jnp.where(q > 0, f_ref[jnp.maximum(q - 1, 0)], 0.0)
        f = mine - nn3(held, pad_rows(k_ref[at], 128))
        f_ref[at] = jnp.where((q <= s) & (lane48 < wide_enough), f, 0.0)

    def solve_row(q):
        at = jnp.maximum(q, 0)
        x = nt3(f_ref[at], pad_rows(linv_ref[at], 128))
        x_ref[at] = jnp.where((q == s) & (lane48 > row48), 0.0, x)

    def store_row(q):
        at = jnp.maximum(q, 0)
        x = jnp.where(q >= 0, x_ref[at], 0.0)
        place(out_ref, x, SLOTS * at, before)
        g_ref[at] = nn3(x, pad_rows(linv_ref[at], 128))

    def step(t, odd, scur, n):
        soff, uoff = (LIVE, 0) if odd else (0, LIVE)
        given = all_ref[t]
        limit = jnp.where(t == NB - 1, 16, LIVE)
        in_s = (lane >= soff) & (lane < soff + LIVE)
        eye = jnp.where(lane == row + soff, 1.0, 0.0)
        a = jnp.where((row < limit) & (lane < soff + limit), scur, eye)
        rest = jnp.where(lane < 2 * LIVE, jnp.where(row < limit, given, 0.0),
                         jnp.where(lane == row + 2 * LIVE, 1.0, 0.0))
        a = jnp.where(in_s, a, rest)
        ut = transposed(given)[uoff : uoff + LIVE]
        tiles = tuple(a[8 * v : 8 * v + 8] for v in range(LIVE // 8))
        state = pivots(0, soff, (tiles, tiles), spread_ref, rows_ref)

        store_row(t - 3)
        solve_row(t - 2)
        reduce_row(t - 1)
        coming = all_ref[jnp.minimum(t + 1, NB - 1)]
        coming_n = jnp.max(jnp.where(lanes_of((8, 128)) >= 3 * LIVE, coming[0:8], 0.0))
        n = jnp.where(t == NB - 1, jnp.minimum(n, 16.0), n)
        for p in range(1, LIVE // 8):
            state = lax.cond(
                n > 8.0 * p,
                lambda st, p=p: pivots(p, soff, st, spread_ref, rows_ref),
                lambda st: st,
                state,
            )
        tiles, saved = state
        k = jnp.concatenate(tiles, 0)
        snext = coming - nn3(ut, pad_rows(k, 128))
        linv_ref[t] = left(jnp.concatenate(saved, 0), 2 * LIVE)
        k_ref[t + 1] = left(k, uoff)
        return snext, coming_n

    @pl.when(upper | member)
    def _():
        k_ref[0] = jnp.zeros((LIVE, 128), F32)
        linv_ref[0] = jnp.zeros((LIVE, 128), F32)
        f_ref[0] = jnp.zeros((SLOTS, 128), F32)
        x_ref[0] = jnp.zeros((SLOTS, 128), F32)
        first = all_ref[0]
        n = jnp.max(jnp.where(lanes_of((8, 128)) >= 3 * LIVE, first[0:8], 0.0))

        def pair(i, carry):
            carry = step(2 * i, False, *carry)
            return step(2 * i + 1, True, *carry)

        lax.fori_loop(0, NB // 2, pair, (first, n))
        store_row(NB - 3)
        solve_row(NB - 2)
        reduce_row(NB - 1)
        store_row(NB - 2)
        solve_row(NB - 1)
        store_row(NB - 1)

    @pl.when(upper)
    def _():
        dead = jnp.where((row48 == lane48) & (row48 >= LIVE), 1.0, 0.0)
        place(out_ref, dead, SLOTS * s, before)

    @pl.when(member)
    def _():
        def put(block, pos):
            base = pos // 128 * 128
            shifted = pltpu.roll(pad_lanes(block, 256), pos - base, 1)
            if pos < DONE:
                shifted = jnp.where(lanes_of((SLOTS, 256)) + base >= DONE, shifted, 0.0)
            out_ref[:, base : base + 256] -= shifted

        late = lane >= 16
        last = jnp.where(row < 16, all_ref[NB - 1], 0.0)
        own = jnp.where(late, left(last, LIVE), 0.0)
        over = jnp.where(late, left(all_ref[NB - 2], LIVE), 0.0)
        y = None
        for t in range(NB - 1, -1, -1):
            if y is None:
                y = g_ref[t]
                put(nn3(y, pad_rows(left(last, 0), 128)), SLOTS * NB)
                put(nn3(y, pad_rows(own, 128)), SLOTS * (NB - 1))
            else:
                y = g_ref[t] - nt3(y, pad_rows(k_ref[t + 1], 128))
            if t == NB - 2:
                put(nn3(y, pad_rows(over, 128)), SLOTS * (NB - 1))
            rising = pad_rows(left(all_ref[t], 2 * LIVE), 128)
            put(nt3(y, rising), SLOTS * (t + NU))

    @pl.when(s >= 21)
    def _():
        targets = [s, s - NU, s + NU, s - 1, s + 1]
        valid = [True, g > 0, g < NG - 1, u > 0, u < NU - 1]
        for k in range(5):
            pos = SLOTS * jnp.clip(targets[k], 0, NG * NU - 1)
            place(out_ref, jnp.where(valid[k], blocks_ref[k], 0.0), pos, after)

    @pl.when(s == 21)
    def _():
        out_ref[0:16, DONE:] = jnp.zeros((16, NC - DONE), F32)


def factor(everyone, blocks):
    vmem = pl.BlockSpec(memory_space=pltpu.VMEM)
    return pl.pallas_call(
        factor_kernel,
        out_shape=jax.ShapeDtypeStruct((SLOTS, NC), F32),
        in_specs=[vmem, vmem],
        out_specs=vmem,
        scratch_shapes=[
            pltpu.VMEM((NB, LIVE, 128), F32),
            pltpu.VMEM((NB + 1, LIVE, 128), F32),
            pltpu.VMEM((NB, SLOTS, 128), F32),
            pltpu.VMEM((NB, SLOTS, 128), F32),
            pltpu.VMEM((NB, SLOTS, 128), F32),
            pltpu.VMEM((LIVE // 8, 8, 8, 128), F32),
            pltpu.VMEM((LIVE // 8, 8, 128), F32),
        ],
        compiler_params=pltpu.CompilerParams(vmem_limit_bytes=40 * 2**20),
        name="factor",
    )(everyone, blocks)


def per_device(modes, counts, kappa, react):
    blocks, everyone = assemble(counts, modes, kappa, react)
    return factor(everyone, blocks)


def solution(mesh):
    in_specs = (
        P(None, "grp", "sub", None),
        P(("grp", "sub")),
        P("grp", "sub", None),
        P("grp", "sub", None),
    )
    out_specs = P(("grp", "sub"), None)
    return jax.shard_map(
        per_device, mesh=mesh, in_specs=in_specs, out_specs=out_specs, check_vma=False
    )
```

```python
import jax
import jax.numpy as jnp
from jax import lax
from jax.experimental import pallas as pl
from jax.experimental.pallas import tpu as pltpu
from jax.sharding import PartitionSpec as P

F32 = jnp.float32
BF16 = jnp.bfloat16
MESH = pl.DeviceIdType.MESH
NG, NU = 4, 32
CX, CY, NZ = 16, 16, 256
SLOTS, LIVE = 48, 40
NB = 22
DONE = 1024
NC = SLOTS * NG * NU


def nt(a, b, precision=None):
    return lax.dot_general(
        a, b, (((1,), (1,)), ((), ())), preferred_element_type=F32, precision=precision
    )


def lanes_of(shape):
    return lax.broadcasted_iota(jnp.int32, shape, len(shape) - 1)


def rows_of(shape):
    return lax.broadcasted_iota(jnp.int32, shape, len(shape) - 2)


def split(x):
    hi = x.astype(BF16)
    return hi, (x - hi.astype(F32)).astype(BF16)


def pad_rows(x, rows):
    return jnp.concatenate([x, jnp.zeros((rows - x.shape[0], x.shape[1]), x.dtype)], 0)


def pad_lanes(x, lanes):
    return jnp.concatenate([x, jnp.zeros((x.shape[0], lanes - x.shape[1]), x.dtype)], 1)


def transposed(x):
    return jnp.transpose(pad_rows(x, 128))


def assemble_kernel(
    count_ref, modes_ref, kappa_ref, react_ref, blocks_ref, all_ref,
    raw, kappa, react, field, masked, wx, wy, wz, diag, edge, halo, face_x, face_y,
    local0, local1, gram, side, slots,
    raw_sem, cell_sem, halo_send, halo_recv, face_send, face_recv,
    y_sem, x_send, x_recv, z_send, z_recv, core_send, core_recv,
):
    g, u = lax.axis_index("grp"), lax.axis_index("sub")
    partners = [
        (lax.rem(g + NG - 1, NG), u),
        (lax.rem(g + 1, NG), u),
        (g, lax.rem(u + NU - 1, NU)),
        (g, lax.rem(u + 1, NU)),
    ]
    inside = [g > 0, g < NG - 1, u > 0, u < NU - 1]
    mirror = [1, 0, 3, 2]
    px, pz, pc = u // 8, lax.rem(u // 2, 4), lax.rem(u, 2)
    joined = (g < 2) & (u < 24)

    def at(x, z, c):
        return (g, x * 8 + z * 2 + c)

    x_partner = [lax.rem(px + i, 3) for i in (1, 2)]
    z_partner = [lax.rem(pz + i, 4) for i in (1, 2, 3)]

    def fetch(x):
        return pltpu.make_async_copy(
            modes_ref.at[pl.ds(0, LIVE), x], raw.at[x], raw_sem.at[x]
        )

    cells = [
        pltpu.make_async_copy(kappa_ref, kappa, cell_sem.at[0]),
        pltpu.make_async_copy(react_ref, react, cell_sem.at[1]),
    ]
    cells[0].start()
    for x in range(CX):
        fetch(x).start()
    cells[1].start()

    barrier = pltpu.get_barrier_semaphore()

    def greet(device):
        pl.semaphore_signal(barrier, inc=1, device_id=device, device_id_type=MESH)

    for partner in partners:
        greet(partner)

    @pl.when(joined)
    def _():
        for x in x_partner:
            greet(at(x, pz, pc))
        for z in z_partner:
            greet(at(px, z, pc))
        greet(at(px, pz, 1 - pc))

    count = count_ref[0]
    cells[0].wait()
    kap = kappa[...].astype(F32)
    edge[0] = kap[0]
    edge[1] = kap[CX - 1]
    for x in range(CX):
        edge[2, x : x + 1] = kap[x, 0:1]
        edge[3, x : x + 1] = kap[x, CY - 1 : CY]
    pl.semaphore_wait(barrier, jnp.where(joined, 10, 4))

    def halo_copy(k):
        return pltpu.make_async_remote_copy(
            src_ref=edge.at[k], dst_ref=halo.at[mirror[k]],
            send_sem=halo_send.at[k], recv_sem=halo_recv.at[mirror[k]],
            device_id=partners[k], device_id_type=MESH,
        )

    for k in range(4):
        halo_copy(k).start()

    live = rows_of((CY, LIVE, NZ)) < count

    def turn(x, carry):
        fetch(x).wait()
        plane = jnp.swapaxes(raw[x].astype(F32), 0, 1)
        plane = jnp.where(live, plane, 0.0)
        field[x] = plane
        for y in range(CY):
            r, c = SLOTS * (y % 4), NZ * (y // 4)
            masked[x, r : r + SLOTS, c : c + NZ] = pad_rows(plane[y], SLOTS).astype(BF16)
        return carry

    lax.fori_loop(0, CX, turn, 0)

    sources = [
        masked.at[0],
        masked.at[CX - 1],
        masked.at[:, pl.ds(0, SLOTS), pl.ds(0, NZ)],
        masked.at[:, pl.ds(3 * SLOTS, SLOTS), pl.ds(3 * NZ, NZ)],
    ]
    landings = [face_x.at[0], face_x.at[1], face_y.at[0], face_y.at[1]]

    def face_copy(k):
        return pltpu.make_async_remote_copy(
            src_ref=sources[k], dst_ref=landings[mirror[k]],
            send_sem=face_send.at[k], recv_sem=face_recv.at[mirror[k]],
            device_id=partners[k], device_id_type=MESH,
        )

    for k in range(4):
        face_copy(k).start()

    plane0 = jnp.zeros((CY, NZ), F32)
    row0 = jnp.zeros((1, NZ), F32)
    last = lanes_of((CY, NZ)) == NZ - 1
    first = lanes_of((CY, NZ)) == 0
    wx[0] = plane0
    wx[CX] = plane0
    for x in range(CX - 1):
        wx[x + 1] = 0.5 * (kap[x] + kap[x + 1])
    for x in range(CX):
        k = kap[x]
        wy[x, 0:1] = row0
        wy[x, 1:CY] = 0.5 * (k[: CY - 1] + k[1:])
        wy[x, CY : CY + 1] = row0
        wz[x] = jnp.where(last, 0.0, 0.5 * (k + pltpu.roll(k, NZ - 1, 1)))
    cells[1].wait()
    for k in range(4):
        halo_copy(k).wait_recv()
    ext = [jnp.where(inside[k], halo[k], 0.0) for k in range(4)]
    bound = [0.5 * (edge[k] + ext[k]) for k in range(4)]
    for x in range(CX):
        k = kap[x]
        w = wz[x]
        below = jnp.where(first, 0.5 * k, pltpu.roll(w, 1, 1))
        above = jnp.where(last, 0.5 * k, w)
        dx = (bound[0] if x == 0 else wx[x]) + (bound[1] if x == CX - 1 else wx[x + 1])
        dy = wy[x, 0:CY] + wy[x, 1 : CY + 1]
        dy = dy + jnp.concatenate(
            [bound[2][x : x + 1], jnp.zeros((CY - 2, NZ), F32), bound[3][x : x + 1]], 0
        )
        diag[x] = react[x].astype(F32) + dx + dy + (below + above)

    def apply(x, local):
        before, after = jnp.maximum(x - 1, 0), jnp.minimum(x + 1, CX - 1)
        behind, v = None, field[x, 0]
        for y in range(CY):
            ahead = field[x, y + 1] if y < CY - 1 else None
            out = diag[x, y : y + 1] * v
            out = out - wx[x, y : y + 1] * field[before, y]
            out = out - wx[x + 1, y : y + 1] * field[after, y]
            if y > 0:
                out = out - wy[x, y : y + 1] * behind
            if y < CY - 1:
                out = out - wy[x, y + 1 : y + 2] * ahead
            w = wz[x, y : y + 1]
            out = out - w * pltpu.roll(v, NZ - 1, 1)
            out = out - pltpu.roll(w * v, 1, 1)
            r, c = SLOTS * (y % 4), NZ * (y // 4)
            local[r : r + SLOTS, c : c + NZ] = pad_rows(out, SLOTS).astype(BF16)
            behind, v = v, ahead

    def collect(total):
        total_lanes = lanes_of((SLOTS, 128))
        out = jnp.zeros((SLOTS, 128), F32)
        for i in range(4):
            part = total[SLOTS * i : SLOTS * (i + 1), :]
            part = pltpu.roll(part, 256 - SLOTS * i, 1) if i else part
            out = out + part[:, :128]
        return jnp.where(total_lanes < SLOTS, out, 0.0)

    gram[...] = jnp.zeros_like(gram)
    local1[...] = jnp.zeros_like(local1)

    def pair(i, carry):
        x = 2 * i
        gram[:, 0:192] += nt(masked[jnp.maximum(x - 1, 0)], local1[...])
        apply(x, local0)
        gram[:, 0:192] += nt(masked[x], local0[...])
        apply(x + 1, local1)
        return carry

    lax.fori_loop(0, CX // 2, pair, 0)
    gram[:, 0:192] += nt(masked[CX - 1], local1[...])
    own = collect(gram)
    spot, slot = lanes_of((SLOTS, 128)), rows_of((SLOTS, 128))
    own = own + jnp.where((spot == slot) & (slot >= count), 1.0, 0.0)

    found = []
    for k in range(4):
        weight = bound[k]
        for i in range(16):
            mine = field[0 if k == 0 else CX - 1, i] if k < 2 else field[i, 0 if k == 2 else CY - 1]
            hi, lo = split(pad_rows(mine * weight[i : i + 1], SLOTS))
            r, c = SLOTS * (i % 4), NZ * (i // 4)
            local0[r : r + SLOTS, c : c + NZ] = hi
            local1[r : r + SLOTS, c : c + NZ] = lo
        face_copy(mirror[k]).wait_recv()
        if k < 2:
            other = face_x[k]
            total = nt(local0[...], other) + nt(local1[...], other)
        else:
            total = jnp.zeros((192, 192), F32)
            for q in range(4):
                other = face_y[k - 2, 4 * q : 4 * q + 4].reshape(192, NZ)
                cols = slice(NZ * q, NZ * (q + 1))
                total = total + nt(local0[:, cols], other) + nt(local1[:, cols], other)
        side[:, 0:192] = -total
        found.append(jnp.where(inside[k], collect(side), 0.0))

    blocks = [own] + found
    for k in range(5):
        blocks_ref[k] = blocks[k]
    sym = 0.5 * (blocks[0] + transposed(blocks[0])[:SLOTS])
    up = transposed(blocks[2])[:SLOTS]
    lane = lanes_of((SLOTS, 128))
    sym = jnp.where(lane < LIVE, sym, 0.0)
    blocks_ref[5] = sym
    ahead = blocks[4]
    odd = pc == 1
    payload = jnp.where(odd, ahead, sym) + pltpu.roll(jnp.where(odd, sym, ahead), LIVE, 1)
    payload = payload + pltpu.roll(up, 2 * LIVE, 1)
    payload = jnp.where(lane >= 3 * LIVE, count.astype(F32), payload)

    def y_copy():
        return pltpu.make_async_remote_copy(
            src_ref=slots.at[px, pz, pc], dst_ref=slots.at[px, pz, pc],
            send_sem=y_sem.at[0], recv_sem=y_sem.at[1],
            device_id=(1, u), device_id_type=MESH,
        )

    def x_copy(i, x):
        return pltpu.make_async_remote_copy(
            src_ref=slots.at[px, pz, pc], dst_ref=slots.at[px, pz, pc],
            send_sem=x_send.at[i], recv_sem=x_recv.at[px],
            device_id=at(x, pz, pc), device_id_type=MESH,
        )

    def x_land(x):
        return pltpu.make_async_remote_copy(
            src_ref=slots.at[x, pz, pc], dst_ref=slots.at[x, pz, pc],
            send_sem=x_send.at[0], recv_sem=x_recv.at[x],
            device_id=at(x, pz, pc), device_id_type=MESH,
        )

    def z_copy(i, z):
        return pltpu.make_async_remote_copy(
            src_ref=slots.at[:, pz, pc], dst_ref=slots.at[:, pz, pc],
            send_sem=z_send.at[i], recv_sem=z_recv.at[pz],
            device_id=at(px, z, pc), device_id_type=MESH,
        )

    def z_land(z):
        return pltpu.make_async_remote_copy(
            src_ref=slots.at[:, z, pc], dst_ref=slots.at[:, z, pc],
            send_sem=z_send.at[0], recv_sem=z_recv.at[z],
            device_id=at(px, z, pc), device_id_type=MESH,
        )

    def core_copy(z):
        return pltpu.make_async_remote_copy(
            src_ref=slots.at[:, z, pc], dst_ref=slots.at[:, z, pc],
            send_sem=core_send.at[z], recv_sem=core_recv.at[z],
            device_id=at(px, pz, 1 - pc), device_id_type=MESH,
        )

    def core_land(z):
        return pltpu.make_async_remote_copy(
            src_ref=slots.at[:, z, 1 - pc], dst_ref=slots.at[:, z, 1 - pc],
            send_sem=core_send.at[z], recv_sem=core_recv.at[z],
            device_id=at(px, pz, 1 - pc), device_id_type=MESH,
        )

    @pl.when(joined)
    def _():
        @pl.when(g == 0)
        def _():
            slots[px, pz, pc] = payload[:LIVE]
            y_copy().start()

        @pl.when(g == 1)
        def _():
            y_copy().wait_recv()

        for i, x in enumerate(x_partner):
            x_copy(i, x).start()
        for x in x_partner:
            x_land(x).wait_recv()
        for i, z in enumerate(z_partner):
            z_copy(i, z).start()
        core_copy(pz).start()
        for z in z_partner:
            z_land(z).wait_recv()
            core_copy(z).start()
        for z in [pz] + z_partner:
            core_land(z).wait_recv()
        for x in range(3):
            for z in range(4):
                for c in range(2):
                    all_ref[x * 8 + z * 2 + c] = slots[x, z, c]

        @pl.when(g == 0)
        def _():
            y_copy().wait_send()

        for i, x in enumerate(x_partner):
            x_copy(i, x).wait_send()
        for i, z in enumerate(z_partner):
            z_copy(i, z).wait_send()
        for z in [pz] + z_partner:
            core_copy(z).wait_send()

    for k in range(4):
        halo_copy(k).wait_send()
        face_copy(k).wait_send()


def assemble(count, modes, kappa, react):
    vmem = pl.BlockSpec(memory_space=pltpu.VMEM)
    hbm = pl.BlockSpec(memory_space=pltpu.HBM)
    dma = pltpu.SemaphoreType.DMA
    return pl.pallas_call(
        assemble_kernel,
        out_shape=(
            jax.ShapeDtypeStruct((6, SLOTS, 128), F32),
            jax.ShapeDtypeStruct((24, LIVE, 128), F32),
        ),
        in_specs=[pl.BlockSpec(memory_space=pltpu.SMEM), hbm, hbm, hbm],
        out_specs=(vmem, vmem),
        scratch_shapes=[
            pltpu.VMEM((CX, LIVE, CY, NZ), BF16),
            pltpu.VMEM((CX, CY, NZ), BF16),
            pltpu.VMEM((CX, CY, NZ), BF16),
            pltpu.VMEM((CX, CY, LIVE, NZ), F32),
            pltpu.VMEM((CX, 4 * SLOTS, 4 * NZ), BF16),
            pltpu.VMEM((CX + 1, CY, NZ), F32),
            pltpu.VMEM((CX, 24, NZ), F32),
            pltpu.VMEM((CX, CY, NZ), F32),
            pltpu.VMEM((CX, CY, NZ), F32),
            pltpu.VMEM((4, 16, NZ), F32),
            pltpu.VMEM((4, 16, NZ), F32),
            pltpu.VMEM((2, 4 * SLOTS, 4 * NZ), BF16),
            pltpu.VMEM((2, 16, SLOTS, NZ), BF16),
            pltpu.VMEM((4 * SLOTS, 4 * NZ), BF16),
            pltpu.VMEM((4 * SLOTS, 4 * NZ), BF16),
            pltpu.VMEM((4 * SLOTS, 256), F32),
            pltpu.VMEM((4 * SLOTS, 256), F32),
            pltpu.VMEM((3, 4, 2, LIVE, 128), F32),
            dma((CX,)),
            dma((2,)),
            dma((4,)),
            dma((4,)),
            dma((4,)),
            dma((4,)),
            dma((2,)),
            dma((2,)),
            dma((3,)),
            dma((3,)),
            dma((4,)),
            dma((4,)),
            dma((4,)),
        ],
        compiler_params=pltpu.CompilerParams(
            collective_id=0, has_side_effects=True, vmem_limit_bytes=50 * 2**20
        ),
        name="assemble",
    )(count, modes, kappa, react)


def dot3(a, b, dims):
    ah, al = split(a)
    bh, bl = split(b)
    dot = lambda p, q: lax.dot_general(p, q, (dims, ((), ())), preferred_element_type=F32)
    return dot(ah, bh) + (dot(ah, bl) + dot(al, bh))


def nn3(a, b):
    return dot3(a, b, ((1,), (0,)))


def nt3(a, b):
    return dot3(a, b, ((1,), (1,)))


def wide(x):
    return jnp.broadcast_to(x, (8, 128))


def pivots(p, soff, state, spread_ref, rows_ref, side_ref):
    tiles, saved = (list(part) for part in state)
    sub = rows_of((8, 128))
    at = soff + 8 * p
    column = lambda v, c: wide(tiles[v][:, c : c + 1])
    if p == 0:
        for c in range(8):
            spread_ref[p, c] = column(p, at + c)
    rows_ref[p] = tiles[p]
    d = {(i, j): wide(spread_ref[p, j, i : i + 1]) for i in range(8) for j in range(i, 8)}
    rows = [wide(rows_ref[p, c : c + 1]) for c in range(8)]
    follow = p + 1 < LIVE // 8
    if follow:
        under = [column(p + 1, at + c) for c in range(8)]
        coming = [column(p + 1, at + 8 + c) for c in range(8)]
    others = [v for v in range(LIVE // 8) if v not in (p, p + 1)]
    factors = {v: [column(v, at + c) for c in range(8)] for v in others}
    low, rinv = {}, []
    for c in range(8):
        rinv.append(lax.rsqrt(d[c, c]))
        for i in range(c + 1, 8):
            low[c, i] = d[c, i] * rinv[c]
        for i in range(c + 1, 8):
            for j in range(i, 8):
                d[i, j] = d[i, j] - low[c, i] * low[c, j]
        rows[c] = rows[c] * rinv[c]
        saved[p] = jnp.where(sub == c, rows[c], saved[p])
        for i in range(c + 1, 8):
            rows[i] = rows[i] - low[c, i] * rows[c]
        if follow:
            under[c] = under[c] * rinv[c]
            side_ref[p, c] = under[c]
            for i in range(c + 1, 8):
                under[i] = under[i] - low[c, i] * under[c]
            for i in range(8):
                coming[i] = coming[i] - under[c] * wide(side_ref[p, c, i : i + 1])
            tiles[p + 1] = tiles[p + 1] - under[c] * rows[c]
    if follow:
        for c in range(8):
            spread_ref[p + 1, c] = coming[c]
    z = rows
    for c in range(7, -1, -1):
        z[c] = z[c] * rinv[c]
        for i in range(c):
            z[i] = z[i] - low[i, c] * z[c]
    for v in others:
        terms = [factors[v][c] * z[c] for c in range(8)]
        while len(terms) > 1:
            terms = [terms[i] + terms[i + 1] for i in range(0, len(terms), 2)]
        tiles[v] = tiles[v] - terms[0]
    for c in range(8):
        tiles[p] = jnp.where(sub == c, z[c], tiles[p])
    return tuple(tiles), tuple(saved)


def place(out_ref, block, pos, keep):
    base = jnp.minimum((pos // 128) * 128, NC - 256)
    base = pl.multiple_of(base, 128)
    shifted = pltpu.roll(pad_lanes(block, 256), pos - base, 1)
    cols = lanes_of((SLOTS, 256)) + base
    out_ref[:, pl.ds(base, 256)] += jnp.where(keep(cols), shifted, 0.0)


def factor_kernel(all_ref, blocks_ref, out_ref, linv_ref, k_ref, g_ref, f_ref, x_ref, spread_ref, rows_ref, side_ref):
    g, u = lax.axis_index("grp"), lax.axis_index("sub")
    s = g * NU + u
    upper = s <= 21
    member = (s == 21) | (s == 22) | ((s >= NU) & (s < NU + NB))
    lane = lanes_of((LIVE, 128))
    row = rows_of((LIVE, 128))
    lane48 = lanes_of((SLOTS, 128))
    row48 = rows_of((SLOTS, 128))
    out_ref[...] = jnp.zeros_like(out_ref)
    before = lambda cols: cols < DONE
    after = lambda cols: cols >= DONE

    def left(x, by):
        x = pltpu.roll(x, 128 - by, 1) if by else x
        return jnp.where(lanes_of(x.shape) < LIVE, x, 0.0)

    def put(block, pos, late):
        base = pos // 128 * 128
        shifted = pltpu.roll(pad_lanes(block, 256), pos - base, 1) if pos > base else (
            pad_lanes(block, 256)
        )
        if base < DONE < base + 256:
            cols = lanes_of((SLOTS, 256)) + base
            shifted = jnp.where(cols >= DONE if late else cols < DONE, shifted, 0.0)
        out_ref[:, base : base + 256] += shifted

    def reduce_row(q):
        at, wide_enough = jnp.maximum(q, 0), jnp.where(q == NB - 1, 16, LIVE)
        mine = jnp.where(q == s, blocks_ref[5], 0.0)
        mine = jnp.where(q == s - 1, blocks_ref[3], mine)
        mine = jnp.where(q == s - NU, blocks_ref[1], mine)
        held = jnp.where(q > 0, f_ref[jnp.maximum(q - 1, 0)], 0.0)
        f = mine - nn3(held, pad_rows(k_ref[at], 128))
        f_ref[at] = jnp.where((q <= s) & (lane48 < wide_enough), f, 0.0)

    def solve_row(q):
        at = jnp.maximum(q, 0)
        x = nt3(f_ref[at], pad_rows(linv_ref[at], 128))
        x_ref[at] = jnp.where((q == s) & (lane48 > row48), 0.0, x)

    def double_row(q):
        at = jnp.maximum(q, 0)
        x = x_ref[at]
        g_ref[at] = nn3(x, pad_rows(linv_ref[at], 128))

    def step(t, odd, scur, n):
        soff, uoff = (LIVE, 0) if odd else (0, LIVE)
        given = all_ref[t]
        limit = jnp.where(t == NB - 1, 16, LIVE)
        in_s = (lane >= soff) & (lane < soff + LIVE)
        eye = jnp.where(lane == row + soff, 1.0, 0.0)
        a = jnp.where((row < limit) & (lane < soff + limit), scur, eye)
        rest = jnp.where(lane < 2 * LIVE, jnp.where(row < limit, given, 0.0),
                         jnp.where(lane == row + 2 * LIVE, 1.0, 0.0))
        a = jnp.where(in_s, a, rest)
        ut = transposed(given)[uoff : uoff + LIVE]
        tiles = tuple(a[8 * v : 8 * v + 8] for v in range(LIVE // 8))
        state = pivots(0, soff, (tiles, tiles), spread_ref, rows_ref, side_ref)

        double_row(t - 3)
        solve_row(t - 2)
        reduce_row(t - 1)
        coming = all_ref[jnp.minimum(t + 1, NB - 1)]
        coming_n = jnp.max(jnp.where(lanes_of((8, 128)) >= 3 * LIVE, coming[0:8], 0.0))
        n = jnp.where(t == NB - 1, jnp.minimum(n, 16.0), n)
        for p in range(1, LIVE // 8):
            state = lax.cond(
                n > 8.0 * p,
                lambda st, p=p: pivots(p, soff, st, spread_ref, rows_ref, side_ref),
                lambda st: st,
                state,
            )
        tiles, saved = state
        k = jnp.concatenate(tiles, 0)
        snext = coming - nn3(ut, pad_rows(k, 128))
        linv_ref[t] = left(jnp.concatenate(saved, 0), 2 * LIVE)
        k_ref[t + 1] = left(k, uoff)
        return snext, coming_n

    @pl.when(upper | member)
    def _():
        k_ref[0] = jnp.zeros((LIVE, 128), F32)
        linv_ref[0] = jnp.zeros((LIVE, 128), F32)
        f_ref[0] = jnp.zeros((SLOTS, 128), F32)
        x_ref[0] = jnp.zeros((SLOTS, 128), F32)
        first = all_ref[0]
        n = jnp.max(jnp.where(lanes_of((8, 128)) >= 3 * LIVE, first[0:8], 0.0))

        def pair(i, carry):
            carry = step(2 * i, False, *carry)
            return step(2 * i + 1, True, *carry)

        lax.fori_loop(0, NB // 2, pair, (first, n))
        double_row(NB - 3)
        solve_row(NB - 2)
        reduce_row(NB - 1)
        double_row(NB - 2)
        solve_row(NB - 1)
        double_row(NB - 1)
        for t in range(NB):
            put(x_ref[t], SLOTS * t, False)

    @pl.when(upper)
    def _():
        dead = jnp.where((row48 == lane48) & (row48 >= LIVE), 1.0, 0.0)
        place(out_ref, dead, SLOTS * s, before)

    @pl.when(member)
    def _():
        late = lane >= 16
        last = jnp.where(row < 16, all_ref[NB - 1], 0.0)
        own = jnp.where(late, left(last, LIVE), 0.0)
        over = jnp.where(late, left(all_ref[NB - 2], LIVE), 0.0)
        y = None
        for t in range(NB - 1, -1, -1):
            if y is None:
                y = g_ref[t]
                put(-nn3(y, pad_rows(left(last, 0), 128)), SLOTS * NB, True)
                put(-nn3(y, pad_rows(own, 128)), SLOTS * (NB - 1), True)
            else:
                y = g_ref[t] - nt3(y, pad_rows(k_ref[t + 1], 128))
            if t == NB - 2:
                put(-nn3(y, pad_rows(over, 128)), SLOTS * (NB - 1), True)
            rising = pad_rows(left(all_ref[t], 2 * LIVE), 128)
            put(-nt3(y, rising), SLOTS * (t + NU), True)

    @pl.when(s >= 21)
    def _():
        targets = [s, s - NU, s + NU, s - 1, s + 1]
        valid = [True, g > 0, g < NG - 1, u > 0, u < NU - 1]
        for k in range(5):
            pos = SLOTS * jnp.clip(targets[k], 0, NG * NU - 1)
            place(out_ref, jnp.where(valid[k], blocks_ref[k], 0.0), pos, after)

    @pl.when(s == 21)
    def _():
        out_ref[0:16, DONE:] = jnp.zeros((16, NC - DONE), F32)


def factor(everyone, blocks):
    vmem = pl.BlockSpec(memory_space=pltpu.VMEM)
    return pl.pallas_call(
        factor_kernel,
        out_shape=jax.ShapeDtypeStruct((SLOTS, NC), F32),
        in_specs=[vmem, vmem],
        out_specs=vmem,
        scratch_shapes=[
            pltpu.VMEM((NB, LIVE, 128), F32),
            pltpu.VMEM((NB + 1, LIVE, 128), F32),
            pltpu.VMEM((NB, SLOTS, 128), F32),
            pltpu.VMEM((NB, SLOTS, 128), F32),
            pltpu.VMEM((NB, SLOTS, 128), F32),
            pltpu.VMEM((LIVE // 8, 8, 8, 128), F32),
            pltpu.VMEM((LIVE // 8, 8, 128), F32),
            pltpu.VMEM((LIVE // 8, 8, 8, 128), F32),
        ],
        compiler_params=pltpu.CompilerParams(vmem_limit_bytes=40 * 2**20),
        name="factor",
    )(everyone, blocks)


def per_device(modes, counts, kappa, react):
    blocks, everyone = assemble(counts, modes, kappa, react)
    return factor(everyone, blocks)


def solution(mesh):
    in_specs = (
        P(None, "grp", "sub", None),
        P(("grp", "sub")),
        P("grp", "sub", None),
        P("grp", "sub", None),
    )
    out_specs = P(("grp", "sub"), None)
    return jax.shard_map(
        per_device, mesh=mesh, in_specs=in_specs, out_specs=out_specs, check_vma=False
    )
```

```python
import jax
import jax.numpy as jnp
from jax import lax
from jax.experimental import pallas as pl
from jax.experimental.pallas import tpu as pltpu
from jax.sharding import PartitionSpec as P

F32 = jnp.float32
BF16 = jnp.bfloat16
MESH = pl.DeviceIdType.MESH
NG, NU = 4, 32
CX, CY, NZ = 16, 16, 256
SLOTS, LIVE = 48, 40
NB = 22
DONE = 1024
GROUP = 24
GRAM = 4 * LIVE
NC = SLOTS * NG * NU


def nt(a, b, precision=None):
    return lax.dot_general(
        a, b, (((1,), (1,)), ((), ())), preferred_element_type=F32, precision=precision
    )


def lanes_of(shape):
    return lax.broadcasted_iota(jnp.int32, shape, len(shape) - 1)


def rows_of(shape):
    return lax.broadcasted_iota(jnp.int32, shape, len(shape) - 2)


def split(x):
    hi = x.astype(BF16)
    return hi, (x - hi.astype(F32)).astype(BF16)


def pad_rows(x, rows):
    return jnp.concatenate([x, jnp.zeros((rows - x.shape[0], x.shape[1]), x.dtype)], 0)


def pad_lanes(x, lanes):
    return jnp.concatenate([x, jnp.zeros((x.shape[0], lanes - x.shape[1]), x.dtype)], 1)


def transposed(x):
    return jnp.transpose(pad_rows(x, 128))


def assemble_kernel(
    count_ref, modes_ref, kappa_ref, react_ref, blocks_ref, links_ref, pivots_ref,
    raw, kappa, react, field, masked, wx, wy, wz, diag, edge, halo, face_x, face_y,
    local0, local1, high, low, gram, side, links, pivs,
    raw_sem, cell_sem, halo_send, halo_recv, face_send, face_recv,
    up_sem, link_send, link_recv, core_sem, piv_send, piv_recv,
):
    g, u = lax.axis_index("grp"), lax.axis_index("sub")
    partners = [
        (lax.rem(g + NG - 1, NG), u),
        (lax.rem(g + 1, NG), u),
        (g, lax.rem(u + NU - 1, NU)),
        (g, lax.rem(u + 1, NU)),
    ]
    inside = [g > 0, g < NG - 1, u > 0, u < NU - 1]
    mirror = [1, 0, 3, 2]
    chip, core = u // 2, lax.rem(u, 2)
    joined = (g < 2) & (u < GROUP)

    def fetch(x):
        return pltpu.make_async_copy(
            modes_ref.at[pl.ds(0, LIVE), x], raw.at[x], raw_sem.at[x]
        )

    cells = [
        pltpu.make_async_copy(kappa_ref, kappa, cell_sem.at[0]),
        pltpu.make_async_copy(react_ref, react, cell_sem.at[1]),
    ]
    cells[0].start()
    for x in [0, CX - 1] + list(range(1, CX - 1)):
        fetch(x).start()
    cells[1].start()

    barrier = pltpu.get_barrier_semaphore()

    def greet(device):
        pl.semaphore_signal(barrier, inc=1, device_id=device, device_id_type=MESH)

    for partner in partners:
        greet(partner)

    def others(count, me, act):
        def body(v, carry):
            @pl.when(v != me)
            def _():
                act(v)
            return carry

        lax.fori_loop(0, count, body, 0)

    @pl.when(joined)
    def _():
        others(GROUP, u, lambda v: greet((g, v)))

    count = count_ref[0]
    cells[0].wait()
    kap = kappa[...].astype(F32)
    edge[0] = kap[0]
    edge[1] = kap[CX - 1]
    for x in range(CX):
        edge[2, x : x + 1] = kap[x, 0:1]
        edge[3, x : x + 1] = kap[x, CY - 1 : CY]

    live = rows_of((CY, LIVE, NZ)) < count

    def turn(x):
        fetch(x).wait()
        plane = jnp.swapaxes(raw[x].astype(F32), 0, 1)
        plane = jnp.where(live, plane, 0.0)
        field[x] = plane
        for y in range(0, CY, 2):
            r, c = LIVE * (y % 4), NZ * (y // 4)
            two = jnp.concatenate([plane[y], plane[y + 1]], 0)
            masked[x, r : r + 2 * LIVE, c : c + NZ] = two.astype(BF16)

    turn(0)
    turn(CX - 1)
    pl.semaphore_wait(barrier, jnp.where(joined, GROUP + 3, 4))

    def halo_copy(k):
        return pltpu.make_async_remote_copy(
            src_ref=edge.at[k], dst_ref=halo.at[mirror[k]],
            send_sem=halo_send.at[k], recv_sem=halo_recv.at[mirror[k]],
            device_id=partners[k], device_id_type=MESH,
        )

    sources = [
        masked.at[0],
        masked.at[CX - 1],
        masked.at[:, pl.ds(0, SLOTS), pl.ds(0, NZ)],
        masked.at[:, pl.ds(GRAM - SLOTS, SLOTS), pl.ds(3 * NZ, NZ)],
    ]
    landings = [face_x.at[0], face_x.at[1], face_y.at[0], face_y.at[1]]

    def face_copy(k):
        return pltpu.make_async_remote_copy(
            src_ref=sources[k], dst_ref=landings[mirror[k]],
            send_sem=face_send.at[k], recv_sem=face_recv.at[mirror[k]],
            device_id=partners[k], device_id_type=MESH,
        )

    for k in range(4):
        halo_copy(k).start()
    face_copy(0).start()
    face_copy(1).start()

    def turn_next(x, carry):
        turn(x)
        return carry

    lax.fori_loop(1, CX - 1, turn_next, 0)
    face_copy(2).start()
    face_copy(3).start()

    plane0 = jnp.zeros((CY, NZ), F32)
    row0 = jnp.zeros((1, NZ), F32)
    last = lanes_of((CY, NZ)) == NZ - 1
    first = lanes_of((CY, NZ)) == 0
    wx[0] = plane0
    wx[CX] = plane0
    for x in range(CX - 1):
        wx[x + 1] = 0.5 * (kap[x] + kap[x + 1])
    for x in range(CX):
        k = kap[x]
        wy[x, 0:1] = row0
        wy[x, 1:CY] = 0.5 * (k[: CY - 1] + k[1:])
        wy[x, CY : CY + 1] = row0
        wz[x] = jnp.where(last, 0.0, 0.5 * (k + pltpu.roll(k, NZ - 1, 1)))
    cells[1].wait()
    for k in range(4):
        halo_copy(k).wait_recv()
    ext = [jnp.where(inside[k], halo[k], 0.0) for k in range(4)]
    bound = [0.5 * (edge[k] + ext[k]) for k in range(4)]
    for x in range(CX):
        k = kap[x]
        w = wz[x]
        below = jnp.where(first, 0.5 * k, pltpu.roll(w, 1, 1))
        above = jnp.where(last, 0.5 * k, w)
        dx = (bound[0] if x == 0 else wx[x]) + (bound[1] if x == CX - 1 else wx[x + 1])
        dy = wy[x, 0:CY] + wy[x, 1 : CY + 1]
        dy = dy + jnp.concatenate(
            [bound[2][x : x + 1], jnp.zeros((CY - 2, NZ), F32), bound[3][x : x + 1]], 0
        )
        diag[x] = react[x].astype(F32) + dx + dy + (below + above)

    def apply(x, local):
        before, after = jnp.maximum(x - 1, 0), jnp.minimum(x + 1, CX - 1)
        behind, v, done = None, field[x, 0], None
        for y in range(CY):
            ahead = field[x, y + 1] if y < CY - 1 else None
            out = diag[x, y : y + 1] * v
            out = out - wx[x, y : y + 1] * field[before, y]
            out = out - wx[x + 1, y : y + 1] * field[after, y]
            if y > 0:
                out = out - wy[x, y : y + 1] * behind
            if y < CY - 1:
                out = out - wy[x, y + 1 : y + 2] * ahead
            w = wz[x, y : y + 1]
            out = out - w * pltpu.roll(v, NZ - 1, 1)
            out = out - pltpu.roll(w * v, 1, 1)
            if y % 2:
                r, c = LIVE * (y % 4 - 1), NZ * (y // 4)
                two = jnp.concatenate([done, out], 0)
                local[r : r + 2 * LIVE, c : c + NZ] = two.astype(BF16)
            done = out
            behind, v = v, ahead

    def collect(total, step, start):
        out = jnp.zeros((LIVE, 128), F32)
        for i in range(4):
            part, by = total[LIVE * i : LIVE * (i + 1), :], step * i + start
            part = pltpu.roll(part, 256 - by, 1) if by else part
            out = out + part[:, :128]
        return jnp.where(lanes_of((LIVE, 128)) < LIVE, out, 0.0)

    gram[...] = jnp.zeros_like(gram)

    def pairs(begin, end):
        local1[...] = jnp.zeros_like(local1)

        def pair(i, carry):
            x = 2 * i
            gram[:, 0:GRAM] += nt(masked[jnp.maximum(x - 1, 0)], local1[...])
            apply(x, local0)
            gram[:, 0:GRAM] += nt(masked[x], local0[...])
            apply(x + 1, local1)
            return carry

        lax.fori_loop(begin, end, pair, 0)
        gram[:, 0:GRAM] += nt(masked[2 * end - 1], local1[...])

    pairs(0, 4)

    found = []
    for k in range(4):
        weight = bound[k]
        for i in range(0, 16, 2):
            two = []
            for j in (i, i + 1):
                mine = field[0 if k == 0 else CX - 1, j] if k < 2 else (
                    field[j, 0 if k == 2 else CY - 1]
                )
                two.append(mine * weight[j : j + 1])
            hi, lo = split(jnp.concatenate(two, 0))
            r, c = LIVE * (i % 4), NZ * (i // 4)
            high[r : r + 2 * LIVE, c : c + NZ] = hi
            low[r : r + 2 * LIVE, c : c + NZ] = lo
        face_copy(mirror[k]).wait_recv()
        if k < 2:
            other = face_x[k]
            side[:, 0:GRAM] = -(nt(high[...], other) + nt(low[...], other))
            block = collect(side, LIVE, 0)
        else:
            total = jnp.zeros((GRAM, 4 * SLOTS), F32)
            for q in range(4):
                other = face_y[k - 2, 4 * q : 4 * q + 4].reshape(4 * SLOTS, NZ)
                cols = slice(NZ * q, NZ * (q + 1))
                total = total + nt(high[:, cols], other) + nt(low[:, cols], other)
            side[:, 0 : 4 * SLOTS] = -total
            block = collect(side, SLOTS, SLOTS - LIVE if k == 2 else 0)
        found.append(jnp.where(inside[k], block, 0.0))
    for k in range(4):
        blocks_ref[k + 1] = pad_rows(found[k], SLOTS)

    lane = lanes_of((LIVE, 128))
    odd = core == 1
    ahead = found[3]
    ahead_t = transposed(ahead)[:LIVE]
    message = jnp.where(odd, ahead, ahead_t) + pltpu.roll(jnp.where(odd, ahead_t, ahead), LIVE, 1)
    message = message + pltpu.roll(transposed(found[1])[:LIVE], 2 * LIVE, 1)
    message = jnp.where(lane >= 3 * LIVE, count.astype(F32), message)

    def up_copy(ref, i):
        return pltpu.make_async_remote_copy(
            src_ref=ref, dst_ref=ref, send_sem=up_sem.at[i], recv_sem=up_sem.at[i + 2],
            device_id=(1, u), device_id_type=MESH,
        )

    def link_copy(to, owner):
        return pltpu.make_async_remote_copy(
            src_ref=links.at[owner, core], dst_ref=links.at[owner, core],
            send_sem=link_send.at[to], recv_sem=link_recv.at[owner],
            device_id=(g, 2 * to + core), device_id_type=MESH,
        )

    def core_copy(c):
        return pltpu.make_async_remote_copy(
            src_ref=links.at[:, c], dst_ref=links.at[:, c],
            send_sem=core_sem.at[0], recv_sem=core_sem.at[1],
            device_id=(g, 2 * chip + 1 - core), device_id_type=MESH,
        )

    def piv_copy(to, owner):
        return pltpu.make_async_remote_copy(
            src_ref=pivs.at[owner], dst_ref=pivs.at[owner],
            send_sem=piv_send.at[to], recv_sem=piv_recv.at[owner],
            device_id=(g, to), device_id_type=MESH,
        )

    link_up, piv_up = up_copy(links.at[chip, core], 0), up_copy(pivs.at[u], 1)

    @pl.when(joined & (g == 0))
    def _():
        links[chip, core] = message
        link_up.start()

    pairs(4, 6)

    @pl.when(joined)
    def _():
        @pl.when(g == 1)
        def _():
            link_up.wait_recv()

        others(GROUP // 2, chip, lambda v: link_copy(v, chip).start())

    pairs(6, 8)
    own = pad_rows(collect(gram, LIVE, 0), SLOTS)
    spot, slot = lanes_of((SLOTS, 128)), rows_of((SLOTS, 128))
    own = own + jnp.where((spot == slot) & (slot >= count), 1.0, 0.0)
    sym = jnp.where(spot < LIVE, 0.5 * (own + transposed(own)[:SLOTS]), 0.0)
    blocks_ref[0] = own
    blocks_ref[5] = sym

    @pl.when(joined & (g == 0))
    def _():
        packed = sym[0:16] + pltpu.roll(sym[16:32], LIVE, 1)
        pivs[u] = packed + pltpu.roll(pad_rows(sym[32:40], 16), 2 * LIVE, 1)
        piv_up.start()

    @pl.when(joined)
    def _():
        @pl.when(g == 1)
        def _():
            piv_up.wait_recv()

        others(GROUP, u, lambda v: piv_copy(v, u).start())
        others(GROUP // 2, chip, lambda v: link_copy(chip, v).wait_recv())
        core_copy(core).start()
        others(GROUP, u, lambda v: piv_copy(u, v).wait_recv())
        core_copy(1 - core).wait_recv()
        for v in range(GROUP):
            links_ref[v] = links[v // 2, v % 2]
            pivots_ref[v] = pivs[v]
        others(GROUP // 2, chip, lambda v: link_copy(v, chip).wait_send())
        others(GROUP, u, lambda v: piv_copy(v, u).wait_send())
        core_copy(core).wait_send()

    @pl.when(joined & (g == 0))
    def _():
        link_up.wait_send()
        piv_up.wait_send()

    for k in range(4):
        halo_copy(k).wait_send()
        face_copy(k).wait_send()


def assemble(count, modes, kappa, react):
    vmem = pl.BlockSpec(memory_space=pltpu.VMEM)
    hbm = pl.BlockSpec(memory_space=pltpu.HBM)
    dma = pltpu.SemaphoreType.DMA
    return pl.pallas_call(
        assemble_kernel,
        out_shape=(
            jax.ShapeDtypeStruct((6, SLOTS, 128), F32),
            jax.ShapeDtypeStruct((GROUP, LIVE, 128), F32),
            jax.ShapeDtypeStruct((GROUP, 16, 128), F32),
        ),
        in_specs=[pl.BlockSpec(memory_space=pltpu.SMEM), hbm, hbm, hbm],
        out_specs=(vmem, vmem, vmem),
        scratch_shapes=[
            pltpu.VMEM((CX, LIVE, CY, NZ), BF16),
            pltpu.VMEM((CX, CY, NZ), BF16),
            pltpu.VMEM((CX, CY, NZ), BF16),
            pltpu.VMEM((CX, CY, LIVE, NZ), F32),
            pltpu.VMEM((CX, GRAM, 4 * NZ), BF16),
            pltpu.VMEM((CX + 1, CY, NZ), F32),
            pltpu.VMEM((CX, 24, NZ), F32),
            pltpu.VMEM((CX, CY, NZ), F32),
            pltpu.VMEM((CX, CY, NZ), F32),
            pltpu.VMEM((4, 16, NZ), F32),
            pltpu.VMEM((4, 16, NZ), F32),
            pltpu.VMEM((2, GRAM, 4 * NZ), BF16),
            pltpu.VMEM((2, 16, SLOTS, NZ), BF16),
            pltpu.VMEM((GRAM, 4 * NZ), BF16),
            pltpu.VMEM((GRAM, 4 * NZ), BF16),
            pltpu.VMEM((GRAM, 4 * NZ), BF16),
            pltpu.VMEM((GRAM, 4 * NZ), BF16),
            pltpu.VMEM((GRAM, 256), F32),
            pltpu.VMEM((GRAM, 256), F32),
            pltpu.VMEM((GROUP // 2, 2, LIVE, 128), F32),
            pltpu.VMEM((GROUP, 16, 128), F32),
            dma((CX,)),
            dma((2,)),
            dma((4,)),
            dma((4,)),
            dma((4,)),
            dma((4,)),
            dma((4,)),
            dma((GROUP // 2,)),
            dma((GROUP // 2,)),
            dma((2,)),
            dma((GROUP,)),
            dma((GROUP,)),
        ],
        compiler_params=pltpu.CompilerParams(
            collective_id=0, has_side_effects=True, vmem_limit_bytes=50 * 2**20
        ),
        name="assemble",
    )(count, modes, kappa, react)


def dot3(a, b, dims):
    ah, al = split(a)
    bh, bl = split(b)
    dot = lambda p, q: lax.dot_general(p, q, (dims, ((), ())), preferred_element_type=F32)
    return dot(ah, bh) + (dot(ah, bl) + dot(al, bh))


def nn3(a, b):
    return dot3(a, b, ((1,), (0,)))


def nt3(a, b):
    return dot3(a, b, ((1,), (1,)))


def wide(x):
    return jnp.broadcast_to(x, (8, 128))


def pivots(p, soff, state, spread_ref, rows_ref, side_ref):
    tiles, saved = (list(part) for part in state)
    sub = rows_of((8, 128))
    at = soff + 8 * p
    column = lambda v, c: wide(tiles[v][:, c : c + 1])
    if p == 0:
        for c in range(8):
            spread_ref[p, c] = column(p, at + c)
    rows_ref[p] = tiles[p]
    d = {(i, j): wide(spread_ref[p, j, i : i + 1]) for i in range(8) for j in range(i, 8)}
    rows = [wide(rows_ref[p, c : c + 1]) for c in range(8)]
    follow = p + 1 < LIVE // 8
    if follow:
        under = [column(p + 1, at + c) for c in range(8)]
        coming = [column(p + 1, at + 8 + c) for c in range(8)]
    others = [v for v in range(LIVE // 8) if v not in (p, p + 1)]
    factors = {v: [column(v, at + c) for c in range(8)] for v in others}
    low, rinv = {}, []
    for c in range(8):
        rinv.append(lax.rsqrt(d[c, c]))
        for i in range(c + 1, 8):
            low[c, i] = d[c, i] * rinv[c]
        for i in range(c + 1, 8):
            for j in range(i, 8):
                d[i, j] = d[i, j] - low[c, i] * low[c, j]
        rows[c] = rows[c] * rinv[c]
        saved[p] = jnp.where(sub == c, rows[c], saved[p])
        for i in range(c + 1, 8):
            rows[i] = rows[i] - low[c, i] * rows[c]
        if follow:
            under[c] = under[c] * rinv[c]
            side_ref[p, c] = under[c]
            for i in range(c + 1, 8):
                under[i] = under[i] - low[c, i] * under[c]
            for i in range(8):
                coming[i] = coming[i] - under[c] * wide(side_ref[p, c, i : i + 1])
            tiles[p + 1] = tiles[p + 1] - under[c] * rows[c]
    if follow:
        for c in range(8):
            spread_ref[p + 1, c] = coming[c]
    z = rows
    for c in range(7, -1, -1):
        z[c] = z[c] * rinv[c]
        for i in range(c):
            z[i] = z[i] - low[i, c] * z[c]
    for v in others:
        terms = [factors[v][c] * z[c] for c in range(8)]
        while len(terms) > 1:
            terms = [terms[i] + terms[i + 1] for i in range(0, len(terms), 2)]
        tiles[v] = tiles[v] - terms[0]
    for c in range(8):
        tiles[p] = jnp.where(sub == c, z[c], tiles[p])
    return tuple(tiles), tuple(saved)


def place(out_ref, block, pos, keep):
    base = jnp.minimum((pos // 128) * 128, NC - 256)
    base = pl.multiple_of(base, 128)
    shifted = pltpu.roll(pad_lanes(block, 256), pos - base, 1)
    cols = lanes_of((SLOTS, 256)) + base
    out_ref[:, pl.ds(base, 256)] += jnp.where(keep(cols), shifted, 0.0)


def factor_kernel(
    links_ref, pivots_ref, blocks_ref, out_ref, linv_ref, k_ref, g_ref, f_ref, x_ref, spread_ref, rows_ref, side_ref,
):
    g, u = lax.axis_index("grp"), lax.axis_index("sub")
    s = g * NU + u
    upper = s <= 21
    member = (s == 21) | (s == 22) | ((s >= NU) & (s < NU + NB))
    lane = lanes_of((LIVE, 128))
    row = rows_of((LIVE, 128))
    lane48 = lanes_of((SLOTS, 128))
    row48 = rows_of((SLOTS, 128))
    out_ref[...] = jnp.zeros_like(out_ref)
    before = lambda cols: cols < DONE
    after = lambda cols: cols >= DONE

    def left(x, by):
        x = pltpu.roll(x, 128 - by, 1) if by else x
        return jnp.where(lanes_of(x.shape) < LIVE, x, 0.0)

    def put(block, pos, late):
        base = pos // 128 * 128
        shifted = pltpu.roll(pad_lanes(block, 256), pos - base, 1) if pos > base else (
            pad_lanes(block, 256)
        )
        if base < DONE < base + 256:
            cols = lanes_of((SLOTS, 256)) + base
            shifted = jnp.where(cols >= DONE if late else cols < DONE, shifted, 0.0)
        out_ref[:, base : base + 256] += shifted

    def reduce_row(q):
        at, wide_enough = jnp.maximum(q, 0), jnp.where(q == NB - 1, 16, LIVE)
        mine = jnp.where(q == s, blocks_ref[5], 0.0)
        mine = jnp.where(q == s - 1, blocks_ref[3], mine)
        mine = jnp.where(q == s - NU, blocks_ref[1], mine)
        held = jnp.where(q > 0, f_ref[jnp.maximum(q - 1, 0)], 0.0)
        f = mine - nn3(held, pad_rows(k_ref[at], 128))
        f_ref[at] = jnp.where((q <= s) & (lane48 < wide_enough), f, 0.0)

    def solve_row(q):
        at = jnp.maximum(q, 0)
        x = nt3(f_ref[at], pad_rows(linv_ref[at], 128))
        x_ref[at] = jnp.where((q == s) & (lane48 > row48), 0.0, x)

    def double_row(q):
        at = jnp.maximum(q, 0)
        x = x_ref[at]
        g_ref[at] = nn3(x, pad_rows(linv_ref[at], 128))

    def pivot_block(t, at):
        packed = pivots_ref[t]
        parts = []
        for i in range(3):
            by = (at - LIVE * i) % 128
            parts.append(pltpu.roll(packed, by, 1) if by else packed)
        block = jnp.concatenate([parts[0], parts[1], parts[2][:8]], 0)
        return jnp.where((lane >= at) & (lane < at + LIVE), block, 0.0)

    def live_count(t):
        return jnp.max(jnp.where(lanes_of((8, 128)) >= 3 * LIVE, links_ref[t][0:8], 0.0))

    def at_rows(x, start):
        above = jnp.zeros((start, 128), F32)
        return pad_rows(jnp.concatenate([above, x], 0) if start else x, 128)

    def step(t, odd, scur, n):
        soff, uoff = (LIVE, 0) if odd else (0, LIVE)
        given = links_ref[t]
        limit = jnp.where(t == NB - 1, 16, LIVE)
        in_s = (lane >= soff) & (lane < soff + LIVE)
        in_u = (lane >= uoff) & (lane < uoff + LIVE)
        eye = jnp.where(lane == row + soff, 1.0, 0.0)
        a = jnp.where((row < limit) & (lane < soff + limit), scur, eye)
        rest = jnp.where(lane == row + 2 * LIVE, 1.0, 0.0)
        rest = jnp.where(in_u, jnp.where(row < limit, given, 0.0), rest)
        a = jnp.where(in_s, a, rest)
        ut = jnp.where(in_s, given, 0.0)
        tiles = tuple(a[8 * v : 8 * v + 8] for v in range(LIVE // 8))
        state = pivots(0, soff, (tiles, tiles), spread_ref, rows_ref, side_ref)

        double_row(t - 3)
        solve_row(t - 2)
        reduce_row(t - 1)
        following = jnp.minimum(t + 1, NB - 1)
        coming, coming_n = pivot_block(following, uoff), live_count(following)
        n = jnp.where(t == NB - 1, jnp.minimum(n, 16.0), n)
        for p in range(1, LIVE // 8):
            state = lax.cond(
                n > 8.0 * p,
                lambda st, p=p: pivots(p, soff, st, spread_ref, rows_ref, side_ref),
                lambda st: st,
                state,
            )
        tiles, saved = state
        k = jnp.concatenate(tiles, 0)
        snext = coming - nn3(ut, at_rows(k, soff))
        linv_ref[t] = left(jnp.concatenate(saved, 0), 2 * LIVE)
        k_ref[t + 1] = left(k, uoff)
        return snext, coming_n

    @pl.when(upper | member)
    def _():
        k_ref[0] = jnp.zeros((LIVE, 128), F32)
        linv_ref[0] = jnp.zeros((LIVE, 128), F32)
        f_ref[0] = jnp.zeros((SLOTS, 128), F32)
        x_ref[0] = jnp.zeros((SLOTS, 128), F32)
        def pair(i, carry):
            carry = step(2 * i, False, *carry)
            return step(2 * i + 1, True, *carry)

        lax.fori_loop(0, NB // 2, pair, (pivot_block(0, 0), live_count(0)))
        double_row(NB - 3)
        solve_row(NB - 2)
        reduce_row(NB - 1)
        double_row(NB - 2)
        solve_row(NB - 1)
        double_row(NB - 1)
        for t in range(NB):
            put(x_ref[t], SLOTS * t, False)

    @pl.when(upper)
    def _():
        dead = jnp.where((row48 == lane48) & (row48 >= LIVE), 1.0, 0.0)
        place(out_ref, dead, SLOTS * s, before)

    @pl.when(member)
    def _():
        late = lane >= 16
        last = jnp.where(row < 16, links_ref[NB - 1], 0.0)
        own = jnp.where(late & (row < 16), pivot_block(NB - 1, 0), 0.0)
        over = jnp.where(late, left(links_ref[NB - 2], LIVE), 0.0)
        y = None
        for t in range(NB - 1, -1, -1):
            if y is None:
                y = g_ref[t]
                put(-nn3(y, pad_rows(left(last, 0), 128)), SLOTS * NB, True)
                put(-nn3(y, pad_rows(own, 128)), SLOTS * (NB - 1), True)
            else:
                y = g_ref[t] - nt3(y, pad_rows(k_ref[t + 1], 128))
            if t == NB - 2:
                put(-nn3(y, pad_rows(over, 128)), SLOTS * (NB - 1), True)
            rising = pad_rows(left(links_ref[t], 2 * LIVE), 128)
            put(-nt3(y, rising), SLOTS * (t + NU), True)

    @pl.when(s >= 21)
    def _():
        targets = [s, s - NU, s + NU, s - 1, s + 1]
        valid = [True, g > 0, g < NG - 1, u > 0, u < NU - 1]
        for k in range(5):
            pos = SLOTS * jnp.clip(targets[k], 0, NG * NU - 1)
            place(out_ref, jnp.where(valid[k], blocks_ref[k], 0.0), pos, after)

    @pl.when(s == 21)
    def _():
        out_ref[0:16, DONE:] = jnp.zeros((16, NC - DONE), F32)


def factor(links, pivs, blocks):
    vmem = pl.BlockSpec(memory_space=pltpu.VMEM)
    return pl.pallas_call(
        factor_kernel,
        out_shape=jax.ShapeDtypeStruct((SLOTS, NC), F32),
        in_specs=[vmem, vmem, vmem],
        out_specs=vmem,
        scratch_shapes=[
            pltpu.VMEM((NB, LIVE, 128), F32),
            pltpu.VMEM((NB + 1, LIVE, 128), F32),
            pltpu.VMEM((NB, SLOTS, 128), F32),
            pltpu.VMEM((NB, SLOTS, 128), F32),
            pltpu.VMEM((NB, SLOTS, 128), F32),
            pltpu.VMEM((LIVE // 8, 8, 8, 128), F32),
            pltpu.VMEM((LIVE // 8, 8, 128), F32),
            pltpu.VMEM((LIVE // 8, 8, 8, 128), F32),
        ],
        compiler_params=pltpu.CompilerParams(vmem_limit_bytes=40 * 2**20),
        name="factor",
    )(links, pivs, blocks)


def per_device(modes, counts, kappa, react):
    blocks, links, pivs = assemble(counts, modes, kappa, react)
    return factor(links, pivs, blocks)


def solution(mesh):
    in_specs = (
        P(None, "grp", "sub", None),
        P(("grp", "sub")),
        P("grp", "sub", None),
        P("grp", "sub", None),
    )
    out_specs = P(("grp", "sub"), None)
    return jax.shard_map(
        per_device, mesh=mesh, in_specs=in_specs, out_specs=out_specs, check_vma=False
    )
```

```python
import jax
import jax.numpy as jnp
from jax import lax
from jax.experimental import pallas as pl
from jax.experimental.pallas import tpu as pltpu
from jax.sharding import PartitionSpec as P

F32 = jnp.float32
BF16 = jnp.bfloat16
MESH = pl.DeviceIdType.MESH
NG, NU = 4, 32
CX, CY, NZ = 16, 16, 256
SLOTS, LIVE = 48, 40
NB = 22
DONE = 1024
GROUP = 24
GRAM = 4 * LIVE
NC = SLOTS * NG * NU


def nt(a, b, precision=None):
    return lax.dot_general(
        a, b, (((1,), (1,)), ((), ())), preferred_element_type=F32, precision=precision
    )


def lanes_of(shape):
    return lax.broadcasted_iota(jnp.int32, shape, len(shape) - 1)


def rows_of(shape):
    return lax.broadcasted_iota(jnp.int32, shape, len(shape) - 2)


def split(x):
    hi = x.astype(BF16)
    return hi, (x - hi.astype(F32)).astype(BF16)


def pad_rows(x, rows):
    return jnp.concatenate([x, jnp.zeros((rows - x.shape[0], x.shape[1]), x.dtype)], 0)


def pad_lanes(x, lanes):
    return jnp.concatenate([x, jnp.zeros((x.shape[0], lanes - x.shape[1]), x.dtype)], 1)


def transposed(x):
    return jnp.transpose(pad_rows(x, 128))


def assemble_kernel(
    count_ref, modes_ref, kappa_ref, react_ref, blocks_ref, links_ref, pivots_ref,
    raw, kappa, react, field, masked, wx, wy, wz, diag, edge, halo, face_x, face_y,
    local0, local1, high, low, gram, side, links, pivs, order, turned,
    raw_sem, cell_sem, halo_send, halo_recv, face_send, face_recv,
    up_sem, link_send, link_recv, core_sem, piv_send, piv_recv,
):
    g, u = lax.axis_index("grp"), lax.axis_index("sub")
    partners = [
        (lax.rem(g + NG - 1, NG), u),
        (lax.rem(g + 1, NG), u),
        (g, lax.rem(u + NU - 1, NU)),
        (g, lax.rem(u + 1, NU)),
    ]
    inside = [g > 0, g < NG - 1, u > 0, u < NU - 1]
    mirror = [1, 0, 3, 2]
    chip, core = u // 2, lax.rem(u, 2)
    joined = (g < 2) & (u < GROUP)

    def fetch(x):
        return pltpu.make_async_copy(
            modes_ref.at[pl.ds(0, LIVE), x], raw.at[x], raw_sem.at[x]
        )

    cells = [
        pltpu.make_async_copy(kappa_ref, kappa, cell_sem.at[0]),
        pltpu.make_async_copy(react_ref, react, cell_sem.at[1]),
    ]
    cells[0].start()
    for x in [0, CX - 1] + list(range(1, CX - 1)):
        fetch(x).start()
    cells[1].start()

    barrier = pltpu.get_barrier_semaphore()

    def greet(device):
        pl.semaphore_signal(barrier, inc=1, device_id=device, device_id_type=MESH)

    for partner in partners:
        greet(partner)

    def others(count, me, act):
        def body(v, carry):
            @pl.when(v != me)
            def _():
                act(v)
            return carry

        lax.fori_loop(0, count, body, 0)

    @pl.when(joined)
    def _():
        others(GROUP, u, lambda v: greet((g, v)))

    def ones_where(mask):
        return jnp.where(mask, 1.0, 0.0).astype(BF16)

    count = count_ref[0]
    z_from, z_to = rows_of((NZ, NZ)), lanes_of((NZ, NZ))
    order[...] = ones_where(z_from == jnp.where(z_to < 128, 2 * z_to, 2 * z_to - 255))
    r_to, r_from = rows_of((128, 128)), lanes_of((128, 128))
    slot8 = r_to & 7
    for i in range(LIVE // 8):
        turned[i] = ones_where((r_from == slot8 * 16 + (r_to >> 3)) & (slot8 + 8 * i < count))

    def ordered(x):
        return jnp.dot(x.reshape(-1, NZ), order[...], preferred_element_type=F32)

    cells[0].wait()
    kap = ordered(kappa[...]).reshape(CX, CY, NZ)
    edge[0] = kap[0]
    edge[1] = kap[CX - 1]
    for x in range(CX):
        edge[2, x : x + 1] = kap[x, 0:1]
        edge[3, x : x + 1] = kap[x, CY - 1 : CY]

    def turn(x):
        fetch(x).wait()
        flat = ordered(raw[x]).astype(BF16)
        parts = [
            jnp.dot(turned[i], flat[128 * i : 128 * (i + 1)], preferred_element_type=F32)
            for i in range(LIVE // 8)
        ]
        for y in range(0, CY, 2):
            r, c = LIVE * (y % 4), NZ * (y // 4)
            two = [jnp.concatenate([p[8 * w : 8 * w + 8] for p in parts], 0) for w in (y, y + 1)]
            field[x, y], field[x, y + 1] = two
            masked[x, r : r + 2 * LIVE, c : c + NZ] = jnp.concatenate(two, 0).astype(BF16)

    turn(0)
    turn(CX - 1)
    pl.semaphore_wait(barrier, jnp.where(joined, GROUP + 3, 4))

    def halo_copy(k):
        return pltpu.make_async_remote_copy(
            src_ref=edge.at[k], dst_ref=halo.at[mirror[k]],
            send_sem=halo_send.at[k], recv_sem=halo_recv.at[mirror[k]],
            device_id=partners[k], device_id_type=MESH,
        )

    sources = [
        masked.at[0],
        masked.at[CX - 1],
        masked.at[:, pl.ds(0, SLOTS), pl.ds(0, NZ)],
        masked.at[:, pl.ds(GRAM - SLOTS, SLOTS), pl.ds(3 * NZ, NZ)],
    ]
    landings = [face_x.at[0], face_x.at[1], face_y.at[0], face_y.at[1]]

    def face_copy(k):
        return pltpu.make_async_remote_copy(
            src_ref=sources[k], dst_ref=landings[mirror[k]],
            send_sem=face_send.at[k], recv_sem=face_recv.at[mirror[k]],
            device_id=partners[k], device_id_type=MESH,
        )

    for k in range(4):
        halo_copy(k).start()
    face_copy(0).start()
    face_copy(1).start()

    def turn_next(x, carry):
        turn(x)
        return carry

    lax.fori_loop(1, CX - 1, turn_next, 0)
    face_copy(2).start()
    face_copy(3).start()

    plane0 = jnp.zeros((CY, NZ), F32)
    row0 = jnp.zeros((1, NZ), F32)
    half = lanes_of((CY, 128))
    wx[0] = plane0
    wx[CX] = plane0
    for x in range(CX - 1):
        wx[x + 1] = 0.5 * (kap[x] + kap[x + 1])
    for x in range(CX):
        k = kap[x]
        wy[x, 0:1] = row0
        wy[x, 1:CY] = 0.5 * (k[: CY - 1] + k[1:])
        wy[x, CY : CY + 1] = row0
        even, uneven = k[:, :128], k[:, 128:]
        wz[x, :, 0:128] = 0.5 * (even + uneven)
        wz[x, :, 128:] = jnp.where(half == 127, 0.0, 0.5 * (uneven + pltpu.roll(even, 127, 1)))
    cells[1].wait()
    reac = ordered(react[...]).reshape(CX, CY, NZ)
    for k in range(4):
        halo_copy(k).wait_recv()
    ext = [jnp.where(inside[k], halo[k], 0.0) for k in range(4)]
    bound = [0.5 * (edge[k] + ext[k]) for k in range(4)]
    for x in range(CX):
        k = kap[x]
        inner, outer = wz[x, :, 0:128], wz[x, :, 128:]
        below = jnp.where(half == 0, 0.5 * k[:, :128], pltpu.roll(outer, 1, 1))
        above = jnp.where(half == 127, 0.5 * k[:, 128:], outer)
        dz = jnp.concatenate([below + inner, inner + above], 1)
        dx = (bound[0] if x == 0 else wx[x]) + (bound[1] if x == CX - 1 else wx[x + 1])
        dy = wy[x, 0:CY] + wy[x, 1 : CY + 1]
        dy = dy + jnp.concatenate(
            [bound[2][x : x + 1], jnp.zeros((CY - 2, NZ), F32), bound[3][x : x + 1]], 0
        )
        diag[x] = reac[x] + dx + dy + dz

    def apply(x, local):
        before, after = jnp.maximum(x - 1, 0), jnp.minimum(x + 1, CX - 1)
        behind, v, done = None, field[x, 0], None
        for y in range(CY):
            ahead = field[x, y + 1] if y < CY - 1 else None
            out = diag[x, y : y + 1] * v
            out = out - wx[x, y : y + 1] * field[before, y]
            out = out - wx[x + 1, y : y + 1] * field[after, y]
            if y > 0:
                out = out - wy[x, y : y + 1] * behind
            if y < CY - 1:
                out = out - wy[x, y + 1 : y + 2] * ahead
            even, uneven = v[:, :128], v[:, 128:]
            inner, outer = wz[x, y : y + 1, 0:128], wz[x, y : y + 1, 128:]
            out = out - jnp.concatenate(
                [
                    inner * uneven + pltpu.roll(outer * uneven, 1, 1),
                    inner * even + outer * pltpu.roll(even, 127, 1),
                ],
                1,
            )
            if y % 2:
                r, c = LIVE * (y % 4 - 1), NZ * (y // 4)
                two = jnp.concatenate([done, out], 0)
                local[r : r + 2 * LIVE, c : c + NZ] = two.astype(BF16)
            done = out
            behind, v = v, ahead

    def collect(total, step, start):
        out = jnp.zeros((LIVE, 128), F32)
        for i in range(4):
            part, by = total[LIVE * i : LIVE * (i + 1), :], step * i + start
            part = pltpu.roll(part, 256 - by, 1) if by else part
            out = out + part[:, :128]
        return jnp.where(lanes_of((LIVE, 128)) < LIVE, out, 0.0)

    gram[...] = jnp.zeros_like(gram)

    def pairs(begin, end):
        local1[...] = jnp.zeros_like(local1)

        def pair(i, carry):
            x = 2 * i
            gram[:, 0:GRAM] += nt(masked[jnp.maximum(x - 1, 0)], local1[...])
            apply(x, local0)
            gram[:, 0:GRAM] += nt(masked[x], local0[...])
            apply(x + 1, local1)
            return carry

        lax.fori_loop(begin, end, pair, 0)
        gram[:, 0:GRAM] += nt(masked[2 * end - 1], local1[...])

    pairs(0, 5)

    found = []
    for k in range(4):
        weight = bound[k]
        for i in range(0, 16, 2):
            two = []
            for j in (i, i + 1):
                mine = field[0 if k == 0 else CX - 1, j] if k < 2 else (
                    field[j, 0 if k == 2 else CY - 1]
                )
                two.append(mine * weight[j : j + 1])
            hi, lo = split(jnp.concatenate(two, 0))
            r, c = LIVE * (i % 4), NZ * (i // 4)
            high[r : r + 2 * LIVE, c : c + NZ] = hi
            low[r : r + 2 * LIVE, c : c + NZ] = lo
        face_copy(mirror[k]).wait_recv()
        if k < 2:
            other = face_x[k]
            side[:, 0:GRAM] = -(nt(high[...], other) + nt(low[...], other))
            block = collect(side, LIVE, 0)
        else:
            total = jnp.zeros((GRAM, 4 * SLOTS), F32)
            for q in range(4):
                other = face_y[k - 2, 4 * q : 4 * q + 4].reshape(4 * SLOTS, NZ)
                cols = slice(NZ * q, NZ * (q + 1))
                total = total + nt(high[:, cols], other) + nt(low[:, cols], other)
            side[:, 0 : 4 * SLOTS] = -total
            block = collect(side, SLOTS, SLOTS - LIVE if k == 2 else 0)
        found.append(jnp.where(inside[k], block, 0.0))
    for k in range(4):
        blocks_ref[k + 1] = pad_rows(found[k], SLOTS)

    lane = lanes_of((LIVE, 128))
    odd = core == 1
    ahead = found[3]
    ahead_t = transposed(ahead)[:LIVE]
    message = jnp.where(odd, ahead, ahead_t) + pltpu.roll(jnp.where(odd, ahead_t, ahead), LIVE, 1)
    message = message + pltpu.roll(transposed(found[1])[:LIVE], 2 * LIVE, 1)
    message = jnp.where(lane >= 3 * LIVE, count.astype(F32), message)

    def up_copy(ref, i):
        return pltpu.make_async_remote_copy(
            src_ref=ref, dst_ref=ref, send_sem=up_sem.at[i], recv_sem=up_sem.at[i + 2],
            device_id=(1, u), device_id_type=MESH,
        )

    def link_copy(to, owner):
        return pltpu.make_async_remote_copy(
            src_ref=links.at[owner, core], dst_ref=links.at[owner, core],
            send_sem=link_send.at[to], recv_sem=link_recv.at[owner],
            device_id=(g, 2 * to + core), device_id_type=MESH,
        )

    def core_copy(c):
        return pltpu.make_async_remote_copy(
            src_ref=links.at[:, c], dst_ref=links.at[:, c],
            send_sem=core_sem.at[0], recv_sem=core_sem.at[1],
            device_id=(g, 2 * chip + 1 - core), device_id_type=MESH,
        )

    def piv_copy(to, owner):
        return pltpu.make_async_remote_copy(
            src_ref=pivs.at[owner], dst_ref=pivs.at[owner],
            send_sem=piv_send.at[to], recv_sem=piv_recv.at[owner],
            device_id=(g, to), device_id_type=MESH,
        )

    link_up, piv_up = up_copy(links.at[chip, core], 0), up_copy(pivs.at[u], 1)

    @pl.when(joined & (g == 0))
    def _():
        links[chip, core] = message
        link_up.start()

    pairs(5, 7)

    @pl.when(joined)
    def _():
        @pl.when(g == 1)
        def _():
            link_up.wait_recv()

        others(GROUP // 2, chip, lambda v: link_copy(v, chip).start())

    pairs(7, 8)
    own = pad_rows(collect(gram, LIVE, 0), SLOTS)
    spot, slot = lanes_of((SLOTS, 128)), rows_of((SLOTS, 128))
    own = own + jnp.where((spot == slot) & (slot >= count), 1.0, 0.0)
    sym = jnp.where(spot < LIVE, 0.5 * (own + transposed(own)[:SLOTS]), 0.0)
    blocks_ref[0] = own
    blocks_ref[5] = sym

    @pl.when(joined & (g == 0))
    def _():
        packed = sym[0:16] + pltpu.roll(sym[16:32], LIVE, 1)
        pivs[u] = packed + pltpu.roll(pad_rows(sym[32:40], 16), 2 * LIVE, 1)
        piv_up.start()

    @pl.when(joined)
    def _():
        @pl.when(g == 1)
        def _():
            piv_up.wait_recv()

        others(GROUP, u, lambda v: piv_copy(v, u).start())
        others(GROUP // 2, chip, lambda v: link_copy(chip, v).wait_recv())
        core_copy(core).start()
        others(GROUP, u, lambda v: piv_copy(u, v).wait_recv())
        core_copy(1 - core).wait_recv()
        for v in range(GROUP):
            links_ref[v] = links[v // 2, v % 2]
            pivots_ref[v] = pivs[v]
        others(GROUP // 2, chip, lambda v: link_copy(v, chip).wait_send())
        others(GROUP, u, lambda v: piv_copy(v, u).wait_send())
        core_copy(core).wait_send()

    @pl.when(joined & (g == 0))
    def _():
        link_up.wait_send()
        piv_up.wait_send()

    for k in range(4):
        halo_copy(k).wait_send()
        face_copy(k).wait_send()


def assemble(count, modes, kappa, react):
    vmem = pl.BlockSpec(memory_space=pltpu.VMEM)
    hbm = pl.BlockSpec(memory_space=pltpu.HBM)
    dma = pltpu.SemaphoreType.DMA
    return pl.pallas_call(
        assemble_kernel,
        out_shape=(
            jax.ShapeDtypeStruct((6, SLOTS, 128), F32),
            jax.ShapeDtypeStruct((GROUP, LIVE, 128), F32),
            jax.ShapeDtypeStruct((GROUP, 16, 128), F32),
        ),
        in_specs=[pl.BlockSpec(memory_space=pltpu.SMEM), hbm, hbm, hbm],
        out_specs=(vmem, vmem, vmem),
        scratch_shapes=[
            pltpu.VMEM((CX, LIVE, CY, NZ), BF16),
            pltpu.VMEM((CX, CY, NZ), BF16),
            pltpu.VMEM((CX, CY, NZ), BF16),
            pltpu.VMEM((CX, CY, LIVE, NZ), F32),
            pltpu.VMEM((CX, GRAM, 4 * NZ), BF16),
            pltpu.VMEM((CX + 1, CY, NZ), F32),
            pltpu.VMEM((CX, 24, NZ), F32),
            pltpu.VMEM((CX, CY, NZ), F32),
            pltpu.VMEM((CX, CY, NZ), F32),
            pltpu.VMEM((4, 16, NZ), F32),
            pltpu.VMEM((4, 16, NZ), F32),
            pltpu.VMEM((2, GRAM, 4 * NZ), BF16),
            pltpu.VMEM((2, 16, SLOTS, NZ), BF16),
            pltpu.VMEM((GRAM, 4 * NZ), BF16),
            pltpu.VMEM((GRAM, 4 * NZ), BF16),
            pltpu.VMEM((GRAM, 4 * NZ), BF16),
            pltpu.VMEM((GRAM, 4 * NZ), BF16),
            pltpu.VMEM((GRAM, 256), F32),
            pltpu.VMEM((GRAM, 256), F32),
            pltpu.VMEM((GROUP // 2, 2, LIVE, 128), F32),
            pltpu.VMEM((GROUP, 16, 128), F32),
            pltpu.VMEM((NZ, NZ), BF16),
            pltpu.VMEM((LIVE // 8, 128, 128), BF16),
            dma((CX,)),
            dma((2,)),
            dma((4,)),
            dma((4,)),
            dma((4,)),
            dma((4,)),
            dma((4,)),
            dma((GROUP // 2,)),
            dma((GROUP // 2,)),
            dma((2,)),
            dma((GROUP,)),
            dma((GROUP,)),
        ],
        compiler_params=pltpu.CompilerParams(
            collective_id=0, has_side_effects=True, vmem_limit_bytes=50 * 2**20
        ),
        name="assemble",
    )(count, modes, kappa, react)


def dot3(a, b, dims):
    ah, al = split(a)
    bh, bl = split(b)
    dot = lambda p, q: lax.dot_general(p, q, (dims, ((), ())), preferred_element_type=F32)
    return dot(ah, bh) + (dot(ah, bl) + dot(al, bh))


def nn3(a, b):
    return dot3(a, b, ((1,), (0,)))


def nt3(a, b):
    return dot3(a, b, ((1,), (1,)))


def wide(x):
    return jnp.broadcast_to(x, (8, 128))


def pivots(p, soff, state, spread_ref, rows_ref, side_ref):
    tiles, saved = (list(part) for part in state)
    sub = rows_of((8, 128))
    at = soff + 8 * p
    column = lambda v, c: wide(tiles[v][:, c : c + 1])
    if p == 0:
        for c in range(8):
            spread_ref[p, c] = column(p, at + c)
    rows_ref[p] = tiles[p]
    d = {(i, j): wide(spread_ref[p, j, i : i + 1]) for i in range(8) for j in range(i, 8)}
    rows = [wide(rows_ref[p, c : c + 1]) for c in range(8)]
    follow = p + 1 < LIVE // 8
    if follow:
        under = [column(p + 1, at + c) for c in range(8)]
        coming = [column(p + 1, at + 8 + c) for c in range(8)]
    others = [v for v in range(LIVE // 8) if v not in (p, p + 1)]
    factors = {v: [column(v, at + c) for c in range(8)] for v in others}
    low, rinv = {}, []
    for c in range(8):
        rinv.append(lax.rsqrt(d[c, c]))
        for i in range(c + 1, 8):
            low[c, i] = d[c, i] * rinv[c]
        for i in range(c + 1, 8):
            for j in range(i, 8):
                d[i, j] = d[i, j] - low[c, i] * low[c, j]
        rows[c] = rows[c] * rinv[c]
        saved[p] = jnp.where(sub == c, rows[c], saved[p])
        for i in range(c + 1, 8):
            rows[i] = rows[i] - low[c, i] * rows[c]
        if follow:
            under[c] = under[c] * rinv[c]
            side_ref[p, c] = under[c]
            for i in range(c + 1, 8):
                under[i] = under[i] - low[c, i] * under[c]
            for i in range(8):
                coming[i] = coming[i] - under[c] * wide(side_ref[p, c, i : i + 1])
            tiles[p + 1] = tiles[p + 1] - under[c] * rows[c]
    if follow:
        for c in range(8):
            spread_ref[p + 1, c] = coming[c]
    z = rows
    for c in range(7, -1, -1):
        z[c] = z[c] * rinv[c]
        for i in range(c):
            z[i] = z[i] - low[i, c] * z[c]
    for v in others:
        terms = [factors[v][c] * z[c] for c in range(8)]
        while len(terms) > 1:
            terms = [terms[i] + terms[i + 1] for i in range(0, len(terms), 2)]
        tiles[v] = tiles[v] - terms[0]
    for c in range(8):
        tiles[p] = jnp.where(sub == c, z[c], tiles[p])
    return tuple(tiles), tuple(saved)


def place(out_ref, block, pos, keep):
    base = jnp.minimum((pos // 128) * 128, NC - 256)
    base = pl.multiple_of(base, 128)
    shifted = pltpu.roll(pad_lanes(block, 256), pos - base, 1)
    cols = lanes_of((SLOTS, 256)) + base
    out_ref[:, pl.ds(base, 256)] += jnp.where(keep(cols), shifted, 0.0)


def factor_kernel(
    links_ref, pivots_ref, blocks_ref, out_ref, linv_ref, k_ref, g_ref, f_ref, x_ref, spread_ref, rows_ref, side_ref,
):
    g, u = lax.axis_index("grp"), lax.axis_index("sub")
    s = g * NU + u
    upper = s <= 21
    member = (s == 21) | (s == 22) | ((s >= NU) & (s < NU + NB))
    lane = lanes_of((LIVE, 128))
    row = rows_of((LIVE, 128))
    lane48 = lanes_of((SLOTS, 128))
    row48 = rows_of((SLOTS, 128))
    out_ref[...] = jnp.zeros_like(out_ref)
    before = lambda cols: cols < DONE
    after = lambda cols: cols >= DONE

    def left(x, by):
        x = pltpu.roll(x, 128 - by, 1) if by else x
        return jnp.where(lanes_of(x.shape) < LIVE, x, 0.0)

    def put(block, pos, late):
        base = pos // 128 * 128
        shifted = pltpu.roll(pad_lanes(block, 256), pos - base, 1) if pos > base else (
            pad_lanes(block, 256)
        )
        if base < DONE < base + 256:
            cols = lanes_of((SLOTS, 256)) + base
            shifted = jnp.where(cols >= DONE if late else cols < DONE, shifted, 0.0)
        out_ref[:, base : base + 256] += shifted

    def reduce_row(q):
        at, wide_enough = jnp.maximum(q, 0), jnp.where(q == NB - 1, 16, LIVE)
        mine = jnp.where(q == s, blocks_ref[5], 0.0)
        mine = jnp.where(q == s - 1, blocks_ref[3], mine)
        mine = jnp.where(q == s - NU, blocks_ref[1], mine)
        held = jnp.where(q > 0, f_ref[jnp.maximum(q - 1, 0)], 0.0)
        f = mine - nn3(held, pad_rows(k_ref[at], 128))
        f_ref[at] = jnp.where((q <= s) & (lane48 < wide_enough), f, 0.0)

    def solve_row(q):
        at = jnp.maximum(q, 0)
        x = nt3(f_ref[at], pad_rows(linv_ref[at], 128))
        x_ref[at] = jnp.where((q == s) & (lane48 > row48), 0.0, x)

    def double_row(q):
        at = jnp.maximum(q, 0)
        x = x_ref[at]
        g_ref[at] = nn3(x, pad_rows(linv_ref[at], 128))

    def pivot_block(t, at):
        packed = pivots_ref[t]
        parts = []
        for i in range(3):
            by = (at - LIVE * i) % 128
            parts.append(pltpu.roll(packed, by, 1) if by else packed)
        block = jnp.concatenate([parts[0], parts[1], parts[2][:8]], 0)
        return jnp.where((lane >= at) & (lane < at + LIVE), block, 0.0)

    def live_count(t):
        return jnp.max(jnp.where(lanes_of((8, 128)) >= 3 * LIVE, links_ref[t][0:8], 0.0))

    def at_rows(x, start):
        above = jnp.zeros((start, 128), F32)
        return pad_rows(jnp.concatenate([above, x], 0) if start else x, 128)

    def step(t, odd, scur, n):
        soff, uoff = (LIVE, 0) if odd else (0, LIVE)
        given = links_ref[t]
        limit = jnp.where(t == NB - 1, 16, LIVE)
        in_s = (lane >= soff) & (lane < soff + LIVE)
        in_u = (lane >= uoff) & (lane < uoff + LIVE)
        eye = jnp.where(lane == row + soff, 1.0, 0.0)
        a = jnp.where((row < limit) & (lane < soff + limit), scur, eye)
        rest = jnp.where(lane == row + 2 * LIVE, 1.0, 0.0)
        rest = jnp.where(in_u, jnp.where(row < limit, given, 0.0), rest)
        a = jnp.where(in_s, a, rest)
        ut = jnp.where(in_s, given, 0.0)
        tiles = tuple(a[8 * v : 8 * v + 8] for v in range(LIVE // 8))
        state = pivots(0, soff, (tiles, tiles), spread_ref, rows_ref, side_ref)

        double_row(t - 3)
        solve_row(t - 2)
        reduce_row(t - 1)
        following = jnp.minimum(t + 1, NB - 1)
        coming, coming_n = pivot_block(following, uoff), live_count(following)
        n = jnp.where(t == NB - 1, jnp.minimum(n, 16.0), n)
        for p in range(1, LIVE // 8):
            state = lax.cond(
                n > 8.0 * p,
                lambda st, p=p: pivots(p, soff, st, spread_ref, rows_ref, side_ref),
                lambda st: st,
                state,
            )
        tiles, saved = state
        k = jnp.concatenate(tiles, 0)
        snext = coming - nn3(ut, at_rows(k, soff))
        linv_ref[t] = left(jnp.concatenate(saved, 0), 2 * LIVE)
        k_ref[t + 1] = left(k, uoff)
        return snext, coming_n

    @pl.when(upper | member)
    def _():
        k_ref[0] = jnp.zeros((LIVE, 128), F32)
        linv_ref[0] = jnp.zeros((LIVE, 128), F32)
        f_ref[0] = jnp.zeros((SLOTS, 128), F32)
        x_ref[0] = jnp.zeros((SLOTS, 128), F32)
        def pair(i, carry):
            carry = step(2 * i, False, *carry)
            return step(2 * i + 1, True, *carry)

        lax.fori_loop(0, NB // 2, pair, (pivot_block(0, 0), live_count(0)))
        double_row(NB - 3)
        solve_row(NB - 2)
        reduce_row(NB - 1)
        double_row(NB - 2)
        solve_row(NB - 1)
        double_row(NB - 1)
        for t in range(NB):
            put(x_ref[t], SLOTS * t, False)

    @pl.when(upper)
    def _():
        dead = jnp.where((row48 == lane48) & (row48 >= LIVE), 1.0, 0.0)
        place(out_ref, dead, SLOTS * s, before)

    @pl.when(member)
    def _():
        late = lane >= 16
        last = jnp.where(row < 16, links_ref[NB - 1], 0.0)
        own = jnp.where(late & (row < 16), pivot_block(NB - 1, 0), 0.0)
        over = jnp.where(late, left(links_ref[NB - 2], LIVE), 0.0)
        y = None
        for t in range(NB - 1, -1, -1):
            if y is None:
                y = g_ref[t]
                put(-nn3(y, pad_rows(left(last, 0), 128)), SLOTS * NB, True)
                put(-nn3(y, pad_rows(own, 128)), SLOTS * (NB - 1), True)
            else:
                y = g_ref[t] - nt3(y, pad_rows(k_ref[t + 1], 128))
            if t == NB - 2:
                put(-nn3(y, pad_rows(over, 128)), SLOTS * (NB - 1), True)
            rising = pad_rows(left(links_ref[t], 2 * LIVE), 128)
            put(-nt3(y, rising), SLOTS * (t + NU), True)

    @pl.when(s >= 21)
    def _():
        targets = [s, s - NU, s + NU, s - 1, s + 1]
        valid = [True, g > 0, g < NG - 1, u > 0, u < NU - 1]
        for k in range(5):
            pos = SLOTS * jnp.clip(targets[k], 0, NG * NU - 1)
            place(out_ref, jnp.where(valid[k], blocks_ref[k], 0.0), pos, after)

    @pl.when(s == 21)
    def _():
        out_ref[0:16, DONE:] = jnp.zeros((16, NC - DONE), F32)


def factor(links, pivs, blocks):
    vmem = pl.BlockSpec(memory_space=pltpu.VMEM)
    return pl.pallas_call(
        factor_kernel,
        out_shape=jax.ShapeDtypeStruct((SLOTS, NC), F32),
        in_specs=[vmem, vmem, vmem],
        out_specs=vmem,
        scratch_shapes=[
            pltpu.VMEM((NB, LIVE, 128), F32),
            pltpu.VMEM((NB + 1, LIVE, 128), F32),
            pltpu.VMEM((NB, SLOTS, 128), F32),
            pltpu.VMEM((NB, SLOTS, 128), F32),
            pltpu.VMEM((NB, SLOTS, 128), F32),
            pltpu.VMEM((LIVE // 8, 8, 8, 128), F32),
            pltpu.VMEM((LIVE // 8, 8, 128), F32),
            pltpu.VMEM((LIVE // 8, 8, 8, 128), F32),
        ],
        compiler_params=pltpu.CompilerParams(vmem_limit_bytes=40 * 2**20),
        name="factor",
    )(links, pivs, blocks)


def per_device(modes, counts, kappa, react):
    blocks, links, pivs = assemble(counts, modes, kappa, react)
    return factor(links, pivs, blocks)


def solution(mesh):
    in_specs = (
        P(None, "grp", "sub", None),
        P(("grp", "sub")),
        P("grp", "sub", None),
        P("grp", "sub", None),
    )
    out_specs = P(("grp", "sub"), None)
    return jax.shard_map(
        per_device, mesh=mesh, in_specs=in_specs, out_specs=out_specs, check_vma=False
    )
```

```python
import jax
import jax.numpy as jnp
from jax import lax
from jax.experimental import pallas as pl
from jax.experimental.pallas import tpu as pltpu
from jax.sharding import PartitionSpec as P

F32 = jnp.float32
BF16 = jnp.bfloat16
MESH = pl.DeviceIdType.MESH
NG, NU = 4, 32
CX, CY, NZ = 16, 16, 256
SLOTS, LIVE = 48, 40
NB = 22
DONE = 1024
GROUP = 24
NC = SLOTS * NG * NU


def nt(a, b, precision=None):
    return lax.dot_general(
        a, b, (((1,), (1,)), ((), ())), preferred_element_type=F32, precision=precision
    )


def lanes_of(shape):
    return lax.broadcasted_iota(jnp.int32, shape, len(shape) - 1)


def rows_of(shape):
    return lax.broadcasted_iota(jnp.int32, shape, len(shape) - 2)


def split(x):
    hi = x.astype(BF16)
    return hi, (x - hi.astype(F32)).astype(BF16)


def pad_rows(x, rows):
    return jnp.concatenate([x, jnp.zeros((rows - x.shape[0], x.shape[1]), x.dtype)], 0)


def pad_lanes(x, lanes):
    return jnp.concatenate([x, jnp.zeros((x.shape[0], lanes - x.shape[1]), x.dtype)], 1)


def transposed(x):
    return jnp.transpose(pad_rows(x, 128))


def assemble_kernel(
    count_ref, modes_ref, kappa_ref, react_ref, blocks_ref, links_ref, pivots_ref,
    raw, kappa, react, field, masked, wx, wy, wz, diag, edge, halo, face_x, face_y,
    high, low, ends, links, pivs, order,
    raw_sem, cell_sem, halo_send, halo_recv, face_send, face_recv,
    up_sem, link_send, link_recv, core_sem, piv_send, piv_recv,
):
    g, u = lax.axis_index("grp"), lax.axis_index("sub")
    partners = [
        (lax.rem(g + NG - 1, NG), u),
        (lax.rem(g + 1, NG), u),
        (g, lax.rem(u + NU - 1, NU)),
        (g, lax.rem(u + 1, NU)),
    ]
    inside = [g > 0, g < NG - 1, u > 0, u < NU - 1]
    mirror = [1, 0, 3, 2]
    chip, core = u // 2, lax.rem(u, 2)
    joined = (g < 2) & (u < GROUP)

    def fetch(x):
        return pltpu.make_async_copy(
            modes_ref.at[pl.ds(0, LIVE), x], raw.at[x], raw_sem.at[x]
        )

    cells = [
        pltpu.make_async_copy(kappa_ref, kappa, cell_sem.at[0]),
        pltpu.make_async_copy(react_ref, react, cell_sem.at[1]),
    ]
    cells[0].start()
    for x in [0, CX - 1] + list(range(1, CX - 1)):
        fetch(x).start()
    cells[1].start()

    barrier = pltpu.get_barrier_semaphore()

    def greet(device):
        pl.semaphore_signal(barrier, inc=1, device_id=device, device_id_type=MESH)

    for partner in partners:
        greet(partner)

    def others(count, me, act):
        for step in range(1, count):
            v = me + step
            act(jnp.where(v >= count, v - count, v))

    @pl.when(joined)
    def _():
        others(GROUP, u, lambda v: greet((g, v)))

    count = count_ref[0]
    z_from, z_to = rows_of((NZ, NZ)), lanes_of((NZ, NZ))
    here = z_from == jnp.where(z_to < 128, 2 * z_to, 2 * z_to - 255)
    order[...] = jnp.where(here, 1.0, 0.0).astype(BF16)

    def ordered(x):
        return jnp.dot(x.reshape(-1, NZ), order[...], preferred_element_type=F32)

    cells[0].wait()
    kap = ordered(kappa[...]).reshape(CX, CY, NZ)
    edge[0] = kap[0]
    edge[1] = kap[CX - 1]
    for x in range(CX):
        edge[2, x : x + 1] = kap[x, 0:1]
        edge[3, x : x + 1] = kap[x, CY - 1 : CY]

    live = rows_of((CY, LIVE, NZ)) < count

    def turn(x, side=None):
        plane = jnp.swapaxes(ordered(raw[x]).reshape(LIVE, CY, NZ), 0, 1)
        plane = jnp.where(live, plane, 0.0)
        field[x] = plane
        for y in range(CY):
            masked[x, :, NZ * y : NZ * (y + 1)] = pad_rows(plane[y], SLOTS).astype(BF16)
        if side is not None:
            for y in range(0, CY, 2):
                two = jnp.concatenate([plane[y], plane[y + 1]], 0)
                ends[side, :, NZ * y // 2 : NZ * (y + 2) // 2] = two.astype(BF16)

    fetch(0).wait()
    fetch(CX - 1).wait()
    turn(0, 0)
    turn(CX - 1, 1)
    pl.semaphore_wait(barrier, jnp.where(joined, GROUP + 3, 4))

    def halo_copy(k):
        return pltpu.make_async_remote_copy(
            src_ref=edge.at[k], dst_ref=halo.at[mirror[k]],
            send_sem=halo_send.at[k], recv_sem=halo_recv.at[mirror[k]],
            device_id=partners[k], device_id_type=MESH,
        )

    sources = [
        ends.at[0],
        ends.at[1],
        masked.at[:, :, pl.ds(0, NZ)],
        masked.at[:, :, pl.ds((CY - 1) * NZ, NZ)],
    ]
    landings = [face_x.at[0], face_x.at[1], face_y.at[0], face_y.at[1]]

    def face_copy(k):
        return pltpu.make_async_remote_copy(
            src_ref=sources[k], dst_ref=landings[mirror[k]],
            send_sem=face_send.at[k], recv_sem=face_recv.at[mirror[k]],
            device_id=partners[k], device_id_type=MESH,
        )

    for k in range(4):
        halo_copy(k).start()
    face_copy(0).start()
    face_copy(1).start()

    def turn_next(i, carry):
        fetch(2 * i + 1).wait()
        fetch(2 * i + 2).wait()
        turn(2 * i + 1)
        turn(2 * i + 2)
        return carry

    lax.fori_loop(0, CX // 2 - 1, turn_next, 0)
    face_copy(2).start()
    face_copy(3).start()

    plane0 = jnp.zeros((CY, NZ), F32)
    row0 = jnp.zeros((1, NZ), F32)
    half = lanes_of((CY, 128))
    wx[0] = plane0
    wx[CX] = plane0
    for x in range(CX - 1):
        wx[x + 1] = 0.5 * (kap[x] + kap[x + 1])
    for x in range(CX):
        k = kap[x]
        wy[x, 0:1] = row0
        wy[x, 1:CY] = 0.5 * (k[: CY - 1] + k[1:])
        wy[x, CY : CY + 1] = row0
        even, uneven = k[:, :128], k[:, 128:]
        wz[x, :, 0:128] = 0.5 * (even + uneven)
        wz[x, :, 128:] = jnp.where(half == 127, 0.0, 0.5 * (uneven + pltpu.roll(even, 127, 1)))
    cells[1].wait()
    reac = ordered(react[...]).reshape(CX, CY, NZ)
    for k in range(4):
        halo_copy(k).wait_recv()
    ext = [jnp.where(inside[k], halo[k], 0.0) for k in range(4)]
    bound = [0.5 * (edge[k] + ext[k]) for k in range(4)]
    for x in range(CX):
        k = kap[x]
        inner, outer = wz[x, :, 0:128], wz[x, :, 128:]
        below = jnp.where(half == 0, 0.5 * k[:, :128], pltpu.roll(outer, 1, 1))
        above = jnp.where(half == 127, 0.5 * k[:, 128:], outer)
        dz = jnp.concatenate([below + inner, inner + above], 1)
        dx = (bound[0] if x == 0 else wx[x]) + (bound[1] if x == CX - 1 else wx[x + 1])
        dy = wy[x, 0:CY] + wy[x, 1 : CY + 1]
        dy = dy + jnp.concatenate(
            [bound[2][x : x + 1], jnp.zeros((CY - 2, NZ), F32), bound[3][x : x + 1]], 0
        )
        diag[x] = reac[x] + dx + dy + dz

    def apply(x, gram):
        before, after = jnp.maximum(x - 1, 0), jnp.minimum(x + 1, CX - 1)
        behind, v = None, field[x, 0]
        for y in range(CY):
            ahead = field[x, y + 1] if y < CY - 1 else None
            out = diag[x, y : y + 1] * v
            out = out - wx[x, y : y + 1] * field[before, y]
            out = out - wx[x + 1, y : y + 1] * field[after, y]
            if y > 0:
                out = out - wy[x, y : y + 1] * behind
            if y < CY - 1:
                out = out - wy[x, y + 1 : y + 2] * ahead
            even, uneven = v[:, :128], v[:, 128:]
            inner, outer = wz[x, y : y + 1, 0:128], wz[x, y : y + 1, 128:]
            out = out - jnp.concatenate(
                [
                    inner * uneven + pltpu.roll(outer * uneven, 1, 1),
                    inner * even + outer * pltpu.roll(even, 127, 1),
                ],
                1,
            )
            local = pad_rows(out, SLOTS).astype(BF16)
            gram = gram + nt(masked[x, :, NZ * y : NZ * (y + 1)], local)
            behind, v = v, ahead
        return gram

    def pairs(begin, end, gram):
        return lax.fori_loop(
            begin, end, lambda i, gram: apply(2 * i + 1, apply(2 * i, gram)), gram
        )

    gram = pairs(0, 5, jnp.zeros((SLOTS, SLOTS), F32))

    found = []
    for k in range(4):
        weight = bound[k]
        total = jnp.zeros((SLOTS, SLOTS), F32)
        if k < 2:
            x = 0 if k == 0 else CX - 1
            for y in range(0, CY, 2):
                two = [field[x, j] * weight[j : j + 1] for j in (y, y + 1)]
                hi, lo = split(jnp.concatenate(two, 0))
                cols = slice(NZ * y // 2, NZ * (y + 2) // 2)
                high[:, cols], low[:, cols] = hi, lo
            face_copy(mirror[k]).wait_recv()
            both = nt(high[...], face_x[k]) + nt(low[...], face_x[k])
            both = pad_lanes(both, 128)
            block = both[:LIVE] + pltpu.roll(both[LIVE:], 128 - LIVE, 1)
            block = jnp.where(lanes_of((LIVE, 128)) < LIVE, block, 0.0)
        else:
            face_copy(mirror[k]).wait_recv()
            for x in range(CX):
                mine = field[x, 0 if k == 2 else CY - 1] * weight[x : x + 1]
                hi, lo = split(pad_rows(mine, SLOTS))
                other = face_y[k - 2, x]
                total = total + (nt(hi, other) + nt(lo, other))
            block = pad_lanes(total, 128)[:LIVE]
        found.append(jnp.where(inside[k], -block, 0.0))
    for k in range(4):
        blocks_ref[k + 1] = pad_rows(found[k], SLOTS)

    lane = lanes_of((LIVE, 128))
    odd = core == 1
    ahead = found[3]
    ahead_t = transposed(ahead)[:LIVE]
    message = jnp.where(odd, ahead, ahead_t) + pltpu.roll(jnp.where(odd, ahead_t, ahead), LIVE, 1)
    message = message + pltpu.roll(transposed(found[1])[:LIVE], 2 * LIVE, 1)
    message = jnp.where(lane >= 3 * LIVE, count.astype(F32), message)

    def up_copy(ref, i):
        return pltpu.make_async_remote_copy(
            src_ref=ref, dst_ref=ref, send_sem=up_sem.at[i], recv_sem=up_sem.at[i + 2],
            device_id=(1, u), device_id_type=MESH,
        )

    def link_copy(to, owner):
        return pltpu.make_async_remote_copy(
            src_ref=links.at[owner, core], dst_ref=links.at[owner, core],
            send_sem=link_send.at[to], recv_sem=link_recv.at[owner],
            device_id=(g, 2 * to + core), device_id_type=MESH,
        )

    def core_copy(c):
        return pltpu.make_async_remote_copy(
            src_ref=links.at[:, c], dst_ref=links.at[:, c],
            send_sem=core_sem.at[0], recv_sem=core_sem.at[1],
            device_id=(g, 2 * chip + 1 - core), device_id_type=MESH,
        )

    def piv_copy(to, owner):
        return pltpu.make_async_remote_copy(
            src_ref=pivs.at[owner], dst_ref=pivs.at[owner],
            send_sem=piv_send.at[to], recv_sem=piv_recv.at[owner],
            device_id=(g, to), device_id_type=MESH,
        )

    link_up, piv_up = up_copy(links.at[chip, core], 0), up_copy(pivs.at[u], 1)

    @pl.when(joined & (g == 0))
    def _():
        links[chip, core] = message
        link_up.start()

    gram = pairs(5, 7, gram)

    @pl.when(joined)
    def _():
        @pl.when(g == 1)
        def _():
            link_up.wait_recv()

        others(GROUP // 2, chip, lambda v: link_copy(v, chip).start())

    own = pad_lanes(pairs(7, 8, gram), 128)
    spot, slot = lanes_of((SLOTS, 128)), rows_of((SLOTS, 128))
    own = own + jnp.where((spot == slot) & (slot >= count), 1.0, 0.0)
    sym = jnp.where(spot < LIVE, 0.5 * (own + transposed(own)[:SLOTS]), 0.0)
    blocks_ref[0] = own
    blocks_ref[5] = sym

    @pl.when(joined & (g == 0))
    def _():
        packed = sym[0:16] + pltpu.roll(sym[16:32], LIVE, 1)
        pivs[u] = packed + pltpu.roll(pad_rows(sym[32:40], 16), 2 * LIVE, 1)
        piv_up.start()

    @pl.when(joined)
    def _():
        @pl.when(g == 1)
        def _():
            piv_up.wait_recv()

        others(GROUP, u, lambda v: piv_copy(v, u).start())
        others(GROUP // 2, chip, lambda v: link_copy(chip, v).wait_recv())
        core_copy(core).start()
        others(GROUP, u, lambda v: piv_copy(u, v).wait_recv())
        core_copy(1 - core).wait_recv()
        for v in range(GROUP):
            links_ref[v] = links[v // 2, v % 2]
            pivots_ref[v] = pivs[v]
        others(GROUP // 2, chip, lambda v: link_copy(v, chip).wait_send())
        others(GROUP, u, lambda v: piv_copy(v, u).wait_send())
        core_copy(core).wait_send()

    @pl.when(joined & (g == 0))
    def _():
        link_up.wait_send()
        piv_up.wait_send()

    for k in range(4):
        halo_copy(k).wait_send()
        face_copy(k).wait_send()


def assemble(count, modes, kappa, react):
    vmem = pl.BlockSpec(memory_space=pltpu.VMEM)
    hbm = pl.BlockSpec(memory_space=pltpu.HBM)
    dma = pltpu.SemaphoreType.DMA
    return pl.pallas_call(
        assemble_kernel,
        out_shape=(
            jax.ShapeDtypeStruct((6, SLOTS, 128), F32),
            jax.ShapeDtypeStruct((GROUP, LIVE, 128), F32),
            jax.ShapeDtypeStruct((GROUP, 16, 128), F32),
        ),
        in_specs=[pl.BlockSpec(memory_space=pltpu.SMEM), hbm, hbm, hbm],
        out_specs=(vmem, vmem, vmem),
        scratch_shapes=[
            pltpu.VMEM((CX, LIVE, CY, NZ), BF16),
            pltpu.VMEM((CX, CY, NZ), BF16),
            pltpu.VMEM((CX, CY, NZ), BF16),
            pltpu.VMEM((CX, CY, LIVE, NZ), F32),
            pltpu.VMEM((CX, SLOTS, CY * NZ), BF16),
            pltpu.VMEM((CX + 1, CY, NZ), F32),
            pltpu.VMEM((CX, 24, NZ), F32),
            pltpu.VMEM((CX, CY, NZ), F32),
            pltpu.VMEM((CX, CY, NZ), F32),
            pltpu.VMEM((4, 16, NZ), F32),
            pltpu.VMEM((4, 16, NZ), F32),
            pltpu.VMEM((2, 2 * LIVE, 8 * NZ), BF16),
            pltpu.VMEM((2, 16, SLOTS, NZ), BF16),
            pltpu.VMEM((2 * LIVE, 8 * NZ), BF16),
            pltpu.VMEM((2 * LIVE, 8 * NZ), BF16),
            pltpu.VMEM((2, 2 * LIVE, 8 * NZ), BF16),
            pltpu.VMEM((GROUP // 2, 2, LIVE, 128), F32),
            pltpu.VMEM((GROUP, 16, 128), F32),
            pltpu.VMEM((NZ, NZ), BF16),
            dma((CX,)),
            dma((2,)),
            dma((4,)),
            dma((4,)),
            dma((4,)),
            dma((4,)),
            dma((4,)),
            dma((GROUP // 2,)),
            dma((GROUP // 2,)),
            dma((2,)),
            dma((GROUP,)),
            dma((GROUP,)),
        ],
        compiler_params=pltpu.CompilerParams(
            collective_id=0, has_side_effects=True, vmem_limit_bytes=50 * 2**20
        ),
        name="assemble",
    )(count, modes, kappa, react)


def dot3(a, b, dims):
    ah, al = split(a)
    bh, bl = split(b)
    dot = lambda p, q: lax.dot_general(p, q, (dims, ((), ())), preferred_element_type=F32)
    return dot(ah, bh) + (dot(ah, bl) + dot(al, bh))


def nn3(a, b):
    return dot3(a, b, ((1,), (0,)))


def nt3(a, b):
    return dot3(a, b, ((1,), (1,)))


def wide(x):
    return jnp.broadcast_to(x, (8, 128))


def pivots(p, soff, state, spread_ref, rows_ref, side_ref):
    tiles, saved = (list(part) for part in state)
    sub = rows_of((8, 128))
    at = soff + 8 * p
    column = lambda v, c: wide(tiles[v][:, c : c + 1])
    if p == 0:
        for c in range(8):
            spread_ref[p, c] = column(p, at + c)
    rows_ref[p] = tiles[p]
    d = {(i, j): wide(spread_ref[p, j, i : i + 1]) for i in range(8) for j in range(i, 8)}
    rows = [wide(rows_ref[p, c : c + 1]) for c in range(8)]
    follow = p + 1 < LIVE // 8
    if follow:
        under = [column(p + 1, at + c) for c in range(8)]
        coming = [column(p + 1, at + 8 + c) for c in range(8)]
    others = [v for v in range(LIVE // 8) if v not in (p, p + 1)]
    factors = {v: [column(v, at + c) for c in range(8)] for v in others}
    low, rinv = {}, []
    for c in range(8):
        rinv.append(lax.rsqrt(d[c, c]))
        for i in range(c + 1, 8):
            low[c, i] = d[c, i] * rinv[c]
        for i in range(c + 1, 8):
            for j in range(i, 8):
                d[i, j] = d[i, j] - low[c, i] * low[c, j]
        rows[c] = rows[c] * rinv[c]
        saved[p] = jnp.where(sub == c, rows[c], saved[p])
        for i in range(c + 1, 8):
            rows[i] = rows[i] - low[c, i] * rows[c]
        if follow:
            under[c] = under[c] * rinv[c]
            side_ref[p, c] = under[c]
            for i in range(c + 1, 8):
                under[i] = under[i] - low[c, i] * under[c]
            for i in range(8):
                coming[i] = coming[i] - under[c] * wide(side_ref[p, c, i : i + 1])
            tiles[p + 1] = tiles[p + 1] - under[c] * rows[c]
    if follow:
        for c in range(8):
            spread_ref[p + 1, c] = coming[c]
    z = rows
    for c in range(7, -1, -1):
        z[c] = z[c] * rinv[c]
        for i in range(c):
            z[i] = z[i] - low[i, c] * z[c]
    for v in others:
        terms = [factors[v][c] * z[c] for c in range(8)]
        while len(terms) > 1:
            terms = [terms[i] + terms[i + 1] for i in range(0, len(terms), 2)]
        tiles[v] = tiles[v] - terms[0]
    for c in range(8):
        tiles[p] = jnp.where(sub == c, z[c], tiles[p])
    return tuple(tiles), tuple(saved)


def place(out_ref, block, pos, keep):
    base = jnp.minimum((pos // 128) * 128, NC - 256)
    base = pl.multiple_of(base, 128)
    shifted = pltpu.roll(pad_lanes(block, 256), pos - base, 1)
    cols = lanes_of((SLOTS, 256)) + base
    out_ref[:, pl.ds(base, 256)] += jnp.where(keep(cols), shifted, 0.0)


def factor_kernel(
    links_ref, pivots_ref, blocks_ref, out_ref, linv_ref, k_ref, g_ref, f_ref, x_ref, spread_ref, rows_ref, side_ref,
):
    g, u = lax.axis_index("grp"), lax.axis_index("sub")
    s = g * NU + u
    upper = s <= 21
    member = (s == 21) | (s == 22) | ((s >= NU) & (s < NU + NB))
    lane = lanes_of((LIVE, 128))
    row = rows_of((LIVE, 128))
    lane48 = lanes_of((SLOTS, 128))
    row48 = rows_of((SLOTS, 128))
    out_ref[...] = jnp.zeros_like(out_ref)
    before = lambda cols: cols < DONE
    after = lambda cols: cols >= DONE

    def left(x, by):
        x = pltpu.roll(x, 128 - by, 1) if by else x
        return jnp.where(lanes_of(x.shape) < LIVE, x, 0.0)

    def put(block, pos, late):
        base = pos // 128 * 128
        shifted = pltpu.roll(pad_lanes(block, 256), pos - base, 1) if pos > base else (
            pad_lanes(block, 256)
        )
        if base < DONE < base + 256:
            cols = lanes_of((SLOTS, 256)) + base
            shifted = jnp.where(cols >= DONE if late else cols < DONE, shifted, 0.0)
        out_ref[:, base : base + 256] += shifted

    def reduce_row(q):
        at, wide_enough = jnp.maximum(q, 0), jnp.where(q == NB - 1, 16, LIVE)
        mine = jnp.where(q == s, blocks_ref[5], 0.0)
        mine = jnp.where(q == s - 1, blocks_ref[3], mine)
        mine = jnp.where(q == s - NU, blocks_ref[1], mine)
        held = jnp.where(q > 0, f_ref[jnp.maximum(q - 1, 0)], 0.0)
        f = mine - nn3(held, pad_rows(k_ref[at], 128))
        f_ref[at] = jnp.where((q <= s) & (lane48 < wide_enough), f, 0.0)

    def solve_row(q):
        at = jnp.maximum(q, 0)
        x = nt3(f_ref[at], pad_rows(linv_ref[at], 128))
        x_ref[at] = jnp.where((q == s) & (lane48 > row48), 0.0, x)

    def double_row(q):
        at = jnp.maximum(q, 0)
        x = x_ref[at]
        g_ref[at] = nn3(x, pad_rows(linv_ref[at], 128))

    def pivot_block(t, at):
        packed = pivots_ref[t]
        parts = []
        for i in range(3):
            by = (at - LIVE * i) % 128
            parts.append(pltpu.roll(packed, by, 1) if by else packed)
        block = jnp.concatenate([parts[0], parts[1], parts[2][:8]], 0)
        return jnp.where((lane >= at) & (lane < at + LIVE), block, 0.0)

    def live_count(t):
        return jnp.max(jnp.where(lanes_of((8, 128)) >= 3 * LIVE, links_ref[t][0:8], 0.0))

    def at_rows(x, start):
        above = jnp.zeros((start, 128), F32)
        return pad_rows(jnp.concatenate([above, x], 0) if start else x, 128)

    def step(t, odd, scur, n):
        soff, uoff = (LIVE, 0) if odd else (0, LIVE)
        given = links_ref[t]
        limit = jnp.where(t == NB - 1, 16, LIVE)
        in_s = (lane >= soff) & (lane < soff + LIVE)
        in_u = (lane >= uoff) & (lane < uoff + LIVE)
        eye = jnp.where(lane == row + soff, 1.0, 0.0)
        a = jnp.where((row < limit) & (lane < soff + limit), scur, eye)
        rest = jnp.where(lane == row + 2 * LIVE, 1.0, 0.0)
        rest = jnp.where(in_u, jnp.where(row < limit, given, 0.0), rest)
        a = jnp.where(in_s, a, rest)
        ut = jnp.where(in_s, given, 0.0)
        tiles = tuple(a[8 * v : 8 * v + 8] for v in range(LIVE // 8))
        state = pivots(0, soff, (tiles, tiles), spread_ref, rows_ref, side_ref)

        double_row(t - 3)
        solve_row(t - 2)
        reduce_row(t - 1)
        following = jnp.minimum(t + 1, NB - 1)
        coming, coming_n = pivot_block(following, uoff), live_count(following)
        n = jnp.where(t == NB - 1, jnp.minimum(n, 16.0), n)
        for p in range(1, LIVE // 8):
            state = lax.cond(
                n > 8.0 * p,
                lambda st, p=p: pivots(p, soff, st, spread_ref, rows_ref, side_ref),
                lambda st: st,
                state,
            )
        tiles, saved = state
        k = jnp.concatenate(tiles, 0)
        snext = coming - nn3(ut, at_rows(k, soff))
        linv_ref[t] = left(jnp.concatenate(saved, 0), 2 * LIVE)
        k_ref[t + 1] = left(k, uoff)
        return snext, coming_n

    @pl.when(upper | member)
    def _():
        k_ref[0] = jnp.zeros((LIVE, 128), F32)
        linv_ref[0] = jnp.zeros((LIVE, 128), F32)
        f_ref[0] = jnp.zeros((SLOTS, 128), F32)
        x_ref[0] = jnp.zeros((SLOTS, 128), F32)
        def pair(i, carry):
            carry = step(2 * i, False, *carry)
            return step(2 * i + 1, True, *carry)

        lax.fori_loop(0, NB // 2, pair, (pivot_block(0, 0), live_count(0)))
        double_row(NB - 3)
        solve_row(NB - 2)
        reduce_row(NB - 1)
        double_row(NB - 2)
        solve_row(NB - 1)
        double_row(NB - 1)
        for t in range(NB):
            put(x_ref[t], SLOTS * t, False)

    @pl.when(upper)
    def _():
        dead = jnp.where((row48 == lane48) & (row48 >= LIVE), 1.0, 0.0)
        place(out_ref, dead, SLOTS * s, before)

    @pl.when(member)
    def _():
        late = lane >= 16
        last = jnp.where(row < 16, links_ref[NB - 1], 0.0)
        own = jnp.where(late & (row < 16), pivot_block(NB - 1, 0), 0.0)
        over = jnp.where(late, left(links_ref[NB - 2], LIVE), 0.0)
        y = None
        for t in range(NB - 1, -1, -1):
            if y is None:
                y = g_ref[t]
                put(-nn3(y, pad_rows(left(last, 0), 128)), SLOTS * NB, True)
                put(-nn3(y, pad_rows(own, 128)), SLOTS * (NB - 1), True)
            else:
                y = g_ref[t] - nt3(y, pad_rows(k_ref[t + 1], 128))
            if t == NB - 2:
                put(-nn3(y, pad_rows(over, 128)), SLOTS * (NB - 1), True)
            rising = pad_rows(left(links_ref[t], 2 * LIVE), 128)
            put(-nt3(y, rising), SLOTS * (t + NU), True)

    @pl.when(s >= 21)
    def _():
        targets = [s, s - NU, s + NU, s - 1, s + 1]
        valid = [True, g > 0, g < NG - 1, u > 0, u < NU - 1]
        for k in range(5):
            pos = SLOTS * jnp.clip(targets[k], 0, NG * NU - 1)
            place(out_ref, jnp.where(valid[k], blocks_ref[k], 0.0), pos, after)

    @pl.when(s == 21)
    def _():
        out_ref[0:16, DONE:] = jnp.zeros((16, NC - DONE), F32)


def factor(links, pivs, blocks):
    vmem = pl.BlockSpec(memory_space=pltpu.VMEM)
    return pl.pallas_call(
        factor_kernel,
        out_shape=jax.ShapeDtypeStruct((SLOTS, NC), F32),
        in_specs=[vmem, vmem, vmem],
        out_specs=vmem,
        scratch_shapes=[
            pltpu.VMEM((NB, LIVE, 128), F32),
            pltpu.VMEM((NB + 1, LIVE, 128), F32),
            pltpu.VMEM((NB, SLOTS, 128), F32),
            pltpu.VMEM((NB, SLOTS, 128), F32),
            pltpu.VMEM((NB, SLOTS, 128), F32),
            pltpu.VMEM((LIVE // 8, 8, 8, 128), F32),
            pltpu.VMEM((LIVE // 8, 8, 128), F32),
            pltpu.VMEM((LIVE // 8, 8, 8, 128), F32),
        ],
        compiler_params=pltpu.CompilerParams(vmem_limit_bytes=40 * 2**20),
        name="factor",
    )(links, pivs, blocks)


def per_device(modes, counts, kappa, react):
    blocks, links, pivs = assemble(counts, modes, kappa, react)
    return factor(links, pivs, blocks)


def solution(mesh):
    in_specs = (
        P(None, "grp", "sub", None),
        P(("grp", "sub")),
        P("grp", "sub", None),
        P("grp", "sub", None),
    )
    out_specs = P(("grp", "sub"), None)
    return jax.shard_map(
        per_device, mesh=mesh, in_specs=in_specs, out_specs=out_specs, check_vma=False
    )
```

```python
import jax
import jax.numpy as jnp
from jax import lax
from jax.experimental import pallas as pl
from jax.experimental.pallas import tpu as pltpu
from jax.sharding import PartitionSpec as P

F32 = jnp.float32
BF16 = jnp.bfloat16
MESH = pl.DeviceIdType.MESH
NG, NU = 4, 32
CX, CY, NZ = 16, 16, 256
SLOTS, LIVE = 48, 40
NB = 22
DONE = 1024
GROUP = 24
NC = SLOTS * NG * NU


def nt(a, b, precision=None):
    return lax.dot_general(
        a, b, (((1,), (1,)), ((), ())), preferred_element_type=F32, precision=precision
    )


def lanes_of(shape):
    return lax.broadcasted_iota(jnp.int32, shape, len(shape) - 1)


def rows_of(shape):
    return lax.broadcasted_iota(jnp.int32, shape, len(shape) - 2)


def split(x):
    hi = x.astype(BF16)
    return hi, (x - hi.astype(F32)).astype(BF16)


def pad_rows(x, rows):
    return jnp.concatenate([x, jnp.zeros((rows - x.shape[0], x.shape[1]), x.dtype)], 0)


def pad_lanes(x, lanes):
    return jnp.concatenate([x, jnp.zeros((x.shape[0], lanes - x.shape[1]), x.dtype)], 1)


def transposed(x):
    return jnp.transpose(pad_rows(x, 128))


def assemble_kernel(
    count_ref, modes_ref, kappa_ref, react_ref, blocks_ref, links_ref, pivots_ref,
    raw, kappa, react, field, masked, wx, wy, wz, diag, edge, halo, face_x, face_y,
    high, low, ends, links, pivs, order,
    raw_sem, cell_sem, halo_send, halo_recv, face_send, face_recv,
    up_sem, link_send, link_recv, core_sem, piv_send, piv_recv,
):
    g, u = lax.axis_index("grp"), lax.axis_index("sub")
    partners = [
        (lax.rem(g + NG - 1, NG), u),
        (lax.rem(g + 1, NG), u),
        (g, lax.rem(u + NU - 1, NU)),
        (g, lax.rem(u + 1, NU)),
    ]
    inside = [g > 0, g < NG - 1, u > 0, u < NU - 1]
    mirror = [1, 0, 3, 2]
    chip, core = u // 2, lax.rem(u, 2)
    joined = (g < 2) & (u < GROUP)

    def fetch(x):
        return pltpu.make_async_copy(
            modes_ref.at[pl.ds(0, LIVE), x], raw.at[x], raw_sem.at[x]
        )

    cells = [
        pltpu.make_async_copy(kappa_ref, kappa, cell_sem.at[0]),
        pltpu.make_async_copy(react_ref, react, cell_sem.at[1]),
    ]
    cells[0].start()
    for x in [0, CX - 1] + list(range(1, CX - 1)):
        fetch(x).start()
    cells[1].start()

    barrier = pltpu.get_barrier_semaphore()

    def greet(device):
        pl.semaphore_signal(barrier, inc=1, device_id=device, device_id_type=MESH)

    for partner in partners:
        greet(partner)

    def others(count, me, act):
        for step in range(1, count):
            v = me + step
            act(jnp.where(v >= count, v - count, v))

    @pl.when(joined)
    def _():
        others(GROUP, u, lambda v: greet((g, v)))

    count = count_ref[0]
    z_from, z_to = rows_of((NZ, NZ)), lanes_of((NZ, NZ))
    here = z_from == jnp.where(z_to < 128, 2 * z_to, 2 * z_to - 255)
    order[...] = jnp.where(here, 1.0, 0.0).astype(BF16)

    def ordered(x):
        return jnp.dot(x.reshape(-1, NZ), order[...], preferred_element_type=F32)

    cells[0].wait()
    kap = ordered(kappa[...]).reshape(CX, CY, NZ)
    edge[0] = kap[0]
    edge[1] = kap[CX - 1]
    for x in range(CX):
        edge[2, x : x + 1] = kap[x, 0:1]
        edge[3, x : x + 1] = kap[x, CY - 1 : CY]

    live = rows_of((CY, LIVE, NZ)) < count

    def turn(x, side=None):
        plane = jnp.swapaxes(ordered(raw[x]).reshape(LIVE, CY, NZ), 0, 1)
        plane = jnp.where(live, plane, 0.0)
        field[x] = plane
        for y in range(CY):
            masked[x, :, NZ * y : NZ * (y + 1)] = pad_rows(plane[y], SLOTS).astype(BF16)
        if side is not None:
            for y in range(0, CY, 2):
                two = jnp.concatenate([plane[y], plane[y + 1]], 0)
                ends[side, :, NZ * y // 2 : NZ * (y + 2) // 2] = two.astype(BF16)

    fetch(0).wait()
    fetch(CX - 1).wait()
    turn(0, 0)
    turn(CX - 1, 1)
    pl.semaphore_wait(barrier, jnp.where(joined, GROUP + 3, 4))

    def halo_copy(k):
        return pltpu.make_async_remote_copy(
            src_ref=edge.at[k], dst_ref=halo.at[mirror[k]],
            send_sem=halo_send.at[k], recv_sem=halo_recv.at[mirror[k]],
            device_id=partners[k], device_id_type=MESH,
        )

    sources = [
        ends.at[0],
        ends.at[1],
        masked.at[:, :, pl.ds(0, NZ)],
        masked.at[:, :, pl.ds((CY - 1) * NZ, NZ)],
    ]
    landings = [face_x.at[0], face_x.at[1], face_y.at[0], face_y.at[1]]

    def face_copy(k):
        return pltpu.make_async_remote_copy(
            src_ref=sources[k], dst_ref=landings[mirror[k]],
            send_sem=face_send.at[k], recv_sem=face_recv.at[mirror[k]],
            device_id=partners[k], device_id_type=MESH,
        )

    for k in range(4):
        halo_copy(k).start()
    face_copy(0).start()
    face_copy(1).start()

    def turn_next(i, carry):
        fetch(2 * i + 1).wait()
        fetch(2 * i + 2).wait()
        turn(2 * i + 1)
        turn(2 * i + 2)
        return carry

    lax.fori_loop(0, CX // 2 - 1, turn_next, 0)
    face_copy(2).start()
    face_copy(3).start()

    plane0 = jnp.zeros((CY, NZ), F32)
    row0 = jnp.zeros((1, NZ), F32)
    half = lanes_of((CY, 128))
    wx[0] = plane0
    wx[CX] = plane0
    for x in range(CX - 1):
        wx[x + 1] = 0.5 * (kap[x] + kap[x + 1])
    for x in range(CX):
        k = kap[x]
        wy[x, 0:1] = row0
        wy[x, 1:CY] = 0.5 * (k[: CY - 1] + k[1:])
        wy[x, CY : CY + 1] = row0
        even, uneven = k[:, :128], k[:, 128:]
        wz[x, :, 0:128] = 0.5 * (even + uneven)
        wz[x, :, 128:] = jnp.where(half == 127, 0.0, 0.5 * (uneven + pltpu.roll(even, 127, 1)))
    cells[1].wait()
    reac = ordered(react[...]).reshape(CX, CY, NZ)
    for k in range(4):
        halo_copy(k).wait_recv()
    ext = [jnp.where(inside[k], halo[k], 0.0) for k in range(4)]
    bound = [0.5 * (edge[k] + ext[k]) for k in range(4)]
    for x in range(CX):
        k = kap[x]
        inner, outer = wz[x, :, 0:128], wz[x, :, 128:]
        below = jnp.where(half == 0, 0.5 * k[:, :128], pltpu.roll(outer, 1, 1))
        above = jnp.where(half == 127, 0.5 * k[:, 128:], outer)
        dz = jnp.concatenate([below + inner, inner + above], 1)
        dx = (bound[0] if x == 0 else wx[x]) + (bound[1] if x == CX - 1 else wx[x + 1])
        dy = wy[x, 0:CY] + wy[x, 1 : CY + 1]
        dy = dy + jnp.concatenate(
            [bound[2][x : x + 1], jnp.zeros((CY - 2, NZ), F32), bound[3][x : x + 1]], 0
        )
        diag[x] = reac[x] + dx + dy + dz

    def apply(x, gram):
        before, after = jnp.maximum(x - 1, 0), jnp.minimum(x + 1, CX - 1)
        behind, v = None, field[x, 0]
        for y in range(CY):
            ahead = field[x, y + 1] if y < CY - 1 else None
            out = diag[x, y : y + 1] * v
            out = out - wx[x, y : y + 1] * field[before, y]
            out = out - wx[x + 1, y : y + 1] * field[after, y]
            if y > 0:
                out = out - wy[x, y : y + 1] * behind
            if y < CY - 1:
                out = out - wy[x, y + 1 : y + 2] * ahead
            even, uneven = v[:, :128], v[:, 128:]
            inner, outer = wz[x, y : y + 1, 0:128], wz[x, y : y + 1, 128:]
            out = out - jnp.concatenate(
                [
                    inner * uneven + pltpu.roll(outer * uneven, 1, 1),
                    inner * even + outer * pltpu.roll(even, 127, 1),
                ],
                1,
            )
            local = pad_rows(out, SLOTS).astype(BF16)
            gram = gram + nt(masked[x, :, NZ * y : NZ * (y + 1)], local)
            behind, v = v, ahead
        return gram

    def pairs(begin, end, gram):
        return lax.fori_loop(
            begin, end, lambda i, gram: apply(2 * i + 1, apply(2 * i, gram)), gram
        )

    gram = pairs(0, 5, jnp.zeros((SLOTS, SLOTS), F32))

    found = []
    for k in range(4):
        weight = bound[k]
        total = jnp.zeros((SLOTS, SLOTS), F32)
        if k < 2:
            x = 0 if k == 0 else CX - 1
            for y in range(0, CY, 2):
                two = [field[x, j] * weight[j : j + 1] for j in (y, y + 1)]
                hi, lo = split(jnp.concatenate(two, 0))
                cols = slice(NZ * y // 2, NZ * (y + 2) // 2)
                high[:, cols], low[:, cols] = hi, lo
            face_copy(mirror[k]).wait_recv()
            both = nt(high[...], face_x[k]) + nt(low[...], face_x[k])
            both = pad_lanes(both, 128)
            block = both[:LIVE] + pltpu.roll(both[LIVE:], 128 - LIVE, 1)
            block = jnp.where(lanes_of((LIVE, 128)) < LIVE, block, 0.0)
        else:
            face_copy(mirror[k]).wait_recv()
            for x in range(CX):
                mine = field[x, 0 if k == 2 else CY - 1] * weight[x : x + 1]
                hi, lo = split(pad_rows(mine, SLOTS))
                other = face_y[k - 2, x]
                total = total + (nt(hi, other) + nt(lo, other))
            block = pad_lanes(total, 128)[:LIVE]
        found.append(jnp.where(inside[k], -block, 0.0))
    for k in range(4):
        blocks_ref[k + 1] = pad_rows(found[k], SLOTS)

    lane = lanes_of((LIVE, 128))
    odd = core == 1
    ahead = found[3]
    ahead_t = transposed(ahead)[:LIVE]
    message = jnp.where(odd, ahead, ahead_t) + pltpu.roll(jnp.where(odd, ahead_t, ahead), LIVE, 1)
    message = message + pltpu.roll(transposed(found[1])[:LIVE], 2 * LIVE, 1)
    message = jnp.where(lane >= 3 * LIVE, count.astype(F32), message)

    def up_copy(ref, i):
        return pltpu.make_async_remote_copy(
            src_ref=ref, dst_ref=ref, send_sem=up_sem.at[i], recv_sem=up_sem.at[i + 2],
            device_id=(1, u), device_id_type=MESH,
        )

    def link_copy(to, owner):
        return pltpu.make_async_remote_copy(
            src_ref=links.at[owner, core], dst_ref=links.at[owner, core],
            send_sem=link_send.at[to], recv_sem=link_recv.at[owner],
            device_id=(g, 2 * to + core), device_id_type=MESH,
        )

    def core_copy(c):
        return pltpu.make_async_remote_copy(
            src_ref=links.at[:, c], dst_ref=links.at[:, c],
            send_sem=core_sem.at[0], recv_sem=core_sem.at[1],
            device_id=(g, 2 * chip + 1 - core), device_id_type=MESH,
        )

    def piv_copy(to, owner):
        return pltpu.make_async_remote_copy(
            src_ref=pivs.at[owner], dst_ref=pivs.at[owner],
            send_sem=piv_send.at[to], recv_sem=piv_recv.at[owner],
            device_id=(g, to), device_id_type=MESH,
        )

    link_up, piv_up = up_copy(links.at[chip, core], 0), up_copy(pivs.at[u], 1)

    @pl.when(joined & (g == 0))
    def _():
        links[chip, core] = message
        link_up.start()

    gram = pairs(5, 7, gram)

    @pl.when(joined)
    def _():
        @pl.when(g == 1)
        def _():
            link_up.wait_recv()

        others(GROUP // 2, chip, lambda v: link_copy(v, chip).start())

    own = pad_lanes(pairs(7, 8, gram), 128)
    spot, slot = lanes_of((SLOTS, 128)), rows_of((SLOTS, 128))
    own = own + jnp.where((spot == slot) & (slot >= count), 1.0, 0.0)
    sym = jnp.where(spot < LIVE, 0.5 * (own + transposed(own)[:SLOTS]), 0.0)
    blocks_ref[0] = own
    blocks_ref[5] = sym

    @pl.when(joined & (g == 0))
    def _():
        packed = sym[0:16] + pltpu.roll(sym[16:32], LIVE, 1)
        pivs[u] = packed + pltpu.roll(pad_rows(sym[32:40], 16), 2 * LIVE, 1)
        piv_up.start()

    @pl.when(joined)
    def _():
        @pl.when(g == 1)
        def _():
            piv_up.wait_recv()

        others(GROUP, u, lambda v: piv_copy(v, u).start())
        others(GROUP // 2, chip, lambda v: link_copy(chip, v).wait_recv())
        core_copy(core).start()
        others(GROUP, u, lambda v: piv_copy(u, v).wait_recv())
        core_copy(1 - core).wait_recv()
        for v in range(GROUP):
            links_ref[v] = links[v // 2, v % 2]
            pivots_ref[v] = pivs[v]
        others(GROUP // 2, chip, lambda v: link_copy(v, chip).wait_send())
        others(GROUP, u, lambda v: piv_copy(v, u).wait_send())
        core_copy(core).wait_send()

    @pl.when(joined & (g == 0))
    def _():
        link_up.wait_send()
        piv_up.wait_send()

    for k in range(4):
        halo_copy(k).wait_send()
        face_copy(k).wait_send()


def assemble(count, modes, kappa, react):
    vmem = pl.BlockSpec(memory_space=pltpu.VMEM)
    hbm = pl.BlockSpec(memory_space=pltpu.HBM)
    dma = pltpu.SemaphoreType.DMA
    return pl.pallas_call(
        assemble_kernel,
        out_shape=(
            jax.ShapeDtypeStruct((6, SLOTS, 128), F32),
            jax.ShapeDtypeStruct((GROUP, LIVE, 128), F32),
            jax.ShapeDtypeStruct((GROUP, 16, 128), F32),
        ),
        in_specs=[pl.BlockSpec(memory_space=pltpu.SMEM), hbm, hbm, hbm],
        out_specs=(vmem, vmem, vmem),
        scratch_shapes=[
            pltpu.VMEM((CX, LIVE, CY, NZ), BF16),
            pltpu.VMEM((CX, CY, NZ), BF16),
            pltpu.VMEM((CX, CY, NZ), BF16),
            pltpu.VMEM((CX, CY, LIVE, NZ), F32),
            pltpu.VMEM((CX, SLOTS, CY * NZ), BF16),
            pltpu.VMEM((CX + 1, CY, NZ), F32),
            pltpu.VMEM((CX, 24, NZ), F32),
            pltpu.VMEM((CX, CY, NZ), F32),
            pltpu.VMEM((CX, CY, NZ), F32),
            pltpu.VMEM((4, 16, NZ), F32),
            pltpu.VMEM((4, 16, NZ), F32),
            pltpu.VMEM((2, 2 * LIVE, 8 * NZ), BF16),
            pltpu.VMEM((2, 16, SLOTS, NZ), BF16),
            pltpu.VMEM((2 * LIVE, 8 * NZ), BF16),
            pltpu.VMEM((2 * LIVE, 8 * NZ), BF16),
            pltpu.VMEM((2, 2 * LIVE, 8 * NZ), BF16),
            pltpu.VMEM((GROUP // 2, 2, LIVE, 128), F32),
            pltpu.VMEM((GROUP, 16, 128), F32),
            pltpu.VMEM((NZ, NZ), BF16),
            dma((CX,)),
            dma((2,)),
            dma((4,)),
            dma((4,)),
            dma((4,)),
            dma((4,)),
            dma((4,)),
            dma((GROUP // 2,)),
            dma((GROUP // 2,)),
            dma((2,)),
            dma((GROUP,)),
            dma((GROUP,)),
        ],
        compiler_params=pltpu.CompilerParams(
            collective_id=0, has_side_effects=True, vmem_limit_bytes=50 * 2**20
        ),
        name="assemble",
    )(count, modes, kappa, react)


def halves(x, rows, axis):
    hi, lo = split(pad_rows(x, rows) if x.shape[0] < rows else x)
    return jnp.concatenate([hi, lo], axis)


def joined_halves(out, rows):
    tall = out.shape[0] // 2
    return out[:rows, :128] + (out[:rows, 128:] + out[tall : tall + rows, :128])


def nn3(a, b):
    left = halves(a, SLOTS, 0)
    out = jnp.dot(left, halves(b, 128, 1), preferred_element_type=F32)
    return joined_halves(out, a.shape[0])


def nt3(a, b):
    out = nt(halves(a, SLOTS, 0), halves(b, 128, 0))
    return joined_halves(out, a.shape[0])


def wide(x):
    return jnp.broadcast_to(x, (8, 128))


def pivots(p, soff, state, spread_ref, rows_ref, side_ref):
    tiles, saved = (list(part) for part in state)
    sub = rows_of((8, 128))
    at = soff + 8 * p
    column = lambda v, c: wide(tiles[v][:, c : c + 1])
    if p == 0:
        for c in range(8):
            spread_ref[p, c] = column(p, at + c)
    rows_ref[p] = tiles[p]
    d = {(i, j): wide(spread_ref[p, j, i : i + 1]) for i in range(8) for j in range(i, 8)}
    rows = [wide(rows_ref[p, c : c + 1]) for c in range(8)]
    follow = p + 1 < LIVE // 8
    if follow:
        under = [column(p + 1, at + c) for c in range(8)]
        coming = [column(p + 1, at + 8 + c) for c in range(8)]
    others = [v for v in range(LIVE // 8) if v not in (p, p + 1)]
    factors = {v: [column(v, at + c) for c in range(8)] for v in others}
    low, rinv = {}, []
    for c in range(8):
        rinv.append(lax.rsqrt(d[c, c]))
        for i in range(c + 1, 8):
            low[c, i] = d[c, i] * rinv[c]
        for i in range(c + 1, 8):
            for j in range(i, 8):
                d[i, j] = d[i, j] - low[c, i] * low[c, j]
        rows[c] = rows[c] * rinv[c]
        saved[p] = jnp.where(sub == c, rows[c], saved[p])
        for i in range(c + 1, 8):
            rows[i] = rows[i] - low[c, i] * rows[c]
        if follow:
            under[c] = under[c] * rinv[c]
            side_ref[p, c] = under[c]
            for i in range(c + 1, 8):
                under[i] = under[i] - low[c, i] * under[c]
            for i in range(8):
                coming[i] = coming[i] - under[c] * wide(side_ref[p, c, i : i + 1])
            tiles[p + 1] = tiles[p + 1] - under[c] * rows[c]
    if follow:
        for c in range(8):
            spread_ref[p + 1, c] = coming[c]
    z = rows
    for c in range(7, -1, -1):
        z[c] = z[c] * rinv[c]
        for i in range(c):
            z[i] = z[i] - low[i, c] * z[c]
    for v in others:
        terms = [factors[v][c] * z[c] for c in range(8)]
        while len(terms) > 1:
            terms = [terms[i] + terms[i + 1] for i in range(0, len(terms), 2)]
        tiles[v] = tiles[v] - terms[0]
    for c in range(8):
        tiles[p] = jnp.where(sub == c, z[c], tiles[p])
    return tuple(tiles), tuple(saved)


def place(out_ref, block, pos, keep):
    base = jnp.minimum((pos // 128) * 128, NC - 256)
    base = pl.multiple_of(base, 128)
    shifted = pltpu.roll(pad_lanes(block, 256), pos - base, 1)
    cols = lanes_of((SLOTS, 256)) + base
    out_ref[:, pl.ds(base, 256)] += jnp.where(keep(cols), shifted, 0.0)


def factor_kernel(
    links_ref, pivots_ref, blocks_ref, out_ref, linv_ref, k_ref, g_ref, f_ref, x_ref, spread_ref, rows_ref, side_ref,
):
    g, u = lax.axis_index("grp"), lax.axis_index("sub")
    s = g * NU + u
    upper = s <= 21
    member = (s == 21) | (s == 22) | ((s >= NU) & (s < NU + NB))
    lane = lanes_of((LIVE, 128))
    row = rows_of((LIVE, 128))
    lane48 = lanes_of((SLOTS, 128))
    row48 = rows_of((SLOTS, 128))
    out_ref[...] = jnp.zeros_like(out_ref)
    before = lambda cols: cols < DONE
    after = lambda cols: cols >= DONE

    def left(x, by):
        x = pltpu.roll(x, 128 - by, 1) if by else x
        return jnp.where(lanes_of(x.shape) < LIVE, x, 0.0)

    def put(block, pos, late):
        base = pos // 128 * 128
        shifted = pltpu.roll(pad_lanes(block, 256), pos - base, 1) if pos > base else (
            pad_lanes(block, 256)
        )
        if base < DONE < base + 256:
            cols = lanes_of((SLOTS, 256)) + base
            shifted = jnp.where(cols >= DONE if late else cols < DONE, shifted, 0.0)
        out_ref[:, base : base + 256] += shifted

    def reduce_row(q):
        at, wide_enough = jnp.maximum(q, 0), jnp.where(q == NB - 1, 16, LIVE)
        mine = jnp.where(q == s, blocks_ref[5], 0.0)
        mine = jnp.where(q == s - 1, blocks_ref[3], mine)
        mine = jnp.where(q == s - NU, blocks_ref[1], mine)
        held = jnp.where(q > 0, f_ref[jnp.maximum(q - 1, 0)], 0.0)
        f = mine - nn3(held, pad_rows(k_ref[at], 128))
        f_ref[at] = jnp.where((q <= s) & (lane48 < wide_enough), f, 0.0)

    def solve_row(q):
        at = jnp.maximum(q, 0)
        x = nt3(f_ref[at], pad_rows(linv_ref[at], 128))
        x_ref[at] = jnp.where((q == s) & (lane48 > row48), 0.0, x)

    def double_row(q):
        at = jnp.maximum(q, 0)
        x = x_ref[at]
        g_ref[at] = nn3(x, pad_rows(linv_ref[at], 128))

    def pivot_block(t, at):
        packed = pivots_ref[t]
        parts = []
        for i in range(3):
            by = (at - LIVE * i) % 128
            parts.append(pltpu.roll(packed, by, 1) if by else packed)
        block = jnp.concatenate([parts[0], parts[1], parts[2][:8]], 0)
        return jnp.where((lane >= at) & (lane < at + LIVE), block, 0.0)

    def live_count(t):
        return jnp.max(jnp.where(lanes_of((8, 128)) >= 3 * LIVE, links_ref[t][0:8], 0.0))

    def at_rows(x, start):
        above = jnp.zeros((start, 128), F32)
        return pad_rows(jnp.concatenate([above, x], 0) if start else x, 128)

    def step(t, odd, scur, n):
        soff, uoff = (LIVE, 0) if odd else (0, LIVE)
        given = links_ref[t]
        limit = jnp.where(t == NB - 1, 16, LIVE)
        in_s = (lane >= soff) & (lane < soff + LIVE)
        in_u = (lane >= uoff) & (lane < uoff + LIVE)
        eye = jnp.where(lane == row + soff, 1.0, 0.0)
        a = jnp.where((row < limit) & (lane < soff + limit), scur, eye)
        rest = jnp.where(lane == row + 2 * LIVE, 1.0, 0.0)
        rest = jnp.where(in_u, jnp.where(row < limit, given, 0.0), rest)
        a = jnp.where(in_s, a, rest)
        ut = jnp.where(in_s, given, 0.0)
        tiles = tuple(a[8 * v : 8 * v + 8] for v in range(LIVE // 8))
        state = pivots(0, soff, (tiles, tiles), spread_ref, rows_ref, side_ref)

        double_row(t - 3)
        solve_row(t - 2)
        reduce_row(t - 1)
        following = jnp.minimum(t + 1, NB - 1)
        coming, coming_n = pivot_block(following, uoff), live_count(following)
        n = jnp.where(t == NB - 1, jnp.minimum(n, 16.0), n)
        for p in range(1, LIVE // 8):
            state = lax.cond(
                n > 8.0 * p,
                lambda st, p=p: pivots(p, soff, st, spread_ref, rows_ref, side_ref),
                lambda st: st,
                state,
            )
        tiles, saved = state
        k = jnp.concatenate(tiles, 0)
        snext = coming - nn3(ut, at_rows(k, soff))
        linv_ref[t] = left(jnp.concatenate(saved, 0), 2 * LIVE)
        k_ref[t + 1] = left(k, uoff)
        return snext, coming_n

    @pl.when(upper | member)
    def _():
        k_ref[0] = jnp.zeros((LIVE, 128), F32)
        linv_ref[0] = jnp.zeros((LIVE, 128), F32)
        f_ref[0] = jnp.zeros((SLOTS, 128), F32)
        x_ref[0] = jnp.zeros((SLOTS, 128), F32)
        def pair(i, carry):
            carry = step(2 * i, False, *carry)
            return step(2 * i + 1, True, *carry)

        lax.fori_loop(0, NB // 2, pair, (pivot_block(0, 0), live_count(0)))
        double_row(NB - 3)
        solve_row(NB - 2)
        reduce_row(NB - 1)
        double_row(NB - 2)
        solve_row(NB - 1)
        double_row(NB - 1)
        for t in range(NB):
            put(x_ref[t], SLOTS * t, False)

    @pl.when(upper)
    def _():
        dead = jnp.where((row48 == lane48) & (row48 >= LIVE), 1.0, 0.0)
        place(out_ref, dead, SLOTS * s, before)

    @pl.when(member)
    def _():
        late = lane >= 16
        last = jnp.where(row < 16, links_ref[NB - 1], 0.0)
        own = jnp.where(late & (row < 16), pivot_block(NB - 1, 0), 0.0)
        over = jnp.where(late, left(links_ref[NB - 2], LIVE), 0.0)
        y = None
        for t in range(NB - 1, -1, -1):
            if y is None:
                y = g_ref[t]
                put(-nn3(y, pad_rows(left(last, 0), 128)), SLOTS * NB, True)
                put(-nn3(y, pad_rows(own, 128)), SLOTS * (NB - 1), True)
            else:
                y = g_ref[t] - nt3(y, pad_rows(k_ref[t + 1], 128))
            if t == NB - 2:
                put(-nn3(y, pad_rows(over, 128)), SLOTS * (NB - 1), True)
            rising = pad_rows(left(links_ref[t], 2 * LIVE), 128)
            put(-nt3(y, rising), SLOTS * (t + NU), True)

    @pl.when(s >= 21)
    def _():
        targets = [s, s - NU, s + NU, s - 1, s + 1]
        valid = [True, g > 0, g < NG - 1, u > 0, u < NU - 1]
        for k in range(5):
            pos = SLOTS * jnp.clip(targets[k], 0, NG * NU - 1)
            place(out_ref, jnp.where(valid[k], blocks_ref[k], 0.0), pos, after)

    @pl.when(s == 21)
    def _():
        out_ref[0:16, DONE:] = jnp.zeros((16, NC - DONE), F32)


def factor(links, pivs, blocks):
    vmem = pl.BlockSpec(memory_space=pltpu.VMEM)
    return pl.pallas_call(
        factor_kernel,
        out_shape=jax.ShapeDtypeStruct((SLOTS, NC), F32),
        in_specs=[vmem, vmem, vmem],
        out_specs=vmem,
        scratch_shapes=[
            pltpu.VMEM((NB, LIVE, 128), F32),
            pltpu.VMEM((NB + 1, LIVE, 128), F32),
            pltpu.VMEM((NB, SLOTS, 128), F32),
            pltpu.VMEM((NB, SLOTS, 128), F32),
            pltpu.VMEM((NB, SLOTS, 128), F32),
            pltpu.VMEM((LIVE // 8, 8, 8, 128), F32),
            pltpu.VMEM((LIVE // 8, 8, 128), F32),
            pltpu.VMEM((LIVE // 8, 8, 8, 128), F32),
        ],
        compiler_params=pltpu.CompilerParams(vmem_limit_bytes=40 * 2**20),
        name="factor",
    )(links, pivs, blocks)


def per_device(modes, counts, kappa, react):
    blocks, links, pivs = assemble(counts, modes, kappa, react)
    return factor(links, pivs, blocks)


def solution(mesh):
    in_specs = (
        P(None, "grp", "sub", None),
        P(("grp", "sub")),
        P("grp", "sub", None),
        P("grp", "sub", None),
    )
    out_specs = P(("grp", "sub"), None)
    return jax.shard_map(
        per_device, mesh=mesh, in_specs=in_specs, out_specs=out_specs, check_vma=False
    )
```

```python
import jax
import jax.numpy as jnp
from jax import lax
from jax.experimental import pallas as pl
from jax.experimental.pallas import tpu as pltpu
from jax.sharding import PartitionSpec as P

F32 = jnp.float32
BF16 = jnp.bfloat16
MESH = pl.DeviceIdType.MESH
NG, NU = 4, 32
CX, CY, NZ = 16, 16, 256
SLOTS, LIVE = 48, 40
NB = 22
DONE = 1024
GROUP = 24
NC = SLOTS * NG * NU


def nt(a, b, precision=None):
    return lax.dot_general(
        a, b, (((1,), (1,)), ((), ())), preferred_element_type=F32, precision=precision
    )


def lanes_of(shape):
    return lax.broadcasted_iota(jnp.int32, shape, len(shape) - 1)


def rows_of(shape):
    return lax.broadcasted_iota(jnp.int32, shape, len(shape) - 2)


def split(x):
    hi = x.astype(BF16)
    return hi, (x - hi.astype(F32)).astype(BF16)


def pad_rows(x, rows):
    return jnp.concatenate([x, jnp.zeros((rows - x.shape[0], x.shape[1]), x.dtype)], 0)


def pad_lanes(x, lanes):
    return jnp.concatenate([x, jnp.zeros((x.shape[0], lanes - x.shape[1]), x.dtype)], 1)


def transposed(x):
    return jnp.transpose(pad_rows(x, 128))


def assemble_kernel(
    count_ref, modes_ref, kappa_ref, react_ref, blocks_ref, links_ref, pivots_ref,
    raw, kappa, react, field, masked, wx, wy, wz, diag, edge, halo, face_x, face_y,
    high, low, ends, links, pivs, order,
    raw_sem, cell_sem, halo_send, halo_recv, face_send, face_recv,
    up_sem, link_send, link_recv, core_sem, piv_send, piv_recv,
):
    g, u = lax.axis_index("grp"), lax.axis_index("sub")
    partners = [
        (lax.rem(g + NG - 1, NG), u),
        (lax.rem(g + 1, NG), u),
        (g, lax.rem(u + NU - 1, NU)),
        (g, lax.rem(u + 1, NU)),
    ]
    inside = [g > 0, g < NG - 1, u > 0, u < NU - 1]
    mirror = [1, 0, 3, 2]
    chip, core = u // 2, lax.rem(u, 2)
    joined = (g < 2) & (u < GROUP)

    def fetch(x):
        return pltpu.make_async_copy(
            modes_ref.at[pl.ds(0, LIVE), x], raw.at[x], raw_sem.at[x]
        )

    cells = [
        pltpu.make_async_copy(kappa_ref, kappa, cell_sem.at[0]),
        pltpu.make_async_copy(react_ref, react, cell_sem.at[1]),
    ]
    cells[0].start()
    for x in [0, CX - 1] + list(range(1, CX - 1)):
        fetch(x).start()
    cells[1].start()

    barrier = pltpu.get_barrier_semaphore()

    def greet(device):
        pl.semaphore_signal(barrier, inc=1, device_id=device, device_id_type=MESH)

    for partner in partners:
        greet(partner)

    def others(count, me, act):
        for step in range(1, count):
            v = me + step
            act(jnp.where(v >= count, v - count, v))

    @pl.when(joined)
    def _():
        others(GROUP, u, lambda v: greet((g, v)))

    count = count_ref[0]
    z_from, z_to = rows_of((NZ, NZ)), lanes_of((NZ, NZ))
    here = z_from == jnp.where(z_to < 128, 2 * z_to, 2 * z_to - 255)
    order[...] = jnp.where(here, 1.0, 0.0).astype(BF16)

    def ordered(x):
        return jnp.dot(x.reshape(-1, NZ), order[...], preferred_element_type=F32)

    cells[0].wait()
    kap = ordered(kappa[...]).reshape(CX, CY, NZ)
    edge[0] = kap[0]
    edge[1] = kap[CX - 1]
    for x in range(CX):
        edge[2, x : x + 1] = kap[x, 0:1]
        edge[3, x : x + 1] = kap[x, CY - 1 : CY]

    live = rows_of((CY, LIVE, NZ)) < count

    def turn(x, side=None):
        plane = jnp.swapaxes(ordered(raw[x]).reshape(LIVE, CY, NZ), 0, 1)
        plane = jnp.where(live, plane, 0.0)
        field[x] = plane
        for y in range(CY):
            masked[x, :, NZ * y : NZ * (y + 1)] = pad_rows(plane[y], SLOTS).astype(BF16)
        if side is not None:
            for y in range(0, CY, 2):
                two = jnp.concatenate([plane[y], plane[y + 1]], 0)
                ends[side, :, NZ * y // 2 : NZ * (y + 2) // 2] = two.astype(BF16)

    fetch(0).wait()
    fetch(CX - 1).wait()
    turn(0, 0)
    turn(CX - 1, 1)
    pl.semaphore_wait(barrier, jnp.where(joined, GROUP + 3, 4))

    def halo_copy(k):
        return pltpu.make_async_remote_copy(
            src_ref=edge.at[k], dst_ref=halo.at[mirror[k]],
            send_sem=halo_send.at[k], recv_sem=halo_recv.at[mirror[k]],
            device_id=partners[k], device_id_type=MESH,
        )

    sources = [
        ends.at[0],
        ends.at[1],
        masked.at[:, :, pl.ds(0, NZ)],
        masked.at[:, :, pl.ds((CY - 1) * NZ, NZ)],
    ]
    landings = [face_x.at[0], face_x.at[1], face_y.at[0], face_y.at[1]]

    def face_copy(k):
        return pltpu.make_async_remote_copy(
            src_ref=sources[k], dst_ref=landings[mirror[k]],
            send_sem=face_send.at[k], recv_sem=face_recv.at[mirror[k]],
            device_id=partners[k], device_id_type=MESH,
        )

    for k in range(4):
        halo_copy(k).start()
    face_copy(0).start()
    face_copy(1).start()

    def turn_next(i, carry):
        fetch(2 * i + 1).wait()
        fetch(2 * i + 2).wait()
        turn(2 * i + 1)
        turn(2 * i + 2)
        return carry

    lax.fori_loop(0, CX // 2 - 1, turn_next, 0)
    face_copy(2).start()
    face_copy(3).start()

    plane0 = jnp.zeros((CY, NZ), F32)
    row0 = jnp.zeros((1, NZ), F32)
    half = lanes_of((CY, 128))
    wx[0] = plane0
    wx[CX] = plane0
    for x in range(CX - 1):
        wx[x + 1] = 0.5 * (kap[x] + kap[x + 1])
    for x in range(CX):
        k = kap[x]
        wy[x, 0:1] = row0
        wy[x, 1:CY] = 0.5 * (k[: CY - 1] + k[1:])
        wy[x, CY : CY + 1] = row0
        even, uneven = k[:, :128], k[:, 128:]
        wz[x, :, 0:128] = 0.5 * (even + uneven)
        wz[x, :, 128:] = jnp.where(half == 127, 0.0, 0.5 * (uneven + pltpu.roll(even, 127, 1)))
    cells[1].wait()
    reac = ordered(react[...]).reshape(CX, CY, NZ)
    for k in range(4):
        halo_copy(k).wait_recv()
    ext = [jnp.where(inside[k], halo[k], 0.0) for k in range(4)]
    bound = [0.5 * (edge[k] + ext[k]) for k in range(4)]
    for x in range(CX):
        k = kap[x]
        inner, outer = wz[x, :, 0:128], wz[x, :, 128:]
        below = jnp.where(half == 0, 0.5 * k[:, :128], pltpu.roll(outer, 1, 1))
        above = jnp.where(half == 127, 0.5 * k[:, 128:], outer)
        dz = jnp.concatenate([below + inner, inner + above], 1)
        dx = (bound[0] if x == 0 else wx[x]) + (bound[1] if x == CX - 1 else wx[x + 1])
        dy = wy[x, 0:CY] + wy[x, 1 : CY + 1]
        dy = dy + jnp.concatenate(
            [bound[2][x : x + 1], jnp.zeros((CY - 2, NZ), F32), bound[3][x : x + 1]], 0
        )
        diag[x] = reac[x] + dx + dy + dz

    def apply(x, gram):
        before, after = jnp.maximum(x - 1, 0), jnp.minimum(x + 1, CX - 1)
        behind, v = None, field[x, 0]
        for y in range(CY):
            ahead = field[x, y + 1] if y < CY - 1 else None
            out = diag[x, y : y + 1] * v
            out = out - wx[x, y : y + 1] * field[before, y]
            out = out - wx[x + 1, y : y + 1] * field[after, y]
            if y > 0:
                out = out - wy[x, y : y + 1] * behind
            if y < CY - 1:
                out = out - wy[x, y + 1 : y + 2] * ahead
            even, uneven = v[:, :128], v[:, 128:]
            inner, outer = wz[x, y : y + 1, 0:128], wz[x, y : y + 1, 128:]
            out = out - jnp.concatenate(
                [
                    inner * uneven + pltpu.roll(outer * uneven, 1, 1),
                    inner * even + outer * pltpu.roll(even, 127, 1),
                ],
                1,
            )
            local = pad_rows(out, SLOTS).astype(BF16)
            gram = gram + nt(masked[x, :, NZ * y : NZ * (y + 1)], local)
            behind, v = v, ahead
        return gram

    gram = lax.fori_loop(
        0, CX // 2, lambda i, gram: apply(2 * i + 1, apply(2 * i, gram)),
        jnp.zeros((SLOTS, SLOTS), F32),
    )
    own = pad_lanes(gram, 128)
    spot, slot = lanes_of((SLOTS, 128)), rows_of((SLOTS, 128))
    own = own + jnp.where((spot == slot) & (slot >= count), 1.0, 0.0)
    sym = jnp.where(spot < LIVE, 0.5 * (own + transposed(own)[:SLOTS]), 0.0)

    def up_copy(ref, i):
        return pltpu.make_async_remote_copy(
            src_ref=ref, dst_ref=ref, send_sem=up_sem.at[i], recv_sem=up_sem.at[i + 2],
            device_id=(1, u), device_id_type=MESH,
        )

    def link_copy(to, owner):
        return pltpu.make_async_remote_copy(
            src_ref=links.at[owner, core], dst_ref=links.at[owner, core],
            send_sem=link_send.at[to], recv_sem=link_recv.at[owner],
            device_id=(g, 2 * to + core), device_id_type=MESH,
        )

    def core_copy(c):
        return pltpu.make_async_remote_copy(
            src_ref=links.at[:, c], dst_ref=links.at[:, c],
            send_sem=core_sem.at[0], recv_sem=core_sem.at[1],
            device_id=(g, 2 * chip + 1 - core), device_id_type=MESH,
        )

    def piv_copy(to, owner):
        return pltpu.make_async_remote_copy(
            src_ref=pivs.at[owner], dst_ref=pivs.at[owner],
            send_sem=piv_send.at[to], recv_sem=piv_recv.at[owner],
            device_id=(g, to), device_id_type=MESH,
        )

    link_up, piv_up = up_copy(links.at[chip, core], 0), up_copy(pivs.at[u], 1)

    @pl.when(joined & (g == 0))
    def _():
        packed = sym[0:16] + pltpu.roll(sym[16:32], LIVE, 1)
        pivs[u] = packed + pltpu.roll(pad_rows(sym[32:40], 16), 2 * LIVE, 1)
        piv_up.start()
        others(GROUP, u, lambda v: piv_copy(v, u).start())

    def coupling(k):
        weight = bound[k]
        total = jnp.zeros((SLOTS, SLOTS), F32)
        if k < 2:
            x = 0 if k == 0 else CX - 1
            for y in range(0, CY, 2):
                two = [field[x, j] * weight[j : j + 1] for j in (y, y + 1)]
                hi, lo = split(jnp.concatenate(two, 0))
                cols = slice(NZ * y // 2, NZ * (y + 2) // 2)
                high[:, cols], low[:, cols] = hi, lo
            face_copy(mirror[k]).wait_recv()
            both = nt(high[...], face_x[k]) + nt(low[...], face_x[k])
            both = pad_lanes(both, 128)
            block = both[:LIVE] + pltpu.roll(both[LIVE:], 128 - LIVE, 1)
            block = jnp.where(lanes_of((LIVE, 128)) < LIVE, block, 0.0)
        else:
            face_copy(mirror[k]).wait_recv()
            for x in range(CX):
                mine = field[x, 0 if k == 2 else CY - 1] * weight[x : x + 1]
                hi, lo = split(pad_rows(mine, SLOTS))
                other = face_y[k - 2, x]
                total = total + (nt(hi, other) + nt(lo, other))
            block = pad_lanes(total, 128)[:LIVE]
        return jnp.where(inside[k], -block, 0.0)

    found = {k: coupling(k) for k in (1, 3)}
    lane = lanes_of((LIVE, 128))
    odd = core == 1
    ahead = found[3]
    ahead_t = transposed(ahead)[:LIVE]
    message = jnp.where(odd, ahead, ahead_t) + pltpu.roll(jnp.where(odd, ahead_t, ahead), LIVE, 1)
    message = message + pltpu.roll(transposed(found[1])[:LIVE], 2 * LIVE, 1)
    message = jnp.where(lane >= 3 * LIVE, count.astype(F32), message)

    @pl.when(joined & (g == 0))
    def _():
        links[chip, core] = message
        link_up.start()
        others(GROUP // 2, chip, lambda v: link_copy(v, chip).start())

    @pl.when(joined & (g == 1))
    def _():
        piv_up.wait_recv()
        others(GROUP, u, lambda v: piv_copy(v, u).start())
        link_up.wait_recv()
        others(GROUP // 2, chip, lambda v: link_copy(v, chip).start())

    for k in (0, 2):
        found[k] = coupling(k)
    blocks_ref[0] = own
    for k in range(4):
        blocks_ref[k + 1] = pad_rows(found[k], SLOTS)
    blocks_ref[5] = sym

    @pl.when(joined)
    def _():
        others(GROUP // 2, chip, lambda v: link_copy(chip, v).wait_recv())
        core_copy(core).start()
        others(GROUP, u, lambda v: piv_copy(u, v).wait_recv())
        core_copy(1 - core).wait_recv()
        for v in range(GROUP):
            links_ref[v] = links[v // 2, v % 2]
            pivots_ref[v] = pivs[v]
        others(GROUP // 2, chip, lambda v: link_copy(v, chip).wait_send())
        others(GROUP, u, lambda v: piv_copy(v, u).wait_send())
        core_copy(core).wait_send()

    @pl.when(joined & (g == 0))
    def _():
        link_up.wait_send()
        piv_up.wait_send()

    for k in range(4):
        halo_copy(k).wait_send()
        face_copy(k).wait_send()


def assemble(count, modes, kappa, react):
    vmem = pl.BlockSpec(memory_space=pltpu.VMEM)
    hbm = pl.BlockSpec(memory_space=pltpu.HBM)
    dma = pltpu.SemaphoreType.DMA
    return pl.pallas_call(
        assemble_kernel,
        out_shape=(
            jax.ShapeDtypeStruct((6, SLOTS, 128), F32),
            jax.ShapeDtypeStruct((GROUP, LIVE, 128), F32),
            jax.ShapeDtypeStruct((GROUP, 16, 128), F32),
        ),
        in_specs=[pl.BlockSpec(memory_space=pltpu.SMEM), hbm, hbm, hbm],
        out_specs=(vmem, vmem, vmem),
        scratch_shapes=[
            pltpu.VMEM((CX, LIVE, CY, NZ), BF16),
            pltpu.VMEM((CX, CY, NZ), BF16),
            pltpu.VMEM((CX, CY, NZ), BF16),
            pltpu.VMEM((CX, CY, LIVE, NZ), F32),
            pltpu.VMEM((CX, SLOTS, CY * NZ), BF16),
            pltpu.VMEM((CX + 1, CY, NZ), F32),
            pltpu.VMEM((CX, 24, NZ), F32),
            pltpu.VMEM((CX, CY, NZ), F32),
            pltpu.VMEM((CX, CY, NZ), F32),
            pltpu.VMEM((4, 16, NZ), F32),
            pltpu.VMEM((4, 16, NZ), F32),
            pltpu.VMEM((2, 2 * LIVE, 8 * NZ), BF16),
            pltpu.VMEM((2, 16, SLOTS, NZ), BF16),
            pltpu.VMEM((2 * LIVE, 8 * NZ), BF16),
            pltpu.VMEM((2 * LIVE, 8 * NZ), BF16),
            pltpu.VMEM((2, 2 * LIVE, 8 * NZ), BF16),
            pltpu.VMEM((GROUP // 2, 2, LIVE, 128), F32),
            pltpu.VMEM((GROUP, 16, 128), F32),
            pltpu.VMEM((NZ, NZ), BF16),
            dma((CX,)),
            dma((2,)),
            dma((4,)),
            dma((4,)),
            dma((4,)),
            dma((4,)),
            dma((4,)),
            dma((GROUP // 2,)),
            dma((GROUP // 2,)),
            dma((2,)),
            dma((GROUP,)),
            dma((GROUP,)),
        ],
        compiler_params=pltpu.CompilerParams(
            collective_id=0, has_side_effects=True, vmem_limit_bytes=50 * 2**20
        ),
        name="assemble",
    )(count, modes, kappa, react)


def halves(x, rows, axis):
    hi, lo = split(pad_rows(x, rows) if x.shape[0] < rows else x)
    return jnp.concatenate([hi, lo], axis)


def joined_halves(out, rows):
    tall = out.shape[0] // 2
    return out[:rows, :128] + (out[:rows, 128:] + out[tall : tall + rows, :128])


def nn3(a, b):
    left = halves(a, SLOTS, 0)
    out = jnp.dot(left, halves(b, 128, 1), preferred_element_type=F32)
    return joined_halves(out, a.shape[0])


def nt3(a, b):
    out = nt(halves(a, SLOTS, 0), halves(b, 128, 0))
    return joined_halves(out, a.shape[0])


def wide(x):
    return jnp.broadcast_to(x, (8, 128))


def pivots(p, soff, state, spread_ref, rows_ref, side_ref):
    tiles, saved = (list(part) for part in state)
    sub = rows_of((8, 128))
    at = soff + 8 * p
    column = lambda v, c: wide(tiles[v][:, c : c + 1])
    if p == 0:
        for c in range(8):
            spread_ref[p, c] = column(p, at + c)
    rows_ref[p] = tiles[p]
    d = {(i, j): wide(spread_ref[p, j, i : i + 1]) for i in range(8) for j in range(i, 8)}
    rows = [wide(rows_ref[p, c : c + 1]) for c in range(8)]
    follow = p + 1 < LIVE // 8
    if follow:
        under = [column(p + 1, at + c) for c in range(8)]
        coming = [column(p + 1, at + 8 + c) for c in range(8)]
    others = [v for v in range(LIVE // 8) if v not in (p, p + 1)]
    factors = {v: [column(v, at + c) for c in range(8)] for v in others}
    low, rinv = {}, []
    for c in range(8):
        rinv.append(lax.rsqrt(d[c, c]))
        for i in range(c + 1, 8):
            low[c, i] = d[c, i] * rinv[c]
        for i in range(c + 1, 8):
            for j in range(i, 8):
                d[i, j] = d[i, j] - low[c, i] * low[c, j]
        rows[c] = rows[c] * rinv[c]
        saved[p] = jnp.where(sub == c, rows[c], saved[p])
        for i in range(c + 1, 8):
            rows[i] = rows[i] - low[c, i] * rows[c]
        if follow:
            under[c] = under[c] * rinv[c]
            side_ref[p, c] = under[c]
            for i in range(c + 1, 8):
                under[i] = under[i] - low[c, i] * under[c]
            for i in range(8):
                coming[i] = coming[i] - under[c] * wide(side_ref[p, c, i : i + 1])
            tiles[p + 1] = tiles[p + 1] - under[c] * rows[c]
    if follow:
        for c in range(8):
            spread_ref[p + 1, c] = coming[c]
    z = rows
    for c in range(7, -1, -1):
        z[c] = z[c] * rinv[c]
        for i in range(c):
            z[i] = z[i] - low[i, c] * z[c]
    for v in others:
        terms = [factors[v][c] * z[c] for c in range(8)]
        while len(terms) > 1:
            terms = [terms[i] + terms[i + 1] for i in range(0, len(terms), 2)]
        tiles[v] = tiles[v] - terms[0]
    for c in range(8):
        tiles[p] = jnp.where(sub == c, z[c], tiles[p])
    return tuple(tiles), tuple(saved)


def place(out_ref, block, pos, keep):
    base = jnp.minimum((pos // 128) * 128, NC - 256)
    base = pl.multiple_of(base, 128)
    shifted = pltpu.roll(pad_lanes(block, 256), pos - base, 1)
    cols = lanes_of((SLOTS, 256)) + base
    out_ref[:, pl.ds(base, 256)] += jnp.where(keep(cols), shifted, 0.0)


def factor_kernel(
    links_ref, pivots_ref, blocks_ref, out_ref, linv_ref, k_ref, g_ref, f_ref, x_ref, spread_ref, rows_ref, side_ref,
):
    g, u = lax.axis_index("grp"), lax.axis_index("sub")
    s = g * NU + u
    upper = s <= 21
    member = (s == 21) | (s == 22) | ((s >= NU) & (s < NU + NB))
    lane = lanes_of((LIVE, 128))
    row = rows_of((LIVE, 128))
    lane48 = lanes_of((SLOTS, 128))
    row48 = rows_of((SLOTS, 128))
    out_ref[...] = jnp.zeros_like(out_ref)
    before = lambda cols: cols < DONE
    after = lambda cols: cols >= DONE

    def left(x, by):
        x = pltpu.roll(x, 128 - by, 1) if by else x
        return jnp.where(lanes_of(x.shape) < LIVE, x, 0.0)

    def put(block, pos, late):
        base = pos // 128 * 128
        shifted = pltpu.roll(pad_lanes(block, 256), pos - base, 1) if pos > base else (
            pad_lanes(block, 256)
        )
        if base < DONE < base + 256:
            cols = lanes_of((SLOTS, 256)) + base
            shifted = jnp.where(cols >= DONE if late else cols < DONE, shifted, 0.0)
        out_ref[:, base : base + 256] += shifted

    def reduce_row(q):
        at, wide_enough = jnp.maximum(q, 0), jnp.where(q == NB - 1, 16, LIVE)
        mine = jnp.where(q == s, blocks_ref[5], 0.0)
        mine = jnp.where(q == s - 1, blocks_ref[3], mine)
        mine = jnp.where(q == s - NU, blocks_ref[1], mine)
        held = jnp.where(q > 0, f_ref[jnp.maximum(q - 1, 0)], 0.0)
        f = mine - nn3(held, pad_rows(k_ref[at], 128))
        f_ref[at] = jnp.where((q <= s) & (lane48 < wide_enough), f, 0.0)

    def solve_row(q):
        at = jnp.maximum(q, 0)
        x = nt3(f_ref[at], pad_rows(linv_ref[at], 128))
        x_ref[at] = jnp.where((q == s) & (lane48 > row48), 0.0, x)

    def double_row(q):
        at = jnp.maximum(q, 0)
        x = x_ref[at]
        g_ref[at] = nn3(x, pad_rows(linv_ref[at], 128))

    def pivot_block(t, at):
        packed = pivots_ref[t]
        parts = []
        for i in range(3):
            by = (at - LIVE * i) % 128
            parts.append(pltpu.roll(packed, by, 1) if by else packed)
        block = jnp.concatenate([parts[0], parts[1], parts[2][:8]], 0)
        return jnp.where((lane >= at) & (lane < at + LIVE), block, 0.0)

    def live_count(t):
        return jnp.max(jnp.where(lanes_of((8, 128)) >= 3 * LIVE, links_ref[t][0:8], 0.0))

    def at_rows(x, start):
        above = jnp.zeros((start, 128), F32)
        return pad_rows(jnp.concatenate([above, x], 0) if start else x, 128)

    def step(t, odd, scur, n):
        soff, uoff = (LIVE, 0) if odd else (0, LIVE)
        given = links_ref[t]
        limit = jnp.where(t == NB - 1, 16, LIVE)
        in_s = (lane >= soff) & (lane < soff + LIVE)
        in_u = (lane >= uoff) & (lane < uoff + LIVE)
        eye = jnp.where(lane == row + soff, 1.0, 0.0)
        a = jnp.where((row < limit) & (lane < soff + limit), scur, eye)
        rest = jnp.where(lane == row + 2 * LIVE, 1.0, 0.0)
        rest = jnp.where(in_u, jnp.where(row < limit, given, 0.0), rest)
        a = jnp.where(in_s, a, rest)
        ut = jnp.where(in_s, given, 0.0)
        tiles = tuple(a[8 * v : 8 * v + 8] for v in range(LIVE // 8))
        state = pivots(0, soff, (tiles, tiles), spread_ref, rows_ref, side_ref)

        double_row(t - 3)
        solve_row(t - 2)
        reduce_row(t - 1)
        following = jnp.minimum(t + 1, NB - 1)
        coming, coming_n = pivot_block(following, uoff), live_count(following)
        n = jnp.where(t == NB - 1, jnp.minimum(n, 16.0), n)
        for p in range(1, LIVE // 8):
            state = lax.cond(
                n > 8.0 * p,
                lambda st, p=p: pivots(p, soff, st, spread_ref, rows_ref, side_ref),
                lambda st: st,
                state,
            )
        tiles, saved = state
        k = jnp.concatenate(tiles, 0)
        snext = coming - nn3(ut, at_rows(k, soff))
        linv_ref[t] = left(jnp.concatenate(saved, 0), 2 * LIVE)
        k_ref[t + 1] = left(k, uoff)
        return snext, coming_n

    @pl.when(upper | member)
    def _():
        k_ref[0] = jnp.zeros((LIVE, 128), F32)
        linv_ref[0] = jnp.zeros((LIVE, 128), F32)
        f_ref[0] = jnp.zeros((SLOTS, 128), F32)
        x_ref[0] = jnp.zeros((SLOTS, 128), F32)
        def pair(i, carry):
            carry = step(2 * i, False, *carry)
            return step(2 * i + 1, True, *carry)

        lax.fori_loop(0, NB // 2, pair, (pivot_block(0, 0), live_count(0)))
        double_row(NB - 3)
        solve_row(NB - 2)
        reduce_row(NB - 1)
        double_row(NB - 2)
        solve_row(NB - 1)
        double_row(NB - 1)
        for t in range(NB):
            put(x_ref[t], SLOTS * t, False)

    @pl.when(upper)
    def _():
        dead = jnp.where((row48 == lane48) & (row48 >= LIVE), 1.0, 0.0)
        place(out_ref, dead, SLOTS * s, before)

    @pl.when(member)
    def _():
        late = lane >= 16
        last = jnp.where(row < 16, links_ref[NB - 1], 0.0)
        own = jnp.where(late & (row < 16), pivot_block(NB - 1, 0), 0.0)
        over = jnp.where(late, left(links_ref[NB - 2], LIVE), 0.0)
        y = None
        for t in range(NB - 1, -1, -1):
            if y is None:
                y = g_ref[t]
                put(-nn3(y, pad_rows(left(last, 0), 128)), SLOTS * NB, True)
                put(-nn3(y, pad_rows(own, 128)), SLOTS * (NB - 1), True)
            else:
                y = g_ref[t] - nt3(y, pad_rows(k_ref[t + 1], 128))
            if t == NB - 2:
                put(-nn3(y, pad_rows(over, 128)), SLOTS * (NB - 1), True)
            rising = pad_rows(left(links_ref[t], 2 * LIVE), 128)
            put(-nt3(y, rising), SLOTS * (t + NU), True)

    @pl.when(s >= 21)
    def _():
        targets = [s, s - NU, s + NU, s - 1, s + 1]
        valid = [True, g > 0, g < NG - 1, u > 0, u < NU - 1]
        for k in range(5):
            pos = SLOTS * jnp.clip(targets[k], 0, NG * NU - 1)
            place(out_ref, jnp.where(valid[k], blocks_ref[k], 0.0), pos, after)

    @pl.when(s == 21)
    def _():
        out_ref[0:16, DONE:] = jnp.zeros((16, NC - DONE), F32)


def factor(links, pivs, blocks):
    vmem = pl.BlockSpec(memory_space=pltpu.VMEM)
    return pl.pallas_call(
        factor_kernel,
        out_shape=jax.ShapeDtypeStruct((SLOTS, NC), F32),
        in_specs=[vmem, vmem, vmem],
        out_specs=vmem,
        scratch_shapes=[
            pltpu.VMEM((NB, LIVE, 128), F32),
            pltpu.VMEM((NB + 1, LIVE, 128), F32),
            pltpu.VMEM((NB, SLOTS, 128), F32),
            pltpu.VMEM((NB, SLOTS, 128), F32),
            pltpu.VMEM((NB, SLOTS, 128), F32),
            pltpu.VMEM((LIVE // 8, 8, 8, 128), F32),
            pltpu.VMEM((LIVE // 8, 8, 128), F32),
            pltpu.VMEM((LIVE // 8, 8, 8, 128), F32),
        ],
        compiler_params=pltpu.CompilerParams(vmem_limit_bytes=40 * 2**20),
        name="factor",
    )(links, pivs, blocks)


def per_device(modes, counts, kappa, react):
    blocks, links, pivs = assemble(counts, modes, kappa, react)
    return factor(links, pivs, blocks)


def solution(mesh):
    in_specs = (
        P(None, "grp", "sub", None),
        P(("grp", "sub")),
        P("grp", "sub", None),
        P("grp", "sub", None),
    )
    out_specs = P(("grp", "sub"), None)
    return jax.shard_map(
        per_device, mesh=mesh, in_specs=in_specs, out_specs=out_specs, check_vma=False
    )
```

```python
import jax
import jax.numpy as jnp
from jax import lax
from jax.experimental import pallas as pl
from jax.experimental.pallas import tpu as pltpu
from jax.sharding import PartitionSpec as P

F32 = jnp.float32
BF16 = jnp.bfloat16
MESH = pl.DeviceIdType.MESH
NG, NU = 4, 32
CX, CY, NZ = 16, 16, 256
SLOTS, LIVE = 48, 40
NB = 22
DONE = 1024
GROUP = 24
NC = SLOTS * NG * NU


def nt(a, b, precision=None):
    return lax.dot_general(
        a, b, (((1,), (1,)), ((), ())), preferred_element_type=F32, precision=precision
    )


def lanes_of(shape):
    return lax.broadcasted_iota(jnp.int32, shape, len(shape) - 1)


def rows_of(shape):
    return lax.broadcasted_iota(jnp.int32, shape, len(shape) - 2)


def split(x):
    hi = x.astype(BF16)
    return hi, (x - hi.astype(F32)).astype(BF16)


def pad_rows(x, rows):
    return jnp.concatenate([x, jnp.zeros((rows - x.shape[0], x.shape[1]), x.dtype)], 0)


def pad_lanes(x, lanes):
    return jnp.concatenate([x, jnp.zeros((x.shape[0], lanes - x.shape[1]), x.dtype)], 1)


def transposed(x):
    return jnp.transpose(pad_rows(x, 128))


def assemble_kernel(
    count_ref, modes_ref, kappa_ref, react_ref, blocks_ref, links_ref, pivots_ref,
    raw, kappa, react, field, masked, wx, wy, wz, diag, edge, halo, face_x, face_y,
    high, low, ends, links, pivs, order,
    raw_sem, cell_sem, halo_send, halo_recv, face_send, face_recv,
    up_sem, link_send, link_recv, piv_send, piv_recv, cross_send, cross_recv,
):
    g, u = lax.axis_index("grp"), lax.axis_index("sub")
    partners = [
        (lax.rem(g + NG - 1, NG), u),
        (lax.rem(g + 1, NG), u),
        (g, lax.rem(u + NU - 1, NU)),
        (g, lax.rem(u + 1, NU)),
    ]
    inside = [g > 0, g < NG - 1, u > 0, u < NU - 1]
    mirror = [1, 0, 3, 2]
    chip, core = u // 2, lax.rem(u, 2)
    joined = (g < 2) & (u < GROUP)

    def fetch(x):
        return pltpu.make_async_copy(
            modes_ref.at[pl.ds(0, LIVE), x], raw.at[x], raw_sem.at[x]
        )

    cells = [
        pltpu.make_async_copy(kappa_ref, kappa, cell_sem.at[0]),
        pltpu.make_async_copy(react_ref, react, cell_sem.at[1]),
    ]
    cells[0].start()
    for x in [0, CX - 1] + list(range(1, CX - 1)):
        fetch(x).start()
    cells[1].start()

    barrier = pltpu.get_barrier_semaphore()

    def greet(device):
        pl.semaphore_signal(barrier, inc=1, device_id=device, device_id_type=MESH)

    for partner in partners:
        greet(partner)

    def others(count, me, act):
        for step in range(1, count):
            v = me + step
            act(jnp.where(v >= count, v - count, v))

    @pl.when(joined)
    def _():
        others(GROUP // 2, chip, lambda v: greet((g, 2 * v + core)))
        greet((g, 2 * chip + 1 - core))

    count = count_ref[0]
    z_from, z_to = rows_of((NZ, NZ)), lanes_of((NZ, NZ))
    here = z_from == jnp.where(z_to < 128, 2 * z_to, 2 * z_to - 255)
    order[...] = jnp.where(here, 1.0, 0.0).astype(BF16)

    def ordered(x):
        return jnp.dot(x.reshape(-1, NZ), order[...], preferred_element_type=F32)

    cells[0].wait()
    kap = ordered(kappa[...]).reshape(CX, CY, NZ)
    edge[0] = kap[0]
    edge[1] = kap[CX - 1]
    for x in range(CX):
        edge[2, x : x + 1] = kap[x, 0:1]
        edge[3, x : x + 1] = kap[x, CY - 1 : CY]

    live = rows_of((CY, LIVE, NZ)) < count

    def turn(x, side=None):
        plane = jnp.swapaxes(ordered(raw[x]).reshape(LIVE, CY, NZ), 0, 1)
        plane = jnp.where(live, plane, 0.0)
        field[x] = plane
        for y in range(CY):
            masked[x, :, NZ * y : NZ * (y + 1)] = pad_rows(plane[y], SLOTS).astype(BF16)
        if side is not None:
            for y in range(0, CY, 2):
                two = jnp.concatenate([plane[y], plane[y + 1]], 0)
                ends[side, :, NZ * y // 2 : NZ * (y + 2) // 2] = two.astype(BF16)

    fetch(0).wait()
    fetch(CX - 1).wait()
    turn(0, 0)
    turn(CX - 1, 1)
    pl.semaphore_wait(barrier, jnp.where(joined, GROUP // 2 + 4, 4))

    def halo_copy(k):
        return pltpu.make_async_remote_copy(
            src_ref=edge.at[k], dst_ref=halo.at[mirror[k]],
            send_sem=halo_send.at[k], recv_sem=halo_recv.at[mirror[k]],
            device_id=partners[k], device_id_type=MESH,
        )

    sources = [
        ends.at[0],
        ends.at[1],
        masked.at[:, :, pl.ds(0, NZ)],
        masked.at[:, :, pl.ds((CY - 1) * NZ, NZ)],
    ]
    landings = [face_x.at[0], face_x.at[1], face_y.at[0], face_y.at[1]]

    def face_copy(k):
        return pltpu.make_async_remote_copy(
            src_ref=sources[k], dst_ref=landings[mirror[k]],
            send_sem=face_send.at[k], recv_sem=face_recv.at[mirror[k]],
            device_id=partners[k], device_id_type=MESH,
        )

    for k in range(4):
        halo_copy(k).start()
    face_copy(0).start()
    face_copy(1).start()

    def turn_next(i, carry):
        fetch(2 * i + 1).wait()
        fetch(2 * i + 2).wait()
        turn(2 * i + 1)
        turn(2 * i + 2)
        return carry

    lax.fori_loop(0, CX // 2 - 1, turn_next, 0)
    face_copy(2).start()
    face_copy(3).start()

    plane0 = jnp.zeros((CY, NZ), F32)
    row0 = jnp.zeros((1, NZ), F32)
    half = lanes_of((CY, 128))
    wx[0] = plane0
    wx[CX] = plane0
    for x in range(CX - 1):
        wx[x + 1] = 0.5 * (kap[x] + kap[x + 1])
    for x in range(CX):
        k = kap[x]
        wy[x, 0:1] = row0
        wy[x, 1:CY] = 0.5 * (k[: CY - 1] + k[1:])
        wy[x, CY : CY + 1] = row0
        even, uneven = k[:, :128], k[:, 128:]
        wz[x, :, 0:128] = 0.5 * (even + uneven)
        wz[x, :, 128:] = jnp.where(half == 127, 0.0, 0.5 * (uneven + pltpu.roll(even, 127, 1)))
    cells[1].wait()
    reac = ordered(react[...]).reshape(CX, CY, NZ)
    for k in range(4):
        halo_copy(k).wait_recv()
    ext = [jnp.where(inside[k], halo[k], 0.0) for k in range(4)]
    bound = [0.5 * (edge[k] + ext[k]) for k in range(4)]
    for x in range(CX):
        k = kap[x]
        inner, outer = wz[x, :, 0:128], wz[x, :, 128:]
        below = jnp.where(half == 0, 0.5 * k[:, :128], pltpu.roll(outer, 1, 1))
        above = jnp.where(half == 127, 0.5 * k[:, 128:], outer)
        dz = jnp.concatenate([below + inner, inner + above], 1)
        dx = (bound[0] if x == 0 else wx[x]) + (bound[1] if x == CX - 1 else wx[x + 1])
        dy = wy[x, 0:CY] + wy[x, 1 : CY + 1]
        dy = dy + jnp.concatenate(
            [bound[2][x : x + 1], jnp.zeros((CY - 2, NZ), F32), bound[3][x : x + 1]], 0
        )
        diag[x] = reac[x] + dx + dy + dz

    def apply(x, gram):
        before, after = jnp.maximum(x - 1, 0), jnp.minimum(x + 1, CX - 1)
        behind, v = None, field[x, 0]
        for y in range(CY):
            ahead = field[x, y + 1] if y < CY - 1 else None
            out = diag[x, y : y + 1] * v
            out = out - wx[x, y : y + 1] * field[before, y]
            out = out - wx[x + 1, y : y + 1] * field[after, y]
            if y > 0:
                out = out - wy[x, y : y + 1] * behind
            if y < CY - 1:
                out = out - wy[x, y + 1 : y + 2] * ahead
            even, uneven = v[:, :128], v[:, 128:]
            inner, outer = wz[x, y : y + 1, 0:128], wz[x, y : y + 1, 128:]
            out = out - jnp.concatenate(
                [
                    inner * uneven + pltpu.roll(outer * uneven, 1, 1),
                    inner * even + outer * pltpu.roll(even, 127, 1),
                ],
                1,
            )
            local = pad_rows(out, SLOTS).astype(BF16)
            gram = gram + nt(masked[x, :, NZ * y : NZ * (y + 1)], local)
            behind, v = v, ahead
        return gram

    gram = lax.fori_loop(
        0, CX // 2, lambda i, gram: apply(2 * i + 1, apply(2 * i, gram)),
        jnp.zeros((SLOTS, SLOTS), F32),
    )
    own = pad_lanes(gram, 128)
    spot, slot = lanes_of((SLOTS, 128)), rows_of((SLOTS, 128))
    own = own + jnp.where((spot == slot) & (slot >= count), 1.0, 0.0)
    sym = jnp.where(spot < LIVE, 0.5 * (own + transposed(own)[:SLOTS]), 0.0)

    def up_copy(ref, i):
        return pltpu.make_async_remote_copy(
            src_ref=ref, dst_ref=ref, send_sem=up_sem.at[i], recv_sem=up_sem.at[i + 2],
            device_id=(1, u), device_id_type=MESH,
        )

    def link_copy(to, owner):
        return pltpu.make_async_remote_copy(
            src_ref=links.at[owner, core], dst_ref=links.at[owner, core],
            send_sem=link_send.at[to], recv_sem=link_recv.at[owner],
            device_id=(g, 2 * to + core), device_id_type=MESH,
        )

    def piv_copy(to, owner):
        return pltpu.make_async_remote_copy(
            src_ref=pivs.at[owner, core], dst_ref=pivs.at[owner, core],
            send_sem=piv_send.at[to], recv_sem=piv_recv.at[owner],
            device_id=(g, 2 * to + core), device_id_type=MESH,
        )

    def cross_copy(ref, sem):
        return pltpu.make_async_remote_copy(
            src_ref=ref, dst_ref=ref, send_sem=cross_send.at[sem], recv_sem=cross_recv.at[sem],
            device_id=(g, 2 * chip + 1 - core), device_id_type=MESH,
        )

    def cross_link(v, c):
        return cross_copy(links.at[v, c], v)

    def cross_pivs(c):
        return cross_copy(pivs.at[:, c], GROUP // 2)

    link_up, piv_up = up_copy(links.at[chip, core], 0), up_copy(pivs.at[chip, core], 1)

    @pl.when(joined & (g == 0))
    def _():
        packed = sym[0:16] + pltpu.roll(sym[16:32], LIVE, 1)
        pivs[chip, core] = packed + pltpu.roll(pad_rows(sym[32:40], 16), 2 * LIVE, 1)
        piv_up.start()
        others(GROUP // 2, chip, lambda v: piv_copy(v, chip).start())

    def coupling(k):
        weight = bound[k]
        total = jnp.zeros((SLOTS, SLOTS), F32)
        if k < 2:
            x = 0 if k == 0 else CX - 1
            for y in range(0, CY, 2):
                two = [field[x, j] * weight[j : j + 1] for j in (y, y + 1)]
                hi, lo = split(jnp.concatenate(two, 0))
                cols = slice(NZ * y // 2, NZ * (y + 2) // 2)
                high[:, cols], low[:, cols] = hi, lo
            face_copy(mirror[k]).wait_recv()
            both = nt(high[...], face_x[k]) + nt(low[...], face_x[k])
            both = pad_lanes(both, 128)
            block = both[:LIVE] + pltpu.roll(both[LIVE:], 128 - LIVE, 1)
            block = jnp.where(lanes_of((LIVE, 128)) < LIVE, block, 0.0)
        else:
            face_copy(mirror[k]).wait_recv()
            for x in range(CX):
                mine = field[x, 0 if k == 2 else CY - 1] * weight[x : x + 1]
                hi, lo = split(pad_rows(mine, SLOTS))
                other = face_y[k - 2, x]
                total = total + (nt(hi, other) + nt(lo, other))
            block = pad_lanes(total, 128)[:LIVE]
        return jnp.where(inside[k], -block, 0.0)

    found = {k: coupling(k) for k in (1, 3)}
    lane = lanes_of((LIVE, 128))
    odd = core == 1
    ahead = found[3]
    ahead_t = transposed(ahead)[:LIVE]
    message = jnp.where(odd, ahead, ahead_t) + pltpu.roll(jnp.where(odd, ahead_t, ahead), LIVE, 1)
    message = message + pltpu.roll(transposed(found[1])[:LIVE], 2 * LIVE, 1)
    message = jnp.where(lane >= 3 * LIVE, count.astype(F32), message)

    @pl.when(joined & (g == 0))
    def _():
        links[chip, core] = message
        link_up.start()
        others(GROUP // 2, chip, lambda v: link_copy(v, chip).start())

    @pl.when(joined & (g == 1))
    def _():
        piv_up.wait_recv()
        others(GROUP // 2, chip, lambda v: piv_copy(v, chip).start())
        link_up.wait_recv()
        others(GROUP // 2, chip, lambda v: link_copy(v, chip).start())

    for k in (0, 2):
        found[k] = coupling(k)
    blocks_ref[0] = own
    for k in range(4):
        blocks_ref[k + 1] = pad_rows(found[k], SLOTS)
    blocks_ref[5] = sym

    @pl.when(joined)
    def _():
        others(GROUP // 2, chip, lambda v: piv_copy(chip, v).wait_recv())
        cross_pivs(core).start()
        cross_link(chip, core).start()

        def forward(v):
            link_copy(chip, v).wait_recv()
            cross_link(v, core).start()

        others(GROUP // 2, chip, forward)
        cross_pivs(1 - core).wait_recv()
        for v in range(GROUP // 2):
            cross_link(v, 1 - core).wait_recv()
        for v in range(GROUP):
            links_ref[v] = links[v // 2, v % 2]
            pivots_ref[v] = pivs[v // 2, v % 2]
        others(GROUP // 2, chip, lambda v: link_copy(v, chip).wait_send())
        others(GROUP // 2, chip, lambda v: piv_copy(v, chip).wait_send())
        cross_pivs(core).wait_send()
        for v in range(GROUP // 2):
            cross_link(v, core).wait_send()

    @pl.when(joined & (g == 0))
    def _():
        link_up.wait_send()
        piv_up.wait_send()

    for k in range(4):
        halo_copy(k).wait_send()
        face_copy(k).wait_send()


def assemble(count, modes, kappa, react):
    vmem = pl.BlockSpec(memory_space=pltpu.VMEM)
    hbm = pl.BlockSpec(memory_space=pltpu.HBM)
    dma = pltpu.SemaphoreType.DMA
    return pl.pallas_call(
        assemble_kernel,
        out_shape=(
            jax.ShapeDtypeStruct((6, SLOTS, 128), F32),
            jax.ShapeDtypeStruct((GROUP, LIVE, 128), F32),
            jax.ShapeDtypeStruct((GROUP, 16, 128), F32),
        ),
        in_specs=[pl.BlockSpec(memory_space=pltpu.SMEM), hbm, hbm, hbm],
        out_specs=(vmem, vmem, vmem),
        scratch_shapes=[
            pltpu.VMEM((CX, LIVE, CY, NZ), BF16),
            pltpu.VMEM((CX, CY, NZ), BF16),
            pltpu.VMEM((CX, CY, NZ), BF16),
            pltpu.VMEM((CX, CY, LIVE, NZ), F32),
            pltpu.VMEM((CX, SLOTS, CY * NZ), BF16),
            pltpu.VMEM((CX + 1, CY, NZ), F32),
            pltpu.VMEM((CX, 24, NZ), F32),
            pltpu.VMEM((CX, CY, NZ), F32),
            pltpu.VMEM((CX, CY, NZ), F32),
            pltpu.VMEM((4, 16, NZ), F32),
            pltpu.VMEM((4, 16, NZ), F32),
            pltpu.VMEM((2, 2 * LIVE, 8 * NZ), BF16),
            pltpu.VMEM((2, 16, SLOTS, NZ), BF16),
            pltpu.VMEM((2 * LIVE, 8 * NZ), BF16),
            pltpu.VMEM((2 * LIVE, 8 * NZ), BF16),
            pltpu.VMEM((2, 2 * LIVE, 8 * NZ), BF16),
            pltpu.VMEM((GROUP // 2, 2, LIVE, 128), F32),
            pltpu.VMEM((GROUP // 2, 2, 16, 128), F32),
            pltpu.VMEM((NZ, NZ), BF16),
            dma((CX,)),
            dma((2,)),
            dma((4,)),
            dma((4,)),
            dma((4,)),
            dma((4,)),
            dma((4,)),
            dma((GROUP // 2,)),
            dma((GROUP // 2,)),
            dma((GROUP // 2,)),
            dma((GROUP // 2,)),
            dma((GROUP // 2 + 1,)),
            dma((GROUP // 2 + 1,)),
        ],
        compiler_params=pltpu.CompilerParams(
            collective_id=0, has_side_effects=True, vmem_limit_bytes=50 * 2**20
        ),
        name="assemble",
    )(count, modes, kappa, react)


def halves(x, rows, axis):
    hi, lo = split(pad_rows(x, rows) if x.shape[0] < rows else x)
    return jnp.concatenate([hi, lo], axis)


def joined_halves(out, rows):
    tall = out.shape[0] // 2
    return out[:rows, :128] + (out[:rows, 128:] + out[tall : tall + rows, :128])


def nn3(a, b):
    left = halves(a, SLOTS, 0)
    out = jnp.dot(left, halves(b, 128, 1), preferred_element_type=F32)
    return joined_halves(out, a.shape[0])


def nt3(a, b):
    out = nt(halves(a, SLOTS, 0), halves(b, 128, 0))
    return joined_halves(out, a.shape[0])


def wide(x):
    return jnp.broadcast_to(x, (8, 128))


def pivots(p, soff, state, spread_ref, rows_ref, side_ref):
    tiles, saved = (list(part) for part in state)
    sub = rows_of((8, 128))
    at = soff + 8 * p
    column = lambda v, c: wide(tiles[v][:, c : c + 1])
    if p == 0:
        for c in range(8):
            spread_ref[p, c] = column(p, at + c)
    rows_ref[p] = tiles[p]
    d = {(i, j): wide(spread_ref[p, j, i : i + 1]) for i in range(8) for j in range(i, 8)}
    rows = [wide(rows_ref[p, c : c + 1]) for c in range(8)]
    follow = p + 1 < LIVE // 8
    if follow:
        under = [column(p + 1, at + c) for c in range(8)]
        coming = [column(p + 1, at + 8 + c) for c in range(8)]
    others = [v for v in range(LIVE // 8) if v not in (p, p + 1)]
    factors = {v: [column(v, at + c) for c in range(8)] for v in others}
    low, rinv = {}, []
    for c in range(8):
        rinv.append(lax.rsqrt(d[c, c]))
        for i in range(c + 1, 8):
            low[c, i] = d[c, i] * rinv[c]
        for i in range(c + 1, 8):
            for j in range(i, 8):
                d[i, j] = d[i, j] - low[c, i] * low[c, j]
        rows[c] = rows[c] * rinv[c]
        saved[p] = jnp.where(sub == c, rows[c], saved[p])
        for i in range(c + 1, 8):
            rows[i] = rows[i] - low[c, i] * rows[c]
        if follow:
            under[c] = under[c] * rinv[c]
            side_ref[p, c] = under[c]
            for i in range(c + 1, 8):
                under[i] = under[i] - low[c, i] * under[c]
            for i in range(8):
                coming[i] = coming[i] - under[c] * wide(side_ref[p, c, i : i + 1])
            tiles[p + 1] = tiles[p + 1] - under[c] * rows[c]
    if follow:
        for c in range(8):
            spread_ref[p + 1, c] = coming[c]
    z = rows
    for c in range(7, -1, -1):
        z[c] = z[c] * rinv[c]
        for i in range(c):
            z[i] = z[i] - low[i, c] * z[c]
    for v in others:
        terms = [factors[v][c] * z[c] for c in range(8)]
        while len(terms) > 1:
            terms = [terms[i] + terms[i + 1] for i in range(0, len(terms), 2)]
        tiles[v] = tiles[v] - terms[0]
    for c in range(8):
        tiles[p] = jnp.where(sub == c, z[c], tiles[p])
    return tuple(tiles), tuple(saved)


def place(out_ref, block, pos, keep):
    base = jnp.minimum((pos // 128) * 128, NC - 256)
    base = pl.multiple_of(base, 128)
    shifted = pltpu.roll(pad_lanes(block, 256), pos - base, 1)
    cols = lanes_of((SLOTS, 256)) + base
    out_ref[:, pl.ds(base, 256)] += jnp.where(keep(cols), shifted, 0.0)


def factor_kernel(
    links_ref, pivots_ref, blocks_ref, out_ref, linv_ref, k_ref, g_ref, f_ref, x_ref, spread_ref, rows_ref, side_ref,
):
    g, u = lax.axis_index("grp"), lax.axis_index("sub")
    s = g * NU + u
    upper = s <= 21
    member = (s == 21) | (s == 22) | ((s >= NU) & (s < NU + NB))
    lane = lanes_of((LIVE, 128))
    row = rows_of((LIVE, 128))
    lane48 = lanes_of((SLOTS, 128))
    row48 = rows_of((SLOTS, 128))
    out_ref[...] = jnp.zeros_like(out_ref)
    before = lambda cols: cols < DONE
    after = lambda cols: cols >= DONE

    def left(x, by):
        x = pltpu.roll(x, 128 - by, 1) if by else x
        return jnp.where(lanes_of(x.shape) < LIVE, x, 0.0)

    def put(block, pos, late):
        base = pos // 128 * 128
        shifted = pltpu.roll(pad_lanes(block, 256), pos - base, 1) if pos > base else (
            pad_lanes(block, 256)
        )
        if base < DONE < base + 256:
            cols = lanes_of((SLOTS, 256)) + base
            shifted = jnp.where(cols >= DONE if late else cols < DONE, shifted, 0.0)
        out_ref[:, base : base + 256] += shifted

    def reduce_row(q):
        at, wide_enough = jnp.maximum(q, 0), jnp.where(q == NB - 1, 16, LIVE)
        mine = jnp.where(q == s, blocks_ref[5], 0.0)
        mine = jnp.where(q == s - 1, blocks_ref[3], mine)
        mine = jnp.where(q == s - NU, blocks_ref[1], mine)
        held = jnp.where(q > 0, f_ref[jnp.maximum(q - 1, 0)], 0.0)
        f = mine - nn3(held, pad_rows(k_ref[at], 128))
        f_ref[at] = jnp.where((q <= s) & (lane48 < wide_enough), f, 0.0)

    def solve_row(q):
        at = jnp.maximum(q, 0)
        x = nt3(f_ref[at], pad_rows(linv_ref[at], 128))
        x_ref[at] = jnp.where((q == s) & (lane48 > row48), 0.0, x)

    def double_row(q):
        at = jnp.maximum(q, 0)
        x = x_ref[at]
        g_ref[at] = nn3(x, pad_rows(linv_ref[at], 128))

    def pivot_block(t, at):
        packed = pivots_ref[t]
        parts = []
        for i in range(3):
            by = (at - LIVE * i) % 128
            parts.append(pltpu.roll(packed, by, 1) if by else packed)
        block = jnp.concatenate([parts[0], parts[1], parts[2][:8]], 0)
        return jnp.where((lane >= at) & (lane < at + LIVE), block, 0.0)

    def live_count(t):
        return jnp.max(jnp.where(lanes_of((8, 128)) >= 3 * LIVE, links_ref[t][0:8], 0.0))

    def at_rows(x, start):
        above = jnp.zeros((start, 128), F32)
        return pad_rows(jnp.concatenate([above, x], 0) if start else x, 128)

    def step(t, odd, scur, n):
        soff, uoff = (LIVE, 0) if odd else (0, LIVE)
        given = links_ref[t]
        limit = jnp.where(t == NB - 1, 16, LIVE)
        in_s = (lane >= soff) & (lane < soff + LIVE)
        in_u = (lane >= uoff) & (lane < uoff + LIVE)
        eye = jnp.where(lane == row + soff, 1.0, 0.0)
        a = jnp.where((row < limit) & (lane < soff + limit), scur, eye)
        rest = jnp.where(lane == row + 2 * LIVE, 1.0, 0.0)
        rest = jnp.where(in_u, jnp.where(row < limit, given, 0.0), rest)
        a = jnp.where(in_s, a, rest)
        ut = jnp.where(in_s, given, 0.0)
        tiles = tuple(a[8 * v : 8 * v + 8] for v in range(LIVE // 8))
        state = pivots(0, soff, (tiles, tiles), spread_ref, rows_ref, side_ref)

        double_row(t - 3)
        solve_row(t - 2)
        reduce_row(t - 1)
        following = jnp.minimum(t + 1, NB - 1)
        coming, coming_n = pivot_block(following, uoff), live_count(following)
        n = jnp.where(t == NB - 1, jnp.minimum(n, 16.0), n)
        for p in range(1, LIVE // 8):
            state = lax.cond(
                n > 8.0 * p,
                lambda st, p=p: pivots(p, soff, st, spread_ref, rows_ref, side_ref),
                lambda st: st,
                state,
            )
        tiles, saved = state
        k = jnp.concatenate(tiles, 0)
        snext = coming - nn3(ut, at_rows(k, soff))
        linv_ref[t] = left(jnp.concatenate(saved, 0), 2 * LIVE)
        k_ref[t + 1] = left(k, uoff)
        return snext, coming_n

    @pl.when(upper | member)
    def _():
        k_ref[0] = jnp.zeros((LIVE, 128), F32)
        linv_ref[0] = jnp.zeros((LIVE, 128), F32)
        f_ref[0] = jnp.zeros((SLOTS, 128), F32)
        x_ref[0] = jnp.zeros((SLOTS, 128), F32)
        def pair(i, carry):
            carry = step(2 * i, False, *carry)
            return step(2 * i + 1, True, *carry)

        lax.fori_loop(0, NB // 2, pair, (pivot_block(0, 0), live_count(0)))
        double_row(NB - 3)
        solve_row(NB - 2)
        reduce_row(NB - 1)
        double_row(NB - 2)
        solve_row(NB - 1)
        double_row(NB - 1)
        for t in range(NB):
            put(x_ref[t], SLOTS * t, False)

    @pl.when(upper)
    def _():
        dead = jnp.where((row48 == lane48) & (row48 >= LIVE), 1.0, 0.0)
        place(out_ref, dead, SLOTS * s, before)

    @pl.when(member)
    def _():
        late = lane >= 16
        last = jnp.where(row < 16, links_ref[NB - 1], 0.0)
        own = jnp.where(late & (row < 16), pivot_block(NB - 1, 0), 0.0)
        over = jnp.where(late, left(links_ref[NB - 2], LIVE), 0.0)
        y = None
        for t in range(NB - 1, -1, -1):
            if y is None:
                y = g_ref[t]
                put(-nn3(y, pad_rows(left(last, 0), 128)), SLOTS * NB, True)
                put(-nn3(y, pad_rows(own, 128)), SLOTS * (NB - 1), True)
            else:
                y = g_ref[t] - nt3(y, pad_rows(k_ref[t + 1], 128))
            if t == NB - 2:
                put(-nn3(y, pad_rows(over, 128)), SLOTS * (NB - 1), True)
            rising = pad_rows(left(links_ref[t], 2 * LIVE), 128)
            put(-nt3(y, rising), SLOTS * (t + NU), True)

    @pl.when(s >= 21)
    def _():
        targets = [s, s - NU, s + NU, s - 1, s + 1]
        valid = [True, g > 0, g < NG - 1, u > 0, u < NU - 1]
        for k in range(5):
            pos = SLOTS * jnp.clip(targets[k], 0, NG * NU - 1)
            place(out_ref, jnp.where(valid[k], blocks_ref[k], 0.0), pos, after)

    @pl.when(s == 21)
    def _():
        out_ref[0:16, DONE:] = jnp.zeros((16, NC - DONE), F32)


def factor(links, pivs, blocks):
    vmem = pl.BlockSpec(memory_space=pltpu.VMEM)
    return pl.pallas_call(
        factor_kernel,
        out_shape=jax.ShapeDtypeStruct((SLOTS, NC), F32),
        in_specs=[vmem, vmem, vmem],
        out_specs=vmem,
        scratch_shapes=[
            pltpu.VMEM((NB, LIVE, 128), F32),
            pltpu.VMEM((NB + 1, LIVE, 128), F32),
            pltpu.VMEM((NB, SLOTS, 128), F32),
            pltpu.VMEM((NB, SLOTS, 128), F32),
            pltpu.VMEM((NB, SLOTS, 128), F32),
            pltpu.VMEM((LIVE // 8, 8, 8, 128), F32),
            pltpu.VMEM((LIVE // 8, 8, 128), F32),
            pltpu.VMEM((LIVE // 8, 8, 8, 128), F32),
        ],
        compiler_params=pltpu.CompilerParams(vmem_limit_bytes=40 * 2**20),
        name="factor",
    )(links, pivs, blocks)


def per_device(modes, counts, kappa, react):
    kappa = pltpu.with_memory_space_constraint(kappa, pltpu.HBM)
    react = pltpu.with_memory_space_constraint(react, pltpu.HBM)
    blocks, links, pivs = assemble(counts, modes, kappa, react)
    return factor(links, pivs, blocks)


def solution(mesh):
    in_specs = (
        P(None, "grp", "sub", None),
        P(("grp", "sub")),
        P("grp", "sub", None),
        P("grp", "sub", None),
    )
    out_specs = P(("grp", "sub"), None)
    return jax.shard_map(
        per_device, mesh=mesh, in_specs=in_specs, out_specs=out_specs, check_vma=False
    )
```

```python
import jax
import jax.numpy as jnp
from jax import lax
from jax.experimental import pallas as pl
from jax.experimental.pallas import tpu as pltpu
from jax.sharding import PartitionSpec as P

F32 = jnp.float32
BF16 = jnp.bfloat16
MESH = pl.DeviceIdType.MESH
NG, NU = 4, 32
CX, CY, NZ = 16, 16, 256
SLOTS, LIVE = 48, 40
NB = 22
DONE = 1024
GROUP = 24
NC = SLOTS * NG * NU


def nt(a, b, precision=None):
    return lax.dot_general(
        a, b, (((1,), (1,)), ((), ())), preferred_element_type=F32, precision=precision
    )


def lanes_of(shape):
    return lax.broadcasted_iota(jnp.int32, shape, len(shape) - 1)


def rows_of(shape):
    return lax.broadcasted_iota(jnp.int32, shape, len(shape) - 2)


def split(x):
    hi = x.astype(BF16)
    return hi, (x - hi.astype(F32)).astype(BF16)


def pad_rows(x, rows):
    return jnp.concatenate([x, jnp.zeros((rows - x.shape[0], x.shape[1]), x.dtype)], 0)


def pad_lanes(x, lanes):
    return jnp.concatenate([x, jnp.zeros((x.shape[0], lanes - x.shape[1]), x.dtype)], 1)


def transposed(x):
    return jnp.transpose(pad_rows(x, 128))


def assemble_kernel(
    count_ref, modes_ref, kappa_ref, react_ref, blocks_ref, links_ref, pivots_ref,
    raw, kappa, react, field, masked, wx, wy, wz, diag, edge, halo, face_x, face_y,
    high, low, ends, links, pivs, order,
    raw_sem, cell_sem, halo_send, halo_recv, face_send, face_recv,
    up_sem, link_send, link_recv, piv_send, piv_recv, cross_send, cross_recv,
):
    g, u = lax.axis_index("grp"), lax.axis_index("sub")
    partners = [
        (lax.rem(g + NG - 1, NG), u),
        (lax.rem(g + 1, NG), u),
        (g, lax.rem(u + NU - 1, NU)),
        (g, lax.rem(u + 1, NU)),
    ]
    inside = [g > 0, g < NG - 1, u > 0, u < NU - 1]
    mirror = [1, 0, 3, 2]
    chip, core = u // 2, lax.rem(u, 2)
    joined = (g < 2) & (u < GROUP)

    def fetch(x):
        return pltpu.make_async_copy(
            modes_ref.at[pl.ds(0, LIVE), x], raw.at[x], raw_sem.at[x]
        )

    cells = [
        pltpu.make_async_copy(kappa_ref, kappa, cell_sem.at[0]),
        pltpu.make_async_copy(react_ref, react, cell_sem.at[1]),
    ]
    cells[0].start()
    for x in [0, CX - 1] + list(range(1, CX - 1)):
        fetch(x).start()
    cells[1].start()

    barrier = pltpu.get_barrier_semaphore()

    def greet(device):
        pl.semaphore_signal(barrier, inc=1, device_id=device, device_id_type=MESH)

    for partner in partners:
        greet(partner)

    def others(count, me, act):
        for step in range(1, count):
            v = me + step
            act(jnp.where(v >= count, v - count, v))

    @pl.when(joined)
    def _():
        others(GROUP // 2, chip, lambda v: greet((g, 2 * v + core)))
        greet((g, 2 * chip + 1 - core))

    count = count_ref[0]
    z_from, z_to = rows_of((NZ, NZ)), lanes_of((NZ, NZ))
    here = z_from == jnp.where(z_to < 128, 2 * z_to, 2 * z_to - 255)
    order[...] = jnp.where(here, 1.0, 0.0).astype(BF16)

    def ordered(x):
        return jnp.dot(x.reshape(-1, NZ), order[...], preferred_element_type=F32)

    cells[0].wait()
    kap = ordered(kappa[...]).reshape(CX, CY, NZ)
    edge[0] = kap[0]
    edge[1] = kap[CX - 1]
    for x in range(CX):
        edge[2, x : x + 1] = kap[x, 0:1]
        edge[3, x : x + 1] = kap[x, CY - 1 : CY]

    live = rows_of((CY, LIVE, NZ)) < count

    def turn(x, side=None):
        plane = jnp.swapaxes(ordered(raw[x]).reshape(LIVE, CY, NZ), 0, 1)
        plane = jnp.where(live, plane, 0.0)
        field[x] = plane
        for y in range(CY):
            masked[x, :, NZ * y : NZ * (y + 1)] = pad_rows(plane[y], SLOTS).astype(BF16)
        if side is not None:
            for y in range(0, CY, 2):
                two = jnp.concatenate([plane[y], plane[y + 1]], 0)
                ends[side, :, NZ * y // 2 : NZ * (y + 2) // 2] = two.astype(BF16)

    fetch(0).wait()
    fetch(CX - 1).wait()
    turn(0, 0)
    turn(CX - 1, 1)
    pl.semaphore_wait(barrier, jnp.where(joined, GROUP // 2 + 4, 4))

    def halo_copy(k):
        return pltpu.make_async_remote_copy(
            src_ref=edge.at[k], dst_ref=halo.at[mirror[k]],
            send_sem=halo_send.at[k], recv_sem=halo_recv.at[mirror[k]],
            device_id=partners[k], device_id_type=MESH,
        )

    sources = [
        ends.at[0],
        ends.at[1],
        masked.at[:, :, pl.ds(0, NZ)],
        masked.at[:, :, pl.ds((CY - 1) * NZ, NZ)],
    ]
    landings = [face_x.at[0], face_x.at[1], face_y.at[0], face_y.at[1]]

    def face_copy(k):
        return pltpu.make_async_remote_copy(
            src_ref=sources[k], dst_ref=landings[mirror[k]],
            send_sem=face_send.at[k], recv_sem=face_recv.at[mirror[k]],
            device_id=partners[k], device_id_type=MESH,
        )

    for k in range(4):
        halo_copy(k).start()
    face_copy(0).start()
    face_copy(1).start()

    def turn_next(i, carry):
        fetch(2 * i + 1).wait()
        fetch(2 * i + 2).wait()
        turn(2 * i + 1)
        turn(2 * i + 2)
        return carry

    lax.fori_loop(0, CX // 2 - 1, turn_next, 0)
    face_copy(2).start()
    face_copy(3).start()

    plane0 = jnp.zeros((CY, NZ), F32)
    row0 = jnp.zeros((1, NZ), F32)
    half = lanes_of((CY, 128))
    wx[0] = plane0
    wx[CX] = plane0
    for x in range(CX - 1):
        wx[x + 1] = 0.5 * (kap[x] + kap[x + 1])
    for x in range(CX):
        k = kap[x]
        wy[x, 0:1] = row0
        wy[x, 1:CY] = 0.5 * (k[: CY - 1] + k[1:])
        wy[x, CY : CY + 1] = row0
        even, uneven = k[:, :128], k[:, 128:]
        wz[x, :, 0:128] = 0.5 * (even + uneven)
        wz[x, :, 128:] = jnp.where(half == 127, 0.0, 0.5 * (uneven + pltpu.roll(even, 127, 1)))
    cells[1].wait()
    reac = ordered(react[...]).reshape(CX, CY, NZ)
    for k in range(4):
        halo_copy(k).wait_recv()
    ext = [jnp.where(inside[k], halo[k], 0.0) for k in range(4)]
    bound = [0.5 * (edge[k] + ext[k]) for k in range(4)]
    for x in range(CX):
        k = kap[x]
        inner, outer = wz[x, :, 0:128], wz[x, :, 128:]
        below = jnp.where(half == 0, 0.5 * k[:, :128], pltpu.roll(outer, 1, 1))
        above = jnp.where(half == 127, 0.5 * k[:, 128:], outer)
        dz = jnp.concatenate([below + inner, inner + above], 1)
        dx = (bound[0] if x == 0 else wx[x]) + (bound[1] if x == CX - 1 else wx[x + 1])
        dy = wy[x, 0:CY] + wy[x, 1 : CY + 1]
        dy = dy + jnp.concatenate(
            [bound[2][x : x + 1], jnp.zeros((CY - 2, NZ), F32), bound[3][x : x + 1]], 0
        )
        diag[x] = reac[x] + dx + dy + dz

    def apply(x, gram):
        before, after = jnp.maximum(x - 1, 0), jnp.minimum(x + 1, CX - 1)
        behind, v = None, field[x, 0]
        for y in range(CY):
            ahead = field[x, y + 1] if y < CY - 1 else None
            out = diag[x, y : y + 1] * v
            out = out - wx[x, y : y + 1] * field[before, y]
            out = out - wx[x + 1, y : y + 1] * field[after, y]
            if y > 0:
                out = out - wy[x, y : y + 1] * behind
            if y < CY - 1:
                out = out - wy[x, y + 1 : y + 2] * ahead
            even, uneven = v[:, :128], v[:, 128:]
            inner, outer = wz[x, y : y + 1, 0:128], wz[x, y : y + 1, 128:]
            out = out - jnp.concatenate(
                [
                    inner * uneven + pltpu.roll(outer * uneven, 1, 1),
                    inner * even + outer * pltpu.roll(even, 127, 1),
                ],
                1,
            )
            local = pad_rows(out, SLOTS).astype(BF16)
            gram = gram + nt(masked[x, :, NZ * y : NZ * (y + 1)], local)
            behind, v = v, ahead
        return gram

    gram = lax.fori_loop(
        0, CX // 2, lambda i, gram: apply(2 * i + 1, apply(2 * i, gram)),
        jnp.zeros((SLOTS, SLOTS), F32),
    )
    own = pad_lanes(gram, 128)
    spot, slot = lanes_of((SLOTS, 128)), rows_of((SLOTS, 128))
    own = own + jnp.where((spot == slot) & (slot >= count), 1.0, 0.0)
    sym = jnp.where(spot < LIVE, 0.5 * (own + transposed(own)[:SLOTS]), 0.0)

    on_diag = jnp.where((spot == slot) & (spot < LIVE), sym, 0.0)
    scale_lane = lax.rsqrt(jnp.sum(on_diag, axis=0, keepdims=True))
    scale_lane = jnp.where(lanes_of((1, 128)) < LIVE, scale_lane, 1.0)
    scale_row = lax.rsqrt(jnp.sum(on_diag, axis=1, keepdims=True)[:LIVE])

    def up_copy(ref, i):
        return pltpu.make_async_remote_copy(
            src_ref=ref, dst_ref=ref, send_sem=up_sem.at[i], recv_sem=up_sem.at[i + 2],
            device_id=(1, u), device_id_type=MESH,
        )

    def link_copy(to, owner):
        return pltpu.make_async_remote_copy(
            src_ref=links.at[owner, core], dst_ref=links.at[owner, core],
            send_sem=link_send.at[to], recv_sem=link_recv.at[owner],
            device_id=(g, 2 * to + core), device_id_type=MESH,
        )

    def piv_copy(to, owner):
        return pltpu.make_async_remote_copy(
            src_ref=pivs.at[owner, core], dst_ref=pivs.at[owner, core],
            send_sem=piv_send.at[to], recv_sem=piv_recv.at[owner],
            device_id=(g, 2 * to + core), device_id_type=MESH,
        )

    def cross_copy(ref, sem):
        return pltpu.make_async_remote_copy(
            src_ref=ref, dst_ref=ref, send_sem=cross_send.at[sem], recv_sem=cross_recv.at[sem],
            device_id=(g, 2 * chip + 1 - core), device_id_type=MESH,
        )

    def cross_link(v, c):
        return cross_copy(links.at[v, c], v)

    def cross_pivs(c):
        return cross_copy(pivs.at[:, c], GROUP // 2)

    link_up, piv_up = up_copy(links.at[chip, core], 0), up_copy(pivs.at[chip, core], 1)

    @pl.when(joined & (g == 0))
    def _():
        unit = sym[:LIVE] * scale_row * scale_lane
        packed = unit[0:16] + pltpu.roll(unit[16:32], LIVE, 1)
        packed = packed + pltpu.roll(pad_rows(unit[32:40], 16), 2 * LIVE, 1)
        shifted = pltpu.roll(jnp.broadcast_to(scale_lane, (16, 128)), 2 * LIVE, 1)
        wide_lane = lanes_of((16, 128))
        spare = (rows_of((16, 128)) == 8) & (wide_lane >= 2 * LIVE) & (wide_lane < 3 * LIVE)
        pivs[chip, core] = jnp.where(spare, shifted, packed)
        piv_up.start()
        others(GROUP // 2, chip, lambda v: piv_copy(v, chip).start())

    def coupling(k):
        weight = bound[k]
        total = jnp.zeros((SLOTS, SLOTS), F32)
        if k < 2:
            x = 0 if k == 0 else CX - 1
            for y in range(0, CY, 2):
                two = [field[x, j] * weight[j : j + 1] for j in (y, y + 1)]
                hi, lo = split(jnp.concatenate(two, 0))
                cols = slice(NZ * y // 2, NZ * (y + 2) // 2)
                high[:, cols], low[:, cols] = hi, lo
            face_copy(mirror[k]).wait_recv()
            both = nt(high[...], face_x[k]) + nt(low[...], face_x[k])
            both = pad_lanes(both, 128)
            block = both[:LIVE] + pltpu.roll(both[LIVE:], 128 - LIVE, 1)
            block = jnp.where(lanes_of((LIVE, 128)) < LIVE, block, 0.0)
        else:
            face_copy(mirror[k]).wait_recv()
            for x in range(CX):
                mine = field[x, 0 if k == 2 else CY - 1] * weight[x : x + 1]
                hi, lo = split(pad_rows(mine, SLOTS))
                other = face_y[k - 2, x]
                total = total + (nt(hi, other) + nt(lo, other))
            block = pad_lanes(total, 128)[:LIVE]
        return jnp.where(inside[k], -block, 0.0)

    found = {k: coupling(k) for k in (1, 3)}
    lane = lanes_of((LIVE, 128))
    odd = core == 1
    ahead = found[3] * scale_row
    ahead_t = transposed(found[3])[:LIVE] * scale_lane
    rising = transposed(found[1])[:LIVE] * scale_lane
    message = jnp.where(odd, ahead, ahead_t) + pltpu.roll(jnp.where(odd, ahead_t, ahead), LIVE, 1)
    message = message + pltpu.roll(rising, 2 * LIVE, 1)
    message = jnp.where(lane >= 3 * LIVE, count.astype(F32), message)
    message = jnp.where(lane == 3 * LIVE + 1, scale_row, message)

    @pl.when(joined & (g == 0))
    def _():
        links[chip, core] = message
        link_up.start()
        others(GROUP // 2, chip, lambda v: link_copy(v, chip).start())

    @pl.when(joined & (g == 1))
    def _():
        piv_up.wait_recv()
        others(GROUP // 2, chip, lambda v: piv_copy(v, chip).start())
        link_up.wait_recv()
        others(GROUP // 2, chip, lambda v: link_copy(v, chip).start())

    for k in (0, 2):
        found[k] = coupling(k)
    blocks_ref[0] = own
    for k in range(4):
        blocks_ref[k + 1] = pad_rows(found[k], SLOTS)
    blocks_ref[5] = sym

    @pl.when(joined)
    def _():
        others(GROUP // 2, chip, lambda v: piv_copy(chip, v).wait_recv())
        cross_pivs(core).start()
        cross_link(chip, core).start()

        def forward(v):
            link_copy(chip, v).wait_recv()
            cross_link(v, core).start()

        others(GROUP // 2, chip, forward)
        cross_pivs(1 - core).wait_recv()
        for v in range(GROUP // 2):
            cross_link(v, 1 - core).wait_recv()
        for v in range(GROUP):
            links_ref[v] = links[v // 2, v % 2]
            pivots_ref[v] = pivs[v // 2, v % 2]
        others(GROUP // 2, chip, lambda v: link_copy(v, chip).wait_send())
        others(GROUP // 2, chip, lambda v: piv_copy(v, chip).wait_send())
        cross_pivs(core).wait_send()
        for v in range(GROUP // 2):
            cross_link(v, core).wait_send()

    @pl.when(joined & (g == 0))
    def _():
        link_up.wait_send()
        piv_up.wait_send()

    for k in range(4):
        halo_copy(k).wait_send()
        face_copy(k).wait_send()


def assemble(count, modes, kappa, react):
    vmem = pl.BlockSpec(memory_space=pltpu.VMEM)
    hbm = pl.BlockSpec(memory_space=pltpu.HBM)
    dma = pltpu.SemaphoreType.DMA
    return pl.pallas_call(
        assemble_kernel,
        out_shape=(
            jax.ShapeDtypeStruct((6, SLOTS, 128), F32),
            jax.ShapeDtypeStruct((GROUP, LIVE, 128), F32),
            jax.ShapeDtypeStruct((GROUP, 16, 128), F32),
        ),
        in_specs=[pl.BlockSpec(memory_space=pltpu.SMEM), hbm, hbm, hbm],
        out_specs=(vmem, vmem, vmem),
        scratch_shapes=[
            pltpu.VMEM((CX, LIVE, CY, NZ), BF16),
            pltpu.VMEM((CX, CY, NZ), BF16),
            pltpu.VMEM((CX, CY, NZ), BF16),
            pltpu.VMEM((CX, CY, LIVE, NZ), F32),
            pltpu.VMEM((CX, SLOTS, CY * NZ), BF16),
            pltpu.VMEM((CX + 1, CY, NZ), F32),
            pltpu.VMEM((CX, 24, NZ), F32),
            pltpu.VMEM((CX, CY, NZ), F32),
            pltpu.VMEM((CX, CY, NZ), F32),
            pltpu.VMEM((4, 16, NZ), F32),
            pltpu.VMEM((4, 16, NZ), F32),
            pltpu.VMEM((2, 2 * LIVE, 8 * NZ), BF16),
            pltpu.VMEM((2, 16, SLOTS, NZ), BF16),
            pltpu.VMEM((2 * LIVE, 8 * NZ), BF16),
            pltpu.VMEM((2 * LIVE, 8 * NZ), BF16),
            pltpu.VMEM((2, 2 * LIVE, 8 * NZ), BF16),
            pltpu.VMEM((GROUP // 2, 2, LIVE, 128), F32),
            pltpu.VMEM((GROUP // 2, 2, 16, 128), F32),
            pltpu.VMEM((NZ, NZ), BF16),
            dma((CX,)),
            dma((2,)),
            dma((4,)),
            dma((4,)),
            dma((4,)),
            dma((4,)),
            dma((4,)),
            dma((GROUP // 2,)),
            dma((GROUP // 2,)),
            dma((GROUP // 2,)),
            dma((GROUP // 2,)),
            dma((GROUP // 2 + 1,)),
            dma((GROUP // 2 + 1,)),
        ],
        compiler_params=pltpu.CompilerParams(
            collective_id=0, has_side_effects=True, vmem_limit_bytes=50 * 2**20
        ),
        name="assemble",
    )(count, modes, kappa, react)


def halves(x, rows, axis):
    hi, lo = split(pad_rows(x, rows) if x.shape[0] < rows else x)
    return jnp.concatenate([hi, lo], axis)


def joined_halves(out, rows):
    tall = out.shape[0] // 2
    return out[:rows, :128] + (out[:rows, 128:] + out[tall : tall + rows, :128])


def nn3(a, b):
    left = halves(a, SLOTS, 0)
    out = jnp.dot(left, halves(b, 128, 1), preferred_element_type=F32)
    return joined_halves(out, a.shape[0])


def nt3(a, b):
    out = nt(halves(a, SLOTS, 0), halves(b, 128, 0))
    return joined_halves(out, a.shape[0])


def wide(x):
    return jnp.broadcast_to(x, (8, 128))


def pivots(p, soff, state, spread_ref, rows_ref, side_ref):
    tiles, saved = (list(part) for part in state)
    sub = rows_of((8, 128))
    at = soff + 8 * p
    column = lambda v, c: wide(tiles[v][:, c : c + 1])
    if p == 0:
        for c in range(8):
            spread_ref[p, c] = column(p, at + c)
    rows_ref[p] = tiles[p]
    d = {(i, j): wide(spread_ref[p, j, i : i + 1]) for i in range(8) for j in range(i, 8)}
    rows = [wide(rows_ref[p, c : c + 1]) for c in range(8)]
    follow = p + 1 < LIVE // 8
    if follow:
        under = [column(p + 1, at + c) for c in range(8)]
        coming = [column(p + 1, at + 8 + c) for c in range(8)]
    others = [v for v in range(LIVE // 8) if v not in (p, p + 1)]
    factors = {v: [column(v, at + c) for c in range(8)] for v in others}
    alpha, beta, z = {}, {}, list(rows)
    for c in range(0, 8, 2):
        n = c + 1
        a, b, e = d[c, c], d[c, n], d[n, n]
        det = a * e - b * b
        r = pl.reciprocal(det, approx=True)
        for i in range(n + 1, 8):
            top, bottom = e * d[c, i] - b * d[n, i], a * d[n, i] - b * d[c, i]
            alpha[c, i], beta[c, i] = top * r, bottom * r
            for j in range(i, 8):
                if j <= n + 2:
                    d[i, j] = d[i, j] - (top * d[c, j] + bottom * d[n, j]) * r
                else:
                    d[i, j] = d[i, j] - (alpha[c, i] * d[c, j] + beta[c, i] * d[n, j])
        root = lax.rsqrt(a)
        saved[p] = jnp.where(sub == c, rows[c] * root, saved[p])
        second = (rows[n] - (b * root * root) * rows[c]) * (lax.rsqrt(det) * (a * root))
        saved[p] = jnp.where(sub == n, second, saved[p])
        for i in range(n + 1, 8):
            rows[i] = rows[i] - (alpha[c, i] * rows[c] + beta[c, i] * rows[n])
        z[c] = (e * rows[c] - b * rows[n]) * r
        z[n] = (a * rows[n] - b * rows[c]) * r
        if follow:
            first = (e * under[c] - b * under[n]) * r
            other = (a * under[n] - b * under[c]) * r
            side_ref[p, c], side_ref[p, n] = first, other
            for i in range(n + 1, 8):
                under[i] = under[i] - (alpha[c, i] * under[c] + beta[c, i] * under[n])
            for i in range(8):
                coming[i] = coming[i] - (
                    under[c] * wide(side_ref[p, c, i : i + 1])
                    + under[n] * wide(side_ref[p, n, i : i + 1])
                )
            tiles[p + 1] = tiles[p + 1] - (first * rows[c] + other * rows[n])
    if follow:
        for c in range(8):
            spread_ref[p + 1, c] = coming[c]
    for c in range(4, -1, -2):
        for i in range(c + 2, 8):
            z[c] = z[c] - alpha[c, i] * z[i]
            z[c + 1] = z[c + 1] - beta[c, i] * z[i]
    for v in others:
        terms = [factors[v][c] * z[c] for c in range(8)]
        while len(terms) > 1:
            terms = [terms[i] + terms[i + 1] for i in range(0, len(terms), 2)]
        tiles[v] = tiles[v] - terms[0]
    for c in range(8):
        tiles[p] = jnp.where(sub == c, z[c], tiles[p])
    return tuple(tiles), tuple(saved)


def place(out_ref, block, pos, keep):
    base = jnp.minimum((pos // 128) * 128, NC - 256)
    base = pl.multiple_of(base, 128)
    shifted = pltpu.roll(pad_lanes(block, 256), pos - base, 1)
    cols = lanes_of((SLOTS, 256)) + base
    out_ref[:, pl.ds(base, 256)] += jnp.where(keep(cols), shifted, 0.0)


def factor_kernel(
    links_ref, pivots_ref, blocks_ref, out_ref, linv_ref, k_ref, g_ref, f_ref, x_ref, spread_ref, rows_ref, side_ref,
):
    g, u = lax.axis_index("grp"), lax.axis_index("sub")
    s = g * NU + u
    upper = s <= 21
    member = (s == 21) | (s == 22) | ((s >= NU) & (s < NU + NB))
    lane = lanes_of((LIVE, 128))
    row = rows_of((LIVE, 128))
    lane48 = lanes_of((SLOTS, 128))
    row48 = rows_of((SLOTS, 128))
    out_ref[...] = jnp.zeros_like(out_ref)
    before = lambda cols: cols < DONE
    after = lambda cols: cols >= DONE

    def left(x, by):
        x = pltpu.roll(x, 128 - by, 1) if by else x
        return jnp.where(lanes_of(x.shape) < LIVE, x, 0.0)

    def put(block, pos, late):
        base = pos // 128 * 128
        shifted = pltpu.roll(pad_lanes(block, 256), pos - base, 1) if pos > base else (
            pad_lanes(block, 256)
        )
        if base < DONE < base + 256:
            cols = lanes_of((SLOTS, 256)) + base
            shifted = jnp.where(cols >= DONE if late else cols < DONE, shifted, 0.0)
        out_ref[:, base : base + 256] += shifted

    def reduce_row(q):
        at, wide_enough = jnp.maximum(q, 0), jnp.where(q == NB - 1, 16, LIVE)
        mine = jnp.where(q == s, blocks_ref[5], 0.0)
        mine = jnp.where(q == s - 1, blocks_ref[3], mine)
        mine = jnp.where(q == s - NU, blocks_ref[1], mine)
        mine = mine * scale(at, 0)
        held = jnp.where(q > 0, f_ref[jnp.maximum(q - 1, 0)], 0.0)
        f = mine - nn3(held, pad_rows(k_ref[at], 128))
        f_ref[at] = jnp.where((q <= s) & (lane48 < wide_enough), f, 0.0)

    def solve_row(q):
        at = jnp.maximum(q, 0)
        x = nt3(f_ref[at], pad_rows(linv_ref[at], 128))
        x_ref[at] = jnp.where((q == s) & (lane48 > row48), 0.0, x)

    def double_row(q):
        at = jnp.maximum(q, 0)
        x = x_ref[at]
        g_ref[at] = nn3(x, pad_rows(linv_ref[at], 128))

    def pivot_block(t, at):
        packed = pivots_ref[t]
        parts = []
        for i in range(3):
            by = (at - LIVE * i) % 128
            parts.append(pltpu.roll(packed, by, 1) if by else packed)
        block = jnp.concatenate([parts[0], parts[1], parts[2][:8]], 0)
        return jnp.where((lane >= at) & (lane < at + LIVE), block, 0.0)

    def scale(t, at):
        spare = pltpu.roll(pivots_ref[t, 8:16, :], (at - 2 * LIVE) % 128, 1)[0:1]
        lanes = lanes_of((1, 128))
        return jnp.where((lanes >= at) & (lanes < at + LIVE), spare, 1.0)

    def live_count(t):
        return jnp.max(jnp.where(lanes_of((8, 128)) == 3 * LIVE, links_ref[t][0:8], 0.0))

    def at_rows(x, start):
        above = jnp.zeros((start, 128), F32)
        return pad_rows(jnp.concatenate([above, x], 0) if start else x, 128)

    def step(t, odd, scur, n):
        soff, uoff = (LIVE, 0) if odd else (0, LIVE)
        following = jnp.minimum(t + 1, NB - 1)
        given = links_ref[t] * scale(following, uoff)
        limit = jnp.where(t == NB - 1, 16, LIVE)
        in_s = (lane >= soff) & (lane < soff + LIVE)
        in_u = (lane >= uoff) & (lane < uoff + LIVE)
        eye = jnp.where(lane == row + soff, 1.0, 0.0)
        a = jnp.where((row < limit) & (lane < soff + limit), scur, eye)
        rest = jnp.where(lane == row + 2 * LIVE, 1.0, 0.0)
        rest = jnp.where(in_u, jnp.where(row < limit, given, 0.0), rest)
        a = jnp.where(in_s, a, rest)
        ut = jnp.where(in_s, given, 0.0) * links_ref[following, :, 3 * LIVE + 1 : 3 * LIVE + 2]
        tiles = tuple(a[8 * v : 8 * v + 8] for v in range(LIVE // 8))
        state = pivots(0, soff, (tiles, tiles), spread_ref, rows_ref, side_ref)

        double_row(t - 3)
        solve_row(t - 2)
        reduce_row(t - 1)
        coming, coming_n = pivot_block(following, uoff), live_count(following)
        n = jnp.where(t == NB - 1, jnp.minimum(n, 16.0), n)
        for p in range(1, LIVE // 8):
            state = lax.cond(
                n > 8.0 * p,
                lambda st, p=p: pivots(p, soff, st, spread_ref, rows_ref, side_ref),
                lambda st: st,
                state,
            )
        tiles, saved = state
        k = jnp.concatenate(tiles, 0)
        snext = coming - nn3(ut, at_rows(k, soff))
        linv_ref[t] = left(jnp.concatenate(saved, 0), 2 * LIVE)
        k_ref[t + 1] = left(k, uoff)
        return snext, coming_n

    @pl.when(upper | member)
    def _():
        k_ref[0] = jnp.zeros((LIVE, 128), F32)
        linv_ref[0] = jnp.zeros((LIVE, 128), F32)
        f_ref[0] = jnp.zeros((SLOTS, 128), F32)
        x_ref[0] = jnp.zeros((SLOTS, 128), F32)
        def pair(i, carry):
            carry = step(2 * i, False, *carry)
            return step(2 * i + 1, True, *carry)

        lax.fori_loop(0, NB // 2, pair, (pivot_block(0, 0), live_count(0)))
        double_row(NB - 3)
        solve_row(NB - 2)
        reduce_row(NB - 1)
        double_row(NB - 2)
        solve_row(NB - 1)
        double_row(NB - 1)
        for t in range(NB):
            put(x_ref[t], SLOTS * t, False)

    @pl.when(upper)
    def _():
        dead = jnp.where((row48 == lane48) & (row48 >= LIVE), 1.0, 0.0)
        place(out_ref, dead, SLOTS * s, before)

    @pl.when(member)
    def _():
        late = lane >= 16
        last = jnp.where(row < 16, links_ref[NB - 1], 0.0)
        own = jnp.where(late & (row < 16), pivot_block(NB - 1, 0) / scale(NB - 1, 0), 0.0)
        over = jnp.where(late, left(links_ref[NB - 2], LIVE), 0.0)
        y = None
        for t in range(NB - 1, -1, -1):
            if y is None:
                y = g_ref[t]
                put(-nn3(y, pad_rows(left(last, 0), 128)), SLOTS * NB, True)
                put(-nn3(y, pad_rows(own, 128)), SLOTS * (NB - 1), True)
            else:
                y = g_ref[t] - nt3(y, pad_rows(k_ref[t + 1], 128))
            if t == NB - 2:
                put(-nn3(y, pad_rows(over, 128)), SLOTS * (NB - 1), True)
            rising = pad_rows(left(links_ref[t], 2 * LIVE), 128)
            put(-nt3(y, rising), SLOTS * (t + NU), True)

    @pl.when(s >= 21)
    def _():
        targets = [s, s - NU, s + NU, s - 1, s + 1]
        valid = [True, g > 0, g < NG - 1, u > 0, u < NU - 1]
        for k in range(5):
            pos = SLOTS * jnp.clip(targets[k], 0, NG * NU - 1)
            place(out_ref, jnp.where(valid[k], blocks_ref[k], 0.0), pos, after)

    @pl.when(s == 21)
    def _():
        out_ref[0:16, DONE:] = jnp.zeros((16, NC - DONE), F32)


def factor(links, pivs, blocks):
    vmem = pl.BlockSpec(memory_space=pltpu.VMEM)
    return pl.pallas_call(
        factor_kernel,
        out_shape=jax.ShapeDtypeStruct((SLOTS, NC), F32),
        in_specs=[vmem, vmem, vmem],
        out_specs=vmem,
        scratch_shapes=[
            pltpu.VMEM((NB, LIVE, 128), F32),
            pltpu.VMEM((NB + 1, LIVE, 128), F32),
            pltpu.VMEM((NB, SLOTS, 128), F32),
            pltpu.VMEM((NB, SLOTS, 128), F32),
            pltpu.VMEM((NB, SLOTS, 128), F32),
            pltpu.VMEM((LIVE // 8, 8, 8, 128), F32),
            pltpu.VMEM((LIVE // 8, 8, 128), F32),
            pltpu.VMEM((LIVE // 8, 8, 8, 128), F32),
        ],
        compiler_params=pltpu.CompilerParams(vmem_limit_bytes=40 * 2**20),
        name="factor",
    )(links, pivs, blocks)


def per_device(modes, counts, kappa, react):
    kappa = pltpu.with_memory_space_constraint(kappa, pltpu.HBM)
    react = pltpu.with_memory_space_constraint(react, pltpu.HBM)
    blocks, links, pivs = assemble(counts, modes, kappa, react)
    return factor(links, pivs, blocks)


def solution(mesh):
    in_specs = (
        P(None, "grp", "sub", None),
        P(("grp", "sub")),
        P("grp", "sub", None),
        P("grp", "sub", None),
    )
    out_specs = P(("grp", "sub"), None)
    return jax.shard_map(
        per_device, mesh=mesh, in_specs=in_specs, out_specs=out_specs, check_vma=False
    )
```

```python
import jax
import jax.numpy as jnp
from jax import lax
from jax.experimental import pallas as pl
from jax.experimental.pallas import tpu as pltpu
from jax.sharding import PartitionSpec as P

F32 = jnp.float32
BF16 = jnp.bfloat16
MESH = pl.DeviceIdType.MESH
NG, NU = 4, 32
CX, CY, NZ = 16, 16, 256
SLOTS, LIVE = 48, 40
NB = 22
DONE = 1024
GROUP = 24
NC = SLOTS * NG * NU


def nt(a, b, precision=None):
    return lax.dot_general(
        a, b, (((1,), (1,)), ((), ())), preferred_element_type=F32, precision=precision
    )


def lanes_of(shape):
    return lax.broadcasted_iota(jnp.int32, shape, len(shape) - 1)


def rows_of(shape):
    return lax.broadcasted_iota(jnp.int32, shape, len(shape) - 2)


def split(x):
    hi = x.astype(BF16)
    return hi, (x - hi.astype(F32)).astype(BF16)


def pad_rows(x, rows):
    return jnp.concatenate([x, jnp.zeros((rows - x.shape[0], x.shape[1]), x.dtype)], 0)


def pad_lanes(x, lanes):
    return jnp.concatenate([x, jnp.zeros((x.shape[0], lanes - x.shape[1]), x.dtype)], 1)


def transposed(x):
    return jnp.transpose(pad_rows(x, 128))


def assemble_kernel(
    count_ref, modes_ref, kappa_ref, react_ref, blocks_ref, links_ref, pivots_ref,
    raw, kappa, react, field, masked, wx, wy, wz, diag, edge, halo, face_x, face_y,
    high, low, ends, links, pivs, order, upward, part, part_in,
    raw_sem, cell_sem, halo_send, halo_recv, face_send, face_recv, piece_send, piece_recv, part_send, part_recv,
    up_sem, link_send, link_recv, piv_send, piv_recv, cross_send, cross_recv,
):
    g, u = lax.axis_index("grp"), lax.axis_index("sub")
    partners = [
        (lax.rem(g + NG - 1, NG), u),
        (lax.rem(g + 1, NG), u),
        (g, lax.rem(u + NU - 1, NU)),
        (g, lax.rem(u + 1, NU)),
    ]
    inside = [g > 0, g < NG - 1, u > 0, u < NU - 1]
    mirror = [1, 0, 3, 2]
    chip, core = u // 2, lax.rem(u, 2)
    joined = (g < 2) & (u < GROUP)

    def fetch(x):
        return pltpu.make_async_copy(
            modes_ref.at[pl.ds(0, LIVE), x], raw.at[x], raw_sem.at[x]
        )

    cells = [
        pltpu.make_async_copy(kappa_ref, kappa, cell_sem.at[0]),
        pltpu.make_async_copy(react_ref, react, cell_sem.at[1]),
    ]
    cells[0].start()
    for x in [0, CX - 1] + list(range(1, CX - 1)):
        fetch(x).start()
    cells[1].start()

    barrier = pltpu.get_barrier_semaphore()

    def greet(device):
        pl.semaphore_signal(barrier, inc=1, device_id=device, device_id_type=MESH)

    for partner in partners:
        greet(partner)

    def others(count, me, act):
        for step in range(1, count):
            v = me + step
            act(jnp.where(v >= count, v - count, v))

    @pl.when(joined)
    def _():
        others(GROUP // 2, chip, lambda v: greet((g, 2 * v + core)))
        greet((g, 2 * chip + 1 - core))

    count = count_ref[0]
    z_from, z_to = rows_of((NZ, NZ)), lanes_of((NZ, NZ))
    here = z_from == jnp.where(z_to < 128, 2 * z_to, 2 * z_to - 255)
    order[...] = jnp.where(here, 1.0, 0.0).astype(BF16)

    def ordered(x):
        return jnp.dot(x.reshape(-1, NZ), order[...], preferred_element_type=F32)

    cells[0].wait()
    kap = ordered(kappa[...]).reshape(CX, CY, NZ)
    edge[0] = kap[0]
    edge[1] = kap[CX - 1]
    for x in range(CX):
        edge[2, x : x + 1] = kap[x, 0:1]
        edge[3, x : x + 1] = kap[x, CY - 1 : CY]

    live = rows_of((CY, LIVE, NZ)) < count

    def turn(x):
        plane = jnp.swapaxes(ordered(raw[x]).reshape(LIVE, CY, NZ), 0, 1)
        plane = jnp.where(live, plane, 0.0)
        field[x] = plane
        for y in range(CY):
            masked[x, :, NZ * y : NZ * (y + 1)] = pad_rows(plane[y], SLOTS).astype(BF16)
        return plane

    def turn_two(x, w, q):
        fetch(x).wait()
        fetch(w).wait()
        one, two = turn(x), turn(w)
        for side, y in ((2, 0), (3, CY - 1)):
            pair = jnp.concatenate([one[y], two[y]], 0).astype(BF16)
            ends[side, :, pl.ds(pl.multiple_of(q * NZ, NZ), NZ)] = pair
        return one, two

    for side, plane in enumerate(turn_two(0, CX - 1, 0)):
        for y in range(0, CY, 2):
            pair = jnp.concatenate([plane[y], plane[y + 1]], 0).astype(BF16)
            ends[side, :, NZ * y // 2 : NZ * (y + 2) // 2] = pair
    pl.semaphore_wait(barrier, jnp.where(joined, GROUP // 2 + 4, 4))

    def halo_copy(k):
        return pltpu.make_async_remote_copy(
            src_ref=edge.at[k], dst_ref=halo.at[mirror[k]],
            send_sem=halo_send.at[k], recv_sem=halo_recv.at[mirror[k]],
            device_id=partners[k], device_id_type=MESH,
        )

    def face_copy(k):
        return pltpu.make_async_remote_copy(
            src_ref=ends.at[k, :, pl.ds(4 * NZ * k, 4 * NZ)], dst_ref=face_x.at[mirror[k]],
            send_sem=face_send.at[k], recv_sem=face_recv.at[mirror[k]],
            device_id=partners[k], device_id_type=MESH,
        )

    def piece_copy(k, q):
        cols = pl.ds(pl.multiple_of(q * NZ, NZ), NZ)
        return pltpu.make_async_remote_copy(
            src_ref=ends.at[k, :, cols], dst_ref=face_y.at[mirror[k] - 2, :, cols],
            send_sem=piece_send.at[k - 2, q], recv_sem=piece_recv.at[mirror[k] - 2, q],
            device_id=partners[k], device_id_type=MESH,
        )

    for k in range(4):
        halo_copy(k).start()
    face_copy(0).start()
    face_copy(1).start()
    piece_copy(2, 0).start()
    piece_copy(3, 0).start()

    def turn_next(i, carry):
        turn_two(2 * i + 1, 2 * i + 2, i + 1)
        piece_copy(2, i + 1).start()
        piece_copy(3, i + 1).start()
        return carry

    lax.fori_loop(0, CX // 2 - 1, turn_next, 0)

    plane0 = jnp.zeros((CY, NZ), F32)
    row0 = jnp.zeros((1, NZ), F32)
    lane128 = lanes_of((CY, 128))
    wx[0] = plane0
    wx[CX] = plane0
    for x in range(CX - 1):
        wx[x + 1] = 0.5 * (kap[x] + kap[x + 1])
    for x in range(CX):
        k = kap[x]
        wy[x, 0:1] = row0
        wy[x, 1:CY] = 0.5 * (k[: CY - 1] + k[1:])
        wy[x, CY : CY + 1] = row0
        even, uneven = k[:, :128], k[:, 128:]
        wz[x, :, 0:128] = 0.5 * (even + uneven)
        wz[x, :, 128:] = jnp.where(lane128 == 127, 0.0, 0.5 * (uneven + pltpu.roll(even, 127, 1)))
    cells[1].wait()
    reac = ordered(react[...]).reshape(CX, CY, NZ)
    for k in range(4):
        halo_copy(k).wait_recv()
    ext = [jnp.where(inside[k], halo[k], 0.0) for k in range(4)]
    bound = [0.5 * (edge[k] + ext[k]) for k in range(4)]
    for x in range(CX):
        k = kap[x]
        inner, outer = wz[x, :, 0:128], wz[x, :, 128:]
        below = jnp.where(lane128 == 0, 0.5 * k[:, :128], pltpu.roll(outer, 1, 1))
        above = jnp.where(lane128 == 127, 0.5 * k[:, 128:], outer)
        dz = jnp.concatenate([below + inner, inner + above], 1)
        dx = (bound[0] if x == 0 else wx[x]) + (bound[1] if x == CX - 1 else wx[x + 1])
        dy = wy[x, 0:CY] + wy[x, 1 : CY + 1]
        dy = dy + jnp.concatenate(
            [bound[2][x : x + 1], jnp.zeros((CY - 2, NZ), F32), bound[3][x : x + 1]], 0
        )
        diag[x] = reac[x] + dx + dy + dz

    def apply(x, gram):
        before, after = jnp.maximum(x - 1, 0), jnp.minimum(x + 1, CX - 1)
        behind, v = None, field[x, 0]
        for y in range(CY):
            ahead = field[x, y + 1] if y < CY - 1 else None
            out = diag[x, y : y + 1] * v
            out = out - wx[x, y : y + 1] * field[before, y]
            out = out - wx[x + 1, y : y + 1] * field[after, y]
            if y > 0:
                out = out - wy[x, y : y + 1] * behind
            if y < CY - 1:
                out = out - wy[x, y + 1 : y + 2] * ahead
            even, uneven = v[:, :128], v[:, 128:]
            inner, outer = wz[x, y : y + 1, 0:128], wz[x, y : y + 1, 128:]
            out = out - jnp.concatenate(
                [
                    inner * uneven + pltpu.roll(outer * uneven, 1, 1),
                    inner * even + outer * pltpu.roll(even, 127, 1),
                ],
                1,
            )
            local = pad_rows(out, SLOTS).astype(BF16)
            gram = gram + nt(masked[x, :, NZ * y : NZ * (y + 1)], local)
            behind, v = v, ahead
        return gram

    gram = lax.fori_loop(
        0, CX // 2, lambda i, gram: apply(2 * i + 1, apply(2 * i, gram)),
        jnp.zeros((SLOTS, SLOTS), F32),
    )
    own = pad_lanes(gram, 128)
    spot, slot = lanes_of((SLOTS, 128)), rows_of((SLOTS, 128))
    own = own + jnp.where((spot == slot) & (slot >= count), 1.0, 0.0)
    sym = jnp.where(spot < LIVE, 0.5 * (own + transposed(own)[:SLOTS]), 0.0)

    on_diag = jnp.where((spot == slot) & (spot < LIVE), sym, 0.0)
    scale_lane = lax.rsqrt(jnp.sum(on_diag, axis=0, keepdims=True))
    scale_lane = jnp.where(lanes_of((1, 128)) < LIVE, scale_lane, 1.0)
    scale_row = lax.rsqrt(jnp.sum(on_diag, axis=1, keepdims=True)[:LIVE])

    def up_copy(src, dst, i):
        return pltpu.make_async_remote_copy(
            src_ref=src, dst_ref=dst, send_sem=up_sem.at[i], recv_sem=up_sem.at[i + 2],
            device_id=(1, u), device_id_type=MESH,
        )

    def link_copy(to, owner):
        return pltpu.make_async_remote_copy(
            src_ref=links.at[owner, core], dst_ref=links.at[owner, core],
            send_sem=link_send.at[to], recv_sem=link_recv.at[owner],
            device_id=(g, 2 * to + core), device_id_type=MESH,
        )

    def piv_copy(to, owner):
        return pltpu.make_async_remote_copy(
            src_ref=pivs.at[owner, core], dst_ref=pivs.at[owner, core],
            send_sem=piv_send.at[to], recv_sem=piv_recv.at[owner],
            device_id=(g, 2 * to + core), device_id_type=MESH,
        )

    def cross_copy(ref, sem):
        return pltpu.make_async_remote_copy(
            src_ref=ref, dst_ref=ref, send_sem=cross_send.at[sem], recv_sem=cross_recv.at[sem],
            device_id=(g, 2 * chip + 1 - core), device_id_type=MESH,
        )

    def cross_link(v, c):
        return cross_copy(links.at[v, c], v)

    def cross_pivs(c):
        return cross_copy(pivs.at[:, c], GROUP // 2)

    def part_copy(k):
        return pltpu.make_async_remote_copy(
            src_ref=part.at[k], dst_ref=part_in.at[mirror[k]],
            send_sem=part_send.at[k], recv_sem=part_recv.at[mirror[k]],
            device_id=partners[k], device_id_type=MESH,
        )

    link_up = up_copy(upward, links.at[chip, core], 0)
    piv_up = up_copy(pivs.at[chip, core], pivs.at[chip, core], 1)

    @pl.when(joined & (g == 0))
    def _():
        unit = sym[:LIVE] * scale_row * scale_lane
        packed = unit[0:16] + pltpu.roll(unit[16:32], LIVE, 1)
        packed = packed + pltpu.roll(pad_rows(unit[32:40], 16), 2 * LIVE, 1)
        shifted = pltpu.roll(jnp.broadcast_to(scale_lane, (16, 128)), 2 * LIVE, 1)
        wide_lane = lanes_of((16, 128))
        spare = (rows_of((16, 128)) == 8) & (wide_lane >= 2 * LIVE) & (wide_lane < 3 * LIVE)
        pivs[chip, core] = jnp.where(spare, shifted, packed)
        piv_up.start()
        others(GROUP // 2, chip, lambda v: piv_copy(v, chip).start())

    x_order = [0, CX - 1] + list(range(1, CX - 1))

    def coupling(k):
        if k < 2:
            cells = range(8) if k == 1 else range(8, CY)
            mine = [field[0 if k == 0 else CX - 1, y] * bound[k][y : y + 1] for y in cells]
        else:
            mine = [field[x, 0 if k == 2 else CY - 1] * bound[k][x : x + 1] for x in x_order]
        for q in range(len(mine) // 2):
            hi, lo = split(jnp.concatenate(mine[2 * q : 2 * q + 2], 0))
            cols = slice(NZ * q, NZ * (q + 1))
            high[:, cols], low[:, cols] = hi, lo
        width = NZ * len(mine) // 2
        if k < 2:
            face_copy(mirror[k]).wait_recv()
            other = face_x[k]
        else:
            for q in range(8):
                piece_copy(mirror[k], q).wait_recv()
            other = face_y[k - 2]
        both = pad_lanes(nt(high[:, :width], other) + nt(low[:, :width], other), 128)
        block = both[:LIVE] + pltpu.roll(both[LIVE:], 128 - LIVE, 1)
        block = jnp.where(lanes_of((LIVE, 128)) < LIVE, block, 0.0)
        return jnp.where(inside[k], -block, 0.0)

    half = {1: coupling(1), 0: coupling(0)}
    for k in (1, 0):
        part[k] = half[k]
        part_copy(k).start()
    found = {3: coupling(3)}
    lane = lanes_of((LIVE, 128))
    odd = core == 1
    ahead = found[3] * scale_row
    ahead_t = transposed(found[3])[:LIVE] * scale_lane
    message = jnp.where(odd, ahead, ahead_t) + pltpu.roll(jnp.where(odd, ahead_t, ahead), LIVE, 1)
    message = jnp.where(lane >= 3 * LIVE, count.astype(F32), message)
    message = jnp.where(lane == 3 * LIVE + 1, scale_row, message)
    rising = transposed(half[1])[:LIVE] * scale_lane
    message = message + pltpu.roll(rising, 2 * LIVE, 1)

    @pl.when(joined & (g == 0))
    def _():
        upward[...] = message
        link_up.start()

    @pl.when(joined & (g == 1))
    def _():
        piv_up.wait_recv()
        others(GROUP // 2, chip, lambda v: piv_copy(v, chip).start())
        rest = pltpu.roll(half[0], 2 * LIVE, 1) * pivs[chip, core, 8:9]
        link_up.wait_recv()
        in_rest = (lane >= 2 * LIVE) & (lane < 3 * LIVE)
        links[chip, core] = links[chip, core] + jnp.where(in_rest, rest, 0.0)
        others(GROUP // 2, chip, lambda v: link_copy(v, chip).start())

    part_copy(0).wait_recv()
    back = jnp.where(inside[1], part_in[1], 0.0)
    found[1] = half[1] + transposed(back)[:LIVE]

    @pl.when(joined & (g == 0))
    def _():
        links[chip, core] = message + pltpu.roll(back * scale_lane, 2 * LIVE, 1)
        others(GROUP // 2, chip, lambda v: link_copy(v, chip).start())

    found[2] = coupling(2)
    part_copy(1).wait_recv()
    found[0] = half[0] + transposed(jnp.where(inside[0], part_in[0], 0.0))[:LIVE]
    blocks_ref[0] = own
    for k in range(4):
        blocks_ref[k + 1] = pad_rows(found[k], SLOTS)
    blocks_ref[5] = sym

    @pl.when(joined)
    def _():
        others(GROUP // 2, chip, lambda v: piv_copy(chip, v).wait_recv())
        cross_pivs(core).start()
        cross_link(chip, core).start()

        def forward(v):
            link_copy(chip, v).wait_recv()
            cross_link(v, core).start()

        others(GROUP // 2, chip, forward)
        cross_pivs(1 - core).wait_recv()
        for v in range(GROUP // 2):
            cross_link(v, 1 - core).wait_recv()
        for v in range(GROUP):
            links_ref[v] = links[v // 2, v % 2]
            pivots_ref[v] = pivs[v // 2, v % 2]
        others(GROUP // 2, chip, lambda v: link_copy(v, chip).wait_send())
        others(GROUP // 2, chip, lambda v: piv_copy(v, chip).wait_send())
        cross_pivs(core).wait_send()
        for v in range(GROUP // 2):
            cross_link(v, core).wait_send()

    @pl.when(joined & (g == 0))
    def _():
        link_up.wait_send()
        piv_up.wait_send()

    for k in range(4):
        halo_copy(k).wait_send()
    for k in range(2):
        face_copy(k).wait_send()
        part_copy(k).wait_send()
        for q in range(8):
            piece_copy(k + 2, q).wait_send()


def assemble(count, modes, kappa, react):
    vmem = pl.BlockSpec(memory_space=pltpu.VMEM)
    hbm = pl.BlockSpec(memory_space=pltpu.HBM)
    dma = pltpu.SemaphoreType.DMA
    return pl.pallas_call(
        assemble_kernel,
        out_shape=(
            jax.ShapeDtypeStruct((6, SLOTS, 128), F32),
            jax.ShapeDtypeStruct((GROUP, LIVE, 128), F32),
            jax.ShapeDtypeStruct((GROUP, 16, 128), F32),
        ),
        in_specs=[pl.BlockSpec(memory_space=pltpu.SMEM), hbm, hbm, hbm],
        out_specs=(vmem, vmem, vmem),
        scratch_shapes=[
            pltpu.VMEM((CX, LIVE, CY, NZ), BF16),
            pltpu.VMEM((CX, CY, NZ), BF16),
            pltpu.VMEM((CX, CY, NZ), BF16),
            pltpu.VMEM((CX, CY, LIVE, NZ), F32),
            pltpu.VMEM((CX, SLOTS, CY * NZ), BF16),
            pltpu.VMEM((CX + 1, CY, NZ), F32),
            pltpu.VMEM((CX, 24, NZ), F32),
            pltpu.VMEM((CX, CY, NZ), F32),
            pltpu.VMEM((CX, CY, NZ), F32),
            pltpu.VMEM((4, 16, NZ), F32),
            pltpu.VMEM((4, 16, NZ), F32),
            pltpu.VMEM((2, 2 * LIVE, 4 * NZ), BF16),
            pltpu.VMEM((2, 2 * LIVE, 8 * NZ), BF16),
            pltpu.VMEM((2 * LIVE, 8 * NZ), BF16),
            pltpu.VMEM((2 * LIVE, 8 * NZ), BF16),
            pltpu.VMEM((4, 2 * LIVE, 8 * NZ), BF16),
            pltpu.VMEM((GROUP // 2, 2, LIVE, 128), F32),
            pltpu.VMEM((GROUP // 2, 2, 16, 128), F32),
            pltpu.VMEM((NZ, NZ), BF16),
            pltpu.VMEM((LIVE, 128), F32),
            pltpu.VMEM((2, LIVE, 128), F32),
            pltpu.VMEM((2, LIVE, 128), F32),
            dma((CX,)),
            dma((2,)),
            dma((4,)),
            dma((4,)),
            dma((2,)),
            dma((2,)),
            dma((2, 8)),
            dma((2, 8)),
            dma((2,)),
            dma((2,)),
            dma((4,)),
            dma((GROUP // 2,)),
            dma((GROUP // 2,)),
            dma((GROUP // 2,)),
            dma((GROUP // 2,)),
            dma((GROUP // 2 + 1,)),
            dma((GROUP // 2 + 1,)),
        ],
        compiler_params=pltpu.CompilerParams(
            collective_id=0, has_side_effects=True, vmem_limit_bytes=50 * 2**20
        ),
        name="assemble",
    )(count, modes, kappa, react)


def halves(x, rows, axis):
    hi, lo = split(pad_rows(x, rows) if x.shape[0] < rows else x)
    return jnp.concatenate([hi, lo], axis)


def joined_halves(out, rows):
    tall = out.shape[0] // 2
    return out[:rows, :128] + (out[:rows, 128:] + out[tall : tall + rows, :128])


def nn3(a, b):
    left = halves(a, SLOTS, 0)
    out = jnp.dot(left, halves(b, 128, 1), preferred_element_type=F32)
    return joined_halves(out, a.shape[0])


def nt3(a, b):
    out = nt(halves(a, SLOTS, 0), halves(b, 128, 0))
    return joined_halves(out, a.shape[0])


def wide(x):
    return jnp.broadcast_to(x, (8, 128))


def pivots(p, soff, state, spread_ref, rows_ref, side_ref):
    tiles, saved = (list(part) for part in state)
    sub = rows_of((8, 128))
    at = soff + 8 * p
    column = lambda v, c: wide(tiles[v][:, c : c + 1])
    if p == 0:
        for c in range(8):
            spread_ref[p, c] = column(p, at + c)
    rows_ref[p] = tiles[p]
    d = {(i, j): wide(spread_ref[p, j, i : i + 1]) for i in range(8) for j in range(i, 8)}
    rows = [wide(rows_ref[p, c : c + 1]) for c in range(8)]
    follow = p + 1 < LIVE // 8
    if follow:
        under = [column(p + 1, at + c) for c in range(8)]
        coming = [column(p + 1, at + 8 + c) for c in range(8)]
    others = [v for v in range(LIVE // 8) if v not in (p, p + 1)]
    factors = {v: [column(v, at + c) for c in range(8)] for v in others}
    alpha, beta, z = {}, {}, list(rows)
    for c in range(0, 8, 2):
        n = c + 1
        a, b, e = d[c, c], d[c, n], d[n, n]
        det = a * e - b * b
        r = pl.reciprocal(det, approx=True)
        for i in range(n + 1, 8):
            top, bottom = e * d[c, i] - b * d[n, i], a * d[n, i] - b * d[c, i]
            alpha[c, i], beta[c, i] = top * r, bottom * r
            for j in range(i, 8):
                if j <= n + 2:
                    d[i, j] = d[i, j] - (top * d[c, j] + bottom * d[n, j]) * r
                else:
                    d[i, j] = d[i, j] - (alpha[c, i] * d[c, j] + beta[c, i] * d[n, j])
        root = lax.rsqrt(a)
        saved[p] = jnp.where(sub == c, rows[c] * root, saved[p])
        second = (rows[n] - (b * root * root) * rows[c]) * (lax.rsqrt(det) * (a * root))
        saved[p] = jnp.where(sub == n, second, saved[p])
        for i in range(n + 1, 8):
            rows[i] = rows[i] - (alpha[c, i] * rows[c] + beta[c, i] * rows[n])
        z[c] = (e * rows[c] - b * rows[n]) * r
        z[n] = (a * rows[n] - b * rows[c]) * r
        if follow:
            first = (e * under[c] - b * under[n]) * r
            other = (a * under[n] - b * under[c]) * r
            side_ref[p, c], side_ref[p, n] = first, other
            for i in range(n + 1, 8):
                under[i] = under[i] - (alpha[c, i] * under[c] + beta[c, i] * under[n])
            for i in range(8):
                coming[i] = coming[i] - (
                    under[c] * wide(side_ref[p, c, i : i + 1])
                    + under[n] * wide(side_ref[p, n, i : i + 1])
                )
            tiles[p + 1] = tiles[p + 1] - (first * rows[c] + other * rows[n])
    if follow:
        for c in range(8):
            spread_ref[p + 1, c] = coming[c]
    for c in range(4, -1, -2):
        for i in range(c + 2, 8):
            z[c] = z[c] - alpha[c, i] * z[i]
            z[c + 1] = z[c + 1] - beta[c, i] * z[i]
    for v in others:
        terms = [factors[v][c] * z[c] for c in range(8)]
        while len(terms) > 1:
            terms = [terms[i] + terms[i + 1] for i in range(0, len(terms), 2)]
        tiles[v] = tiles[v] - terms[0]
    for c in range(8):
        tiles[p] = jnp.where(sub == c, z[c], tiles[p])
    return tuple(tiles), tuple(saved)


def place(out_ref, block, pos, keep):
    base = jnp.minimum((pos // 128) * 128, NC - 256)
    base = pl.multiple_of(base, 128)
    shifted = pltpu.roll(pad_lanes(block, 256), pos - base, 1)
    cols = lanes_of((SLOTS, 256)) + base
    out_ref[:, pl.ds(base, 256)] += jnp.where(keep(cols), shifted, 0.0)


def factor_kernel(
    links_ref, pivots_ref, blocks_ref, out_ref, linv_ref, k_ref, g_ref, f_ref, x_ref, spread_ref, rows_ref, side_ref,
):
    g, u = lax.axis_index("grp"), lax.axis_index("sub")
    s = g * NU + u
    upper = s <= 21
    member = (s == 21) | (s == 22) | ((s >= NU) & (s < NU + NB))
    lane = lanes_of((LIVE, 128))
    row = rows_of((LIVE, 128))
    lane48 = lanes_of((SLOTS, 128))
    row48 = rows_of((SLOTS, 128))
    out_ref[...] = jnp.zeros_like(out_ref)
    before = lambda cols: cols < DONE
    after = lambda cols: cols >= DONE

    def left(x, by):
        x = pltpu.roll(x, 128 - by, 1) if by else x
        return jnp.where(lanes_of(x.shape) < LIVE, x, 0.0)

    def put(block, pos, late):
        base = pos // 128 * 128
        shifted = pltpu.roll(pad_lanes(block, 256), pos - base, 1) if pos > base else (
            pad_lanes(block, 256)
        )
        if base < DONE < base + 256:
            cols = lanes_of((SLOTS, 256)) + base
            shifted = jnp.where(cols >= DONE if late else cols < DONE, shifted, 0.0)
        out_ref[:, base : base + 256] += shifted

    def reduce_row(q):
        at, wide_enough = jnp.maximum(q, 0), jnp.where(q == NB - 1, 16, LIVE)
        mine = jnp.where(q == s, blocks_ref[5], 0.0)
        mine = jnp.where(q == s - 1, blocks_ref[3], mine)
        mine = jnp.where(q == s - NU, blocks_ref[1], mine)
        mine = mine * scale(at, 0)
        held = jnp.where(q > 0, f_ref[jnp.maximum(q - 1, 0)], 0.0)
        f = mine - nn3(held, pad_rows(k_ref[at], 128))
        f_ref[at] = jnp.where((q <= s) & (lane48 < wide_enough), f, 0.0)

    def solve_row(q):
        at = jnp.maximum(q, 0)
        x = nt3(f_ref[at], pad_rows(linv_ref[at], 128))
        x_ref[at] = jnp.where((q == s) & (lane48 > row48), 0.0, x)

    def double_row(q):
        at = jnp.maximum(q, 0)
        x = x_ref[at]
        g_ref[at] = nn3(x, pad_rows(linv_ref[at], 128))

    def pivot_block(t, at):
        packed = pivots_ref[t]
        parts = []
        for i in range(3):
            by = (at - LIVE * i) % 128
            parts.append(pltpu.roll(packed, by, 1) if by else packed)
        block = jnp.concatenate([parts[0], parts[1], parts[2][:8]], 0)
        return jnp.where((lane >= at) & (lane < at + LIVE), block, 0.0)

    def scale(t, at):
        spare = pltpu.roll(pivots_ref[t, 8:16, :], (at - 2 * LIVE) % 128, 1)[0:1]
        lanes = lanes_of((1, 128))
        return jnp.where((lanes >= at) & (lanes < at + LIVE), spare, 1.0)

    def live_count(t):
        return jnp.max(jnp.where(lanes_of((8, 128)) == 3 * LIVE, links_ref[t][0:8], 0.0))

    def at_rows(x, start):
        above = jnp.zeros((start, 128), F32)
        return pad_rows(jnp.concatenate([above, x], 0) if start else x, 128)

    def step(t, odd, scur, n):
        soff, uoff = (LIVE, 0) if odd else (0, LIVE)
        following = jnp.minimum(t + 1, NB - 1)
        given = links_ref[t] * scale(following, uoff)
        limit = jnp.where(t == NB - 1, 16, LIVE)
        in_s = (lane >= soff) & (lane < soff + LIVE)
        in_u = (lane >= uoff) & (lane < uoff + LIVE)
        eye = jnp.where(lane == row + soff, 1.0, 0.0)
        a = jnp.where((row < limit) & (lane < soff + limit), scur, eye)
        rest = jnp.where(lane == row + 2 * LIVE, 1.0, 0.0)
        rest = jnp.where(in_u, jnp.where(row < limit, given, 0.0), rest)
        a = jnp.where(in_s, a, rest)
        ut = jnp.where(in_s, given, 0.0) * links_ref[following, :, 3 * LIVE + 1 : 3 * LIVE + 2]
        tiles = tuple(a[8 * v : 8 * v + 8] for v in range(LIVE // 8))
        state = pivots(0, soff, (tiles, tiles), spread_ref, rows_ref, side_ref)

        double_row(t - 3)
        solve_row(t - 2)
        reduce_row(t - 1)
        coming, coming_n = pivot_block(following, uoff), live_count(following)
        n = jnp.where(t == NB - 1, jnp.minimum(n, 16.0), n)
        for p in range(1, LIVE // 8):
            state = lax.cond(
                n > 8.0 * p,
                lambda st, p=p: pivots(p, soff, st, spread_ref, rows_ref, side_ref),
                lambda st: st,
                state,
            )
        tiles, saved = state
        k = jnp.concatenate(tiles, 0)
        snext = coming - nn3(ut, at_rows(k, soff))
        linv_ref[t] = left(jnp.concatenate(saved, 0), 2 * LIVE)
        k_ref[t + 1] = left(k, uoff)
        return snext, coming_n

    @pl.when(upper | member)
    def _():
        k_ref[0] = jnp.zeros((LIVE, 128), F32)
        linv_ref[0] = jnp.zeros((LIVE, 128), F32)
        f_ref[0] = jnp.zeros((SLOTS, 128), F32)
        x_ref[0] = jnp.zeros((SLOTS, 128), F32)
        def pair(i, carry):
            carry = step(2 * i, False, *carry)
            return step(2 * i + 1, True, *carry)

        lax.fori_loop(0, NB // 2, pair, (pivot_block(0, 0), live_count(0)))
        double_row(NB - 3)
        solve_row(NB - 2)
        reduce_row(NB - 1)
        double_row(NB - 2)
        solve_row(NB - 1)
        double_row(NB - 1)
        for t in range(NB):
            put(x_ref[t], SLOTS * t, False)

    @pl.when(upper)
    def _():
        dead = jnp.where((row48 == lane48) & (row48 >= LIVE), 1.0, 0.0)
        place(out_ref, dead, SLOTS * s, before)

    @pl.when(member)
    def _():
        late = lane >= 16
        last = jnp.where(row < 16, links_ref[NB - 1], 0.0)
        own = jnp.where(late & (row < 16), pivot_block(NB - 1, 0) / scale(NB - 1, 0), 0.0)
        over = jnp.where(late, left(links_ref[NB - 2], LIVE), 0.0)
        y = None
        for t in range(NB - 1, -1, -1):
            if y is None:
                y = g_ref[t]
                put(-nn3(y, pad_rows(left(last, 0), 128)), SLOTS * NB, True)
                put(-nn3(y, pad_rows(own, 128)), SLOTS * (NB - 1), True)
            else:
                y = g_ref[t] - nt3(y, pad_rows(k_ref[t + 1], 128))
            if t == NB - 2:
                put(-nn3(y, pad_rows(over, 128)), SLOTS * (NB - 1), True)
            rising = pad_rows(left(links_ref[t], 2 * LIVE), 128)
            put(-nt3(y, rising), SLOTS * (t + NU), True)

    @pl.when(s >= 21)
    def _():
        targets = [s, s - NU, s + NU, s - 1, s + 1]
        valid = [True, g > 0, g < NG - 1, u > 0, u < NU - 1]
        for k in range(5):
            pos = SLOTS * jnp.clip(targets[k], 0, NG * NU - 1)
            place(out_ref, jnp.where(valid[k], blocks_ref[k], 0.0), pos, after)

    @pl.when(s == 21)
    def _():
        out_ref[0:16, DONE:] = jnp.zeros((16, NC - DONE), F32)


def factor(links, pivs, blocks):
    vmem = pl.BlockSpec(memory_space=pltpu.VMEM)
    return pl.pallas_call(
        factor_kernel,
        out_shape=jax.ShapeDtypeStruct((SLOTS, NC), F32),
        in_specs=[vmem, vmem, vmem],
        out_specs=vmem,
        scratch_shapes=[
            pltpu.VMEM((NB, LIVE, 128), F32),
            pltpu.VMEM((NB + 1, LIVE, 128), F32),
            pltpu.VMEM((NB, SLOTS, 128), F32),
            pltpu.VMEM((NB, SLOTS, 128), F32),
            pltpu.VMEM((NB, SLOTS, 128), F32),
            pltpu.VMEM((LIVE // 8, 8, 8, 128), F32),
            pltpu.VMEM((LIVE // 8, 8, 128), F32),
            pltpu.VMEM((LIVE // 8, 8, 8, 128), F32),
        ],
        compiler_params=pltpu.CompilerParams(vmem_limit_bytes=40 * 2**20),
        name="factor",
    )(links, pivs, blocks)


def per_device(modes, counts, kappa, react):
    kappa = pltpu.with_memory_space_constraint(kappa, pltpu.HBM)
    react = pltpu.with_memory_space_constraint(react, pltpu.HBM)
    blocks, links, pivs = assemble(counts, modes, kappa, react)
    return factor(links, pivs, blocks)


def solution(mesh):
    in_specs = (
        P(None, "grp", "sub", None),
        P(("grp", "sub")),
        P("grp", "sub", None),
        P("grp", "sub", None),
    )
    out_specs = P(("grp", "sub"), None)
    return jax.shard_map(
        per_device, mesh=mesh, in_specs=in_specs, out_specs=out_specs, check_vma=False
    )
```

```python
import jax
import jax.numpy as jnp
from jax import lax
from jax.experimental import pallas as pl
from jax.experimental.pallas import tpu as pltpu
from jax.sharding import PartitionSpec as P

F32 = jnp.float32
BF16 = jnp.bfloat16
MESH = pl.DeviceIdType.MESH
NG, NU = 4, 32
CX, CY, NZ = 16, 16, 256
SLOTS, LIVE = 48, 40
NB = 22
DONE = 1024
GROUP = 24
NC = SLOTS * NG * NU


def nt(a, b, precision=None):
    return lax.dot_general(
        a, b, (((1,), (1,)), ((), ())), preferred_element_type=F32, precision=precision
    )


def lanes_of(shape):
    return lax.broadcasted_iota(jnp.int32, shape, len(shape) - 1)


def rows_of(shape):
    return lax.broadcasted_iota(jnp.int32, shape, len(shape) - 2)


def split(x):
    hi = x.astype(BF16)
    return hi, (x - hi.astype(F32)).astype(BF16)


def pad_rows(x, rows):
    return jnp.concatenate([x, jnp.zeros((rows - x.shape[0], x.shape[1]), x.dtype)], 0)


def pad_lanes(x, lanes):
    return jnp.concatenate([x, jnp.zeros((x.shape[0], lanes - x.shape[1]), x.dtype)], 1)


def transposed(x):
    return jnp.transpose(pad_rows(x, 128))


def assemble_kernel(
    count_ref, modes_ref, kappa_ref, react_ref, blocks_ref, links_ref, pivots_ref,
    raw, kappa, react, field, masked, wx, wy, wz, diag, edge, halo, face_x, face_y,
    high, low, ends, links, pivs, order,
    raw_sem, cell_sem, halo_send, halo_recv, face_send, face_recv,
    up_sem, link_send, link_recv, piv_send, piv_recv, cross_send, cross_recv,
):
    g, u = lax.axis_index("grp"), lax.axis_index("sub")
    partners = [
        (lax.rem(g + NG - 1, NG), u),
        (lax.rem(g + 1, NG), u),
        (g, lax.rem(u + NU - 1, NU)),
        (g, lax.rem(u + 1, NU)),
    ]
    inside = [g > 0, g < NG - 1, u > 0, u < NU - 1]
    mirror = [1, 0, 3, 2]
    chip, core = u // 2, lax.rem(u, 2)
    joined = (g < 2) & (u < GROUP)

    def fetch(x):
        return pltpu.make_async_copy(
            modes_ref.at[pl.ds(0, LIVE), x], raw.at[x], raw_sem.at[x]
        )

    cells = [
        pltpu.make_async_copy(kappa_ref, kappa, cell_sem.at[0]),
        pltpu.make_async_copy(react_ref, react, cell_sem.at[1]),
    ]
    fetch(0).start()
    fetch(CX - 1).start()
    cells[0].start()
    for x in range(1, CX - 1):
        fetch(x).start()
    cells[1].start()

    barrier = pltpu.get_barrier_semaphore()

    def greet(device):
        pl.semaphore_signal(barrier, inc=1, device_id=device, device_id_type=MESH)

    for partner in partners:
        greet(partner)

    def others(count, me, act):
        for step in range(1, count):
            v = me + step
            act(jnp.where(v >= count, v - count, v))

    @pl.when(joined)
    def _():
        others(GROUP // 2, chip, lambda v: greet((g, 2 * v + core)))
        greet((g, 2 * chip + 1 - core))

    count = count_ref[0]
    z_from, z_to = rows_of((NZ, NZ)), lanes_of((NZ, NZ))
    here = z_from == jnp.where(z_to < 128, 2 * z_to, 2 * z_to - 255)
    order[...] = jnp.where(here, 1.0, 0.0).astype(BF16)

    def ordered(x):
        return jnp.dot(x.reshape(-1, NZ), order[...], preferred_element_type=F32)

    live = rows_of((CY, LIVE, NZ)) < count

    def turn(x, side=None):
        plane = jnp.swapaxes(ordered(raw[x]).reshape(LIVE, CY, NZ), 0, 1)
        plane = jnp.where(live, plane, 0.0)
        field[x] = plane
        for y in range(CY):
            masked[x, :, NZ * y : NZ * (y + 1)] = pad_rows(plane[y], SLOTS).astype(BF16)
        if side is not None:
            for y in range(0, CY, 2):
                two = jnp.concatenate([plane[y], plane[y + 1]], 0)
                ends[side, :, NZ * y // 2 : NZ * (y + 2) // 2] = two.astype(BF16)

    fetch(0).wait()
    fetch(CX - 1).wait()
    turn(0, 0)
    turn(CX - 1, 1)
    cells[0].wait()
    kap = ordered(kappa[...]).reshape(CX, CY, NZ)
    edge[0] = kap[0]
    edge[1] = kap[CX - 1]
    for x in range(CX):
        edge[2, x : x + 1] = kap[x, 0:1]
        edge[3, x : x + 1] = kap[x, CY - 1 : CY]
    pl.semaphore_wait(barrier, jnp.where(joined, GROUP // 2 + 4, 4))

    def halo_copy(k):
        return pltpu.make_async_remote_copy(
            src_ref=edge.at[k], dst_ref=halo.at[mirror[k]],
            send_sem=halo_send.at[k], recv_sem=halo_recv.at[mirror[k]],
            device_id=partners[k], device_id_type=MESH,
        )

    sources = [
        ends.at[0],
        ends.at[1],
        masked.at[:, :, pl.ds(0, NZ)],
        masked.at[:, :, pl.ds((CY - 1) * NZ, NZ)],
    ]
    landings = [face_x.at[0], face_x.at[1], face_y.at[0], face_y.at[1]]

    def face_copy(k):
        return pltpu.make_async_remote_copy(
            src_ref=sources[k], dst_ref=landings[mirror[k]],
            send_sem=face_send.at[k], recv_sem=face_recv.at[mirror[k]],
            device_id=partners[k], device_id_type=MESH,
        )

    for k in range(4):
        halo_copy(k).start()
    face_copy(0).start()
    face_copy(1).start()

    def turn_next(i, carry):
        fetch(2 * i + 1).wait()
        fetch(2 * i + 2).wait()
        turn(2 * i + 1)
        turn(2 * i + 2)
        return carry

    lax.fori_loop(0, CX // 2 - 1, turn_next, 0)
    face_copy(2).start()
    face_copy(3).start()

    plane0 = jnp.zeros((CY, NZ), F32)
    row0 = jnp.zeros((1, NZ), F32)
    half = lanes_of((CY, 128))
    wx[0] = plane0
    wx[CX] = plane0
    for x in range(CX - 1):
        wx[x + 1] = 0.5 * (kap[x] + kap[x + 1])
    for x in range(CX):
        k = kap[x]
        wy[x, 0:1] = row0
        wy[x, 1:CY] = 0.5 * (k[: CY - 1] + k[1:])
        wy[x, CY : CY + 1] = row0
        even, uneven = k[:, :128], k[:, 128:]
        wz[x, :, 0:128] = 0.5 * (even + uneven)
        wz[x, :, 128:] = jnp.where(half == 127, 0.0, 0.5 * (uneven + pltpu.roll(even, 127, 1)))
    cells[1].wait()
    reac = ordered(react[...]).reshape(CX, CY, NZ)
    for k in range(4):
        halo_copy(k).wait_recv()
    ext = [jnp.where(inside[k], halo[k], 0.0) for k in range(4)]
    bound = [0.5 * (edge[k] + ext[k]) for k in range(4)]
    for x in range(CX):
        k = kap[x]
        inner, outer = wz[x, :, 0:128], wz[x, :, 128:]
        below = jnp.where(half == 0, 0.5 * k[:, :128], pltpu.roll(outer, 1, 1))
        above = jnp.where(half == 127, 0.5 * k[:, 128:], outer)
        dz = jnp.concatenate([below + inner, inner + above], 1)
        dx = (bound[0] if x == 0 else wx[x]) + (bound[1] if x == CX - 1 else wx[x + 1])
        dy = wy[x, 0:CY] + wy[x, 1 : CY + 1]
        dy = dy + jnp.concatenate(
            [bound[2][x : x + 1], jnp.zeros((CY - 2, NZ), F32), bound[3][x : x + 1]], 0
        )
        diag[x] = reac[x] + dx + dy + dz

    def apply(x, gram):
        before, after = jnp.maximum(x - 1, 0), jnp.minimum(x + 1, CX - 1)
        behind, v = None, field[x, 0]
        for y in range(CY):
            ahead = field[x, y + 1] if y < CY - 1 else None
            out = diag[x, y : y + 1] * v
            out = out - wx[x, y : y + 1] * field[before, y]
            out = out - wx[x + 1, y : y + 1] * field[after, y]
            if y > 0:
                out = out - wy[x, y : y + 1] * behind
            if y < CY - 1:
                out = out - wy[x, y + 1 : y + 2] * ahead
            even, uneven = v[:, :128], v[:, 128:]
            inner, outer = wz[x, y : y + 1, 0:128], wz[x, y : y + 1, 128:]
            out = out - jnp.concatenate(
                [
                    inner * uneven + pltpu.roll(outer * uneven, 1, 1),
                    inner * even + outer * pltpu.roll(even, 127, 1),
                ],
                1,
            )
            local = pad_rows(out, SLOTS).astype(BF16)
            gram = gram + nt(masked[x, :, NZ * y : NZ * (y + 1)], local)
            behind, v = v, ahead
        return gram

    gram = lax.fori_loop(
        0, CX // 2, lambda i, gram: apply(2 * i + 1, apply(2 * i, gram)),
        jnp.zeros((SLOTS, SLOTS), F32),
    )
    own = pad_lanes(gram, 128)
    spot, slot = lanes_of((SLOTS, 128)), rows_of((SLOTS, 128))
    own = own + jnp.where((spot == slot) & (slot >= count), 1.0, 0.0)
    sym = jnp.where(spot < LIVE, 0.5 * (own + transposed(own)[:SLOTS]), 0.0)

    on_diag = jnp.where((spot == slot) & (spot < LIVE), sym, 0.0)
    scale_lane = lax.rsqrt(jnp.sum(on_diag, axis=0, keepdims=True))
    scale_lane = jnp.where(lanes_of((1, 128)) < LIVE, scale_lane, 1.0)
    scale_row = lax.rsqrt(jnp.sum(on_diag, axis=1, keepdims=True)[:LIVE])

    def up_copy(ref, i):
        return pltpu.make_async_remote_copy(
            src_ref=ref, dst_ref=ref, send_sem=up_sem.at[i], recv_sem=up_sem.at[i + 2],
            device_id=(1, u), device_id_type=MESH,
        )

    def link_copy(to, owner):
        return pltpu.make_async_remote_copy(
            src_ref=links.at[owner, core], dst_ref=links.at[owner, core],
            send_sem=link_send.at[to], recv_sem=link_recv.at[owner],
            device_id=(g, 2 * to + core), device_id_type=MESH,
        )

    def piv_copy(to, owner):
        return pltpu.make_async_remote_copy(
            src_ref=pivs.at[owner, core], dst_ref=pivs.at[owner, core],
            send_sem=piv_send.at[to], recv_sem=piv_recv.at[owner],
            device_id=(g, 2 * to + core), device_id_type=MESH,
        )

    def cross_copy(ref, sem):
        return pltpu.make_async_remote_copy(
            src_ref=ref, dst_ref=ref, send_sem=cross_send.at[sem], recv_sem=cross_recv.at[sem],
            device_id=(g, 2 * chip + 1 - core), device_id_type=MESH,
        )

    def cross_link(v, c):
        return cross_copy(links.at[v, c], v)

    def cross_pivs(c):
        return cross_copy(pivs.at[:, c], GROUP // 2)

    link_up, piv_up = up_copy(links.at[chip, core], 0), up_copy(pivs.at[chip, core], 1)

    @pl.when(joined & (g == 0))
    def _():
        unit = sym[:LIVE] * scale_row * scale_lane
        packed = unit[0:16] + pltpu.roll(unit[16:32], LIVE, 1)
        packed = packed + pltpu.roll(pad_rows(unit[32:40], 16), 2 * LIVE, 1)
        shifted = pltpu.roll(jnp.broadcast_to(scale_lane, (16, 128)), 2 * LIVE, 1)
        wide_lane = lanes_of((16, 128))
        spare = (rows_of((16, 128)) == 8) & (wide_lane >= 2 * LIVE) & (wide_lane < 3 * LIVE)
        pivs[chip, core] = jnp.where(spare, shifted, packed)
        piv_up.start()
        others(GROUP // 2, chip, lambda v: piv_copy(v, chip).start())

    def coupling(k):
        weight = bound[k]
        total = jnp.zeros((SLOTS, SLOTS), F32)
        if k < 2:
            x = 0 if k == 0 else CX - 1
            for y in range(0, CY, 2):
                two = [field[x, j] * weight[j : j + 1] for j in (y, y + 1)]
                hi, lo = split(jnp.concatenate(two, 0))
                cols = slice(NZ * y // 2, NZ * (y + 2) // 2)
                high[:, cols], low[:, cols] = hi, lo
            face_copy(mirror[k]).wait_recv()
            both = nt(high[...], face_x[k]) + nt(low[...], face_x[k])
            both = pad_lanes(both, 128)
            block = both[:LIVE] + pltpu.roll(both[LIVE:], 128 - LIVE, 1)
            block = jnp.where(lanes_of((LIVE, 128)) < LIVE, block, 0.0)
        else:
            face_copy(mirror[k]).wait_recv()
            for x in range(CX):
                mine = field[x, 0 if k == 2 else CY - 1] * weight[x : x + 1]
                hi, lo = split(pad_rows(mine, SLOTS))
                other = face_y[k - 2, x]
                total = total + (nt(hi, other) + nt(lo, other))
            block = pad_lanes(total, 128)[:LIVE]
        return jnp.where(inside[k], -block, 0.0)

    found = {k: coupling(k) for k in (1, 3)}
    lane = lanes_of((LIVE, 128))
    odd = core == 1
    ahead = found[3] * scale_row
    ahead_t = transposed(found[3])[:LIVE] * scale_lane
    rising = transposed(found[1])[:LIVE] * scale_lane
    message = jnp.where(odd, ahead, ahead_t) + pltpu.roll(jnp.where(odd, ahead_t, ahead), LIVE, 1)
    message = message + pltpu.roll(rising, 2 * LIVE, 1)
    message = jnp.where(lane >= 3 * LIVE, count.astype(F32), message)
    message = jnp.where(lane == 3 * LIVE + 1, scale_row, message)

    @pl.when(joined & (g == 0))
    def _():
        links[chip, core] = message
        link_up.start()
        others(GROUP // 2, chip, lambda v: link_copy(v, chip).start())

    @pl.when(joined & (g == 1))
    def _():
        piv_up.wait_recv()
        others(GROUP // 2, chip, lambda v: piv_copy(v, chip).start())
        link_up.wait_recv()
        others(GROUP // 2, chip, lambda v: link_copy(v, chip).start())

    for k in (0, 2):
        found[k] = coupling(k)
    blocks_ref[0] = own
    for k in range(4):
        blocks_ref[k + 1] = pad_rows(found[k], SLOTS)
    blocks_ref[5] = sym

    @pl.when(joined)
    def _():
        others(GROUP // 2, chip, lambda v: piv_copy(chip, v).wait_recv())
        cross_pivs(core).start()
        cross_link(chip, core).start()

        def forward(v):
            link_copy(chip, v).wait_recv()
            cross_link(v, core).start()

        others(GROUP // 2, chip, forward)
        cross_pivs(1 - core).wait_recv()
        for v in range(GROUP // 2):
            cross_link(v, 1 - core).wait_recv()
        for v in range(GROUP):
            links_ref[v] = links[v // 2, v % 2]
            pivots_ref[v] = pivs[v // 2, v % 2]
        others(GROUP // 2, chip, lambda v: link_copy(v, chip).wait_send())
        others(GROUP // 2, chip, lambda v: piv_copy(v, chip).wait_send())
        cross_pivs(core).wait_send()
        for v in range(GROUP // 2):
            cross_link(v, core).wait_send()

    @pl.when(joined & (g == 0))
    def _():
        link_up.wait_send()
        piv_up.wait_send()

    for k in range(4):
        halo_copy(k).wait_send()
        face_copy(k).wait_send()


def assemble(count, modes, kappa, react):
    vmem = pl.BlockSpec(memory_space=pltpu.VMEM)
    hbm = pl.BlockSpec(memory_space=pltpu.HBM)
    dma = pltpu.SemaphoreType.DMA
    return pl.pallas_call(
        assemble_kernel,
        out_shape=(
            jax.ShapeDtypeStruct((6, SLOTS, 128), F32),
            jax.ShapeDtypeStruct((GROUP, LIVE, 128), F32),
            jax.ShapeDtypeStruct((GROUP, 16, 128), F32),
        ),
        in_specs=[pl.BlockSpec(memory_space=pltpu.SMEM), hbm, hbm, hbm],
        out_specs=(vmem, vmem, vmem),
        scratch_shapes=[
            pltpu.VMEM((CX, LIVE, CY, NZ), BF16),
            pltpu.VMEM((CX, CY, NZ), BF16),
            pltpu.VMEM((CX, CY, NZ), BF16),
            pltpu.VMEM((CX, CY, LIVE, NZ), F32),
            pltpu.VMEM((CX, SLOTS, CY * NZ), BF16),
            pltpu.VMEM((CX + 1, CY, NZ), F32),
            pltpu.VMEM((CX, 24, NZ), F32),
            pltpu.VMEM((CX, CY, NZ), F32),
            pltpu.VMEM((CX, CY, NZ), F32),
            pltpu.VMEM((4, 16, NZ), F32),
            pltpu.VMEM((4, 16, NZ), F32),
            pltpu.VMEM((2, 2 * LIVE, 8 * NZ), BF16),
            pltpu.VMEM((2, 16, SLOTS, NZ), BF16),
            pltpu.VMEM((2 * LIVE, 8 * NZ), BF16),
            pltpu.VMEM((2 * LIVE, 8 * NZ), BF16),
            pltpu.VMEM((2, 2 * LIVE, 8 * NZ), BF16),
            pltpu.VMEM((GROUP // 2, 2, LIVE, 128), F32),
            pltpu.VMEM((GROUP // 2, 2, 16, 128), F32),
            pltpu.VMEM((NZ, NZ), BF16),
            dma((CX,)),
            dma((2,)),
            dma((4,)),
            dma((4,)),
            dma((4,)),
            dma((4,)),
            dma((4,)),
            dma((GROUP // 2,)),
            dma((GROUP // 2,)),
            dma((GROUP // 2,)),
            dma((GROUP // 2,)),
            dma((GROUP // 2 + 1,)),
            dma((GROUP // 2 + 1,)),
        ],
        compiler_params=pltpu.CompilerParams(
            collective_id=0, has_side_effects=True, vmem_limit_bytes=50 * 2**20
        ),
        name="assemble",
    )(count, modes, kappa, react)


def halves(x, rows, axis):
    hi, lo = split(pad_rows(x, rows) if x.shape[0] < rows else x)
    return jnp.concatenate([hi, lo], axis)


def joined_halves(out, rows):
    tall = out.shape[0] // 2
    return out[:rows, :128] + (out[:rows, 128:] + out[tall : tall + rows, :128])


def nn3(a, b):
    left = halves(a, SLOTS, 0)
    out = jnp.dot(left, halves(b, 128, 1), preferred_element_type=F32)
    return joined_halves(out, a.shape[0])


def nt3(a, b):
    out = nt(halves(a, SLOTS, 0), halves(b, 128, 0))
    return joined_halves(out, a.shape[0])


def wide(x):
    return jnp.broadcast_to(x, (8, 128))


def pivots(p, soff, state, spread_ref, rows_ref, side_ref):
    tiles, saved = (list(part) for part in state)
    sub = rows_of((8, 128))
    at = soff + 8 * p
    column = lambda v, c: wide(tiles[v][:, c : c + 1])
    if p == 0:
        for c in range(8):
            spread_ref[p, c] = column(p, at + c)
    rows_ref[p] = tiles[p]
    d = {(i, j): wide(spread_ref[p, j, i : i + 1]) for i in range(8) for j in range(i, 8)}
    rows = [wide(rows_ref[p, c : c + 1]) for c in range(8)]
    follow = p + 1 < LIVE // 8
    if follow:
        under = [column(p + 1, at + c) for c in range(8)]
        coming = [column(p + 1, at + 8 + c) for c in range(8)]
    others = [v for v in range(LIVE // 8) if v not in (p, p + 1)]
    factors = {v: [column(v, at + c) for c in range(8)] for v in others}
    alpha, beta, z = {}, {}, list(rows)
    for c in range(0, 8, 2):
        n = c + 1
        a, b, e = d[c, c], d[c, n], d[n, n]
        det = a * e - b * b
        r = pl.reciprocal(det, approx=True)
        for i in range(n + 1, 8):
            top, bottom = e * d[c, i] - b * d[n, i], a * d[n, i] - b * d[c, i]
            alpha[c, i], beta[c, i] = top * r, bottom * r
            for j in range(i, 8):
                if j <= n + 2:
                    d[i, j] = d[i, j] - (top * d[c, j] + bottom * d[n, j]) * r
                else:
                    d[i, j] = d[i, j] - (alpha[c, i] * d[c, j] + beta[c, i] * d[n, j])
        root = lax.rsqrt(a)
        saved[p] = jnp.where(sub == c, rows[c] * root, saved[p])
        second = (rows[n] - (b * root * root) * rows[c]) * (lax.rsqrt(det) * (a * root))
        saved[p] = jnp.where(sub == n, second, saved[p])
        for i in range(n + 1, 8):
            rows[i] = rows[i] - (alpha[c, i] * rows[c] + beta[c, i] * rows[n])
        z[c] = (e * rows[c] - b * rows[n]) * r
        z[n] = (a * rows[n] - b * rows[c]) * r
        if follow:
            first = (e * under[c] - b * under[n]) * r
            other = (a * under[n] - b * under[c]) * r
            side_ref[p, c], side_ref[p, n] = first, other
            for i in range(n + 1, 8):
                under[i] = under[i] - (alpha[c, i] * under[c] + beta[c, i] * under[n])
            for i in range(8):
                coming[i] = coming[i] - (
                    under[c] * wide(side_ref[p, c, i : i + 1])
                    + under[n] * wide(side_ref[p, n, i : i + 1])
                )
            tiles[p + 1] = tiles[p + 1] - (first * rows[c] + other * rows[n])
    if follow:
        for c in range(8):
            spread_ref[p + 1, c] = coming[c]
    for c in range(4, -1, -2):
        for i in range(c + 2, 8):
            z[c] = z[c] - alpha[c, i] * z[i]
            z[c + 1] = z[c + 1] - beta[c, i] * z[i]
    for v in others:
        terms = [factors[v][c] * z[c] for c in range(8)]
        while len(terms) > 1:
            terms = [terms[i] + terms[i + 1] for i in range(0, len(terms), 2)]
        tiles[v] = tiles[v] - terms[0]
    for c in range(8):
        tiles[p] = jnp.where(sub == c, z[c], tiles[p])
    return tuple(tiles), tuple(saved)


def place(out_ref, block, pos, keep):
    base = jnp.minimum((pos // 128) * 128, NC - 256)
    base = pl.multiple_of(base, 128)
    shifted = pltpu.roll(pad_lanes(block, 256), pos - base, 1)
    cols = lanes_of((SLOTS, 256)) + base
    out_ref[:, pl.ds(base, 256)] += jnp.where(keep(cols), shifted, 0.0)


def factor_kernel(
    links_ref, pivots_ref, blocks_ref, out_ref, linv_ref, k_ref, g_ref, f_ref, x_ref, spread_ref, rows_ref, side_ref,
):
    g, u = lax.axis_index("grp"), lax.axis_index("sub")
    s = g * NU + u
    upper = s <= 21
    member = (s == 21) | (s == 22) | ((s >= NU) & (s < NU + NB))
    lane = lanes_of((LIVE, 128))
    row = rows_of((LIVE, 128))
    lane48 = lanes_of((SLOTS, 128))
    row48 = rows_of((SLOTS, 128))
    out_ref[...] = jnp.zeros_like(out_ref)
    before = lambda cols: cols < DONE
    after = lambda cols: cols >= DONE

    def left(x, by):
        x = pltpu.roll(x, 128 - by, 1) if by else x
        return jnp.where(lanes_of(x.shape) < LIVE, x, 0.0)

    def put(block, pos, late):
        base = pos // 128 * 128
        shifted = pltpu.roll(pad_lanes(block, 256), pos - base, 1) if pos > base else (
            pad_lanes(block, 256)
        )
        if base < DONE < base + 256:
            cols = lanes_of((SLOTS, 256)) + base
            shifted = jnp.where(cols >= DONE if late else cols < DONE, shifted, 0.0)
        out_ref[:, base : base + 256] += shifted

    def reduce_row(q):
        at, wide_enough = jnp.maximum(q, 0), jnp.where(q == NB - 1, 16, LIVE)
        mine = jnp.where(q == s, blocks_ref[5], 0.0)
        mine = jnp.where(q == s - 1, blocks_ref[3], mine)
        mine = jnp.where(q == s - NU, blocks_ref[1], mine)
        mine = mine * scale(at, 0)
        held = jnp.where(q > 0, f_ref[jnp.maximum(q - 1, 0)], 0.0)
        f = mine - nn3(held, pad_rows(k_ref[at], 128))
        f_ref[at] = jnp.where((q <= s) & (lane48 < wide_enough), f, 0.0)

    def solve_row(q):
        at = jnp.maximum(q, 0)
        x = nt3(f_ref[at], pad_rows(linv_ref[at], 128))
        x_ref[at] = jnp.where((q == s) & (lane48 > row48), 0.0, x)

    def double_row(q):
        at = jnp.maximum(q, 0)
        x = x_ref[at]
        g_ref[at] = nn3(x, pad_rows(linv_ref[at], 128))

    def pivot_block(t, at):
        packed = pivots_ref[t]
        parts = []
        for i in range(3):
            by = (at - LIVE * i) % 128
            parts.append(pltpu.roll(packed, by, 1) if by else packed)
        block = jnp.concatenate([parts[0], parts[1], parts[2][:8]], 0)
        return jnp.where((lane >= at) & (lane < at + LIVE), block, 0.0)

    def scale(t, at):
        spare = pltpu.roll(pivots_ref[t, 8:16, :], (at - 2 * LIVE) % 128, 1)[0:1]
        lanes = lanes_of((1, 128))
        return jnp.where((lanes >= at) & (lanes < at + LIVE), spare, 1.0)

    def live_count(t):
        return jnp.max(jnp.where(lanes_of((8, 128)) == 3 * LIVE, links_ref[t][0:8], 0.0))

    def at_rows(x, start):
        above = jnp.zeros((start, 128), F32)
        return pad_rows(jnp.concatenate([above, x], 0) if start else x, 128)

    def step(t, odd, scur, n):
        soff, uoff = (LIVE, 0) if odd else (0, LIVE)
        following = jnp.minimum(t + 1, NB - 1)
        given = links_ref[t] * scale(following, uoff)
        limit = jnp.where(t == NB - 1, 16, LIVE)
        in_s = (lane >= soff) & (lane < soff + LIVE)
        in_u = (lane >= uoff) & (lane < uoff + LIVE)
        eye = jnp.where(lane == row + soff, 1.0, 0.0)
        a = jnp.where((row < limit) & (lane < soff + limit), scur, eye)
        rest = jnp.where(lane == row + 2 * LIVE, 1.0, 0.0)
        rest = jnp.where(in_u, jnp.where(row < limit, given, 0.0), rest)
        a = jnp.where(in_s, a, rest)
        ut = jnp.where(in_s, given, 0.0) * links_ref[following, :, 3 * LIVE + 1 : 3 * LIVE + 2]
        tiles = tuple(a[8 * v : 8 * v + 8] for v in range(LIVE // 8))
        state = pivots(0, soff, (tiles, tiles), spread_ref, rows_ref, side_ref)
        state = pivots(1, soff, state, spread_ref, rows_ref, side_ref)

        double_row(t - 3)
        solve_row(t - 2)
        reduce_row(t - 1)
        coming, coming_n = pivot_block(following, uoff), live_count(following)
        n = jnp.where(t == NB - 1, jnp.minimum(n, 16.0), n)
        for p in range(2, LIVE // 8):
            state = lax.cond(
                n > 8.0 * p,
                lambda st, p=p: pivots(p, soff, st, spread_ref, rows_ref, side_ref),
                lambda st: st,
                state,
            )
        tiles, saved = state
        k = jnp.concatenate(tiles, 0)
        snext = coming - nn3(ut, at_rows(k, soff))
        linv_ref[t] = left(jnp.concatenate(saved, 0), 2 * LIVE)
        k_ref[t + 1] = left(k, uoff)
        return snext, coming_n

    @pl.when(upper | member)
    def _():
        k_ref[0] = jnp.zeros((LIVE, 128), F32)
        linv_ref[0] = jnp.zeros((LIVE, 128), F32)
        f_ref[0] = jnp.zeros((SLOTS, 128), F32)
        x_ref[0] = jnp.zeros((SLOTS, 128), F32)
        def pair(i, carry):
            carry = step(2 * i, False, *carry)
            return step(2 * i + 1, True, *carry)

        lax.fori_loop(0, NB // 2, pair, (pivot_block(0, 0), live_count(0)))
        double_row(NB - 3)
        solve_row(NB - 2)
        reduce_row(NB - 1)
        double_row(NB - 2)
        solve_row(NB - 1)
        double_row(NB - 1)
        for t in range(NB):
            put(x_ref[t], SLOTS * t, False)

    @pl.when(upper)
    def _():
        dead = jnp.where((row48 == lane48) & (row48 >= LIVE), 1.0, 0.0)
        place(out_ref, dead, SLOTS * s, before)

    @pl.when(member)
    def _():
        late = lane >= 16
        last = jnp.where(row < 16, links_ref[NB - 1], 0.0)
        own = jnp.where(late & (row < 16), pivot_block(NB - 1, 0) / scale(NB - 1, 0), 0.0)
        over = jnp.where(late, left(links_ref[NB - 2], LIVE), 0.0)
        y = None
        for t in range(NB - 1, -1, -1):
            if y is None:
                y = g_ref[t]
                put(-nn3(y, pad_rows(left(last, 0), 128)), SLOTS * NB, True)
                put(-nn3(y, pad_rows(own, 128)), SLOTS * (NB - 1), True)
            else:
                y = g_ref[t] - nt3(y, pad_rows(k_ref[t + 1], 128))
            if t == NB - 2:
                put(-nn3(y, pad_rows(over, 128)), SLOTS * (NB - 1), True)
            rising = pad_rows(left(links_ref[t], 2 * LIVE), 128)
            put(-nt3(y, rising), SLOTS * (t + NU), True)

    @pl.when(s >= 21)
    def _():
        targets = [s, s - NU, s + NU, s - 1, s + 1]
        valid = [True, g > 0, g < NG - 1, u > 0, u < NU - 1]
        for k in range(5):
            pos = SLOTS * jnp.clip(targets[k], 0, NG * NU - 1)
            place(out_ref, jnp.where(valid[k], blocks_ref[k], 0.0), pos, after)

    @pl.when(s == 21)
    def _():
        out_ref[0:16, DONE:] = jnp.zeros((16, NC - DONE), F32)


def factor(links, pivs, blocks):
    vmem = pl.BlockSpec(memory_space=pltpu.VMEM)
    return pl.pallas_call(
        factor_kernel,
        out_shape=jax.ShapeDtypeStruct((SLOTS, NC), F32),
        in_specs=[vmem, vmem, vmem],
        out_specs=vmem,
        scratch_shapes=[
            pltpu.VMEM((NB, LIVE, 128), F32),
            pltpu.VMEM((NB + 1, LIVE, 128), F32),
            pltpu.VMEM((NB, SLOTS, 128), F32),
            pltpu.VMEM((NB, SLOTS, 128), F32),
            pltpu.VMEM((NB, SLOTS, 128), F32),
            pltpu.VMEM((LIVE // 8, 8, 8, 128), F32),
            pltpu.VMEM((LIVE // 8, 8, 128), F32),
            pltpu.VMEM((LIVE // 8, 8, 8, 128), F32),
        ],
        compiler_params=pltpu.CompilerParams(vmem_limit_bytes=40 * 2**20),
        name="factor",
    )(links, pivs, blocks)


def per_device(modes, counts, kappa, react):
    kappa = pltpu.with_memory_space_constraint(kappa, pltpu.HBM)
    react = pltpu.with_memory_space_constraint(react, pltpu.HBM)
    blocks, links, pivs = assemble(counts, modes, kappa, react)
    return factor(links, pivs, blocks)


def solution(mesh):
    in_specs = (
        P(None, "grp", "sub", None),
        P(("grp", "sub")),
        P("grp", "sub", None),
        P("grp", "sub", None),
    )
    out_specs = P(("grp", "sub"), None)
    return jax.shard_map(
        per_device, mesh=mesh, in_specs=in_specs, out_specs=out_specs, check_vma=False
    )
```

```python
import jax
import jax.numpy as jnp
from jax import lax
from jax.experimental import pallas as pl
from jax.experimental.pallas import tpu as pltpu
from jax.sharding import PartitionSpec as P

F32 = jnp.float32
BF16 = jnp.bfloat16
MESH = pl.DeviceIdType.MESH
NG, NU = 4, 32
CX, CY, NZ = 16, 16, 256
SLOTS, LIVE = 48, 40
NB = 22
DONE = 1024
GROUP = 24
NC = SLOTS * NG * NU


def nt(a, b, precision=None):
    return lax.dot_general(
        a, b, (((1,), (1,)), ((), ())), preferred_element_type=F32, precision=precision
    )


def lanes_of(shape):
    return lax.broadcasted_iota(jnp.int32, shape, len(shape) - 1)


def rows_of(shape):
    return lax.broadcasted_iota(jnp.int32, shape, len(shape) - 2)


def split(x):
    hi = x.astype(BF16)
    return hi, (x - hi.astype(F32)).astype(BF16)


def pad_rows(x, rows):
    return jnp.concatenate([x, jnp.zeros((rows - x.shape[0], x.shape[1]), x.dtype)], 0)


def pad_lanes(x, lanes):
    return jnp.concatenate([x, jnp.zeros((x.shape[0], lanes - x.shape[1]), x.dtype)], 1)


def transposed(x):
    return jnp.transpose(pad_rows(x, 128))


def assemble_kernel(
    count_ref, modes_ref, kappa_ref, react_ref, blocks_ref, links_ref, pivots_ref,
    raw, kappa, react, field, masked, wx, wy, wz, diag, edge, halo, face_x, face_y,
    high, low, ends, links, pivs, order,
    raw_sem, cell_sem, halo_send, halo_recv, face_send, face_recv,
    up_sem, link_send, link_recv, piv_send, piv_recv, cross_send, cross_recv,
):
    g, u = lax.axis_index("grp"), lax.axis_index("sub")
    partners = [
        (lax.rem(g + NG - 1, NG), u),
        (lax.rem(g + 1, NG), u),
        (g, lax.rem(u + NU - 1, NU)),
        (g, lax.rem(u + 1, NU)),
    ]
    inside = [g > 0, g < NG - 1, u > 0, u < NU - 1]
    mirror = [1, 0, 3, 2]
    chip, core = u // 2, lax.rem(u, 2)
    joined = (g < 2) & (u < GROUP)

    def fetch(x):
        return pltpu.make_async_copy(
            modes_ref.at[pl.ds(0, LIVE), x], raw.at[x], raw_sem.at[x]
        )

    cells = [
        pltpu.make_async_copy(kappa_ref, kappa, cell_sem.at[0]),
        pltpu.make_async_copy(react_ref, react, cell_sem.at[1]),
    ]
    fetch(0).start()
    fetch(CX - 1).start()
    cells[0].start()
    for x in range(1, CX - 1):
        fetch(x).start()
    cells[1].start()

    barrier = pltpu.get_barrier_semaphore()

    def greet(device):
        pl.semaphore_signal(barrier, inc=1, device_id=device, device_id_type=MESH)

    for partner in partners:
        greet(partner)

    def others(count, me, act):
        for step in range(1, count):
            v = me + step
            act(jnp.where(v >= count, v - count, v))

    @pl.when(joined)
    def _():
        others(GROUP // 2, chip, lambda v: greet((g, 2 * v + core)))
        greet((g, 2 * chip + 1 - core))

    count = count_ref[0]
    z_from, z_to = rows_of((NZ, NZ)), lanes_of((NZ, NZ))
    here = z_from == jnp.where(z_to < 128, 2 * z_to, 2 * z_to - 255)
    order[...] = jnp.where(here, 1.0, 0.0).astype(BF16)

    def ordered(x):
        return jnp.dot(x.reshape(-1, NZ), order[...], preferred_element_type=F32)

    live = rows_of((CY, LIVE, NZ)) < count

    def turn(x, side=None):
        plane = jnp.swapaxes(ordered(raw[x]).reshape(LIVE, CY, NZ), 0, 1)
        plane = jnp.where(live, plane, 0.0)
        field[x] = plane
        for y in range(CY):
            masked[x, :, NZ * y : NZ * (y + 1)] = pad_rows(plane[y], SLOTS).astype(BF16)
        if side is not None:
            for y in range(0, CY, 2):
                two = jnp.concatenate([plane[y], plane[y + 1]], 0)
                ends[side, :, NZ * y // 2 : NZ * (y + 2) // 2] = two.astype(BF16)

    fetch(0).wait()
    fetch(CX - 1).wait()
    turn(0, 0)
    turn(CX - 1, 1)
    cells[0].wait()
    kap = ordered(kappa[...]).reshape(CX, CY, NZ)
    edge[0] = kap[0]
    edge[1] = kap[CX - 1]
    for x in range(CX):
        edge[2, x : x + 1] = kap[x, 0:1]
        edge[3, x : x + 1] = kap[x, CY - 1 : CY]
    pl.semaphore_wait(barrier, jnp.where(joined, GROUP // 2 + 4, 4))

    def halo_copy(k):
        return pltpu.make_async_remote_copy(
            src_ref=edge.at[k], dst_ref=halo.at[mirror[k]],
            send_sem=halo_send.at[k], recv_sem=halo_recv.at[mirror[k]],
            device_id=partners[k], device_id_type=MESH,
        )

    sources = [
        ends.at[0],
        ends.at[1],
        masked.at[:, :, pl.ds(0, NZ)],
        masked.at[:, :, pl.ds((CY - 1) * NZ, NZ)],
    ]
    landings = [face_x.at[0], face_x.at[1], face_y.at[0], face_y.at[1]]

    def face_copy(k):
        return pltpu.make_async_remote_copy(
            src_ref=sources[k], dst_ref=landings[mirror[k]],
            send_sem=face_send.at[k], recv_sem=face_recv.at[mirror[k]],
            device_id=partners[k], device_id_type=MESH,
        )

    for k in range(4):
        halo_copy(k).start()
    face_copy(0).start()
    face_copy(1).start()

    def turn_next(i, carry):
        fetch(2 * i + 1).wait()
        fetch(2 * i + 2).wait()
        turn(2 * i + 1)
        turn(2 * i + 2)
        return carry

    lax.fori_loop(0, CX // 2 - 1, turn_next, 0)
    face_copy(2).start()
    face_copy(3).start()

    plane0 = jnp.zeros((CY, NZ), F32)
    row0 = jnp.zeros((1, NZ), F32)
    half = lanes_of((CY, 128))
    wx[0] = plane0
    wx[CX] = plane0
    for x in range(CX - 1):
        wx[x + 1] = 0.5 * (kap[x] + kap[x + 1])
    for x in range(CX):
        k = kap[x]
        wy[x, 0:1] = row0
        wy[x, 1:CY] = 0.5 * (k[: CY - 1] + k[1:])
        wy[x, CY : CY + 1] = row0
        even, uneven = k[:, :128], k[:, 128:]
        wz[x, :, 0:128] = 0.5 * (even + uneven)
        wz[x, :, 128:] = jnp.where(half == 127, 0.0, 0.5 * (uneven + pltpu.roll(even, 127, 1)))
    cells[1].wait()
    reac = ordered(react[...]).reshape(CX, CY, NZ)
    for k in range(4):
        halo_copy(k).wait_recv()
    ext = [jnp.where(inside[k], halo[k], 0.0) for k in range(4)]
    bound = [0.5 * (edge[k] + ext[k]) for k in range(4)]
    for x in range(CX):
        k = kap[x]
        inner, outer = wz[x, :, 0:128], wz[x, :, 128:]
        below = jnp.where(half == 0, 0.5 * k[:, :128], pltpu.roll(outer, 1, 1))
        above = jnp.where(half == 127, 0.5 * k[:, 128:], outer)
        dz = jnp.concatenate([below + inner, inner + above], 1)
        dx = (bound[0] if x == 0 else wx[x]) + (bound[1] if x == CX - 1 else wx[x + 1])
        dy = wy[x, 0:CY] + wy[x, 1 : CY + 1]
        dy = dy + jnp.concatenate(
            [bound[2][x : x + 1], jnp.zeros((CY - 2, NZ), F32), bound[3][x : x + 1]], 0
        )
        diag[x] = reac[x] + dx + dy + dz

    def apply(x, gram):
        before, after = jnp.maximum(x - 1, 0), jnp.minimum(x + 1, CX - 1)
        behind, v = None, field[x, 0]
        for y in range(CY):
            ahead = field[x, y + 1] if y < CY - 1 else None
            out = diag[x, y : y + 1] * v
            out = out - wx[x, y : y + 1] * field[before, y]
            out = out - wx[x + 1, y : y + 1] * field[after, y]
            if y > 0:
                out = out - wy[x, y : y + 1] * behind
            if y < CY - 1:
                out = out - wy[x, y + 1 : y + 2] * ahead
            even, uneven = v[:, :128], v[:, 128:]
            inner, outer = wz[x, y : y + 1, 0:128], wz[x, y : y + 1, 128:]
            out = out - jnp.concatenate(
                [
                    inner * uneven + pltpu.roll(outer * uneven, 1, 1),
                    inner * even + outer * pltpu.roll(even, 127, 1),
                ],
                1,
            )
            local = pad_rows(out, SLOTS).astype(BF16)
            gram = gram + nt(masked[x, :, NZ * y : NZ * (y + 1)], local)
            behind, v = v, ahead
        return gram

    gram = lax.fori_loop(
        0, CX // 2, lambda i, gram: apply(2 * i + 1, apply(2 * i, gram)),
        jnp.zeros((SLOTS, SLOTS), F32),
    )
    own = pad_lanes(gram, 128)
    spot, slot = lanes_of((SLOTS, 128)), rows_of((SLOTS, 128))
    own = own + jnp.where((spot == slot) & (slot >= count), 1.0, 0.0)
    sym = jnp.where(spot < LIVE, 0.5 * (own + transposed(own)[:SLOTS]), 0.0)

    on_diag = jnp.where((spot == slot) & (spot < LIVE), sym, 0.0)
    scale_lane = lax.rsqrt(jnp.sum(on_diag, axis=0, keepdims=True))
    scale_lane = jnp.where(lanes_of((1, 128)) < LIVE, scale_lane, 1.0)
    scale_row = lax.rsqrt(jnp.sum(on_diag, axis=1, keepdims=True)[:LIVE])

    def up_copy(ref, i):
        return pltpu.make_async_remote_copy(
            src_ref=ref, dst_ref=ref, send_sem=up_sem.at[i], recv_sem=up_sem.at[i + 2],
            device_id=(1, u), device_id_type=MESH,
        )

    def link_copy(to, owner):
        return pltpu.make_async_remote_copy(
            src_ref=links.at[owner, core], dst_ref=links.at[owner, core],
            send_sem=link_send.at[to], recv_sem=link_recv.at[owner],
            device_id=(g, 2 * to + core), device_id_type=MESH,
        )

    def piv_copy(to, owner):
        return pltpu.make_async_remote_copy(
            src_ref=pivs.at[owner, core], dst_ref=pivs.at[owner, core],
            send_sem=piv_send.at[to], recv_sem=piv_recv.at[owner],
            device_id=(g, 2 * to + core), device_id_type=MESH,
        )

    def cross_copy(ref, sem):
        return pltpu.make_async_remote_copy(
            src_ref=ref, dst_ref=ref, send_sem=cross_send.at[sem], recv_sem=cross_recv.at[sem],
            device_id=(g, 2 * chip + 1 - core), device_id_type=MESH,
        )

    def cross_link(v, c):
        return cross_copy(links.at[v, c], v)

    def cross_pivs(c):
        return cross_copy(pivs.at[:, c], GROUP // 2)

    link_up, piv_up = up_copy(links.at[chip, core], 0), up_copy(pivs.at[chip, core], 1)

    @pl.when(joined & (g == 0))
    def _():
        unit = sym[:LIVE] * scale_row * scale_lane
        packed = unit[0:16] + pltpu.roll(unit[16:32], LIVE, 1)
        packed = packed + pltpu.roll(pad_rows(unit[32:40], 16), 2 * LIVE, 1)
        shifted = pltpu.roll(jnp.broadcast_to(scale_lane, (16, 128)), 2 * LIVE, 1)
        wide_lane = lanes_of((16, 128))
        spare = (rows_of((16, 128)) == 8) & (wide_lane >= 2 * LIVE) & (wide_lane < 3 * LIVE)
        pivs[chip, core] = jnp.where(spare, shifted, packed)
        piv_up.start()
        others(GROUP // 2, chip, lambda v: piv_copy(v, chip).start())

    def coupling(k):
        weight = bound[k]
        total = jnp.zeros((SLOTS, SLOTS), F32)
        if k < 2:
            x = 0 if k == 0 else CX - 1
            for y in range(0, CY, 2):
                two = [field[x, j] * weight[j : j + 1] for j in (y, y + 1)]
                hi, lo = split(jnp.concatenate(two, 0))
                cols = slice(NZ * y // 2, NZ * (y + 2) // 2)
                high[:, cols], low[:, cols] = hi, lo
            face_copy(mirror[k]).wait_recv()
            both = nt(high[...], face_x[k]) + nt(low[...], face_x[k])
            both = pad_lanes(both, 128)
            block = both[:LIVE] + pltpu.roll(both[LIVE:], 128 - LIVE, 1)
            block = jnp.where(lanes_of((LIVE, 128)) < LIVE, block, 0.0)
        else:
            face_copy(mirror[k]).wait_recv()
            for x in range(CX):
                mine = field[x, 0 if k == 2 else CY - 1] * weight[x : x + 1]
                hi, lo = split(pad_rows(mine, SLOTS))
                other = face_y[k - 2, x]
                total = total + (nt(hi, other) + nt(lo, other))
            block = pad_lanes(total, 128)[:LIVE]
        return jnp.where(inside[k], -block, 0.0)

    found = {k: coupling(k) for k in (1, 3)}
    lane = lanes_of((LIVE, 128))
    odd = core == 1
    ahead = found[3] * scale_row
    ahead_t = transposed(found[3])[:LIVE] * scale_lane
    rising = transposed(found[1])[:LIVE] * scale_lane
    message = jnp.where(odd, ahead, ahead_t) + pltpu.roll(jnp.where(odd, ahead_t, ahead), LIVE, 1)
    message = message + pltpu.roll(rising, 2 * LIVE, 1)
    message = jnp.where(lane >= 3 * LIVE, count.astype(F32), message)
    message = jnp.where(lane == 3 * LIVE + 1, scale_row, message)

    @pl.when(joined & (g == 0))
    def _():
        links[chip, core] = message
        link_up.start()
        others(GROUP // 2, chip, lambda v: link_copy(v, chip).start())

    @pl.when(joined & (g == 1))
    def _():
        piv_up.wait_recv()
        others(GROUP // 2, chip, lambda v: piv_copy(v, chip).start())
        link_up.wait_recv()
        others(GROUP // 2, chip, lambda v: link_copy(v, chip).start())

    for k in (0, 2):
        found[k] = coupling(k)
    blocks_ref[0] = own
    for k in range(4):
        blocks_ref[k + 1] = pad_rows(found[k], SLOTS)
    blocks_ref[5] = sym

    @pl.when(joined)
    def _():
        others(GROUP // 2, chip, lambda v: piv_copy(chip, v).wait_recv())
        cross_pivs(core).start()
        cross_link(chip, core).start()

        def forward(v):
            link_copy(chip, v).wait_recv()
            cross_link(v, core).start()

        others(GROUP // 2, chip, forward)
        cross_pivs(1 - core).wait_recv()
        for v in range(GROUP // 2):
            cross_link(v, 1 - core).wait_recv()
        for v in range(GROUP):
            links_ref[v] = links[v // 2, v % 2]
            pivots_ref[v] = pivs[v // 2, v % 2]
        others(GROUP // 2, chip, lambda v: link_copy(v, chip).wait_send())
        others(GROUP // 2, chip, lambda v: piv_copy(v, chip).wait_send())
        cross_pivs(core).wait_send()
        for v in range(GROUP // 2):
            cross_link(v, core).wait_send()

    @pl.when(joined & (g == 0))
    def _():
        link_up.wait_send()
        piv_up.wait_send()

    for k in range(4):
        halo_copy(k).wait_send()
        face_copy(k).wait_send()


def assemble(count, modes, kappa, react):
    vmem = pl.BlockSpec(memory_space=pltpu.VMEM)
    hbm = pl.BlockSpec(memory_space=pltpu.HBM)
    dma = pltpu.SemaphoreType.DMA
    return pl.pallas_call(
        assemble_kernel,
        out_shape=(
            jax.ShapeDtypeStruct((6, SLOTS, 128), F32),
            jax.ShapeDtypeStruct((GROUP, LIVE, 128), F32),
            jax.ShapeDtypeStruct((GROUP, 16, 128), F32),
        ),
        in_specs=[pl.BlockSpec(memory_space=pltpu.SMEM), hbm, hbm, hbm],
        out_specs=(vmem, vmem, vmem),
        scratch_shapes=[
            pltpu.VMEM((CX, LIVE, CY, NZ), BF16),
            pltpu.VMEM((CX, CY, NZ), BF16),
            pltpu.VMEM((CX, CY, NZ), BF16),
            pltpu.VMEM((CX, CY, LIVE, NZ), F32),
            pltpu.VMEM((CX, SLOTS, CY * NZ), BF16),
            pltpu.VMEM((CX + 1, CY, NZ), F32),
            pltpu.VMEM((CX, 24, NZ), F32),
            pltpu.VMEM((CX, CY, NZ), F32),
            pltpu.VMEM((CX, CY, NZ), F32),
            pltpu.VMEM((4, 16, NZ), F32),
            pltpu.VMEM((4, 16, NZ), F32),
            pltpu.VMEM((2, 2 * LIVE, 8 * NZ), BF16),
            pltpu.VMEM((2, 16, SLOTS, NZ), BF16),
            pltpu.VMEM((2 * LIVE, 8 * NZ), BF16),
            pltpu.VMEM((2 * LIVE, 8 * NZ), BF16),
            pltpu.VMEM((2, 2 * LIVE, 8 * NZ), BF16),
            pltpu.VMEM((GROUP // 2, 2, LIVE, 128), F32),
            pltpu.VMEM((GROUP // 2, 2, 16, 128), F32),
            pltpu.VMEM((NZ, NZ), BF16),
            dma((CX,)),
            dma((2,)),
            dma((4,)),
            dma((4,)),
            dma((4,)),
            dma((4,)),
            dma((4,)),
            dma((GROUP // 2,)),
            dma((GROUP // 2,)),
            dma((GROUP // 2,)),
            dma((GROUP // 2,)),
            dma((GROUP // 2 + 1,)),
            dma((GROUP // 2 + 1,)),
        ],
        compiler_params=pltpu.CompilerParams(
            collective_id=0, has_side_effects=True, vmem_limit_bytes=50 * 2**20
        ),
        name="assemble",
    )(count, modes, kappa, react)


def halves(x, rows, axis):
    hi, lo = split(pad_rows(x, rows) if x.shape[0] < rows else x)
    return jnp.concatenate([hi, lo], axis)


def joined_halves(out, rows):
    tall = out.shape[0] // 2
    return out[:rows, :128] + (out[:rows, 128:] + out[tall : tall + rows, :128])


def nn3(a, b):
    left = halves(a, SLOTS, 0)
    out = jnp.dot(left, halves(b, 128, 1), preferred_element_type=F32)
    return joined_halves(out, a.shape[0])


def nt3(a, b):
    out = nt(halves(a, SLOTS, 0), halves(b, 128, 0))
    return joined_halves(out, a.shape[0])


def wide(x):
    return jnp.broadcast_to(x, (8, 128))


def pivots(p, soff, state, spread_ref, rows_ref, side_ref):
    tiles, saved = (list(part) for part in state)
    sub = rows_of((8, 128))
    at = soff + 8 * p
    column = lambda v, c: wide(tiles[v][:, c : c + 1])
    if p == 0:
        for c in range(8):
            spread_ref[p, c] = column(p, at + c)
    rows_ref[p] = tiles[p]
    d = {(i, j): wide(spread_ref[p, j, i : i + 1]) for i in range(8) for j in range(i, 8)}
    rows = [wide(rows_ref[p, c : c + 1]) for c in range(8)]
    follow = p + 1 < LIVE // 8
    if follow:
        under = [column(p + 1, at + c) for c in range(8)]
        coming = [column(p + 1, at + 8 + c) for c in range(8)]
    others = [v for v in range(LIVE // 8) if v not in (p, p + 1)]
    factors = {v: [column(v, at + c) for c in range(8)] for v in others}
    alpha, beta, z = {}, {}, list(rows)
    for c in range(0, 8, 2):
        n = c + 1
        a, b, e = d[c, c], d[c, n], d[n, n]
        det = a * e - b * b
        r = pl.reciprocal(det, approx=True)
        for i in range(n + 1, 8):
            top, bottom = e * d[c, i] - b * d[n, i], a * d[n, i] - b * d[c, i]
            alpha[c, i], beta[c, i] = top * r, bottom * r
            for j in range(i, 8):
                if j <= n + 2:
                    d[i, j] = d[i, j] - (top * d[c, j] + bottom * d[n, j]) * r
                else:
                    d[i, j] = d[i, j] - (alpha[c, i] * d[c, j] + beta[c, i] * d[n, j])
        root = lax.rsqrt(a)
        saved[p] = jnp.where(sub == c, rows[c] * root, saved[p])
        second = (rows[n] - (b * root * root) * rows[c]) * (lax.rsqrt(det) * (a * root))
        saved[p] = jnp.where(sub == n, second, saved[p])
        for i in range(n + 1, 8):
            rows[i] = rows[i] - (alpha[c, i] * rows[c] + beta[c, i] * rows[n])
        z[c] = (e * rows[c] - b * rows[n]) * r
        z[n] = (a * rows[n] - b * rows[c]) * r
        if follow:
            first = (e * under[c] - b * under[n]) * r
            other = (a * under[n] - b * under[c]) * r
            side_ref[p, c], side_ref[p, n] = first, other
            for i in range(n + 1, 8):
                under[i] = under[i] - (alpha[c, i] * under[c] + beta[c, i] * under[n])
            for i in range(8):
                coming[i] = coming[i] - (
                    under[c] * wide(side_ref[p, c, i : i + 1])
                    + under[n] * wide(side_ref[p, n, i : i + 1])
                )
            tiles[p + 1] = tiles[p + 1] - (first * rows[c] + other * rows[n])
    if follow:
        for c in range(8):
            spread_ref[p + 1, c] = coming[c]
    for c in range(4, -1, -2):
        for i in range(c + 2, 8):
            z[c] = z[c] - alpha[c, i] * z[i]
            z[c + 1] = z[c + 1] - beta[c, i] * z[i]
    for v in others:
        terms = [factors[v][c] * z[c] for c in range(8)]
        while len(terms) > 1:
            terms = [terms[i] + terms[i + 1] for i in range(0, len(terms), 2)]
        tiles[v] = tiles[v] - terms[0]
    for c in range(8):
        tiles[p] = jnp.where(sub == c, z[c], tiles[p])
    return tuple(tiles), tuple(saved)


def place(out_ref, block, pos, keep):
    base = jnp.minimum((pos // 128) * 128, NC - 256)
    base = pl.multiple_of(base, 128)
    shifted = pltpu.roll(pad_lanes(block, 256), pos - base, 1)
    cols = lanes_of((SLOTS, 256)) + base
    out_ref[:, pl.ds(base, 256)] += jnp.where(keep(cols), shifted, 0.0)


def factor_kernel(
    links_ref, pivots_ref, blocks_ref, out_ref, linv_ref, k_ref, g_ref, f_ref, x_ref, spread_ref, rows_ref, side_ref,
):
    g, u = lax.axis_index("grp"), lax.axis_index("sub")
    s = g * NU + u
    upper = s <= 21
    member = (s == 21) | (s == 22) | ((s >= NU) & (s < NU + NB))
    lane = lanes_of((LIVE, 128))
    row = rows_of((LIVE, 128))
    lane48 = lanes_of((SLOTS, 128))
    row48 = rows_of((SLOTS, 128))
    out_ref[...] = jnp.zeros_like(out_ref)
    before = lambda cols: cols < DONE
    after = lambda cols: cols >= DONE

    def left(x, by):
        x = pltpu.roll(x, 128 - by, 1) if by else x
        return jnp.where(lanes_of(x.shape) < LIVE, x, 0.0)

    def put(block, pos, late):
        base = pos // 128 * 128
        shifted = pltpu.roll(pad_lanes(block, 256), pos - base, 1) if pos > base else (
            pad_lanes(block, 256)
        )
        if base < DONE < base + 256:
            cols = lanes_of((SLOTS, 256)) + base
            shifted = jnp.where(cols >= DONE if late else cols < DONE, shifted, 0.0)
        out_ref[:, base : base + 256] += shifted

    def reduce_row(q):
        at, wide_enough = jnp.maximum(q, 0), jnp.where(q == NB - 1, 16, LIVE)
        mine = jnp.where(q == s, blocks_ref[5], 0.0)
        mine = jnp.where(q == s - 1, blocks_ref[3], mine)
        mine = jnp.where(q == s - NU, blocks_ref[1], mine)
        mine = mine * scale(at, 0)
        held = jnp.where(q > 0, f_ref[jnp.maximum(q - 1, 0)], 0.0)
        f = mine - nn3(held, pad_rows(k_ref[at], 128))
        f_ref[at] = jnp.where((q <= s) & (lane48 < wide_enough), f, 0.0)

    def solve_row(q):
        at = jnp.maximum(q, 0)
        x = nt3(f_ref[at], pad_rows(linv_ref[at], 128))
        x_ref[at] = jnp.where((q == s) & (lane48 > row48), 0.0, x)

    def double_row(q):
        at = jnp.maximum(q, 0)
        x = x_ref[at]
        g_ref[at] = nn3(x, pad_rows(linv_ref[at], 128))

    def pivot_block(t, at):
        packed = pivots_ref[t]
        parts = []
        for i in range(3):
            by = (at - LIVE * i) % 128
            parts.append(pltpu.roll(packed, by, 1) if by else packed)
        block = jnp.concatenate([parts[0], parts[1], parts[2][:8]], 0)
        return jnp.where((lane >= at) & (lane < at + LIVE), block, 0.0)

    def scale(t, at):
        spare = pltpu.roll(pivots_ref[t, 8:16, :], (at - 2 * LIVE) % 128, 1)[0:1]
        lanes = lanes_of((1, 128))
        return jnp.where((lanes >= at) & (lanes < at + LIVE), spare, 1.0)

    def live_count(t):
        return jnp.max(jnp.where(lanes_of((8, 128)) == 3 * LIVE, links_ref[t][0:8], 0.0))

    def at_rows(x, start):
        above = jnp.zeros((start, 128), F32)
        return pad_rows(jnp.concatenate([above, x], 0) if start else x, 128)

    def step(t, odd, scur, n):
        soff, uoff = (LIVE, 0) if odd else (0, LIVE)
        following = jnp.minimum(t + 1, NB - 1)
        given = links_ref[t] * scale(following, uoff)
        limit = jnp.where(t == NB - 1, 16, LIVE)
        in_s = (lane >= soff) & (lane < soff + LIVE)
        in_u = (lane >= uoff) & (lane < uoff + LIVE)
        eye = jnp.where(lane == row + soff, 1.0, 0.0)
        a = jnp.where((row < limit) & (lane < soff + limit), scur, eye)
        rest = jnp.where(lane == row + 2 * LIVE, 1.0, 0.0)
        rest = jnp.where(in_u, jnp.where(row < limit, given, 0.0), rest)
        a = jnp.where(in_s, a, rest)
        ut = jnp.where(in_s, given, 0.0) * links_ref[following, :, 3 * LIVE + 1 : 3 * LIVE + 2]
        tiles = tuple(a[8 * v : 8 * v + 8] for v in range(LIVE // 8))
        state = pivots(0, soff, (tiles, tiles), spread_ref, rows_ref, side_ref)

        coming, coming_n = pivot_block(following, uoff), live_count(following)
        n = jnp.where(t == NB - 1, jnp.minimum(n, 16.0), n)
        for p in range(1, LIVE // 8):
            state = lax.cond(
                n > 8.0 * p,
                lambda st, p=p: pivots(p, soff, st, spread_ref, rows_ref, side_ref),
                lambda st: st,
                state,
            )
        double_row(t - 3)
        solve_row(t - 2)
        reduce_row(t - 1)
        tiles, saved = state
        k = jnp.concatenate(tiles, 0)
        snext = coming - nn3(ut, at_rows(k, soff))
        linv_ref[t] = left(jnp.concatenate(saved, 0), 2 * LIVE)
        k_ref[t + 1] = left(k, uoff)
        return snext, coming_n

    @pl.when(upper | member)
    def _():
        k_ref[0] = jnp.zeros((LIVE, 128), F32)
        linv_ref[0] = jnp.zeros((LIVE, 128), F32)
        f_ref[0] = jnp.zeros((SLOTS, 128), F32)
        x_ref[0] = jnp.zeros((SLOTS, 128), F32)
        def pair(i, carry):
            carry = step(2 * i, False, *carry)
            return step(2 * i + 1, True, *carry)

        lax.fori_loop(0, NB // 2, pair, (pivot_block(0, 0), live_count(0)))
        double_row(NB - 3)
        solve_row(NB - 2)
        reduce_row(NB - 1)
        double_row(NB - 2)
        solve_row(NB - 1)
        double_row(NB - 1)
        for t in range(NB):
            put(x_ref[t], SLOTS * t, False)

    @pl.when(upper)
    def _():
        dead = jnp.where((row48 == lane48) & (row48 >= LIVE), 1.0, 0.0)
        place(out_ref, dead, SLOTS * s, before)

    @pl.when(member)
    def _():
        late = lane >= 16
        last = jnp.where(row < 16, links_ref[NB - 1], 0.0)
        own = jnp.where(late & (row < 16), pivot_block(NB - 1, 0) / scale(NB - 1, 0), 0.0)
        over = jnp.where(late, left(links_ref[NB - 2], LIVE), 0.0)
        y = None
        for t in range(NB - 1, -1, -1):
            if y is None:
                y = g_ref[t]
                put(-nn3(y, pad_rows(left(last, 0), 128)), SLOTS * NB, True)
                put(-nn3(y, pad_rows(own, 128)), SLOTS * (NB - 1), True)
            else:
                y = g_ref[t] - nt3(y, pad_rows(k_ref[t + 1], 128))
            if t == NB - 2:
                put(-nn3(y, pad_rows(over, 128)), SLOTS * (NB - 1), True)
            rising = pad_rows(left(links_ref[t], 2 * LIVE), 128)
            put(-nt3(y, rising), SLOTS * (t + NU), True)

    @pl.when(s >= 21)
    def _():
        targets = [s, s - NU, s + NU, s - 1, s + 1]
        valid = [True, g > 0, g < NG - 1, u > 0, u < NU - 1]
        for k in range(5):
            pos = SLOTS * jnp.clip(targets[k], 0, NG * NU - 1)
            place(out_ref, jnp.where(valid[k], blocks_ref[k], 0.0), pos, after)

    @pl.when(s == 21)
    def _():
        out_ref[0:16, DONE:] = jnp.zeros((16, NC - DONE), F32)


def factor(links, pivs, blocks):
    vmem = pl.BlockSpec(memory_space=pltpu.VMEM)
    return pl.pallas_call(
        factor_kernel,
        out_shape=jax.ShapeDtypeStruct((SLOTS, NC), F32),
        in_specs=[vmem, vmem, vmem],
        out_specs=vmem,
        scratch_shapes=[
            pltpu.VMEM((NB, LIVE, 128), F32),
            pltpu.VMEM((NB + 1, LIVE, 128), F32),
            pltpu.VMEM((NB, SLOTS, 128), F32),
            pltpu.VMEM((NB, SLOTS, 128), F32),
            pltpu.VMEM((NB, SLOTS, 128), F32),
            pltpu.VMEM((LIVE // 8, 8, 8, 128), F32),
            pltpu.VMEM((LIVE // 8, 8, 128), F32),
            pltpu.VMEM((LIVE // 8, 8, 8, 128), F32),
        ],
        compiler_params=pltpu.CompilerParams(vmem_limit_bytes=40 * 2**20),
        name="factor",
    )(links, pivs, blocks)


def per_device(modes, counts, kappa, react):
    kappa = pltpu.with_memory_space_constraint(kappa, pltpu.HBM)
    react = pltpu.with_memory_space_constraint(react, pltpu.HBM)
    blocks, links, pivs = assemble(counts, modes, kappa, react)
    return factor(links, pivs, blocks)


def solution(mesh):
    in_specs = (
        P(None, "grp", "sub", None),
        P(("grp", "sub")),
        P("grp", "sub", None),
        P("grp", "sub", None),
    )
    out_specs = P(("grp", "sub"), None)
    return jax.shard_map(
        per_device, mesh=mesh, in_specs=in_specs, out_specs=out_specs, check_vma=False
    )
```

```python
import jax
import jax.numpy as jnp
from jax import lax
from jax.experimental import pallas as pl
from jax.experimental.pallas import tpu as pltpu
from jax.sharding import PartitionSpec as P

F32 = jnp.float32
BF16 = jnp.bfloat16
MESH = pl.DeviceIdType.MESH
NG, NU = 4, 32
CX, CY, NZ = 16, 16, 256
SLOTS, LIVE = 48, 40
NB = 22
DONE = 1024
GROUP = 24
NC = SLOTS * NG * NU


def nt(a, b, precision=None):
    return lax.dot_general(
        a, b, (((1,), (1,)), ((), ())), preferred_element_type=F32, precision=precision
    )


def lanes_of(shape):
    return lax.broadcasted_iota(jnp.int32, shape, len(shape) - 1)


def rows_of(shape):
    return lax.broadcasted_iota(jnp.int32, shape, len(shape) - 2)


def split(x):
    hi = x.astype(BF16)
    return hi, (x - hi.astype(F32)).astype(BF16)


def pad_rows(x, rows):
    return jnp.concatenate([x, jnp.zeros((rows - x.shape[0], x.shape[1]), x.dtype)], 0)


def pad_lanes(x, lanes):
    return jnp.concatenate([x, jnp.zeros((x.shape[0], lanes - x.shape[1]), x.dtype)], 1)


def transposed(x):
    return jnp.transpose(pad_rows(x, 128))


def assemble_kernel(
    count_ref, modes_ref, kappa_ref, react_ref, blocks_ref, links_ref, pivots_ref,
    raw, kappa, react, field, masked, wx, wy, wz, diag, edge, halo, face_x, face_y,
    high, low, ends, links, pivs, order,
    raw_sem, cell_sem, halo_send, halo_recv, face_send, face_recv,
    up_sem, link_send, link_recv, piv_send, piv_recv, cross_send, cross_recv,
):
    g, u = lax.axis_index("grp"), lax.axis_index("sub")
    partners = [
        (lax.rem(g + NG - 1, NG), u),
        (lax.rem(g + 1, NG), u),
        (g, lax.rem(u + NU - 1, NU)),
        (g, lax.rem(u + 1, NU)),
    ]
    inside = [g > 0, g < NG - 1, u > 0, u < NU - 1]
    mirror = [1, 0, 3, 2]
    chip, core = u // 2, lax.rem(u, 2)
    joined = (g < 2) & (u < GROUP)

    def fetch(x):
        return pltpu.make_async_copy(
            modes_ref.at[pl.ds(0, LIVE), x], raw.at[x], raw_sem.at[x]
        )

    cells = [
        pltpu.make_async_copy(kappa_ref, kappa, cell_sem.at[0]),
        pltpu.make_async_copy(react_ref, react, cell_sem.at[1]),
    ]
    fetch(0).start()
    fetch(CX - 1).start()
    cells[0].start()
    for x in range(1, CX - 1):
        fetch(x).start()
    cells[1].start()

    barrier = pltpu.get_barrier_semaphore()

    def greet(device):
        pl.semaphore_signal(barrier, inc=1, device_id=device, device_id_type=MESH)

    for partner in partners:
        greet(partner)

    def others(count, me, act):
        for step in range(1, count):
            v = me + step
            act(jnp.where(v >= count, v - count, v))

    @pl.when(joined)
    def _():
        others(GROUP // 2, chip, lambda v: greet((g, 2 * v + core)))
        greet((g, 2 * chip + 1 - core))

    count = count_ref[0]
    z_from, z_to = rows_of((NZ, NZ)), lanes_of((NZ, NZ))
    here = z_from == jnp.where(z_to < 128, 2 * z_to, 2 * z_to - 255)
    order[...] = jnp.where(here, 1.0, 0.0).astype(BF16)

    def ordered(x):
        return jnp.dot(x.reshape(-1, NZ), order[...], preferred_element_type=F32)

    live = rows_of((CY, LIVE, NZ)) < count

    def turn(x, side=None):
        plane = jnp.swapaxes(ordered(raw[x]).reshape(LIVE, CY, NZ), 0, 1)
        plane = jnp.where(live, plane, 0.0)
        field[x] = plane
        for y in range(CY):
            masked[x, :, NZ * y : NZ * (y + 1)] = pad_rows(plane[y], SLOTS).astype(BF16)
        if side is not None:
            for y in range(0, CY, 2):
                two = jnp.concatenate([plane[y], plane[y + 1]], 0)
                ends[side, :, NZ * y // 2 : NZ * (y + 2) // 2] = two.astype(BF16)

    fetch(0).wait()
    fetch(CX - 1).wait()
    turn(0, 0)
    turn(CX - 1, 1)
    cells[0].wait()
    kap = ordered(kappa[...]).reshape(CX, CY, NZ)
    edge[0] = kap[0]
    edge[1] = kap[CX - 1]
    for x in range(CX):
        edge[2, x : x + 1] = kap[x, 0:1]
        edge[3, x : x + 1] = kap[x, CY - 1 : CY]
    pl.semaphore_wait(barrier, jnp.where(joined, GROUP // 2 + 4, 4))

    def halo_copy(k):
        return pltpu.make_async_remote_copy(
            src_ref=edge.at[k], dst_ref=halo.at[mirror[k]],
            send_sem=halo_send.at[k], recv_sem=halo_recv.at[mirror[k]],
            device_id=partners[k], device_id_type=MESH,
        )

    sources = [
        ends.at[0],
        ends.at[1],
        masked.at[:, :, pl.ds(0, NZ)],
        masked.at[:, :, pl.ds((CY - 1) * NZ, NZ)],
    ]
    landings = [face_x.at[0], face_x.at[1], face_y.at[0], face_y.at[1]]

    def face_copy(k):
        return pltpu.make_async_remote_copy(
            src_ref=sources[k], dst_ref=landings[mirror[k]],
            send_sem=face_send.at[k], recv_sem=face_recv.at[mirror[k]],
            device_id=partners[k], device_id_type=MESH,
        )

    for k in range(4):
        halo_copy(k).start()
    face_copy(0).start()
    face_copy(1).start()

    def turn_next(i, carry):
        fetch(2 * i + 1).wait()
        fetch(2 * i + 2).wait()
        turn(2 * i + 1)
        turn(2 * i + 2)
        return carry

    lax.fori_loop(0, CX // 2 - 1, turn_next, 0)
    face_copy(2).start()
    face_copy(3).start()

    plane0 = jnp.zeros((CY, NZ), F32)
    row0 = jnp.zeros((1, NZ), F32)
    half = lanes_of((CY, 128))
    wx[0] = plane0
    wx[CX] = plane0
    for x in range(CX - 1):
        wx[x + 1] = 0.5 * (kap[x] + kap[x + 1])
    for x in range(CX):
        k = kap[x]
        wy[x, 0:1] = row0
        wy[x, 1:CY] = 0.5 * (k[: CY - 1] + k[1:])
        wy[x, CY : CY + 1] = row0
        even, uneven = k[:, :128], k[:, 128:]
        wz[x, :, 0:128] = 0.5 * (even + uneven)
        wz[x, :, 128:] = jnp.where(half == 127, 0.0, 0.5 * (uneven + pltpu.roll(even, 127, 1)))
    cells[1].wait()
    reac = ordered(react[...]).reshape(CX, CY, NZ)
    for k in range(4):
        halo_copy(k).wait_recv()
    ext = [jnp.where(inside[k], halo[k], 0.0) for k in range(4)]
    bound = [0.5 * (edge[k] + ext[k]) for k in range(4)]
    for x in range(CX):
        k = kap[x]
        inner, outer = wz[x, :, 0:128], wz[x, :, 128:]
        below = jnp.where(half == 0, 0.5 * k[:, :128], pltpu.roll(outer, 1, 1))
        above = jnp.where(half == 127, 0.5 * k[:, 128:], outer)
        dz = jnp.concatenate([below + inner, inner + above], 1)
        dx = (bound[0] if x == 0 else wx[x]) + (bound[1] if x == CX - 1 else wx[x + 1])
        dy = wy[x, 0:CY] + wy[x, 1 : CY + 1]
        dy = dy + jnp.concatenate(
            [bound[2][x : x + 1], jnp.zeros((CY - 2, NZ), F32), bound[3][x : x + 1]], 0
        )
        diag[x] = reac[x] + dx + dy + dz

    def apply(x, gram):
        before, after = jnp.maximum(x - 1, 0), jnp.minimum(x + 1, CX - 1)
        behind, v = None, field[x, 0]
        for y in range(CY):
            ahead = field[x, y + 1] if y < CY - 1 else None
            out = diag[x, y : y + 1] * v
            out = out - wx[x, y : y + 1] * field[before, y]
            out = out - wx[x + 1, y : y + 1] * field[after, y]
            if y > 0:
                out = out - wy[x, y : y + 1] * behind
            if y < CY - 1:
                out = out - wy[x, y + 1 : y + 2] * ahead
            even, uneven = v[:, :128], v[:, 128:]
            inner, outer = wz[x, y : y + 1, 0:128], wz[x, y : y + 1, 128:]
            out = out - jnp.concatenate(
                [
                    inner * uneven + pltpu.roll(outer * uneven, 1, 1),
                    inner * even + outer * pltpu.roll(even, 127, 1),
                ],
                1,
            )
            local = pad_rows(out, SLOTS).astype(BF16)
            gram = gram + nt(masked[x, :, NZ * y : NZ * (y + 1)], local)
            behind, v = v, ahead
        return gram

    gram = lax.fori_loop(
        0, CX // 2, lambda i, gram: apply(2 * i + 1, apply(2 * i, gram)),
        jnp.zeros((SLOTS, SLOTS), F32),
    )
    own = pad_lanes(gram, 128)
    spot, slot = lanes_of((SLOTS, 128)), rows_of((SLOTS, 128))
    own = own + jnp.where((spot == slot) & (slot >= count), 1.0, 0.0)
    sym = jnp.where(spot < LIVE, 0.5 * (own + transposed(own)[:SLOTS]), 0.0)

    on_diag = jnp.where((spot == slot) & (spot < LIVE), sym, 0.0)
    scale_lane = lax.rsqrt(jnp.sum(on_diag, axis=0, keepdims=True))
    scale_lane = jnp.where(lanes_of((1, 128)) < LIVE, scale_lane, 1.0)
    scale_row = lax.rsqrt(jnp.sum(on_diag, axis=1, keepdims=True)[:LIVE])

    def up_copy(ref, i):
        return pltpu.make_async_remote_copy(
            src_ref=ref, dst_ref=ref, send_sem=up_sem.at[i], recv_sem=up_sem.at[i + 2],
            device_id=(1, u), device_id_type=MESH,
        )

    def link_copy(to, owner):
        return pltpu.make_async_remote_copy(
            src_ref=links.at[owner, core], dst_ref=links.at[owner, core],
            send_sem=link_send.at[to], recv_sem=link_recv.at[owner],
            device_id=(g, 2 * to + core), device_id_type=MESH,
        )

    def piv_copy(to, owner):
        return pltpu.make_async_remote_copy(
            src_ref=pivs.at[owner, core], dst_ref=pivs.at[owner, core],
            send_sem=piv_send.at[to], recv_sem=piv_recv.at[owner],
            device_id=(g, 2 * to + core), device_id_type=MESH,
        )

    def cross_copy(ref, sem):
        return pltpu.make_async_remote_copy(
            src_ref=ref, dst_ref=ref, send_sem=cross_send.at[sem], recv_sem=cross_recv.at[sem],
            device_id=(g, 2 * chip + 1 - core), device_id_type=MESH,
        )

    def cross_link(v, c):
        return cross_copy(links.at[v, c], v)

    def cross_pivs(c):
        return cross_copy(pivs.at[:, c], GROUP // 2)

    link_up, piv_up = up_copy(links.at[chip, core], 0), up_copy(pivs.at[chip, core], 1)

    @pl.when(joined & (g == 0))
    def _():
        unit = sym[:LIVE] * scale_row * scale_lane
        packed = unit[0:16] + pltpu.roll(unit[16:32], LIVE, 1)
        packed = packed + pltpu.roll(pad_rows(unit[32:40], 16), 2 * LIVE, 1)
        shifted = pltpu.roll(jnp.broadcast_to(scale_lane, (16, 128)), 2 * LIVE, 1)
        wide_lane = lanes_of((16, 128))
        spare = (rows_of((16, 128)) == 8) & (wide_lane >= 2 * LIVE) & (wide_lane < 3 * LIVE)
        pivs[chip, core] = jnp.where(spare, shifted, packed)
        piv_up.start()
        others(GROUP // 2, chip, lambda v: piv_copy(v, chip).start())

    def coupling(k):
        weight = bound[k]
        total = jnp.zeros((SLOTS, SLOTS), F32)
        if k < 2:
            x = 0 if k == 0 else CX - 1
            for y in range(0, CY, 2):
                two = [field[x, j] * weight[j : j + 1] for j in (y, y + 1)]
                hi, lo = split(jnp.concatenate(two, 0))
                cols = slice(NZ * y // 2, NZ * (y + 2) // 2)
                high[:, cols], low[:, cols] = hi, lo
            face_copy(mirror[k]).wait_recv()
            both = nt(high[...], face_x[k]) + nt(low[...], face_x[k])
            both = pad_lanes(both, 128)
            block = both[:LIVE] + pltpu.roll(both[LIVE:], 128 - LIVE, 1)
            block = jnp.where(lanes_of((LIVE, 128)) < LIVE, block, 0.0)
        else:
            face_copy(mirror[k]).wait_recv()
            for x in range(CX):
                mine = field[x, 0 if k == 2 else CY - 1] * weight[x : x + 1]
                hi, lo = split(pad_rows(mine, SLOTS))
                other = face_y[k - 2, x]
                total = total + (nt(hi, other) + nt(lo, other))
            block = pad_lanes(total, 128)[:LIVE]
        return jnp.where(inside[k], -block, 0.0)

    found = {k: coupling(k) for k in (1, 3)}
    lane = lanes_of((LIVE, 128))
    odd = core == 1
    ahead = found[3] * scale_row
    ahead_t = transposed(found[3])[:LIVE] * scale_lane
    rising = transposed(found[1])[:LIVE] * scale_lane
    message = jnp.where(odd, ahead, ahead_t) + pltpu.roll(jnp.where(odd, ahead_t, ahead), LIVE, 1)
    message = message + pltpu.roll(rising, 2 * LIVE, 1)
    message = jnp.where(lane >= 3 * LIVE, count.astype(F32), message)
    message = jnp.where(lane == 3 * LIVE + 1, scale_row, message)

    @pl.when(joined & (g == 0))
    def _():
        links[chip, core] = message
        link_up.start()
        others(GROUP // 2, chip, lambda v: link_copy(v, chip).start())

    @pl.when(joined & (g == 1))
    def _():
        piv_up.wait_recv()
        others(GROUP // 2, chip, lambda v: piv_copy(v, chip).start())
        link_up.wait_recv()
        others(GROUP // 2, chip, lambda v: link_copy(v, chip).start())

    for k in (0, 2):
        found[k] = coupling(k)
    blocks_ref[0] = own
    for k in range(4):
        blocks_ref[k + 1] = pad_rows(found[k], SLOTS)
    blocks_ref[5] = sym

    @pl.when(joined)
    def _():
        others(GROUP // 2, chip, lambda v: piv_copy(chip, v).wait_recv())
        cross_pivs(core).start()
        cross_link(chip, core).start()

        def forward(v):
            link_copy(chip, v).wait_recv()
            cross_link(v, core).start()

        others(GROUP // 2, chip, forward)
        cross_pivs(1 - core).wait_recv()
        for v in range(GROUP // 2):
            cross_link(v, 1 - core).wait_recv()
        for v in range(GROUP):
            links_ref[v] = links[v // 2, v % 2]
            pivots_ref[v] = pivs[v // 2, v % 2]
        others(GROUP // 2, chip, lambda v: link_copy(v, chip).wait_send())
        others(GROUP // 2, chip, lambda v: piv_copy(v, chip).wait_send())
        cross_pivs(core).wait_send()
        for v in range(GROUP // 2):
            cross_link(v, core).wait_send()

    @pl.when(joined & (g == 0))
    def _():
        link_up.wait_send()
        piv_up.wait_send()

    for k in range(4):
        halo_copy(k).wait_send()
        face_copy(k).wait_send()


def assemble(count, modes, kappa, react):
    vmem = pl.BlockSpec(memory_space=pltpu.VMEM)
    hbm = pl.BlockSpec(memory_space=pltpu.HBM)
    dma = pltpu.SemaphoreType.DMA
    return pl.pallas_call(
        assemble_kernel,
        out_shape=(
            jax.ShapeDtypeStruct((6, SLOTS, 128), F32),
            jax.ShapeDtypeStruct((GROUP, LIVE, 128), F32),
            jax.ShapeDtypeStruct((GROUP, 16, 128), F32),
        ),
        in_specs=[pl.BlockSpec(memory_space=pltpu.SMEM), hbm, hbm, hbm],
        out_specs=(vmem, vmem, vmem),
        scratch_shapes=[
            pltpu.VMEM((CX, LIVE, CY, NZ), BF16),
            pltpu.VMEM((CX, CY, NZ), BF16),
            pltpu.VMEM((CX, CY, NZ), BF16),
            pltpu.VMEM((CX, CY, LIVE, NZ), F32),
            pltpu.VMEM((CX, SLOTS, CY * NZ), BF16),
            pltpu.VMEM((CX + 1, CY, NZ), F32),
            pltpu.VMEM((CX, 24, NZ), F32),
            pltpu.VMEM((CX, CY, NZ), F32),
            pltpu.VMEM((CX, CY, NZ), F32),
            pltpu.VMEM((4, 16, NZ), F32),
            pltpu.VMEM((4, 16, NZ), F32),
            pltpu.VMEM((2, 2 * LIVE, 8 * NZ), BF16),
            pltpu.VMEM((2, 16, SLOTS, NZ), BF16),
            pltpu.VMEM((2 * LIVE, 8 * NZ), BF16),
            pltpu.VMEM((2 * LIVE, 8 * NZ), BF16),
            pltpu.VMEM((2, 2 * LIVE, 8 * NZ), BF16),
            pltpu.VMEM((GROUP // 2, 2, LIVE, 128), F32),
            pltpu.VMEM((GROUP // 2, 2, 16, 128), F32),
            pltpu.VMEM((NZ, NZ), BF16),
            dma((CX,)),
            dma((2,)),
            dma((4,)),
            dma((4,)),
            dma((4,)),
            dma((4,)),
            dma((4,)),
            dma((GROUP // 2,)),
            dma((GROUP // 2,)),
            dma((GROUP // 2,)),
            dma((GROUP // 2,)),
            dma((GROUP // 2 + 1,)),
            dma((GROUP // 2 + 1,)),
        ],
        compiler_params=pltpu.CompilerParams(
            collective_id=0, has_side_effects=True, vmem_limit_bytes=50 * 2**20
        ),
        name="assemble",
    )(count, modes, kappa, react)


def halves(x, rows, axis):
    hi, lo = split(pad_rows(x, rows) if x.shape[0] < rows else x)
    return jnp.concatenate([hi, lo], axis)


def joined_halves(out, rows):
    tall = out.shape[0] // 2
    return out[:rows, :128] + (out[:rows, 128:] + out[tall : tall + rows, :128])


def nn3(a, b):
    left = halves(a, SLOTS, 0)
    out = jnp.dot(left, halves(b, 128, 1), preferred_element_type=F32)
    return joined_halves(out, a.shape[0])


def nt3(a, b):
    out = nt(halves(a, SLOTS, 0), halves(b, 128, 0))
    return joined_halves(out, a.shape[0])


def wide(x):
    return jnp.broadcast_to(x, (8, 128))


def pivots(p, soff, state, spread_ref, rows_ref, side_ref):
    tiles, saved = (list(part) for part in state)
    sub = rows_of((8, 128))
    at = soff + 8 * p
    column = lambda v, c: wide(tiles[v][:, c : c + 1])
    if p == 0:
        for c in range(8):
            spread_ref[p, c] = column(p, at + c)
    rows_ref[p] = tiles[p]
    d = {(i, j): wide(spread_ref[p, j, i : i + 1]) for i in range(8) for j in range(i, 8)}
    rows = [wide(rows_ref[p, c : c + 1]) for c in range(8)]
    follow = p + 1 < LIVE // 8
    if follow:
        under = [column(p + 1, at + c) for c in range(8)]
        coming = [column(p + 1, at + 8 + c) for c in range(8)]
    others = [v for v in range(LIVE // 8) if v not in (p, p + 1)]
    factors = {v: [column(v, at + c) for c in range(8)] for v in others}
    alpha, beta, z = {}, {}, list(rows)
    for c in range(0, 8, 2):
        n = c + 1
        a, b, e = d[c, c], d[c, n], d[n, n]
        det = a * e - b * b
        r = pl.reciprocal(det, approx=True)
        for i in range(n + 1, 8):
            top, bottom = e * d[c, i] - b * d[n, i], a * d[n, i] - b * d[c, i]
            alpha[c, i], beta[c, i] = top * r, bottom * r
            for j in range(i, 8):
                if j <= n + 2:
                    d[i, j] = d[i, j] - (top * d[c, j] + bottom * d[n, j]) * r
                else:
                    d[i, j] = d[i, j] - (alpha[c, i] * d[c, j] + beta[c, i] * d[n, j])
        root = lax.rsqrt(a)
        saved[p] = jnp.where(sub == c, rows[c] * root, saved[p])
        second = (rows[n] - (b * root * root) * rows[c]) * (lax.rsqrt(det) * (a * root))
        saved[p] = jnp.where(sub == n, second, saved[p])
        for i in range(n + 1, 8):
            rows[i] = rows[i] - (alpha[c, i] * rows[c] + beta[c, i] * rows[n])
        z[c] = (e * rows[c] - b * rows[n]) * r
        z[n] = (a * rows[n] - b * rows[c]) * r
        if follow:
            first = (e * under[c] - b * under[n]) * r
            other = (a * under[n] - b * under[c]) * r
            side_ref[p, c], side_ref[p, n] = first, other
            for i in range(n + 1, 8):
                under[i] = under[i] - (alpha[c, i] * under[c] + beta[c, i] * under[n])
            for i in range(8):
                coming[i] = coming[i] - (
                    under[c] * wide(side_ref[p, c, i : i + 1])
                    + under[n] * wide(side_ref[p, n, i : i + 1])
                )
            tiles[p + 1] = tiles[p + 1] - (first * rows[c] + other * rows[n])
    if follow:
        for c in range(8):
            spread_ref[p + 1, c] = coming[c]
    for c in range(4, -1, -2):
        for i in range(c + 2, 8):
            z[c] = z[c] - alpha[c, i] * z[i]
            z[c + 1] = z[c + 1] - beta[c, i] * z[i]
    for v in others:
        terms = [factors[v][c] * z[c] for c in range(8)]
        while len(terms) > 1:
            terms = [terms[i] + terms[i + 1] for i in range(0, len(terms), 2)]
        tiles[v] = tiles[v] - terms[0]
    for c in range(8):
        tiles[p] = jnp.where(sub == c, z[c], tiles[p])
    return tuple(tiles), tuple(saved)


def place(out_ref, block, pos, keep):
    base = jnp.minimum((pos // 128) * 128, NC - 256)
    base = pl.multiple_of(base, 128)
    shifted = pltpu.roll(pad_lanes(block, 256), pos - base, 1)
    cols = lanes_of((SLOTS, 256)) + base
    out_ref[:, pl.ds(base, 256)] += jnp.where(keep(cols), shifted, 0.0)


def factor_kernel(
    links_ref, pivots_ref, blocks_ref, out_ref, linv_ref, k_ref, g_ref, f_ref, x_ref, spread_ref, rows_ref, side_ref,
):
    g, u = lax.axis_index("grp"), lax.axis_index("sub")
    s = g * NU + u
    upper = s <= 21
    member = (s == 21) | (s == 22) | ((s >= NU) & (s < NU + NB))
    lane = lanes_of((LIVE, 128))
    row = rows_of((LIVE, 128))
    lane48 = lanes_of((SLOTS, 128))
    row48 = rows_of((SLOTS, 128))
    out_ref[...] = jnp.zeros_like(out_ref)
    before = lambda cols: cols < DONE
    after = lambda cols: cols >= DONE

    def left(x, by):
        x = pltpu.roll(x, 128 - by, 1) if by else x
        return jnp.where(lanes_of(x.shape) < LIVE, x, 0.0)

    def put(block, pos, late):
        base = pos // 128 * 128
        shifted = pltpu.roll(pad_lanes(block, 256), pos - base, 1) if pos > base else (
            pad_lanes(block, 256)
        )
        if base < DONE < base + 256:
            cols = lanes_of((SLOTS, 256)) + base
            shifted = jnp.where(cols >= DONE if late else cols < DONE, shifted, 0.0)
        out_ref[:, base : base + 256] += shifted

    def reduce_row(q):
        at, wide_enough = jnp.maximum(q, 0), jnp.where(q == NB - 1, 16, LIVE)
        mine = jnp.where(q == s, blocks_ref[5], 0.0)
        mine = jnp.where(q == s - 1, blocks_ref[3], mine)
        mine = jnp.where(q == s - NU, blocks_ref[1], mine)
        mine = mine * scale(at, 0)
        held = jnp.where(q > 0, f_ref[jnp.maximum(q - 1, 0)], 0.0)
        f = mine - nn3(held, pad_rows(k_ref[at], 128))
        f_ref[at] = jnp.where((q <= s) & (lane48 < wide_enough), f, 0.0)

    def solve_row(q):
        at = jnp.maximum(q, 0)
        x = nt3(f_ref[at], pad_rows(linv_ref[at], 128))
        x_ref[at] = jnp.where((q == s) & (lane48 > row48), 0.0, x)

    def double_row(q):
        at = jnp.maximum(q, 0)
        x = x_ref[at]
        g_ref[at] = nn3(x, pad_rows(linv_ref[at], 128))

    def pivot_block(t, at):
        packed = pivots_ref[t]
        parts = []
        for i in range(3):
            by = (at - LIVE * i) % 128
            parts.append(pltpu.roll(packed, by, 1) if by else packed)
        block = jnp.concatenate([parts[0], parts[1], parts[2][:8]], 0)
        return jnp.where((lane >= at) & (lane < at + LIVE), block, 0.0)

    def scale(t, at):
        spare = pltpu.roll(pivots_ref[t, 8:16, :], (at - 2 * LIVE) % 128, 1)[0:1]
        lanes = lanes_of((1, 128))
        return jnp.where((lanes >= at) & (lanes < at + LIVE), spare, 1.0)

    def live_count(t):
        return jnp.max(jnp.where(lanes_of((8, 128)) == 3 * LIVE, links_ref[t][0:8], 0.0))

    def at_rows(x, start):
        above = jnp.zeros((start, 128), F32)
        return pad_rows(jnp.concatenate([above, x], 0) if start else x, 128)

    def step(t, odd, scur, n):
        soff, uoff = (LIVE, 0) if odd else (0, LIVE)
        following = jnp.minimum(t + 1, NB - 1)
        given = links_ref[t] * scale(following, uoff)
        limit = jnp.where(t == NB - 1, 16, LIVE)
        in_s = (lane >= soff) & (lane < soff + LIVE)
        in_u = (lane >= uoff) & (lane < uoff + LIVE)
        eye = jnp.where(lane == row + soff, 1.0, 0.0)
        a = jnp.where((row < limit) & (lane < soff + limit), scur, eye)
        rest = jnp.where(lane == row + 2 * LIVE, 1.0, 0.0)
        rest = jnp.where(in_u, jnp.where(row < limit, given, 0.0), rest)
        a = jnp.where(in_s, a, rest)
        ut = jnp.where(in_s, given, 0.0) * links_ref[following, :, 3 * LIVE + 1 : 3 * LIVE + 2]
        tiles = tuple(a[8 * v : 8 * v + 8] for v in range(LIVE // 8))
        state = pivots(0, soff, (tiles, tiles), spread_ref, rows_ref, side_ref)
        reduce_row(t - 1)

        coming, coming_n = pivot_block(following, uoff), live_count(following)
        n = jnp.where(t == NB - 1, jnp.minimum(n, 16.0), n)
        for p in range(1, LIVE // 8):
            state = lax.cond(
                n > 8.0 * p,
                lambda st, p=p: pivots(p, soff, st, spread_ref, rows_ref, side_ref),
                lambda st: st,
                state,
            )
        tiles, saved = state
        k = jnp.concatenate(tiles, 0)
        snext = coming - nn3(ut, at_rows(k, soff))
        linv_ref[t] = left(jnp.concatenate(saved, 0), 2 * LIVE)
        k_ref[t + 1] = left(k, uoff)
        return snext, coming_n

    @pl.when(upper | member)
    def _():
        k_ref[0] = jnp.zeros((LIVE, 128), F32)
        linv_ref[0] = jnp.zeros((LIVE, 128), F32)
        f_ref[0] = jnp.zeros((SLOTS, 128), F32)
        x_ref[0] = jnp.zeros((SLOTS, 128), F32)
        def pair(i, carry):
            carry = step(2 * i, False, *carry)
            return step(2 * i + 1, True, *carry)

        lax.fori_loop(0, NB // 2, pair, (pivot_block(0, 0), live_count(0)))
        reduce_row(NB - 1)
        for t in range(NB):
            solve_row(t)
        for t in range(NB):
            double_row(t)
        for t in range(NB):
            put(x_ref[t], SLOTS * t, False)

    @pl.when(upper)
    def _():
        dead = jnp.where((row48 == lane48) & (row48 >= LIVE), 1.0, 0.0)
        place(out_ref, dead, SLOTS * s, before)

    @pl.when(member)
    def _():
        late = lane >= 16
        last = jnp.where(row < 16, links_ref[NB - 1], 0.0)
        own = jnp.where(late & (row < 16), pivot_block(NB - 1, 0) / scale(NB - 1, 0), 0.0)
        over = jnp.where(late, left(links_ref[NB - 2], LIVE), 0.0)
        y = None
        for t in range(NB - 1, -1, -1):
            if y is None:
                y = g_ref[t]
                put(-nn3(y, pad_rows(left(last, 0), 128)), SLOTS * NB, True)
                put(-nn3(y, pad_rows(own, 128)), SLOTS * (NB - 1), True)
            else:
                y = g_ref[t] - nt3(y, pad_rows(k_ref[t + 1], 128))
            if t == NB - 2:
                put(-nn3(y, pad_rows(over, 128)), SLOTS * (NB - 1), True)
            rising = pad_rows(left(links_ref[t], 2 * LIVE), 128)
            put(-nt3(y, rising), SLOTS * (t + NU), True)

    @pl.when(s >= 21)
    def _():
        targets = [s, s - NU, s + NU, s - 1, s + 1]
        valid = [True, g > 0, g < NG - 1, u > 0, u < NU - 1]
        for k in range(5):
            pos = SLOTS * jnp.clip(targets[k], 0, NG * NU - 1)
            place(out_ref, jnp.where(valid[k], blocks_ref[k], 0.0), pos, after)

    @pl.when(s == 21)
    def _():
        out_ref[0:16, DONE:] = jnp.zeros((16, NC - DONE), F32)


def factor(links, pivs, blocks):
    vmem = pl.BlockSpec(memory_space=pltpu.VMEM)
    return pl.pallas_call(
        factor_kernel,
        out_shape=jax.ShapeDtypeStruct((SLOTS, NC), F32),
        in_specs=[vmem, vmem, vmem],
        out_specs=vmem,
        scratch_shapes=[
            pltpu.VMEM((NB, LIVE, 128), F32),
            pltpu.VMEM((NB + 1, LIVE, 128), F32),
            pltpu.VMEM((NB, SLOTS, 128), F32),
            pltpu.VMEM((NB, SLOTS, 128), F32),
            pltpu.VMEM((NB, SLOTS, 128), F32),
            pltpu.VMEM((LIVE // 8, 8, 8, 128), F32),
            pltpu.VMEM((LIVE // 8, 8, 128), F32),
            pltpu.VMEM((LIVE // 8, 8, 8, 128), F32),
        ],
        compiler_params=pltpu.CompilerParams(vmem_limit_bytes=40 * 2**20),
        name="factor",
    )(links, pivs, blocks)


def per_device(modes, counts, kappa, react):
    kappa = pltpu.with_memory_space_constraint(kappa, pltpu.HBM)
    react = pltpu.with_memory_space_constraint(react, pltpu.HBM)
    blocks, links, pivs = assemble(counts, modes, kappa, react)
    return factor(links, pivs, blocks)


def solution(mesh):
    in_specs = (
        P(None, "grp", "sub", None),
        P(("grp", "sub")),
        P("grp", "sub", None),
        P("grp", "sub", None),
    )
    out_specs = P(("grp", "sub"), None)
    return jax.shard_map(
        per_device, mesh=mesh, in_specs=in_specs, out_specs=out_specs, check_vma=False
    )
```

```python
import jax
import jax.numpy as jnp
from jax import lax
from jax.experimental import pallas as pl
from jax.experimental.pallas import tpu as pltpu
from jax.sharding import PartitionSpec as P

F32 = jnp.float32
BF16 = jnp.bfloat16
MESH = pl.DeviceIdType.MESH
NG, NU = 4, 32
CX, CY, NZ = 16, 16, 256
SLOTS, LIVE = 48, 40
NB = 22
DONE = 1024
GROUP = 24
NC = SLOTS * NG * NU


def nt(a, b, precision=None):
    return lax.dot_general(
        a, b, (((1,), (1,)), ((), ())), preferred_element_type=F32, precision=precision
    )


def lanes_of(shape):
    return lax.broadcasted_iota(jnp.int32, shape, len(shape) - 1)


def rows_of(shape):
    return lax.broadcasted_iota(jnp.int32, shape, len(shape) - 2)


def split(x):
    hi = x.astype(BF16)
    return hi, (x - hi.astype(F32)).astype(BF16)


def pad_rows(x, rows):
    return jnp.concatenate([x, jnp.zeros((rows - x.shape[0], x.shape[1]), x.dtype)], 0)


def pad_lanes(x, lanes):
    return jnp.concatenate([x, jnp.zeros((x.shape[0], lanes - x.shape[1]), x.dtype)], 1)


def transposed(x):
    return jnp.transpose(pad_rows(x, 128))


def assemble_kernel(
    count_ref, modes_ref, kappa_ref, react_ref, blocks_ref, links_ref, pivots_ref,
    raw, kappa, react, field, masked, wx, wy, wz, diag, edge, halo, face_x, face_y,
    high, low, ends, links, pivs, order,
    raw_sem, cell_sem, halo_send, halo_recv, face_send, face_recv,
    up_sem, link_send, link_recv, piv_send, piv_recv, cross_send, cross_recv,
):
    g, u = lax.axis_index("grp"), lax.axis_index("sub")
    partners = [
        (lax.rem(g + NG - 1, NG), u),
        (lax.rem(g + 1, NG), u),
        (g, lax.rem(u + NU - 1, NU)),
        (g, lax.rem(u + 1, NU)),
    ]
    inside = [g > 0, g < NG - 1, u > 0, u < NU - 1]
    mirror = [1, 0, 3, 2]
    chip, core = u // 2, lax.rem(u, 2)
    joined = (g < 2) & (u < GROUP)

    def fetch(x):
        return pltpu.make_async_copy(
            modes_ref.at[pl.ds(0, LIVE), x], raw.at[x], raw_sem.at[x]
        )

    cells = [
        pltpu.make_async_copy(kappa_ref, kappa, cell_sem.at[0]),
        pltpu.make_async_copy(react_ref, react, cell_sem.at[1]),
    ]
    fetch(0).start()
    fetch(CX - 1).start()
    cells[0].start()
    for x in range(1, CX - 1):
        fetch(x).start()
    cells[1].start()

    barrier = pltpu.get_barrier_semaphore()

    def greet(device):
        pl.semaphore_signal(barrier, inc=1, device_id=device, device_id_type=MESH)

    for partner in partners:
        greet(partner)

    def others(count, me, act):
        for step in range(1, count):
            v = me + step
            act(jnp.where(v >= count, v - count, v))

    @pl.when(joined)
    def _():
        others(GROUP // 2, chip, lambda v: greet((g, 2 * v + core)))
        greet((g, 2 * chip + 1 - core))

    count = count_ref[0]
    z_from, z_to = rows_of((NZ, NZ)), lanes_of((NZ, NZ))
    here = z_from == jnp.where(z_to < 128, 2 * z_to, 2 * z_to - 255)
    order[...] = jnp.where(here, 1.0, 0.0).astype(BF16)

    def ordered(x):
        return jnp.dot(x.reshape(-1, NZ), order[...], preferred_element_type=F32)

    live = rows_of((CY, LIVE, NZ)) < count

    def turn(x, side=None):
        plane = jnp.swapaxes(ordered(raw[x]).reshape(LIVE, CY, NZ), 0, 1)
        plane = jnp.where(live, plane, 0.0)
        field[x] = plane
        for y in range(CY):
            masked[x, :, NZ * y : NZ * (y + 1)] = pad_rows(plane[y], SLOTS).astype(BF16)
        if side is not None:
            for y in range(0, CY, 2):
                two = jnp.concatenate([plane[y], plane[y + 1]], 0)
                ends[side, :, NZ * y // 2 : NZ * (y + 2) // 2] = two.astype(BF16)

    fetch(0).wait()
    fetch(CX - 1).wait()
    turn(0, 0)
    turn(CX - 1, 1)
    cells[0].wait()
    kap = ordered(kappa[...]).reshape(CX, CY, NZ)
    edge[0] = kap[0]
    edge[1] = kap[CX - 1]
    for x in range(CX):
        edge[2, x : x + 1] = kap[x, 0:1]
        edge[3, x : x + 1] = kap[x, CY - 1 : CY]
    pl.semaphore_wait(barrier, jnp.where(joined, GROUP // 2 + 4, 4))

    def halo_copy(k):
        return pltpu.make_async_remote_copy(
            src_ref=edge.at[k], dst_ref=halo.at[mirror[k]],
            send_sem=halo_send.at[k], recv_sem=halo_recv.at[mirror[k]],
            device_id=partners[k], device_id_type=MESH,
        )

    sources = [
        ends.at[0],
        ends.at[1],
        masked.at[:, :, pl.ds(0, NZ)],
        masked.at[:, :, pl.ds((CY - 1) * NZ, NZ)],
    ]
    landings = [face_x.at[0], face_x.at[1], face_y.at[0], face_y.at[1]]

    def face_copy(k):
        return pltpu.make_async_remote_copy(
            src_ref=sources[k], dst_ref=landings[mirror[k]],
            send_sem=face_send.at[k], recv_sem=face_recv.at[mirror[k]],
            device_id=partners[k], device_id_type=MESH,
        )

    for k in range(4):
        halo_copy(k).start()
    face_copy(0).start()
    face_copy(1).start()

    def turn_next(i, carry):
        fetch(2 * i + 1).wait()
        fetch(2 * i + 2).wait()
        turn(2 * i + 1)
        turn(2 * i + 2)
        return carry

    lax.fori_loop(0, CX // 2 - 1, turn_next, 0)
    face_copy(2).start()
    face_copy(3).start()

    plane0 = jnp.zeros((CY, NZ), F32)
    row0 = jnp.zeros((1, NZ), F32)
    half = lanes_of((CY, 128))
    wx[0] = plane0
    wx[CX] = plane0
    for x in range(CX - 1):
        wx[x + 1] = 0.5 * (kap[x] + kap[x + 1])
    for x in range(CX):
        k = kap[x]
        wy[x, 0:1] = row0
        wy[x, 1:CY] = 0.5 * (k[: CY - 1] + k[1:])
        wy[x, CY : CY + 1] = row0
        even, uneven = k[:, :128], k[:, 128:]
        wz[x, :, 0:128] = 0.5 * (even + uneven)
        wz[x, :, 128:] = jnp.where(half == 127, 0.0, 0.5 * (uneven + pltpu.roll(even, 127, 1)))
    cells[1].wait()
    reac = ordered(react[...]).reshape(CX, CY, NZ)
    for k in range(4):
        halo_copy(k).wait_recv()
    ext = [jnp.where(inside[k], halo[k], 0.0) for k in range(4)]
    bound = [0.5 * (edge[k] + ext[k]) for k in range(4)]
    for x in range(CX):
        k = kap[x]
        inner, outer = wz[x, :, 0:128], wz[x, :, 128:]
        below = jnp.where(half == 0, 0.5 * k[:, :128], pltpu.roll(outer, 1, 1))
        above = jnp.where(half == 127, 0.5 * k[:, 128:], outer)
        dz = jnp.concatenate([below + inner, inner + above], 1)
        dx = (bound[0] if x == 0 else wx[x]) + (bound[1] if x == CX - 1 else wx[x + 1])
        dy = wy[x, 0:CY] + wy[x, 1 : CY + 1]
        dy = dy + jnp.concatenate(
            [bound[2][x : x + 1], jnp.zeros((CY - 2, NZ), F32), bound[3][x : x + 1]], 0
        )
        diag[x] = reac[x] + dx + dy + dz

    def apply(x, gram):
        before, after = jnp.maximum(x - 1, 0), jnp.minimum(x + 1, CX - 1)
        behind, v = None, field[x, 0]
        for y in range(CY):
            ahead = field[x, y + 1] if y < CY - 1 else None
            out = diag[x, y : y + 1] * v
            out = out - wx[x, y : y + 1] * field[before, y]
            out = out - wx[x + 1, y : y + 1] * field[after, y]
            if y > 0:
                out = out - wy[x, y : y + 1] * behind
            if y < CY - 1:
                out = out - wy[x, y + 1 : y + 2] * ahead
            even, uneven = v[:, :128], v[:, 128:]
            inner, outer = wz[x, y : y + 1, 0:128], wz[x, y : y + 1, 128:]
            out = out - jnp.concatenate(
                [
                    inner * uneven + pltpu.roll(outer * uneven, 1, 1),
                    inner * even + outer * pltpu.roll(even, 127, 1),
                ],
                1,
            )
            local = pad_rows(out, SLOTS).astype(BF16)
            gram = gram + nt(masked[x, :, NZ * y : NZ * (y + 1)], local)
            behind, v = v, ahead
        return gram

    gram = lax.fori_loop(
        0, CX // 2, lambda i, gram: apply(2 * i + 1, apply(2 * i, gram)),
        jnp.zeros((SLOTS, SLOTS), F32),
    )
    own = pad_lanes(gram, 128)
    spot, slot = lanes_of((SLOTS, 128)), rows_of((SLOTS, 128))
    own = own + jnp.where((spot == slot) & (slot >= count), 1.0, 0.0)
    sym = jnp.where(spot < LIVE, 0.5 * (own + transposed(own)[:SLOTS]), 0.0)

    def up_copy(ref, i):
        return pltpu.make_async_remote_copy(
            src_ref=ref, dst_ref=ref, send_sem=up_sem.at[i], recv_sem=up_sem.at[i + 2],
            device_id=(1, u), device_id_type=MESH,
        )

    def link_copy(to, owner):
        return pltpu.make_async_remote_copy(
            src_ref=links.at[owner, core], dst_ref=links.at[owner, core],
            send_sem=link_send.at[to], recv_sem=link_recv.at[owner],
            device_id=(g, 2 * to + core), device_id_type=MESH,
        )

    def piv_copy(to, owner):
        return pltpu.make_async_remote_copy(
            src_ref=pivs.at[owner, core], dst_ref=pivs.at[owner, core],
            send_sem=piv_send.at[to], recv_sem=piv_recv.at[owner],
            device_id=(g, 2 * to + core), device_id_type=MESH,
        )

    def cross_copy(ref, sem):
        return pltpu.make_async_remote_copy(
            src_ref=ref, dst_ref=ref, send_sem=cross_send.at[sem], recv_sem=cross_recv.at[sem],
            device_id=(g, 2 * chip + 1 - core), device_id_type=MESH,
        )

    def cross_link(v, c):
        return cross_copy(links.at[v, c], v)

    def cross_pivs(c):
        return cross_copy(pivs.at[:, c], GROUP // 2)

    link_up, piv_up = up_copy(links.at[chip, core], 0), up_copy(pivs.at[chip, core], 1)

    @pl.when(joined & (g == 0))
    def _():
        packed = sym[0:16] + pltpu.roll(sym[16:32], LIVE, 1)
        pivs[chip, core] = packed + pltpu.roll(pad_rows(sym[32:40], 16), 2 * LIVE, 1)
        piv_up.start()
        others(GROUP // 2, chip, lambda v: piv_copy(v, chip).start())

    def coupling(k):
        weight = bound[k]
        total = jnp.zeros((SLOTS, SLOTS), F32)
        if k < 2:
            x = 0 if k == 0 else CX - 1
            for y in range(0, CY, 2):
                two = [field[x, j] * weight[j : j + 1] for j in (y, y + 1)]
                hi, lo = split(jnp.concatenate(two, 0))
                cols = slice(NZ * y // 2, NZ * (y + 2) // 2)
                high[:, cols], low[:, cols] = hi, lo
            face_copy(mirror[k]).wait_recv()
            both = nt(high[...], face_x[k]) + nt(low[...], face_x[k])
            both = pad_lanes(both, 128)
            block = both[:LIVE] + pltpu.roll(both[LIVE:], 128 - LIVE, 1)
            block = jnp.where(lanes_of((LIVE, 128)) < LIVE, block, 0.0)
        else:
            face_copy(mirror[k]).wait_recv()
            for x in range(CX):
                mine = field[x, 0 if k == 2 else CY - 1] * weight[x : x + 1]
                hi, lo = split(pad_rows(mine, SLOTS))
                other = face_y[k - 2, x]
                total = total + (nt(hi, other) + nt(lo, other))
            block = pad_lanes(total, 128)[:LIVE]
        return jnp.where(inside[k], -block, 0.0)

    found = {k: coupling(k) for k in (1, 3)}
    lane = lanes_of((LIVE, 128))
    odd = core == 1
    ahead = found[3]
    ahead_t = transposed(ahead)[:LIVE]
    message = jnp.where(odd, ahead, ahead_t) + pltpu.roll(jnp.where(odd, ahead_t, ahead), LIVE, 1)
    message = message + pltpu.roll(transposed(found[1])[:LIVE], 2 * LIVE, 1)
    message = jnp.where(lane >= 3 * LIVE, count.astype(F32), message)

    @pl.when(joined & (g == 0))
    def _():
        links[chip, core] = message
        link_up.start()
        others(GROUP // 2, chip, lambda v: link_copy(v, chip).start())

    @pl.when(joined & (g == 1))
    def _():
        piv_up.wait_recv()
        others(GROUP // 2, chip, lambda v: piv_copy(v, chip).start())
        link_up.wait_recv()
        others(GROUP // 2, chip, lambda v: link_copy(v, chip).start())

    for k in (0, 2):
        found[k] = coupling(k)
    blocks_ref[0] = own
    for k in range(4):
        blocks_ref[k + 1] = pad_rows(found[k], SLOTS)
    blocks_ref[5] = sym

    @pl.when(joined)
    def _():
        others(GROUP // 2, chip, lambda v: piv_copy(chip, v).wait_recv())
        cross_pivs(core).start()
        cross_link(chip, core).start()

        def forward(v):
            link_copy(chip, v).wait_recv()
            cross_link(v, core).start()

        others(GROUP // 2, chip, forward)
        cross_pivs(1 - core).wait_recv()
        for v in range(GROUP // 2):
            cross_link(v, 1 - core).wait_recv()
        for v in range(GROUP):
            links_ref[v] = links[v // 2, v % 2]
            pivots_ref[v] = pivs[v // 2, v % 2]
        others(GROUP // 2, chip, lambda v: link_copy(v, chip).wait_send())
        others(GROUP // 2, chip, lambda v: piv_copy(v, chip).wait_send())
        cross_pivs(core).wait_send()
        for v in range(GROUP // 2):
            cross_link(v, core).wait_send()

    @pl.when(joined & (g == 0))
    def _():
        link_up.wait_send()
        piv_up.wait_send()

    for k in range(4):
        halo_copy(k).wait_send()
        face_copy(k).wait_send()


def assemble(count, modes, kappa, react):
    vmem = pl.BlockSpec(memory_space=pltpu.VMEM)
    hbm = pl.BlockSpec(memory_space=pltpu.HBM)
    dma = pltpu.SemaphoreType.DMA
    return pl.pallas_call(
        assemble_kernel,
        out_shape=(
            jax.ShapeDtypeStruct((6, SLOTS, 128), F32),
            jax.ShapeDtypeStruct((GROUP, LIVE, 128), F32),
            jax.ShapeDtypeStruct((GROUP, 16, 128), F32),
        ),
        in_specs=[pl.BlockSpec(memory_space=pltpu.SMEM), hbm, hbm, hbm],
        out_specs=(vmem, vmem, vmem),
        scratch_shapes=[
            pltpu.VMEM((CX, LIVE, CY, NZ), BF16),
            pltpu.VMEM((CX, CY, NZ), BF16),
            pltpu.VMEM((CX, CY, NZ), BF16),
            pltpu.VMEM((CX, CY, LIVE, NZ), F32),
            pltpu.VMEM((CX, SLOTS, CY * NZ), BF16),
            pltpu.VMEM((CX + 1, CY, NZ), F32),
            pltpu.VMEM((CX, 24, NZ), F32),
            pltpu.VMEM((CX, CY, NZ), F32),
            pltpu.VMEM((CX, CY, NZ), F32),
            pltpu.VMEM((4, 16, NZ), F32),
            pltpu.VMEM((4, 16, NZ), F32),
            pltpu.VMEM((2, 2 * LIVE, 8 * NZ), BF16),
            pltpu.VMEM((2, 16, SLOTS, NZ), BF16),
            pltpu.VMEM((2 * LIVE, 8 * NZ), BF16),
            pltpu.VMEM((2 * LIVE, 8 * NZ), BF16),
            pltpu.VMEM((2, 2 * LIVE, 8 * NZ), BF16),
            pltpu.VMEM((GROUP // 2, 2, LIVE, 128), F32),
            pltpu.VMEM((GROUP // 2, 2, 16, 128), F32),
            pltpu.VMEM((NZ, NZ), BF16),
            dma((CX,)),
            dma((2,)),
            dma((4,)),
            dma((4,)),
            dma((4,)),
            dma((4,)),
            dma((4,)),
            dma((GROUP // 2,)),
            dma((GROUP // 2,)),
            dma((GROUP // 2,)),
            dma((GROUP // 2,)),
            dma((GROUP // 2 + 1,)),
            dma((GROUP // 2 + 1,)),
        ],
        compiler_params=pltpu.CompilerParams(
            collective_id=0, has_side_effects=True, vmem_limit_bytes=50 * 2**20
        ),
        name="assemble",
    )(count, modes, kappa, react)


def halves(x, rows, axis):
    hi, lo = split(pad_rows(x, rows) if x.shape[0] < rows else x)
    return jnp.concatenate([hi, lo], axis)


def joined_halves(out, rows):
    tall = out.shape[0] // 2
    return out[:rows, :128] + (out[:rows, 128:] + out[tall : tall + rows, :128])


def nn3(a, b):
    left = halves(a, SLOTS, 0)
    out = jnp.dot(left, halves(b, 128, 1), preferred_element_type=F32)
    return joined_halves(out, a.shape[0])


def nt3(a, b):
    out = nt(halves(a, SLOTS, 0), halves(b, 128, 0))
    return joined_halves(out, a.shape[0])


def wide(x):
    return jnp.broadcast_to(x, (8, 128))


def pivots(p, soff, state, spread_ref, rows_ref, side_ref):
    tiles, saved = (list(part) for part in state)
    sub = rows_of((8, 128))
    at = soff + 8 * p
    column = lambda v, c: wide(tiles[v][:, c : c + 1])
    if p == 0:
        for c in range(8):
            spread_ref[p, c] = column(p, at + c)
    rows_ref[p] = tiles[p]
    d = {(i, j): wide(spread_ref[p, j, i : i + 1]) for i in range(8) for j in range(i, 8)}
    rows = [wide(rows_ref[p, c : c + 1]) for c in range(8)]
    follow = p + 1 < LIVE // 8
    if follow:
        under = [column(p + 1, at + c) for c in range(8)]
        coming = [column(p + 1, at + 8 + c) for c in range(8)]
    others = [v for v in range(LIVE // 8) if v not in (p, p + 1)]
    factors = {v: [column(v, at + c) for c in range(8)] for v in others}
    low, rinv = {}, []
    for c in range(8):
        rinv.append(lax.rsqrt(d[c, c]))
        for i in range(c + 1, 8):
            low[c, i] = d[c, i] * rinv[c]
        for i in range(c + 1, 8):
            for j in range(i, 8):
                d[i, j] = d[i, j] - low[c, i] * low[c, j]
        rows[c] = rows[c] * rinv[c]
        saved[p] = jnp.where(sub == c, rows[c], saved[p])
        for i in range(c + 1, 8):
            rows[i] = rows[i] - low[c, i] * rows[c]
        if follow:
            under[c] = under[c] * rinv[c]
            side_ref[p, c] = under[c]
            for i in range(c + 1, 8):
                under[i] = under[i] - low[c, i] * under[c]
            for i in range(8):
                coming[i] = coming[i] - under[c] * wide(side_ref[p, c, i : i + 1])
            tiles[p + 1] = tiles[p + 1] - under[c] * rows[c]
    if follow:
        for c in range(8):
            spread_ref[p + 1, c] = coming[c]
    z = rows
    for c in range(7, -1, -1):
        z[c] = z[c] * rinv[c]
        for i in range(c):
            z[i] = z[i] - low[i, c] * z[c]
    for v in others:
        terms = [factors[v][c] * z[c] for c in range(8)]
        while len(terms) > 1:
            terms = [terms[i] + terms[i + 1] for i in range(0, len(terms), 2)]
        tiles[v] = tiles[v] - terms[0]
    for c in range(8):
        tiles[p] = jnp.where(sub == c, z[c], tiles[p])
    return tuple(tiles), tuple(saved)


def place(out_ref, block, pos, keep):
    base = jnp.minimum((pos // 128) * 128, NC - 256)
    base = pl.multiple_of(base, 128)
    shifted = pltpu.roll(pad_lanes(block, 256), pos - base, 1)
    cols = lanes_of((SLOTS, 256)) + base
    out_ref[:, pl.ds(base, 256)] += jnp.where(keep(cols), shifted, 0.0)


def factor_kernel(
    links_ref, pivots_ref, blocks_ref, out_ref, linv_ref, k_ref, g_ref, f_ref, x_ref, spread_ref, rows_ref, side_ref,
):
    g, u = lax.axis_index("grp"), lax.axis_index("sub")
    s = g * NU + u
    upper = s <= 21
    member = (s == 21) | (s == 22) | ((s >= NU) & (s < NU + NB))
    lane = lanes_of((LIVE, 128))
    row = rows_of((LIVE, 128))
    lane48 = lanes_of((SLOTS, 128))
    row48 = rows_of((SLOTS, 128))
    out_ref[...] = jnp.zeros_like(out_ref)
    before = lambda cols: cols < DONE
    after = lambda cols: cols >= DONE

    def left(x, by):
        x = pltpu.roll(x, 128 - by, 1) if by else x
        return jnp.where(lanes_of(x.shape) < LIVE, x, 0.0)

    def put(block, pos, late):
        base = pos // 128 * 128
        shifted = pltpu.roll(pad_lanes(block, 256), pos - base, 1) if pos > base else (
            pad_lanes(block, 256)
        )
        if base < DONE < base + 256:
            cols = lanes_of((SLOTS, 256)) + base
            shifted = jnp.where(cols >= DONE if late else cols < DONE, shifted, 0.0)
        out_ref[:, base : base + 256] += shifted

    def reduce_row(q):
        at, wide_enough = jnp.maximum(q, 0), jnp.where(q == NB - 1, 16, LIVE)
        mine = jnp.where(q == s, blocks_ref[5], 0.0)
        mine = jnp.where(q == s - 1, blocks_ref[3], mine)
        mine = jnp.where(q == s - NU, blocks_ref[1], mine)
        held = jnp.where(q > 0, f_ref[jnp.maximum(q - 1, 0)], 0.0)
        f = mine - nn3(held, pad_rows(k_ref[at], 128))
        f_ref[at] = jnp.where((q <= s) & (lane48 < wide_enough), f, 0.0)

    def solve_row(q):
        at = jnp.maximum(q, 0)
        x = nt3(f_ref[at], pad_rows(linv_ref[at], 128))
        x_ref[at] = jnp.where((q == s) & (lane48 > row48), 0.0, x)

    def double_row(q):
        at = jnp.maximum(q, 0)
        x = x_ref[at]
        g_ref[at] = nn3(x, pad_rows(linv_ref[at], 128))

    def pivot_block(t, at):
        packed = pivots_ref[t]
        parts = []
        for i in range(3):
            by = (at - LIVE * i) % 128
            parts.append(pltpu.roll(packed, by, 1) if by else packed)
        block = jnp.concatenate([parts[0], parts[1], parts[2][:8]], 0)
        return jnp.where((lane >= at) & (lane < at + LIVE), block, 0.0)

    def live_count(t):
        return jnp.max(jnp.where(lanes_of((8, 128)) >= 3 * LIVE, links_ref[t][0:8], 0.0))

    def at_rows(x, start):
        above = jnp.zeros((start, 128), F32)
        return pad_rows(jnp.concatenate([above, x], 0) if start else x, 128)

    def step(t, odd, scur, n):
        soff, uoff = (LIVE, 0) if odd else (0, LIVE)
        given = links_ref[t]
        limit = jnp.where(t == NB - 1, 16, LIVE)
        in_s = (lane >= soff) & (lane < soff + LIVE)
        in_u = (lane >= uoff) & (lane < uoff + LIVE)
        eye = jnp.where(lane == row + soff, 1.0, 0.0)
        a = jnp.where((row < limit) & (lane < soff + limit), scur, eye)
        rest = jnp.where(lane == row + 2 * LIVE, 1.0, 0.0)
        rest = jnp.where(in_u, jnp.where(row < limit, given, 0.0), rest)
        a = jnp.where(in_s, a, rest)
        ut = jnp.where(in_s, given, 0.0)
        tiles = tuple(a[8 * v : 8 * v + 8] for v in range(LIVE // 8))
        state = pivots(0, soff, (tiles, tiles), spread_ref, rows_ref, side_ref)

        double_row(t - 3)
        solve_row(t - 2)
        reduce_row(t - 1)
        following = jnp.minimum(t + 1, NB - 1)
        coming, coming_n = pivot_block(following, uoff), live_count(following)
        n = jnp.where(t == NB - 1, jnp.minimum(n, 16.0), n)
        for p in range(1, LIVE // 8):
            state = lax.cond(
                n > 8.0 * p,
                lambda st, p=p: pivots(p, soff, st, spread_ref, rows_ref, side_ref),
                lambda st: st,
                state,
            )
        tiles, saved = state
        k = jnp.concatenate(tiles, 0)
        snext = coming - nn3(ut, at_rows(k, soff))
        linv_ref[t] = left(jnp.concatenate(saved, 0), 2 * LIVE)
        k_ref[t + 1] = left(k, uoff)
        return snext, coming_n

    @pl.when(upper | member)
    def _():
        k_ref[0] = jnp.zeros((LIVE, 128), F32)
        linv_ref[0] = jnp.zeros((LIVE, 128), F32)
        f_ref[0] = jnp.zeros((SLOTS, 128), F32)
        x_ref[0] = jnp.zeros((SLOTS, 128), F32)
        def pair(i, carry):
            carry = step(2 * i, False, *carry)
            return step(2 * i + 1, True, *carry)

        lax.fori_loop(0, NB // 2, pair, (pivot_block(0, 0), live_count(0)))
        double_row(NB - 3)
        solve_row(NB - 2)
        reduce_row(NB - 1)
        double_row(NB - 2)
        solve_row(NB - 1)
        double_row(NB - 1)
        for t in range(NB):
            put(x_ref[t], SLOTS * t, False)

    @pl.when(upper)
    def _():
        dead = jnp.where((row48 == lane48) & (row48 >= LIVE), 1.0, 0.0)
        place(out_ref, dead, SLOTS * s, before)

    @pl.when(member)
    def _():
        late = lane >= 16
        last = jnp.where(row < 16, links_ref[NB - 1], 0.0)
        own = jnp.where(late & (row < 16), pivot_block(NB - 1, 0), 0.0)
        over = jnp.where(late, left(links_ref[NB - 2], LIVE), 0.0)
        y = None
        for t in range(NB - 1, -1, -1):
            if y is None:
                y = g_ref[t]
                put(-nn3(y, pad_rows(left(last, 0), 128)), SLOTS * NB, True)
                put(-nn3(y, pad_rows(own, 128)), SLOTS * (NB - 1), True)
            else:
                y = g_ref[t] - nt3(y, pad_rows(k_ref[t + 1], 128))
            if t == NB - 2:
                put(-nn3(y, pad_rows(over, 128)), SLOTS * (NB - 1), True)
            rising = pad_rows(left(links_ref[t], 2 * LIVE), 128)
            put(-nt3(y, rising), SLOTS * (t + NU), True)

    @pl.when(s >= 21)
    def _():
        targets = [s, s - NU, s + NU, s - 1, s + 1]
        valid = [True, g > 0, g < NG - 1, u > 0, u < NU - 1]
        for k in range(5):
            pos = SLOTS * jnp.clip(targets[k], 0, NG * NU - 1)
            place(out_ref, jnp.where(valid[k], blocks_ref[k], 0.0), pos, after)

    @pl.when(s == 21)
    def _():
        out_ref[0:16, DONE:] = jnp.zeros((16, NC - DONE), F32)


def factor(links, pivs, blocks):
    vmem = pl.BlockSpec(memory_space=pltpu.VMEM)
    return pl.pallas_call(
        factor_kernel,
        out_shape=jax.ShapeDtypeStruct((SLOTS, NC), F32),
        in_specs=[vmem, vmem, vmem],
        out_specs=vmem,
        scratch_shapes=[
            pltpu.VMEM((NB, LIVE, 128), F32),
            pltpu.VMEM((NB + 1, LIVE, 128), F32),
            pltpu.VMEM((NB, SLOTS, 128), F32),
            pltpu.VMEM((NB, SLOTS, 128), F32),
            pltpu.VMEM((NB, SLOTS, 128), F32),
            pltpu.VMEM((LIVE // 8, 8, 8, 128), F32),
            pltpu.VMEM((LIVE // 8, 8, 128), F32),
            pltpu.VMEM((LIVE // 8, 8, 8, 128), F32),
        ],
        compiler_params=pltpu.CompilerParams(vmem_limit_bytes=40 * 2**20),
        name="factor",
    )(links, pivs, blocks)


def per_device(modes, counts, kappa, react):
    kappa = pltpu.with_memory_space_constraint(kappa, pltpu.HBM)
    react = pltpu.with_memory_space_constraint(react, pltpu.HBM)
    blocks, links, pivs = assemble(counts, modes, kappa, react)
    return factor(links, pivs, blocks)


def solution(mesh):
    in_specs = (
        P(None, "grp", "sub", None),
        P(("grp", "sub")),
        P("grp", "sub", None),
        P("grp", "sub", None),
    )
    out_specs = P(("grp", "sub"), None)
    return jax.shard_map(
        per_device, mesh=mesh, in_specs=in_specs, out_specs=out_specs, check_vma=False
    )
```

```python
import jax
import jax.numpy as jnp
from jax import lax
from jax.experimental import pallas as pl
from jax.experimental.pallas import tpu as pltpu
from jax.sharding import PartitionSpec as P

F32 = jnp.float32
BF16 = jnp.bfloat16
MESH = pl.DeviceIdType.MESH
NG, NU = 4, 32
CX, CY, NZ = 16, 16, 256
SLOTS, LIVE = 48, 40
NB = 22
DONE = 1024
GROUP = 24
NC = SLOTS * NG * NU


def nt(a, b, precision=None):
    return lax.dot_general(
        a, b, (((1,), (1,)), ((), ())), preferred_element_type=F32, precision=precision
    )


def lanes_of(shape):
    return lax.broadcasted_iota(jnp.int32, shape, len(shape) - 1)


def rows_of(shape):
    return lax.broadcasted_iota(jnp.int32, shape, len(shape) - 2)


def split(x):
    hi = x.astype(BF16)
    return hi, (x - hi.astype(F32)).astype(BF16)


def pad_rows(x, rows):
    return jnp.concatenate([x, jnp.zeros((rows - x.shape[0], x.shape[1]), x.dtype)], 0)


def pad_lanes(x, lanes):
    return jnp.concatenate([x, jnp.zeros((x.shape[0], lanes - x.shape[1]), x.dtype)], 1)


def transposed(x):
    return jnp.transpose(pad_rows(x, 128))


def assemble_kernel(
    count_ref, modes_ref, kappa_ref, react_ref, blocks_ref, links_ref, pivots_ref,
    raw, kappa, react, field, masked, wx, wy, wz, diag, edge, halo, face_x, face_y,
    high, low, ends, links, pivs, order,
    raw_sem, cell_sem, halo_send, halo_recv, face_send, face_recv,
    up_sem, link_send, link_recv, piv_send, piv_recv, cross_send, cross_recv,
):
    g, u = lax.axis_index("grp"), lax.axis_index("sub")
    partners = [
        (lax.rem(g + NG - 1, NG), u),
        (lax.rem(g + 1, NG), u),
        (g, lax.rem(u + NU - 1, NU)),
        (g, lax.rem(u + 1, NU)),
    ]
    inside = [g > 0, g < NG - 1, u > 0, u < NU - 1]
    mirror = [1, 0, 3, 2]
    chip, core = u // 2, lax.rem(u, 2)
    joined = (g < 2) & (u < GROUP)

    def fetch(x):
        return pltpu.make_async_copy(
            modes_ref.at[pl.ds(0, LIVE), x], raw.at[x], raw_sem.at[x]
        )

    cells = [
        pltpu.make_async_copy(kappa_ref, kappa, cell_sem.at[0]),
        pltpu.make_async_copy(react_ref, react, cell_sem.at[1]),
    ]
    fetch(0).start()
    fetch(CX - 1).start()
    cells[0].start()
    for x in range(1, CX - 1):
        fetch(x).start()
    cells[1].start()

    barrier = pltpu.get_barrier_semaphore()

    def greet(device):
        pl.semaphore_signal(barrier, inc=1, device_id=device, device_id_type=MESH)

    for partner in partners:
        greet(partner)

    def others(count, me, act):
        for step in range(1, count):
            v = me + step
            act(jnp.where(v >= count, v - count, v))

    @pl.when(joined)
    def _():
        others(GROUP // 2, chip, lambda v: greet((g, 2 * v + core)))
        greet((g, 2 * chip + 1 - core))

    count = count_ref[0]
    z_from, z_to = rows_of((NZ, NZ)), lanes_of((NZ, NZ))
    here = z_from == jnp.where(z_to < 128, 2 * z_to, 2 * z_to - 255)
    order[...] = jnp.where(here, 1.0, 0.0).astype(BF16)

    def ordered(x):
        return jnp.dot(x.reshape(-1, NZ), order[...], preferred_element_type=F32)

    live = rows_of((CY, LIVE, NZ)) < count

    def turn(x, side=None):
        plane = jnp.swapaxes(ordered(raw[x]).reshape(LIVE, CY, NZ), 0, 1)
        plane = jnp.where(live, plane, 0.0)
        field[x] = plane
        for y in range(CY):
            masked[x, :, NZ * y : NZ * (y + 1)] = pad_rows(plane[y], SLOTS).astype(BF16)
        if side is not None:
            for y in range(0, CY, 2):
                two = jnp.concatenate([plane[y], plane[y + 1]], 0)
                ends[side, :, NZ * y // 2 : NZ * (y + 2) // 2] = two.astype(BF16)

    fetch(0).wait()
    fetch(CX - 1).wait()
    turn(0, 0)
    turn(CX - 1, 1)
    cells[0].wait()
    kap = ordered(kappa[...]).reshape(CX, CY, NZ)
    edge[0] = kap[0]
    edge[1] = kap[CX - 1]
    for x in range(CX):
        edge[2, x : x + 1] = kap[x, 0:1]
        edge[3, x : x + 1] = kap[x, CY - 1 : CY]
    pl.semaphore_wait(barrier, jnp.where(joined, GROUP // 2 + 4, 4))

    def halo_copy(k):
        return pltpu.make_async_remote_copy(
            src_ref=edge.at[k], dst_ref=halo.at[mirror[k]],
            send_sem=halo_send.at[k], recv_sem=halo_recv.at[mirror[k]],
            device_id=partners[k], device_id_type=MESH,
        )

    sources = [
        ends.at[0],
        ends.at[1],
        masked.at[:, :, pl.ds(0, NZ)],
        masked.at[:, :, pl.ds((CY - 1) * NZ, NZ)],
    ]
    landings = [face_x.at[0], face_x.at[1], face_y.at[0], face_y.at[1]]

    def face_copy(k):
        return pltpu.make_async_remote_copy(
            src_ref=sources[k], dst_ref=landings[mirror[k]],
            send_sem=face_send.at[k], recv_sem=face_recv.at[mirror[k]],
            device_id=partners[k], device_id_type=MESH,
        )

    for k in range(4):
        halo_copy(k).start()
    face_copy(0).start()
    face_copy(1).start()

    def turn_next(i, carry):
        fetch(2 * i + 1).wait()
        fetch(2 * i + 2).wait()
        turn(2 * i + 1)
        turn(2 * i + 2)
        return carry

    lax.fori_loop(0, CX // 2 - 1, turn_next, 0)
    face_copy(2).start()
    face_copy(3).start()

    plane0 = jnp.zeros((CY, NZ), F32)
    row0 = jnp.zeros((1, NZ), F32)
    half = lanes_of((CY, 128))
    wx[0] = plane0
    wx[CX] = plane0
    for x in range(CX - 1):
        wx[x + 1] = 0.5 * (kap[x] + kap[x + 1])
    for x in range(CX):
        k = kap[x]
        wy[x, 0:1] = row0
        wy[x, 1:CY] = 0.5 * (k[: CY - 1] + k[1:])
        wy[x, CY : CY + 1] = row0
        even, uneven = k[:, :128], k[:, 128:]
        wz[x, :, 0:128] = 0.5 * (even + uneven)
        wz[x, :, 128:] = jnp.where(half == 127, 0.0, 0.5 * (uneven + pltpu.roll(even, 127, 1)))
    cells[1].wait()
    reac = ordered(react[...]).reshape(CX, CY, NZ)
    for k in range(4):
        halo_copy(k).wait_recv()
    ext = [jnp.where(inside[k], halo[k], 0.0) for k in range(4)]
    bound = [0.5 * (edge[k] + ext[k]) for k in range(4)]
    for x in range(CX):
        k = kap[x]
        inner, outer = wz[x, :, 0:128], wz[x, :, 128:]
        below = jnp.where(half == 0, 0.5 * k[:, :128], pltpu.roll(outer, 1, 1))
        above = jnp.where(half == 127, 0.5 * k[:, 128:], outer)
        dz = jnp.concatenate([below + inner, inner + above], 1)
        dx = (bound[0] if x == 0 else wx[x]) + (bound[1] if x == CX - 1 else wx[x + 1])
        dy = wy[x, 0:CY] + wy[x, 1 : CY + 1]
        dy = dy + jnp.concatenate(
            [bound[2][x : x + 1], jnp.zeros((CY - 2, NZ), F32), bound[3][x : x + 1]], 0
        )
        diag[x] = reac[x] + dx + dy + dz

    def apply(x, gram):
        before, after = jnp.maximum(x - 1, 0), jnp.minimum(x + 1, CX - 1)
        behind, v = None, field[x, 0]
        for y in range(CY):
            ahead = field[x, y + 1] if y < CY - 1 else None
            out = diag[x, y : y + 1] * v
            out = out - wx[x, y : y + 1] * field[before, y]
            out = out - wx[x + 1, y : y + 1] * field[after, y]
            if y > 0:
                out = out - wy[x, y : y + 1] * behind
            if y < CY - 1:
                out = out - wy[x, y + 1 : y + 2] * ahead
            even, uneven = v[:, :128], v[:, 128:]
            inner, outer = wz[x, y : y + 1, 0:128], wz[x, y : y + 1, 128:]
            out = out - jnp.concatenate(
                [
                    inner * uneven + pltpu.roll(outer * uneven, 1, 1),
                    inner * even + outer * pltpu.roll(even, 127, 1),
                ],
                1,
            )
            local = pad_rows(out, SLOTS).astype(BF16)
            gram = gram + nt(masked[x, :, NZ * y : NZ * (y + 1)], local)
            behind, v = v, ahead
        return gram

    gram = lax.fori_loop(
        0, CX // 2, lambda i, gram: apply(2 * i + 1, apply(2 * i, gram)),
        jnp.zeros((SLOTS, SLOTS), F32),
    )
    own = pad_lanes(gram, 128)
    spot, slot = lanes_of((SLOTS, 128)), rows_of((SLOTS, 128))
    own = own + jnp.where((spot == slot) & (slot >= count), 1.0, 0.0)
    sym = jnp.where(spot < LIVE, 0.5 * (own + transposed(own)[:SLOTS]), 0.0)

    def up_copy(ref, i):
        return pltpu.make_async_remote_copy(
            src_ref=ref, dst_ref=ref, send_sem=up_sem.at[i], recv_sem=up_sem.at[i + 2],
            device_id=(1, u), device_id_type=MESH,
        )

    def link_copy(to, owner):
        return pltpu.make_async_remote_copy(
            src_ref=links.at[owner, core], dst_ref=links.at[owner, core],
            send_sem=link_send.at[to], recv_sem=link_recv.at[owner],
            device_id=(g, 2 * to + core), device_id_type=MESH,
        )

    def piv_copy(to, owner):
        return pltpu.make_async_remote_copy(
            src_ref=pivs.at[owner, core], dst_ref=pivs.at[owner, core],
            send_sem=piv_send.at[to], recv_sem=piv_recv.at[owner],
            device_id=(g, 2 * to + core), device_id_type=MESH,
        )

    def cross_copy(ref, sem):
        return pltpu.make_async_remote_copy(
            src_ref=ref, dst_ref=ref, send_sem=cross_send.at[sem], recv_sem=cross_recv.at[sem],
            device_id=(g, 2 * chip + 1 - core), device_id_type=MESH,
        )

    def cross_link(v, c):
        return cross_copy(links.at[v, c], v)

    def cross_pivs(c):
        return cross_copy(pivs.at[:, c], GROUP // 2)

    link_up, piv_up = up_copy(links.at[chip, core], 0), up_copy(pivs.at[chip, core], 1)

    @pl.when(joined & (g == 0))
    def _():
        packed = sym[0:16] + pltpu.roll(sym[16:32], LIVE, 1)
        pivs[chip, core] = packed + pltpu.roll(pad_rows(sym[32:40], 16), 2 * LIVE, 1)
        piv_up.start()
        others(GROUP // 2, chip, lambda v: piv_copy(v, chip).start())

    def coupling(k):
        weight = bound[k]
        total = jnp.zeros((SLOTS, SLOTS), F32)
        if k < 2:
            x = 0 if k == 0 else CX - 1
            for y in range(0, CY, 2):
                two = [field[x, j] * weight[j : j + 1] for j in (y, y + 1)]
                hi, lo = split(jnp.concatenate(two, 0))
                cols = slice(NZ * y // 2, NZ * (y + 2) // 2)
                high[:, cols], low[:, cols] = hi, lo
            face_copy(mirror[k]).wait_recv()
            both = nt(high[...], face_x[k]) + nt(low[...], face_x[k])
            both = pad_lanes(both, 128)
            block = both[:LIVE] + pltpu.roll(both[LIVE:], 128 - LIVE, 1)
            block = jnp.where(lanes_of((LIVE, 128)) < LIVE, block, 0.0)
        else:
            face_copy(mirror[k]).wait_recv()
            for x in range(CX):
                mine = field[x, 0 if k == 2 else CY - 1] * weight[x : x + 1]
                hi, lo = split(pad_rows(mine, SLOTS))
                other = face_y[k - 2, x]
                total = total + (nt(hi, other) + nt(lo, other))
            block = pad_lanes(total, 128)[:LIVE]
        return jnp.where(inside[k], -block, 0.0)

    found = {k: coupling(k) for k in (1, 3)}
    lane = lanes_of((LIVE, 128))
    odd = core == 1
    ahead = found[3]
    ahead_t = transposed(ahead)[:LIVE]
    message = jnp.where(odd, ahead, ahead_t) + pltpu.roll(jnp.where(odd, ahead_t, ahead), LIVE, 1)
    message = message + pltpu.roll(transposed(found[1])[:LIVE], 2 * LIVE, 1)
    message = jnp.where(lane >= 3 * LIVE, count.astype(F32), message)

    @pl.when(joined & (g == 0))
    def _():
        links[chip, core] = message
        link_up.start()
        others(GROUP // 2, chip, lambda v: link_copy(v, chip).start())

    @pl.when(joined & (g == 1))
    def _():
        piv_up.wait_recv()
        others(GROUP // 2, chip, lambda v: piv_copy(v, chip).start())
        link_up.wait_recv()
        others(GROUP // 2, chip, lambda v: link_copy(v, chip).start())

    for k in (0, 2):
        found[k] = coupling(k)
    blocks_ref[0] = own
    for k in range(4):
        blocks_ref[k + 1] = pad_rows(found[k], SLOTS)
    blocks_ref[5] = sym

    @pl.when(joined)
    def _():
        others(GROUP // 2, chip, lambda v: piv_copy(chip, v).wait_recv())
        cross_pivs(core).start()
        cross_link(chip, core).start()

        def forward(v):
            link_copy(chip, v).wait_recv()
            cross_link(v, core).start()

        others(GROUP // 2, chip, forward)
        cross_pivs(1 - core).wait_recv()
        for v in range(GROUP // 2):
            cross_link(v, 1 - core).wait_recv()
        for v in range(GROUP):
            links_ref[v] = links[v // 2, v % 2]
            pivots_ref[v] = pivs[v // 2, v % 2]
        others(GROUP // 2, chip, lambda v: link_copy(v, chip).wait_send())
        others(GROUP // 2, chip, lambda v: piv_copy(v, chip).wait_send())
        cross_pivs(core).wait_send()
        for v in range(GROUP // 2):
            cross_link(v, core).wait_send()

    @pl.when(joined & (g == 0))
    def _():
        link_up.wait_send()
        piv_up.wait_send()

    for k in range(4):
        halo_copy(k).wait_send()
        face_copy(k).wait_send()


def assemble(count, modes, kappa, react):
    vmem = pl.BlockSpec(memory_space=pltpu.VMEM)
    hbm = pl.BlockSpec(memory_space=pltpu.HBM)
    dma = pltpu.SemaphoreType.DMA
    return pl.pallas_call(
        assemble_kernel,
        out_shape=(
            jax.ShapeDtypeStruct((6, SLOTS, 128), F32),
            jax.ShapeDtypeStruct((GROUP, LIVE, 128), F32),
            jax.ShapeDtypeStruct((GROUP, 16, 128), F32),
        ),
        in_specs=[pl.BlockSpec(memory_space=pltpu.SMEM), hbm, hbm, hbm],
        out_specs=(vmem, vmem, vmem),
        scratch_shapes=[
            pltpu.VMEM((CX, LIVE, CY, NZ), BF16),
            pltpu.VMEM((CX, CY, NZ), BF16),
            pltpu.VMEM((CX, CY, NZ), BF16),
            pltpu.VMEM((CX, CY, LIVE, NZ), F32),
            pltpu.VMEM((CX, SLOTS, CY * NZ), BF16),
            pltpu.VMEM((CX + 1, CY, NZ), F32),
            pltpu.VMEM((CX, 24, NZ), F32),
            pltpu.VMEM((CX, CY, NZ), F32),
            pltpu.VMEM((CX, CY, NZ), F32),
            pltpu.VMEM((4, 16, NZ), F32),
            pltpu.VMEM((4, 16, NZ), F32),
            pltpu.VMEM((2, 2 * LIVE, 8 * NZ), BF16),
            pltpu.VMEM((2, 16, SLOTS, NZ), BF16),
            pltpu.VMEM((2 * LIVE, 8 * NZ), BF16),
            pltpu.VMEM((2 * LIVE, 8 * NZ), BF16),
            pltpu.VMEM((2, 2 * LIVE, 8 * NZ), BF16),
            pltpu.VMEM((GROUP // 2, 2, LIVE, 128), F32),
            pltpu.VMEM((GROUP // 2, 2, 16, 128), F32),
            pltpu.VMEM((NZ, NZ), BF16),
            dma((CX,)),
            dma((2,)),
            dma((4,)),
            dma((4,)),
            dma((4,)),
            dma((4,)),
            dma((4,)),
            dma((GROUP // 2,)),
            dma((GROUP // 2,)),
            dma((GROUP // 2,)),
            dma((GROUP // 2,)),
            dma((GROUP // 2 + 1,)),
            dma((GROUP // 2 + 1,)),
        ],
        compiler_params=pltpu.CompilerParams(
            collective_id=0, has_side_effects=True, vmem_limit_bytes=50 * 2**20
        ),
        name="assemble",
    )(count, modes, kappa, react)


def halves(x, rows, axis):
    hi, lo = split(pad_rows(x, rows) if x.shape[0] < rows else x)
    return jnp.concatenate([hi, lo], axis)


def joined_halves(out, rows):
    tall = out.shape[0] // 2
    return out[:rows, :128] + (out[:rows, 128:] + out[tall : tall + rows, :128])


def nn3(a, b):
    depth = b.shape[0]
    left = halves(a, SLOTS, 0)[:, :depth]
    out = jnp.dot(left, halves(b, depth, 1), preferred_element_type=F32)
    return joined_halves(out, a.shape[0])


def nt3(a, b):
    out = nt(halves(a, SLOTS, 0), halves(b, 128, 0))
    return joined_halves(out, a.shape[0])


def wide(x):
    return jnp.broadcast_to(x, (8, 128))


def pivots(p, soff, state, spread_ref, rows_ref, side_ref):
    tiles, saved = (list(part) for part in state)
    sub = rows_of((8, 128))
    at = soff + 8 * p
    column = lambda v, c: wide(tiles[v][:, c : c + 1])
    if p == 0:
        for c in range(8):
            spread_ref[p, c] = column(p, at + c)
    rows_ref[p] = tiles[p]
    d = {(i, j): wide(spread_ref[p, j, i : i + 1]) for i in range(8) for j in range(i, 8)}
    rows = [wide(rows_ref[p, c : c + 1]) for c in range(8)]
    follow = p + 1 < LIVE // 8
    if follow:
        under = [column(p + 1, at + c) for c in range(8)]
        coming = [column(p + 1, at + 8 + c) for c in range(8)]
    others = [v for v in range(LIVE // 8) if v not in (p, p + 1)]
    factors = {v: [column(v, at + c) for c in range(8)] for v in others}
    low, rinv = {}, []
    for c in range(8):
        rinv.append(lax.rsqrt(d[c, c]))
        for i in range(c + 1, 8):
            low[c, i] = d[c, i] * rinv[c]
        for i in range(c + 1, 8):
            for j in range(i, 8):
                d[i, j] = d[i, j] - low[c, i] * low[c, j]
        rows[c] = rows[c] * rinv[c]
        saved[p] = jnp.where(sub == c, rows[c], saved[p])
        for i in range(c + 1, 8):
            rows[i] = rows[i] - low[c, i] * rows[c]
        if follow:
            under[c] = under[c] * rinv[c]
            side_ref[p, c] = under[c]
            for i in range(c + 1, 8):
                under[i] = under[i] - low[c, i] * under[c]
            for i in range(8):
                coming[i] = coming[i] - under[c] * wide(side_ref[p, c, i : i + 1])
            tiles[p + 1] = tiles[p + 1] - under[c] * rows[c]
    if follow:
        for c in range(8):
            spread_ref[p + 1, c] = coming[c]
    z = rows
    for c in range(7, -1, -1):
        z[c] = z[c] * rinv[c]
        for i in range(c):
            z[i] = z[i] - low[i, c] * z[c]
    for v in others:
        terms = [factors[v][c] * z[c] for c in range(8)]
        while len(terms) > 1:
            terms = [terms[i] + terms[i + 1] for i in range(0, len(terms), 2)]
        tiles[v] = tiles[v] - terms[0]
    for c in range(8):
        tiles[p] = jnp.where(sub == c, z[c], tiles[p])
    return tuple(tiles), tuple(saved)


def place(out_ref, block, pos, keep):
    base = jnp.minimum((pos // 128) * 128, NC - 256)
    base = pl.multiple_of(base, 128)
    shifted = pltpu.roll(pad_lanes(block, 256), pos - base, 1)
    cols = lanes_of((SLOTS, 256)) + base
    out_ref[:, pl.ds(base, 256)] += jnp.where(keep(cols), shifted, 0.0)


def factor_kernel(
    links_ref, pivots_ref, blocks_ref, out_ref, linv_ref, k_ref, g_ref, f_ref, x_ref, spread_ref, rows_ref, side_ref,
):
    g, u = lax.axis_index("grp"), lax.axis_index("sub")
    s = g * NU + u
    upper = s <= 21
    member = (s == 21) | (s == 22) | ((s >= NU) & (s < NU + NB))
    lane = lanes_of((LIVE, 128))
    row = rows_of((LIVE, 128))
    lane48 = lanes_of((SLOTS, 128))
    row48 = rows_of((SLOTS, 128))
    out_ref[...] = jnp.zeros_like(out_ref)
    before = lambda cols: cols < DONE
    after = lambda cols: cols >= DONE

    def left(x, by):
        x = pltpu.roll(x, 128 - by, 1) if by else x
        return jnp.where(lanes_of(x.shape) < LIVE, x, 0.0)

    def put(block, pos, late):
        base = pos // 128 * 128
        shifted = pltpu.roll(pad_lanes(block, 256), pos - base, 1) if pos > base else (
            pad_lanes(block, 256)
        )
        if base < DONE < base + 256:
            cols = lanes_of((SLOTS, 256)) + base
            shifted = jnp.where(cols >= DONE if late else cols < DONE, shifted, 0.0)
        out_ref[:, base : base + 256] += shifted

    def reduce_row(q):
        at, wide_enough = jnp.maximum(q, 0), jnp.where(q == NB - 1, 16, LIVE)
        mine = jnp.where(q == s, blocks_ref[5], 0.0)
        mine = jnp.where(q == s - 1, blocks_ref[3], mine)
        mine = jnp.where(q == s - NU, blocks_ref[1], mine)
        held = jnp.where(q > 0, f_ref[jnp.maximum(q - 1, 0)], 0.0)
        f = mine - nn3(held, pad_rows(k_ref[at], SLOTS))
        f_ref[at] = jnp.where((q <= s) & (lane48 < wide_enough), f, 0.0)

    def solve_row(q):
        at = jnp.maximum(q, 0)
        x = nt3(f_ref[at], pad_rows(linv_ref[at], 128))
        x_ref[at] = jnp.where((q == s) & (lane48 > row48), 0.0, x)

    def double_row(q):
        at = jnp.maximum(q, 0)
        x = x_ref[at]
        g_ref[at] = nn3(x, pad_rows(linv_ref[at], SLOTS))

    def pivot_block(t, at):
        packed = pivots_ref[t]
        parts = []
        for i in range(3):
            by = (at - LIVE * i) % 128
            parts.append(pltpu.roll(packed, by, 1) if by else packed)
        block = jnp.concatenate([parts[0], parts[1], parts[2][:8]], 0)
        return jnp.where((lane >= at) & (lane < at + LIVE), block, 0.0)

    def live_count(t):
        return jnp.max(jnp.where(lanes_of((8, 128)) >= 3 * LIVE, links_ref[t][0:8], 0.0))

    def at_rows(x, start):
        above = jnp.zeros((start, 128), F32)
        return jnp.concatenate([above, x], 0) if start else pad_rows(x, SLOTS)

    def step(t, odd, scur, n):
        soff, uoff = (LIVE, 0) if odd else (0, LIVE)
        given = links_ref[t]
        limit = jnp.where(t == NB - 1, 16, LIVE)
        in_s = (lane >= soff) & (lane < soff + LIVE)
        in_u = (lane >= uoff) & (lane < uoff + LIVE)
        eye = jnp.where(lane == row + soff, 1.0, 0.0)
        a = jnp.where((row < limit) & (lane < soff + limit), scur, eye)
        rest = jnp.where(lane == row + 2 * LIVE, 1.0, 0.0)
        rest = jnp.where(in_u, jnp.where(row < limit, given, 0.0), rest)
        a = jnp.where(in_s, a, rest)
        ut = jnp.where(in_s, given, 0.0)
        tiles = tuple(a[8 * v : 8 * v + 8] for v in range(LIVE // 8))
        state = pivots(0, soff, (tiles, tiles), spread_ref, rows_ref, side_ref)

        double_row(t - 3)
        solve_row(t - 2)
        reduce_row(t - 1)
        following = jnp.minimum(t + 1, NB - 1)
        coming, coming_n = pivot_block(following, uoff), live_count(following)
        n = jnp.where(t == NB - 1, jnp.minimum(n, 16.0), n)
        for p in range(1, LIVE // 8):
            state = lax.cond(
                n > 8.0 * p,
                lambda st, p=p: pivots(p, soff, st, spread_ref, rows_ref, side_ref),
                lambda st: st,
                state,
            )
        tiles, saved = state
        k = jnp.concatenate(tiles, 0)
        snext = coming - nn3(ut, at_rows(k, soff))
        linv_ref[t] = left(jnp.concatenate(saved, 0), 2 * LIVE)
        k_ref[t + 1] = left(k, uoff)
        return snext, coming_n

    @pl.when(upper | member)
    def _():
        k_ref[0] = jnp.zeros((LIVE, 128), F32)
        linv_ref[0] = jnp.zeros((LIVE, 128), F32)
        f_ref[0] = jnp.zeros((SLOTS, 128), F32)
        x_ref[0] = jnp.zeros((SLOTS, 128), F32)
        def pair(i, carry):
            carry = step(2 * i, False, *carry)
            return step(2 * i + 1, True, *carry)

        lax.fori_loop(0, NB // 2, pair, (pivot_block(0, 0), live_count(0)))
        double_row(NB - 3)
        solve_row(NB - 2)
        reduce_row(NB - 1)
        double_row(NB - 2)
        solve_row(NB - 1)
        double_row(NB - 1)
        for t in range(NB):
            put(x_ref[t], SLOTS * t, False)

    @pl.when(upper)
    def _():
        dead = jnp.where((row48 == lane48) & (row48 >= LIVE), 1.0, 0.0)
        place(out_ref, dead, SLOTS * s, before)

    @pl.when(member)
    def _():
        late = lane >= 16
        last = jnp.where(row < 16, links_ref[NB - 1], 0.0)
        own = jnp.where(late & (row < 16), pivot_block(NB - 1, 0), 0.0)
        over = jnp.where(late, left(links_ref[NB - 2], LIVE), 0.0)
        y = None
        for t in range(NB - 1, -1, -1):
            if y is None:
                y = g_ref[t]
                put(-nn3(y, pad_rows(left(last, 0), SLOTS)), SLOTS * NB, True)
                put(-nn3(y, pad_rows(own, SLOTS)), SLOTS * (NB - 1), True)
            else:
                y = g_ref[t] - nt3(y, pad_rows(k_ref[t + 1], 128))
            if t == NB - 2:
                put(-nn3(y, pad_rows(over, SLOTS)), SLOTS * (NB - 1), True)
            rising = pad_rows(left(links_ref[t], 2 * LIVE), 128)
            put(-nt3(y, rising), SLOTS * (t + NU), True)

    @pl.when(s >= 21)
    def _():
        targets = [s, s - NU, s + NU, s - 1, s + 1]
        valid = [True, g > 0, g < NG - 1, u > 0, u < NU - 1]
        for k in range(5):
            pos = SLOTS * jnp.clip(targets[k], 0, NG * NU - 1)
            place(out_ref, jnp.where(valid[k], blocks_ref[k], 0.0), pos, after)

    @pl.when(s == 21)
    def _():
        out_ref[0:16, DONE:] = jnp.zeros((16, NC - DONE), F32)


def factor(links, pivs, blocks):
    vmem = pl.BlockSpec(memory_space=pltpu.VMEM)
    return pl.pallas_call(
        factor_kernel,
        out_shape=jax.ShapeDtypeStruct((SLOTS, NC), F32),
        in_specs=[vmem, vmem, vmem],
        out_specs=vmem,
        scratch_shapes=[
            pltpu.VMEM((NB, LIVE, 128), F32),
            pltpu.VMEM((NB + 1, LIVE, 128), F32),
            pltpu.VMEM((NB, SLOTS, 128), F32),
            pltpu.VMEM((NB, SLOTS, 128), F32),
            pltpu.VMEM((NB, SLOTS, 128), F32),
            pltpu.VMEM((LIVE // 8, 8, 8, 128), F32),
            pltpu.VMEM((LIVE // 8, 8, 128), F32),
            pltpu.VMEM((LIVE // 8, 8, 8, 128), F32),
        ],
        compiler_params=pltpu.CompilerParams(vmem_limit_bytes=40 * 2**20),
        name="factor",
    )(links, pivs, blocks)


def per_device(modes, counts, kappa, react):
    kappa = pltpu.with_memory_space_constraint(kappa, pltpu.HBM)
    react = pltpu.with_memory_space_constraint(react, pltpu.HBM)
    blocks, links, pivs = assemble(counts, modes, kappa, react)
    return factor(links, pivs, blocks)


def solution(mesh):
    in_specs = (
        P(None, "grp", "sub", None),
        P(("grp", "sub")),
        P("grp", "sub", None),
        P("grp", "sub", None),
    )
    out_specs = P(("grp", "sub"), None)
    return jax.shard_map(
        per_device, mesh=mesh, in_specs=in_specs, out_specs=out_specs, check_vma=False
    )
```

```python
import jax
import jax.numpy as jnp
from jax import lax
from jax.experimental import pallas as pl
from jax.experimental.pallas import tpu as pltpu
from jax.sharding import PartitionSpec as P

F32 = jnp.float32
BF16 = jnp.bfloat16
MESH = pl.DeviceIdType.MESH
NG, NU = 4, 32
CX, CY, NZ = 16, 16, 256
SLOTS, LIVE = 48, 40
NB = 22
DONE = 1024
GROUP = 24
NC = SLOTS * NG * NU


def nt(a, b, precision=None):
    return lax.dot_general(
        a, b, (((1,), (1,)), ((), ())), preferred_element_type=F32, precision=precision
    )


def lanes_of(shape):
    return lax.broadcasted_iota(jnp.int32, shape, len(shape) - 1)


def rows_of(shape):
    return lax.broadcasted_iota(jnp.int32, shape, len(shape) - 2)


def split(x):
    hi = x.astype(BF16)
    return hi, (x - hi.astype(F32)).astype(BF16)


def pad_rows(x, rows):
    return jnp.concatenate([x, jnp.zeros((rows - x.shape[0], x.shape[1]), x.dtype)], 0)


def pad_lanes(x, lanes):
    return jnp.concatenate([x, jnp.zeros((x.shape[0], lanes - x.shape[1]), x.dtype)], 1)


def transposed(x):
    return jnp.transpose(pad_rows(x, 128))


def assemble_kernel(
    count_ref, modes_ref, kappa_ref, react_ref, blocks_ref, links_ref, pivots_ref,
    raw, kappa, react, field, masked, wx, wy, wz, diag, edge, halo, face_x, face_y,
    high, low, ends, links, pivs, order,
    raw_sem, cell_sem, halo_send, halo_recv, face_send, face_recv,
    up_sem, link_send, link_recv, piv_send, piv_recv, cross_send, cross_recv,
):
    g, u = lax.axis_index("grp"), lax.axis_index("sub")
    partners = [
        (lax.rem(g + NG - 1, NG), u),
        (lax.rem(g + 1, NG), u),
        (g, lax.rem(u + NU - 1, NU)),
        (g, lax.rem(u + 1, NU)),
    ]
    inside = [g > 0, g < NG - 1, u > 0, u < NU - 1]
    mirror = [1, 0, 3, 2]
    chip, core = u // 2, lax.rem(u, 2)
    joined = (g < 2) & (u < GROUP)

    def fetch(x):
        return pltpu.make_async_copy(
            modes_ref.at[pl.ds(0, LIVE), x], raw.at[x], raw_sem.at[x]
        )

    cells = [
        pltpu.make_async_copy(kappa_ref, kappa, cell_sem.at[0]),
        pltpu.make_async_copy(react_ref, react, cell_sem.at[1]),
    ]
    fetch(0).start()
    fetch(CX - 1).start()
    cells[0].start()
    for x in range(1, CX - 1):
        fetch(x).start()
    cells[1].start()

    barrier = pltpu.get_barrier_semaphore()

    def greet(device):
        pl.semaphore_signal(barrier, inc=1, device_id=device, device_id_type=MESH)

    for partner in partners:
        greet(partner)

    def others(count, me, act):
        for step in range(1, count):
            v = me + step
            act(jnp.where(v >= count, v - count, v))

    @pl.when(joined)
    def _():
        others(GROUP // 2, chip, lambda v: greet((g, 2 * v + core)))
        greet((g, 2 * chip + 1 - core))

    count = count_ref[0]
    z_from, z_to = rows_of((NZ, NZ)), lanes_of((NZ, NZ))
    here = z_from == jnp.where(z_to < 128, 2 * z_to, 2 * z_to - 255)
    order[...] = jnp.where(here, 1.0, 0.0).astype(BF16)

    def ordered(x):
        return jnp.dot(x.reshape(-1, NZ), order[...], preferred_element_type=F32)

    live = rows_of((CY, LIVE, NZ)) < count

    def turn(x, side=None):
        plane = jnp.swapaxes(ordered(raw[x]).reshape(LIVE, CY, NZ), 0, 1)
        plane = jnp.where(live, plane, 0.0)
        field[x] = plane
        for y in range(CY):
            masked[x, :, NZ * y : NZ * (y + 1)] = pad_rows(plane[y], SLOTS).astype(BF16)
        if side is not None:
            for y in range(0, CY, 2):
                two = jnp.concatenate([plane[y], plane[y + 1]], 0)
                ends[side, :, NZ * y // 2 : NZ * (y + 2) // 2] = two.astype(BF16)

    fetch(0).wait()
    fetch(CX - 1).wait()
    turn(0, 0)
    turn(CX - 1, 1)
    cells[0].wait()
    kap = ordered(kappa[...]).reshape(CX, CY, NZ)
    edge[0] = kap[0]
    edge[1] = kap[CX - 1]
    for x in range(CX):
        edge[2, x : x + 1] = kap[x, 0:1]
        edge[3, x : x + 1] = kap[x, CY - 1 : CY]
    pl.semaphore_wait(barrier, jnp.where(joined, GROUP // 2 + 4, 4))

    def halo_copy(k):
        return pltpu.make_async_remote_copy(
            src_ref=edge.at[k], dst_ref=halo.at[mirror[k]],
            send_sem=halo_send.at[k], recv_sem=halo_recv.at[mirror[k]],
            device_id=partners[k], device_id_type=MESH,
        )

    sources = [
        ends.at[0],
        ends.at[1],
        masked.at[:, :, pl.ds(0, NZ)],
        masked.at[:, :, pl.ds((CY - 1) * NZ, NZ)],
    ]
    landings = [face_x.at[0], face_x.at[1], face_y.at[0], face_y.at[1]]

    def face_copy(k):
        return pltpu.make_async_remote_copy(
            src_ref=sources[k], dst_ref=landings[mirror[k]],
            send_sem=face_send.at[k], recv_sem=face_recv.at[mirror[k]],
            device_id=partners[k], device_id_type=MESH,
        )

    for k in range(4):
        halo_copy(k).start()
    face_copy(0).start()
    face_copy(1).start()

    def turn_next(i, carry):
        fetch(2 * i + 1).wait()
        fetch(2 * i + 2).wait()
        turn(2 * i + 1)
        turn(2 * i + 2)
        return carry

    lax.fori_loop(0, CX // 2 - 1, turn_next, 0)
    face_copy(2).start()
    face_copy(3).start()

    plane0 = jnp.zeros((CY, NZ), F32)
    row0 = jnp.zeros((1, NZ), F32)
    half = lanes_of((CY, 128))
    wx[0] = plane0
    wx[CX] = plane0
    for x in range(CX - 1):
        wx[x + 1] = 0.5 * (kap[x] + kap[x + 1])
    for x in range(CX):
        k = kap[x]
        wy[x, 0:1] = row0
        wy[x, 1:CY] = 0.5 * (k[: CY - 1] + k[1:])
        wy[x, CY : CY + 1] = row0
        even, uneven = k[:, :128], k[:, 128:]
        wz[x, :, 0:128] = 0.5 * (even + uneven)
        wz[x, :, 128:] = jnp.where(half == 127, 0.0, 0.5 * (uneven + pltpu.roll(even, 127, 1)))
    cells[1].wait()
    reac = ordered(react[...]).reshape(CX, CY, NZ)
    for k in range(4):
        halo_copy(k).wait_recv()
    ext = [jnp.where(inside[k], halo[k], 0.0) for k in range(4)]
    bound = [0.5 * (edge[k] + ext[k]) for k in range(4)]
    for x in range(CX):
        k = kap[x]
        inner, outer = wz[x, :, 0:128], wz[x, :, 128:]
        below = jnp.where(half == 0, 0.5 * k[:, :128], pltpu.roll(outer, 1, 1))
        above = jnp.where(half == 127, 0.5 * k[:, 128:], outer)
        dz = jnp.concatenate([below + inner, inner + above], 1)
        dx = (bound[0] if x == 0 else wx[x]) + (bound[1] if x == CX - 1 else wx[x + 1])
        dy = wy[x, 0:CY] + wy[x, 1 : CY + 1]
        dy = dy + jnp.concatenate(
            [bound[2][x : x + 1], jnp.zeros((CY - 2, NZ), F32), bound[3][x : x + 1]], 0
        )
        diag[x] = reac[x] + dx + dy + dz

    def apply(x, gram):
        before, after = jnp.maximum(x - 1, 0), jnp.minimum(x + 1, CX - 1)
        behind, v = None, field[x, 0]
        for y in range(CY):
            ahead = field[x, y + 1] if y < CY - 1 else None
            out = diag[x, y : y + 1] * v
            out = out - wx[x, y : y + 1] * field[before, y]
            out = out - wx[x + 1, y : y + 1] * field[after, y]
            if y > 0:
                out = out - wy[x, y : y + 1] * behind
            if y < CY - 1:
                out = out - wy[x, y + 1 : y + 2] * ahead
            even, uneven = v[:, :128], v[:, 128:]
            inner, outer = wz[x, y : y + 1, 0:128], wz[x, y : y + 1, 128:]
            out = out - jnp.concatenate(
                [
                    inner * uneven + pltpu.roll(outer * uneven, 1, 1),
                    inner * even + outer * pltpu.roll(even, 127, 1),
                ],
                1,
            )
            local = pad_rows(out, SLOTS).astype(BF16)
            gram = gram + nt(masked[x, :, NZ * y : NZ * (y + 1)], local)
            behind, v = v, ahead
        return gram

    gram = lax.fori_loop(
        0, CX // 4,
        lambda i, gram: apply(
            4 * i + 3, apply(4 * i + 2, apply(4 * i + 1, apply(4 * i, gram)))
        ),
        jnp.zeros((SLOTS, SLOTS), F32),
    )
    own = pad_lanes(gram, 128)
    spot, slot = lanes_of((SLOTS, 128)), rows_of((SLOTS, 128))
    own = own + jnp.where((spot == slot) & (slot >= count), 1.0, 0.0)
    sym = jnp.where(spot < LIVE, 0.5 * (own + transposed(own)[:SLOTS]), 0.0)

    def up_copy(ref, i):
        return pltpu.make_async_remote_copy(
            src_ref=ref, dst_ref=ref, send_sem=up_sem.at[i], recv_sem=up_sem.at[i + 2],
            device_id=(1, u), device_id_type=MESH,
        )

    def link_copy(to, owner):
        return pltpu.make_async_remote_copy(
            src_ref=links.at[owner, core], dst_ref=links.at[owner, core],
            send_sem=link_send.at[to], recv_sem=link_recv.at[owner],
            device_id=(g, 2 * to + core), device_id_type=MESH,
        )

    def piv_copy(to, owner):
        return pltpu.make_async_remote_copy(
            src_ref=pivs.at[owner, core], dst_ref=pivs.at[owner, core],
            send_sem=piv_send.at[to], recv_sem=piv_recv.at[owner],
            device_id=(g, 2 * to + core), device_id_type=MESH,
        )

    def cross_copy(ref, sem):
        return pltpu.make_async_remote_copy(
            src_ref=ref, dst_ref=ref, send_sem=cross_send.at[sem], recv_sem=cross_recv.at[sem],
            device_id=(g, 2 * chip + 1 - core), device_id_type=MESH,
        )

    def cross_link(v, c):
        return cross_copy(links.at[v, c], v)

    def cross_pivs(c):
        return cross_copy(pivs.at[:, c], GROUP // 2)

    link_up, piv_up = up_copy(links.at[chip, core], 0), up_copy(pivs.at[chip, core], 1)

    @pl.when(joined & (g == 0))
    def _():
        packed = sym[0:16] + pltpu.roll(sym[16:32], LIVE, 1)
        pivs[chip, core] = packed + pltpu.roll(pad_rows(sym[32:40], 16), 2 * LIVE, 1)
        piv_up.start()
        others(GROUP // 2, chip, lambda v: piv_copy(v, chip).start())

    def coupling(k):
        weight = bound[k]
        total = jnp.zeros((SLOTS, SLOTS), F32)
        if k < 2:
            x = 0 if k == 0 else CX - 1
            for y in range(0, CY, 2):
                two = [field[x, j] * weight[j : j + 1] for j in (y, y + 1)]
                hi, lo = split(jnp.concatenate(two, 0))
                cols = slice(NZ * y // 2, NZ * (y + 2) // 2)
                high[:, cols], low[:, cols] = hi, lo
            face_copy(mirror[k]).wait_recv()
            both = nt(high[...], face_x[k]) + nt(low[...], face_x[k])
            both = pad_lanes(both, 128)
            block = both[:LIVE] + pltpu.roll(both[LIVE:], 128 - LIVE, 1)
            block = jnp.where(lanes_of((LIVE, 128)) < LIVE, block, 0.0)
        else:
            face_copy(mirror[k]).wait_recv()
            for x in range(CX):
                mine = field[x, 0 if k == 2 else CY - 1] * weight[x : x + 1]
                hi, lo = split(pad_rows(mine, SLOTS))
                other = face_y[k - 2, x]
                total = total + (nt(hi, other) + nt(lo, other))
            block = pad_lanes(total, 128)[:LIVE]
        return jnp.where(inside[k], -block, 0.0)

    found = {k: coupling(k) for k in (1, 3)}
    lane = lanes_of((LIVE, 128))
    odd = core == 1
    ahead = found[3]
    ahead_t = transposed(ahead)[:LIVE]
    message = jnp.where(odd, ahead, ahead_t) + pltpu.roll(jnp.where(odd, ahead_t, ahead), LIVE, 1)
    message = message + pltpu.roll(transposed(found[1])[:LIVE], 2 * LIVE, 1)
    message = jnp.where(lane >= 3 * LIVE, count.astype(F32), message)

    @pl.when(joined & (g == 0))
    def _():
        links[chip, core] = message
        link_up.start()
        others(GROUP // 2, chip, lambda v: link_copy(v, chip).start())

    @pl.when(joined & (g == 1))
    def _():
        piv_up.wait_recv()
        others(GROUP // 2, chip, lambda v: piv_copy(v, chip).start())
        link_up.wait_recv()
        others(GROUP // 2, chip, lambda v: link_copy(v, chip).start())

    for k in (0, 2):
        found[k] = coupling(k)
    blocks_ref[0] = own
    for k in range(4):
        blocks_ref[k + 1] = pad_rows(found[k], SLOTS)
    blocks_ref[5] = sym

    @pl.when(joined)
    def _():
        others(GROUP // 2, chip, lambda v: piv_copy(chip, v).wait_recv())
        cross_pivs(core).start()
        cross_link(chip, core).start()

        def forward(v):
            link_copy(chip, v).wait_recv()
            cross_link(v, core).start()

        others(GROUP // 2, chip, forward)
        cross_pivs(1 - core).wait_recv()
        for v in range(GROUP // 2):
            cross_link(v, 1 - core).wait_recv()
        for v in range(GROUP):
            links_ref[v] = links[v // 2, v % 2]
            pivots_ref[v] = pivs[v // 2, v % 2]
        others(GROUP // 2, chip, lambda v: link_copy(v, chip).wait_send())
        others(GROUP // 2, chip, lambda v: piv_copy(v, chip).wait_send())
        cross_pivs(core).wait_send()
        for v in range(GROUP // 2):
            cross_link(v, core).wait_send()

    @pl.when(joined & (g == 0))
    def _():
        link_up.wait_send()
        piv_up.wait_send()

    for k in range(4):
        halo_copy(k).wait_send()
        face_copy(k).wait_send()


def assemble(count, modes, kappa, react):
    vmem = pl.BlockSpec(memory_space=pltpu.VMEM)
    hbm = pl.BlockSpec(memory_space=pltpu.HBM)
    dma = pltpu.SemaphoreType.DMA
    return pl.pallas_call(
        assemble_kernel,
        out_shape=(
            jax.ShapeDtypeStruct((6, SLOTS, 128), F32),
            jax.ShapeDtypeStruct((GROUP, LIVE, 128), F32),
            jax.ShapeDtypeStruct((GROUP, 16, 128), F32),
        ),
        in_specs=[pl.BlockSpec(memory_space=pltpu.SMEM), hbm, hbm, hbm],
        out_specs=(vmem, vmem, vmem),
        scratch_shapes=[
            pltpu.VMEM((CX, LIVE, CY, NZ), BF16),
            pltpu.VMEM((CX, CY, NZ), BF16),
            pltpu.VMEM((CX, CY, NZ), BF16),
            pltpu.VMEM((CX, CY, LIVE, NZ), F32),
            pltpu.VMEM((CX, SLOTS, CY * NZ), BF16),
            pltpu.VMEM((CX + 1, CY, NZ), F32),
            pltpu.VMEM((CX, 24, NZ), F32),
            pltpu.VMEM((CX, CY, NZ), F32),
            pltpu.VMEM((CX, CY, NZ), F32),
            pltpu.VMEM((4, 16, NZ), F32),
            pltpu.VMEM((4, 16, NZ), F32),
            pltpu.VMEM((2, 2 * LIVE, 8 * NZ), BF16),
            pltpu.VMEM((2, 16, SLOTS, NZ), BF16),
            pltpu.VMEM((2 * LIVE, 8 * NZ), BF16),
            pltpu.VMEM((2 * LIVE, 8 * NZ), BF16),
            pltpu.VMEM((2, 2 * LIVE, 8 * NZ), BF16),
            pltpu.VMEM((GROUP // 2, 2, LIVE, 128), F32),
            pltpu.VMEM((GROUP // 2, 2, 16, 128), F32),
            pltpu.VMEM((NZ, NZ), BF16),
            dma((CX,)),
            dma((2,)),
            dma((4,)),
            dma((4,)),
            dma((4,)),
            dma((4,)),
            dma((4,)),
            dma((GROUP // 2,)),
            dma((GROUP // 2,)),
            dma((GROUP // 2,)),
            dma((GROUP // 2,)),
            dma((GROUP // 2 + 1,)),
            dma((GROUP // 2 + 1,)),
        ],
        compiler_params=pltpu.CompilerParams(
            collective_id=0, has_side_effects=True, vmem_limit_bytes=50 * 2**20
        ),
        name="assemble",
    )(count, modes, kappa, react)


def halves(x, rows, axis):
    hi, lo = split(pad_rows(x, rows) if x.shape[0] < rows else x)
    return jnp.concatenate([hi, lo], axis)


def joined_halves(out, rows):
    tall = out.shape[0] // 2
    return out[:rows, :128] + (out[:rows, 128:] + out[tall : tall + rows, :128])


def nn3(a, b):
    depth = b.shape[0]
    left = halves(a, SLOTS, 0)[:, :depth]
    out = jnp.dot(left, halves(b, depth, 1), preferred_element_type=F32)
    return joined_halves(out, a.shape[0])


def nt3(a, b):
    out = nt(halves(a, SLOTS, 0), halves(b, 128, 0))
    return joined_halves(out, a.shape[0])


def wide(x):
    return jnp.broadcast_to(x, (8, 128))


def pivots(p, soff, state, spread_ref, rows_ref, side_ref):
    tiles, saved = (list(part) for part in state)
    sub = rows_of((8, 128))
    at = soff + 8 * p
    column = lambda v, c: wide(tiles[v][:, c : c + 1])
    if p == 0:
        for c in range(8):
            spread_ref[p, c] = column(p, at + c)
    rows_ref[p] = tiles[p]
    d = {(i, j): wide(spread_ref[p, j, i : i + 1]) for i in range(8) for j in range(i, 8)}
    rows = [wide(rows_ref[p, c : c + 1]) for c in range(8)]
    follow = p + 1 < LIVE // 8
    if follow:
        under = [column(p + 1, at + c) for c in range(8)]
        coming = [column(p + 1, at + 8 + c) for c in range(8)]
    others = [v for v in range(LIVE // 8) if v not in (p, p + 1)]
    factors = {v: [column(v, at + c) for c in range(8)] for v in others}
    low, rinv = {}, []
    for c in range(8):
        rinv.append(lax.rsqrt(d[c, c]))
        for i in range(c + 1, 8):
            low[c, i] = d[c, i] * rinv[c]
        for i in range(c + 1, 8):
            for j in range(i, 8):
                d[i, j] = d[i, j] - low[c, i] * low[c, j]
        rows[c] = rows[c] * rinv[c]
        saved[p] = jnp.where(sub == c, rows[c], saved[p])
        for i in range(c + 1, 8):
            rows[i] = rows[i] - low[c, i] * rows[c]
        if follow:
            under[c] = under[c] * rinv[c]
            side_ref[p, c] = under[c]
            for i in range(c + 1, 8):
                under[i] = under[i] - low[c, i] * under[c]
            for i in range(8):
                coming[i] = coming[i] - under[c] * wide(side_ref[p, c, i : i + 1])
            tiles[p + 1] = tiles[p + 1] - under[c] * rows[c]
    if follow:
        for c in range(8):
            spread_ref[p + 1, c] = coming[c]
    z = rows
    for c in range(7, -1, -1):
        z[c] = z[c] * rinv[c]
        for i in range(c):
            z[i] = z[i] - low[i, c] * z[c]
    for v in others:
        terms = [factors[v][c] * z[c] for c in range(8)]
        while len(terms) > 1:
            terms = [terms[i] + terms[i + 1] for i in range(0, len(terms), 2)]
        tiles[v] = tiles[v] - terms[0]
    for c in range(8):
        tiles[p] = jnp.where(sub == c, z[c], tiles[p])
    return tuple(tiles), tuple(saved)


def place(out_ref, block, pos, keep):
    base = jnp.minimum((pos // 128) * 128, NC - 256)
    base = pl.multiple_of(base, 128)
    shifted = pltpu.roll(pad_lanes(block, 256), pos - base, 1)
    cols = lanes_of((SLOTS, 256)) + base
    out_ref[:, pl.ds(base, 256)] += jnp.where(keep(cols), shifted, 0.0)


def factor_kernel(
    links_ref, pivots_ref, blocks_ref, out_ref, linv_ref, k_ref, g_ref, f_ref, x_ref, spread_ref, rows_ref, side_ref,
):
    g, u = lax.axis_index("grp"), lax.axis_index("sub")
    s = g * NU + u
    upper = s <= 21
    member = (s == 21) | (s == 22) | ((s >= NU) & (s < NU + NB))
    lane = lanes_of((LIVE, 128))
    row = rows_of((LIVE, 128))
    lane48 = lanes_of((SLOTS, 128))
    row48 = rows_of((SLOTS, 128))
    out_ref[...] = jnp.zeros_like(out_ref)
    before = lambda cols: cols < DONE
    after = lambda cols: cols >= DONE

    def left(x, by):
        x = pltpu.roll(x, 128 - by, 1) if by else x
        return jnp.where(lanes_of(x.shape) < LIVE, x, 0.0)

    def put(block, pos, late):
        base = pos // 128 * 128
        shifted = pltpu.roll(pad_lanes(block, 256), pos - base, 1) if pos > base else (
            pad_lanes(block, 256)
        )
        if base < DONE < base + 256:
            cols = lanes_of((SLOTS, 256)) + base
            shifted = jnp.where(cols >= DONE if late else cols < DONE, shifted, 0.0)
        out_ref[:, base : base + 256] += shifted

    def reduce_row(q):
        at, wide_enough = jnp.maximum(q, 0), jnp.where(q == NB - 1, 16, LIVE)
        mine = jnp.where(q == s, blocks_ref[5], 0.0)
        mine = jnp.where(q == s - 1, blocks_ref[3], mine)
        mine = jnp.where(q == s - NU, blocks_ref[1], mine)
        held = jnp.where(q > 0, f_ref[jnp.maximum(q - 1, 0)], 0.0)
        f = mine - nn3(held, pad_rows(k_ref[at], SLOTS))
        f_ref[at] = jnp.where((q <= s) & (lane48 < wide_enough), f, 0.0)

    def solve_row(q):
        at = jnp.maximum(q, 0)
        x = nt3(f_ref[at], pad_rows(linv_ref[at], 128))
        x_ref[at] = jnp.where((q == s) & (lane48 > row48), 0.0, x)

    def double_row(q):
        at = jnp.maximum(q, 0)
        x = x_ref[at]
        g_ref[at] = nn3(x, pad_rows(linv_ref[at], SLOTS))

    def pivot_block(t, at):
        packed = pivots_ref[t]
        parts = []
        for i in range(3):
            by = (at - LIVE * i) % 128
            parts.append(pltpu.roll(packed, by, 1) if by else packed)
        block = jnp.concatenate([parts[0], parts[1], parts[2][:8]], 0)
        return jnp.where((lane >= at) & (lane < at + LIVE), block, 0.0)

    def live_count(t):
        return jnp.max(jnp.where(lanes_of((8, 128)) >= 3 * LIVE, links_ref[t][0:8], 0.0))

    def at_rows(x, start):
        above = jnp.zeros((start, 128), F32)
        return jnp.concatenate([above, x], 0) if start else pad_rows(x, SLOTS)

    def step(t, odd, scur, n):
        soff, uoff = (LIVE, 0) if odd else (0, LIVE)
        given = links_ref[t]
        limit = jnp.where(t == NB - 1, 16, LIVE)
        in_s = (lane >= soff) & (lane < soff + LIVE)
        in_u = (lane >= uoff) & (lane < uoff + LIVE)
        eye = jnp.where(lane == row + soff, 1.0, 0.0)
        a = jnp.where((row < limit) & (lane < soff + limit), scur, eye)
        rest = jnp.where(lane == row + 2 * LIVE, 1.0, 0.0)
        rest = jnp.where(in_u, jnp.where(row < limit, given, 0.0), rest)
        a = jnp.where(in_s, a, rest)
        ut = jnp.where(in_s, given, 0.0)
        tiles = tuple(a[8 * v : 8 * v + 8] for v in range(LIVE // 8))
        state = pivots(0, soff, (tiles, tiles), spread_ref, rows_ref, side_ref)

        double_row(t - 3)
        solve_row(t - 2)
        reduce_row(t - 1)
        following = jnp.minimum(t + 1, NB - 1)
        coming, coming_n = pivot_block(following, uoff), live_count(following)
        n = jnp.where(t == NB - 1, jnp.minimum(n, 16.0), n)
        for p in range(1, LIVE // 8):
            state = lax.cond(
                n > 8.0 * p,
                lambda st, p=p: pivots(p, soff, st, spread_ref, rows_ref, side_ref),
                lambda st: st,
                state,
            )
        tiles, saved = state
        k = jnp.concatenate(tiles, 0)
        snext = coming - nn3(ut, at_rows(k, soff))
        linv_ref[t] = left(jnp.concatenate(saved, 0), 2 * LIVE)
        k_ref[t + 1] = left(k, uoff)
        return snext, coming_n

    @pl.when(upper | member)
    def _():
        k_ref[0] = jnp.zeros((LIVE, 128), F32)
        linv_ref[0] = jnp.zeros((LIVE, 128), F32)
        f_ref[0] = jnp.zeros((SLOTS, 128), F32)
        x_ref[0] = jnp.zeros((SLOTS, 128), F32)
        def pair(i, carry):
            carry = step(2 * i, False, *carry)
            return step(2 * i + 1, True, *carry)

        lax.fori_loop(0, NB // 2, pair, (pivot_block(0, 0), live_count(0)))
        double_row(NB - 3)
        solve_row(NB - 2)
        reduce_row(NB - 1)
        double_row(NB - 2)
        solve_row(NB - 1)
        double_row(NB - 1)
        for t in range(NB):
            put(x_ref[t], SLOTS * t, False)

    @pl.when(upper)
    def _():
        dead = jnp.where((row48 == lane48) & (row48 >= LIVE), 1.0, 0.0)
        place(out_ref, dead, SLOTS * s, before)

    @pl.when(member)
    def _():
        late = lane >= 16
        last = jnp.where(row < 16, links_ref[NB - 1], 0.0)
        own = jnp.where(late & (row < 16), pivot_block(NB - 1, 0), 0.0)
        over = jnp.where(late, left(links_ref[NB - 2], LIVE), 0.0)
        y = None
        for t in range(NB - 1, -1, -1):
            if y is None:
                y = g_ref[t]
                put(-nn3(y, pad_rows(left(last, 0), SLOTS)), SLOTS * NB, True)
                put(-nn3(y, pad_rows(own, SLOTS)), SLOTS * (NB - 1), True)
            else:
                y = g_ref[t] - nt3(y, pad_rows(k_ref[t + 1], 128))
            if t == NB - 2:
                put(-nn3(y, pad_rows(over, SLOTS)), SLOTS * (NB - 1), True)
            rising = pad_rows(left(links_ref[t], 2 * LIVE), 128)
            put(-nt3(y, rising), SLOTS * (t + NU), True)

    @pl.when(s >= 21)
    def _():
        targets = [s, s - NU, s + NU, s - 1, s + 1]
        valid = [True, g > 0, g < NG - 1, u > 0, u < NU - 1]
        for k in range(5):
            pos = SLOTS * jnp.clip(targets[k], 0, NG * NU - 1)
            place(out_ref, jnp.where(valid[k], blocks_ref[k], 0.0), pos, after)

    @pl.when(s == 21)
    def _():
        out_ref[0:16, DONE:] = jnp.zeros((16, NC - DONE), F32)


def factor(links, pivs, blocks):
    vmem = pl.BlockSpec(memory_space=pltpu.VMEM)
    return pl.pallas_call(
        factor_kernel,
        out_shape=jax.ShapeDtypeStruct((SLOTS, NC), F32),
        in_specs=[vmem, vmem, vmem],
        out_specs=vmem,
        scratch_shapes=[
            pltpu.VMEM((NB, LIVE, 128), F32),
            pltpu.VMEM((NB + 1, LIVE, 128), F32),
            pltpu.VMEM((NB, SLOTS, 128), F32),
            pltpu.VMEM((NB, SLOTS, 128), F32),
            pltpu.VMEM((NB, SLOTS, 128), F32),
            pltpu.VMEM((LIVE // 8, 8, 8, 128), F32),
            pltpu.VMEM((LIVE // 8, 8, 128), F32),
            pltpu.VMEM((LIVE // 8, 8, 8, 128), F32),
        ],
        compiler_params=pltpu.CompilerParams(vmem_limit_bytes=40 * 2**20),
        name="factor",
    )(links, pivs, blocks)


def per_device(modes, counts, kappa, react):
    kappa = pltpu.with_memory_space_constraint(kappa, pltpu.HBM)
    react = pltpu.with_memory_space_constraint(react, pltpu.HBM)
    blocks, links, pivs = assemble(counts, modes, kappa, react)
    return factor(links, pivs, blocks)


def solution(mesh):
    in_specs = (
        P(None, "grp", "sub", None),
        P(("grp", "sub")),
        P("grp", "sub", None),
        P("grp", "sub", None),
    )
    out_specs = P(("grp", "sub"), None)
    return jax.shard_map(
        per_device, mesh=mesh, in_specs=in_specs, out_specs=out_specs, check_vma=False
    )
```

```python
import jax
import jax.numpy as jnp
from jax import lax
from jax.experimental import pallas as pl
from jax.experimental.pallas import tpu as pltpu
from jax.sharding import PartitionSpec as P

F32 = jnp.float32
BF16 = jnp.bfloat16
MESH = pl.DeviceIdType.MESH
NG, NU = 4, 32
CX, CY, NZ = 16, 16, 256
SLOTS, LIVE = 48, 40
NB = 22
DONE = 1024
GROUP = 24
NC = SLOTS * NG * NU


def nt(a, b, precision=None):
    return lax.dot_general(
        a, b, (((1,), (1,)), ((), ())), preferred_element_type=F32, precision=precision
    )


def lanes_of(shape):
    return lax.broadcasted_iota(jnp.int32, shape, len(shape) - 1)


def rows_of(shape):
    return lax.broadcasted_iota(jnp.int32, shape, len(shape) - 2)


def split(x):
    hi = x.astype(BF16)
    return hi, (x - hi.astype(F32)).astype(BF16)


def pad_rows(x, rows):
    return jnp.concatenate([x, jnp.zeros((rows - x.shape[0], x.shape[1]), x.dtype)], 0)


def pad_lanes(x, lanes):
    return jnp.concatenate([x, jnp.zeros((x.shape[0], lanes - x.shape[1]), x.dtype)], 1)


def transposed(x):
    return jnp.transpose(pad_rows(x, 128))


def assemble_kernel(
    count_ref, modes_ref, kappa_ref, react_ref, blocks_ref, links_ref, pivots_ref,
    raw, kappa, react, field, masked, wx, wy, wz, diag, edge, halo, face_x, face_y,
    high, low, ends, links, pivs, order,
    raw_sem, cell_sem, halo_send, halo_recv, face_send, face_recv,
    up_sem, link_send, link_recv, piv_send, piv_recv, cross_send, cross_recv,
):
    g, u = lax.axis_index("grp"), lax.axis_index("sub")
    partners = [
        (lax.rem(g + NG - 1, NG), u),
        (lax.rem(g + 1, NG), u),
        (g, lax.rem(u + NU - 1, NU)),
        (g, lax.rem(u + 1, NU)),
    ]
    inside = [g > 0, g < NG - 1, u > 0, u < NU - 1]
    mirror = [1, 0, 3, 2]
    chip, core = u // 2, lax.rem(u, 2)
    joined = (g < 2) & (u < GROUP)

    def fetch(x):
        return pltpu.make_async_copy(
            modes_ref.at[pl.ds(0, LIVE), x], raw.at[x], raw_sem.at[x]
        )

    cells = [
        pltpu.make_async_copy(kappa_ref, kappa, cell_sem.at[0]),
        pltpu.make_async_copy(react_ref, react, cell_sem.at[1]),
    ]
    fetch(0).start()
    fetch(CX - 1).start()
    cells[0].start()
    for x in range(1, CX - 1):
        fetch(x).start()
    cells[1].start()

    barrier = pltpu.get_barrier_semaphore()

    def greet(device):
        pl.semaphore_signal(barrier, inc=1, device_id=device, device_id_type=MESH)

    for partner in partners:
        greet(partner)

    def others(count, me, act):
        for step in range(1, count):
            v = me + step
            act(jnp.where(v >= count, v - count, v))

    @pl.when(joined)
    def _():
        others(GROUP // 2, chip, lambda v: greet((g, 2 * v + core)))
        greet((g, 2 * chip + 1 - core))

    count = count_ref[0]
    z_from, z_to = rows_of((NZ, NZ)), lanes_of((NZ, NZ))
    here = z_from == jnp.where(z_to < 128, 2 * z_to, 2 * z_to - 255)
    order[...] = jnp.where(here, 1.0, 0.0).astype(BF16)

    def ordered(x):
        return jnp.dot(x.reshape(-1, NZ), order[...], preferred_element_type=F32)

    live = rows_of((CY, LIVE, NZ)) < count

    def turn(x, side=None):
        plane = jnp.swapaxes(ordered(raw[x]).reshape(LIVE, CY, NZ), 0, 1)
        plane = jnp.where(live, plane, 0.0)
        field[x] = plane
        for y in range(CY):
            masked[x, :, NZ * y : NZ * (y + 1)] = pad_rows(plane[y], SLOTS).astype(BF16)
        if side is not None:
            for y in range(0, CY, 2):
                two = jnp.concatenate([plane[y], plane[y + 1]], 0)
                ends[side, :, NZ * y // 2 : NZ * (y + 2) // 2] = two.astype(BF16)

    fetch(0).wait()
    fetch(CX - 1).wait()
    turn(0, 0)
    turn(CX - 1, 1)
    cells[0].wait()
    kap = ordered(kappa[...]).reshape(CX, CY, NZ)
    edge[0] = kap[0]
    edge[1] = kap[CX - 1]
    for x in range(CX):
        edge[2, x : x + 1] = kap[x, 0:1]
        edge[3, x : x + 1] = kap[x, CY - 1 : CY]
    pl.semaphore_wait(barrier, jnp.where(joined, GROUP // 2 + 4, 4))

    def halo_copy(k):
        return pltpu.make_async_remote_copy(
            src_ref=edge.at[k], dst_ref=halo.at[mirror[k]],
            send_sem=halo_send.at[k], recv_sem=halo_recv.at[mirror[k]],
            device_id=partners[k], device_id_type=MESH,
        )

    sources = [
        ends.at[0],
        ends.at[1],
        masked.at[:, :, pl.ds(0, NZ)],
        masked.at[:, :, pl.ds((CY - 1) * NZ, NZ)],
    ]
    landings = [face_x.at[0], face_x.at[1], face_y.at[0], face_y.at[1]]

    def face_copy(k):
        return pltpu.make_async_remote_copy(
            src_ref=sources[k], dst_ref=landings[mirror[k]],
            send_sem=face_send.at[k], recv_sem=face_recv.at[mirror[k]],
            device_id=partners[k], device_id_type=MESH,
        )

    for k in range(4):
        halo_copy(k).start()
    face_copy(0).start()
    face_copy(1).start()

    def turn_next(i, carry):
        fetch(2 * i + 1).wait()
        fetch(2 * i + 2).wait()
        turn(2 * i + 1)
        turn(2 * i + 2)
        return carry

    lax.fori_loop(0, CX // 2 - 1, turn_next, 0)
    face_copy(2).start()
    face_copy(3).start()

    plane0 = jnp.zeros((CY, NZ), F32)
    row0 = jnp.zeros((1, NZ), F32)
    half = lanes_of((CY, 128))
    wx[0] = plane0
    wx[CX] = plane0
    for x in range(CX - 1):
        wx[x + 1] = 0.5 * (kap[x] + kap[x + 1])
    for x in range(CX):
        k = kap[x]
        wy[x, 0:1] = row0
        wy[x, 1:CY] = 0.5 * (k[: CY - 1] + k[1:])
        wy[x, CY : CY + 1] = row0
        even, uneven = k[:, :128], k[:, 128:]
        wz[x, :, 0:128] = 0.5 * (even + uneven)
        wz[x, :, 128:] = jnp.where(half == 127, 0.0, 0.5 * (uneven + pltpu.roll(even, 127, 1)))
    cells[1].wait()
    reac = ordered(react[...]).reshape(CX, CY, NZ)
    for k in range(4):
        halo_copy(k).wait_recv()
    ext = [jnp.where(inside[k], halo[k], 0.0) for k in range(4)]
    bound = [0.5 * (edge[k] + ext[k]) for k in range(4)]
    for x in range(CX):
        k = kap[x]
        inner, outer = wz[x, :, 0:128], wz[x, :, 128:]
        below = jnp.where(half == 0, 0.5 * k[:, :128], pltpu.roll(outer, 1, 1))
        above = jnp.where(half == 127, 0.5 * k[:, 128:], outer)
        dz = jnp.concatenate([below + inner, inner + above], 1)
        dx = (bound[0] if x == 0 else wx[x]) + (bound[1] if x == CX - 1 else wx[x + 1])
        dy = wy[x, 0:CY] + wy[x, 1 : CY + 1]
        dy = dy + jnp.concatenate(
            [bound[2][x : x + 1], jnp.zeros((CY - 2, NZ), F32), bound[3][x : x + 1]], 0
        )
        diag[x] = reac[x] + dx + dy + dz

    def apply(x, gram):
        before, after = jnp.maximum(x - 1, 0), jnp.minimum(x + 1, CX - 1)
        behind, v = None, field[x, 0]
        for y in range(CY):
            ahead = field[x, y + 1] if y < CY - 1 else None
            out = diag[x, y : y + 1] * v
            out = out - wx[x, y : y + 1] * field[before, y]
            out = out - wx[x + 1, y : y + 1] * field[after, y]
            if y > 0:
                out = out - wy[x, y : y + 1] * behind
            if y < CY - 1:
                out = out - wy[x, y + 1 : y + 2] * ahead
            even, uneven = v[:, :128], v[:, 128:]
            inner, outer = wz[x, y : y + 1, 0:128], wz[x, y : y + 1, 128:]
            out = out - jnp.concatenate(
                [
                    inner * uneven + pltpu.roll(outer * uneven, 1, 1),
                    inner * even + outer * pltpu.roll(even, 127, 1),
                ],
                1,
            )
            local = pad_rows(out, SLOTS).astype(BF16)
            gram = gram + nt(masked[x, :, NZ * y : NZ * (y + 1)], local)
            behind, v = v, ahead
        return gram

    def eight(i, gram):
        for x in range(8):
            gram = apply(8 * i + x, gram)
        return gram

    gram = lax.fori_loop(
        0, CX // 8, eight,
        jnp.zeros((SLOTS, SLOTS), F32),
    )
    own = pad_lanes(gram, 128)
    spot, slot = lanes_of((SLOTS, 128)), rows_of((SLOTS, 128))
    own = own + jnp.where((spot == slot) & (slot >= count), 1.0, 0.0)
    sym = jnp.where(spot < LIVE, 0.5 * (own + transposed(own)[:SLOTS]), 0.0)

    def up_copy(ref, i):
        return pltpu.make_async_remote_copy(
            src_ref=ref, dst_ref=ref, send_sem=up_sem.at[i], recv_sem=up_sem.at[i + 2],
            device_id=(1, u), device_id_type=MESH,
        )

    def link_copy(to, owner):
        return pltpu.make_async_remote_copy(
            src_ref=links.at[owner, core], dst_ref=links.at[owner, core],
            send_sem=link_send.at[to], recv_sem=link_recv.at[owner],
            device_id=(g, 2 * to + core), device_id_type=MESH,
        )

    def piv_copy(to, owner):
        return pltpu.make_async_remote_copy(
            src_ref=pivs.at[owner, core], dst_ref=pivs.at[owner, core],
            send_sem=piv_send.at[to], recv_sem=piv_recv.at[owner],
            device_id=(g, 2 * to + core), device_id_type=MESH,
        )

    def cross_copy(ref, sem):
        return pltpu.make_async_remote_copy(
            src_ref=ref, dst_ref=ref, send_sem=cross_send.at[sem], recv_sem=cross_recv.at[sem],
            device_id=(g, 2 * chip + 1 - core), device_id_type=MESH,
        )

    def cross_link(v, c):
        return cross_copy(links.at[v, c], v)

    def cross_pivs(c):
        return cross_copy(pivs.at[:, c], GROUP // 2)

    link_up, piv_up = up_copy(links.at[chip, core], 0), up_copy(pivs.at[chip, core], 1)

    @pl.when(joined & (g == 0))
    def _():
        packed = sym[0:16] + pltpu.roll(sym[16:32], LIVE, 1)
        pivs[chip, core] = packed + pltpu.roll(pad_rows(sym[32:40], 16), 2 * LIVE, 1)
        piv_up.start()
        others(GROUP // 2, chip, lambda v: piv_copy(v, chip).start())

    def coupling(k):
        weight = bound[k]
        total = jnp.zeros((SLOTS, SLOTS), F32)
        if k < 2:
            x = 0 if k == 0 else CX - 1
            for y in range(0, CY, 2):
                two = [field[x, j] * weight[j : j + 1] for j in (y, y + 1)]
                hi, lo = split(jnp.concatenate(two, 0))
                cols = slice(NZ * y // 2, NZ * (y + 2) // 2)
                high[:, cols], low[:, cols] = hi, lo
            face_copy(mirror[k]).wait_recv()
            both = nt(high[...], face_x[k]) + nt(low[...], face_x[k])
            both = pad_lanes(both, 128)
            block = both[:LIVE] + pltpu.roll(both[LIVE:], 128 - LIVE, 1)
            block = jnp.where(lanes_of((LIVE, 128)) < LIVE, block, 0.0)
        else:
            face_copy(mirror[k]).wait_recv()
            for x in range(CX):
                mine = field[x, 0 if k == 2 else CY - 1] * weight[x : x + 1]
                hi, lo = split(pad_rows(mine, SLOTS))
                other = face_y[k - 2, x]
                total = total + (nt(hi, other) + nt(lo, other))
            block = pad_lanes(total, 128)[:LIVE]
        return jnp.where(inside[k], -block, 0.0)

    found = {k: coupling(k) for k in (1, 3)}
    lane = lanes_of((LIVE, 128))
    odd = core == 1
    ahead = found[3]
    ahead_t = transposed(ahead)[:LIVE]
    message = jnp.where(odd, ahead, ahead_t) + pltpu.roll(jnp.where(odd, ahead_t, ahead), LIVE, 1)
    message = message + pltpu.roll(transposed(found[1])[:LIVE], 2 * LIVE, 1)
    message = jnp.where(lane >= 3 * LIVE, count.astype(F32), message)

    @pl.when(joined & (g == 0))
    def _():
        links[chip, core] = message
        link_up.start()
        others(GROUP // 2, chip, lambda v: link_copy(v, chip).start())

    @pl.when(joined & (g == 1))
    def _():
        piv_up.wait_recv()
        others(GROUP // 2, chip, lambda v: piv_copy(v, chip).start())
        link_up.wait_recv()
        others(GROUP // 2, chip, lambda v: link_copy(v, chip).start())

    for k in (0, 2):
        found[k] = coupling(k)
    blocks_ref[0] = own
    for k in range(4):
        blocks_ref[k + 1] = pad_rows(found[k], SLOTS)
    blocks_ref[5] = sym

    @pl.when(joined)
    def _():
        others(GROUP // 2, chip, lambda v: piv_copy(chip, v).wait_recv())
        cross_pivs(core).start()
        cross_link(chip, core).start()

        def forward(v):
            link_copy(chip, v).wait_recv()
            cross_link(v, core).start()

        others(GROUP // 2, chip, forward)
        cross_pivs(1 - core).wait_recv()
        for v in range(GROUP // 2):
            cross_link(v, 1 - core).wait_recv()
        for v in range(GROUP):
            links_ref[v] = links[v // 2, v % 2]
            pivots_ref[v] = pivs[v // 2, v % 2]
        others(GROUP // 2, chip, lambda v: link_copy(v, chip).wait_send())
        others(GROUP // 2, chip, lambda v: piv_copy(v, chip).wait_send())
        cross_pivs(core).wait_send()
        for v in range(GROUP // 2):
            cross_link(v, core).wait_send()

    @pl.when(joined & (g == 0))
    def _():
        link_up.wait_send()
        piv_up.wait_send()

    for k in range(4):
        halo_copy(k).wait_send()
        face_copy(k).wait_send()


def assemble(count, modes, kappa, react):
    vmem = pl.BlockSpec(memory_space=pltpu.VMEM)
    hbm = pl.BlockSpec(memory_space=pltpu.HBM)
    dma = pltpu.SemaphoreType.DMA
    return pl.pallas_call(
        assemble_kernel,
        out_shape=(
            jax.ShapeDtypeStruct((6, SLOTS, 128), F32),
            jax.ShapeDtypeStruct((GROUP, LIVE, 128), F32),
            jax.ShapeDtypeStruct((GROUP, 16, 128), F32),
        ),
        in_specs=[pl.BlockSpec(memory_space=pltpu.SMEM), hbm, hbm, hbm],
        out_specs=(vmem, vmem, vmem),
        scratch_shapes=[
            pltpu.VMEM((CX, LIVE, CY, NZ), BF16),
            pltpu.VMEM((CX, CY, NZ), BF16),
            pltpu.VMEM((CX, CY, NZ), BF16),
            pltpu.VMEM((CX, CY, LIVE, NZ), F32),
            pltpu.VMEM((CX, SLOTS, CY * NZ), BF16),
            pltpu.VMEM((CX + 1, CY, NZ), F32),
            pltpu.VMEM((CX, 24, NZ), F32),
            pltpu.VMEM((CX, CY, NZ), F32),
            pltpu.VMEM((CX, CY, NZ), F32),
            pltpu.VMEM((4, 16, NZ), F32),
            pltpu.VMEM((4, 16, NZ), F32),
            pltpu.VMEM((2, 2 * LIVE, 8 * NZ), BF16),
            pltpu.VMEM((2, 16, SLOTS, NZ), BF16),
            pltpu.VMEM((2 * LIVE, 8 * NZ), BF16),
            pltpu.VMEM((2 * LIVE, 8 * NZ), BF16),
            pltpu.VMEM((2, 2 * LIVE, 8 * NZ), BF16),
            pltpu.VMEM((GROUP // 2, 2, LIVE, 128), F32),
            pltpu.VMEM((GROUP // 2, 2, 16, 128), F32),
            pltpu.VMEM((NZ, NZ), BF16),
            dma((CX,)),
            dma((2,)),
            dma((4,)),
            dma((4,)),
            dma((4,)),
            dma((4,)),
            dma((4,)),
            dma((GROUP // 2,)),
            dma((GROUP // 2,)),
            dma((GROUP // 2,)),
            dma((GROUP // 2,)),
            dma((GROUP // 2 + 1,)),
            dma((GROUP // 2 + 1,)),
        ],
        compiler_params=pltpu.CompilerParams(
            collective_id=0, has_side_effects=True, vmem_limit_bytes=50 * 2**20
        ),
        name="assemble",
    )(count, modes, kappa, react)


def halves(x, rows, axis):
    hi, lo = split(pad_rows(x, rows) if x.shape[0] < rows else x)
    return jnp.concatenate([hi, lo], axis)


def joined_halves(out, rows):
    tall = out.shape[0] // 2
    return out[:rows, :128] + (out[:rows, 128:] + out[tall : tall + rows, :128])


def nn3(a, b):
    depth = b.shape[0]
    left = halves(a, SLOTS, 0)[:, :depth]
    out = jnp.dot(left, halves(b, depth, 1), preferred_element_type=F32)
    return joined_halves(out, a.shape[0])


def nt3(a, b):
    out = nt(halves(a, SLOTS, 0), halves(b, 128, 0))
    return joined_halves(out, a.shape[0])


def wide(x):
    return jnp.broadcast_to(x, (8, 128))


def pivots(p, soff, state, spread_ref, rows_ref, side_ref):
    tiles, saved = (list(part) for part in state)
    sub = rows_of((8, 128))
    at = soff + 8 * p
    column = lambda v, c: wide(tiles[v][:, c : c + 1])
    if p == 0:
        for c in range(8):
            spread_ref[p, c] = column(p, at + c)
    rows_ref[p] = tiles[p]
    d = {(i, j): wide(spread_ref[p, j, i : i + 1]) for i in range(8) for j in range(i, 8)}
    rows = [wide(rows_ref[p, c : c + 1]) for c in range(8)]
    follow = p + 1 < LIVE // 8
    if follow:
        under = [column(p + 1, at + c) for c in range(8)]
        coming = [column(p + 1, at + 8 + c) for c in range(8)]
    others = [v for v in range(LIVE // 8) if v not in (p, p + 1)]
    factors = {v: [column(v, at + c) for c in range(8)] for v in others}
    low, rinv = {}, []
    for c in range(8):
        rinv.append(lax.rsqrt(d[c, c]))
        for i in range(c + 1, 8):
            low[c, i] = d[c, i] * rinv[c]
        for i in range(c + 1, 8):
            for j in range(i, 8):
                d[i, j] = d[i, j] - low[c, i] * low[c, j]
        rows[c] = rows[c] * rinv[c]
        saved[p] = jnp.where(sub == c, rows[c], saved[p])
        for i in range(c + 1, 8):
            rows[i] = rows[i] - low[c, i] * rows[c]
        if follow:
            under[c] = under[c] * rinv[c]
            side_ref[p, c] = under[c]
            for i in range(c + 1, 8):
                under[i] = under[i] - low[c, i] * under[c]
            for i in range(8):
                coming[i] = coming[i] - under[c] * wide(side_ref[p, c, i : i + 1])
            tiles[p + 1] = tiles[p + 1] - under[c] * rows[c]
    if follow:
        for c in range(8):
            spread_ref[p + 1, c] = coming[c]
    z = rows
    for c in range(7, -1, -1):
        z[c] = z[c] * rinv[c]
        for i in range(c):
            z[i] = z[i] - low[i, c] * z[c]
    for v in others:
        terms = [factors[v][c] * z[c] for c in range(8)]
        while len(terms) > 1:
            terms = [terms[i] + terms[i + 1] for i in range(0, len(terms), 2)]
        tiles[v] = tiles[v] - terms[0]
    for c in range(8):
        tiles[p] = jnp.where(sub == c, z[c], tiles[p])
    return tuple(tiles), tuple(saved)


def place(out_ref, block, pos, keep):
    base = jnp.minimum((pos // 128) * 128, NC - 256)
    base = pl.multiple_of(base, 128)
    shifted = pltpu.roll(pad_lanes(block, 256), pos - base, 1)
    cols = lanes_of((SLOTS, 256)) + base
    out_ref[:, pl.ds(base, 256)] += jnp.where(keep(cols), shifted, 0.0)


def factor_kernel(
    links_ref, pivots_ref, blocks_ref, out_ref, linv_ref, k_ref, g_ref, f_ref, x_ref, spread_ref, rows_ref, side_ref,
):
    g, u = lax.axis_index("grp"), lax.axis_index("sub")
    s = g * NU + u
    upper = s <= 21
    member = (s == 21) | (s == 22) | ((s >= NU) & (s < NU + NB))
    lane = lanes_of((LIVE, 128))
    row = rows_of((LIVE, 128))
    lane48 = lanes_of((SLOTS, 128))
    row48 = rows_of((SLOTS, 128))
    out_ref[...] = jnp.zeros_like(out_ref)
    before = lambda cols: cols < DONE
    after = lambda cols: cols >= DONE

    def left(x, by):
        x = pltpu.roll(x, 128 - by, 1) if by else x
        return jnp.where(lanes_of(x.shape) < LIVE, x, 0.0)

    def put(block, pos, late):
        base = pos // 128 * 128
        shifted = pltpu.roll(pad_lanes(block, 256), pos - base, 1) if pos > base else (
            pad_lanes(block, 256)
        )
        if base < DONE < base + 256:
            cols = lanes_of((SLOTS, 256)) + base
            shifted = jnp.where(cols >= DONE if late else cols < DONE, shifted, 0.0)
        out_ref[:, base : base + 256] += shifted

    def reduce_row(q):
        at, wide_enough = jnp.maximum(q, 0), jnp.where(q == NB - 1, 16, LIVE)
        mine = jnp.where(q == s, blocks_ref[5], 0.0)
        mine = jnp.where(q == s - 1, blocks_ref[3], mine)
        mine = jnp.where(q == s - NU, blocks_ref[1], mine)
        held = jnp.where(q > 0, f_ref[jnp.maximum(q - 1, 0)], 0.0)
        f = mine - nn3(held, pad_rows(k_ref[at], SLOTS))
        f_ref[at] = jnp.where((q <= s) & (lane48 < wide_enough), f, 0.0)

    def solve_row(q):
        at = jnp.maximum(q, 0)
        x = nt3(f_ref[at], pad_rows(linv_ref[at], 128))
        x_ref[at] = jnp.where((q == s) & (lane48 > row48), 0.0, x)

    def double_row(q):
        at = jnp.maximum(q, 0)
        x = x_ref[at]
        g_ref[at] = nn3(x, pad_rows(linv_ref[at], SLOTS))

    def pivot_block(t, at):
        packed = pivots_ref[t]
        parts = []
        for i in range(3):
            by = (at - LIVE * i) % 128
            parts.append(pltpu.roll(packed, by, 1) if by else packed)
        block = jnp.concatenate([parts[0], parts[1], parts[2][:8]], 0)
        return jnp.where((lane >= at) & (lane < at + LIVE), block, 0.0)

    def live_count(t):
        return jnp.max(jnp.where(lanes_of((8, 128)) >= 3 * LIVE, links_ref[t][0:8], 0.0))

    def at_rows(x, start):
        above = jnp.zeros((start, 128), F32)
        return jnp.concatenate([above, x], 0) if start else pad_rows(x, SLOTS)

    def step(t, odd, scur, n):
        soff, uoff = (LIVE, 0) if odd else (0, LIVE)
        given = links_ref[t]
        limit = jnp.where(t == NB - 1, 16, LIVE)
        in_s = (lane >= soff) & (lane < soff + LIVE)
        in_u = (lane >= uoff) & (lane < uoff + LIVE)
        eye = jnp.where(lane == row + soff, 1.0, 0.0)
        a = jnp.where((row < limit) & (lane < soff + limit), scur, eye)
        rest = jnp.where(lane == row + 2 * LIVE, 1.0, 0.0)
        rest = jnp.where(in_u, jnp.where(row < limit, given, 0.0), rest)
        a = jnp.where(in_s, a, rest)
        ut = jnp.where(in_s, given, 0.0)
        tiles = tuple(a[8 * v : 8 * v + 8] for v in range(LIVE // 8))
        state = pivots(0, soff, (tiles, tiles), spread_ref, rows_ref, side_ref)

        double_row(t - 3)
        solve_row(t - 2)
        reduce_row(t - 1)
        following = jnp.minimum(t + 1, NB - 1)
        coming, coming_n = pivot_block(following, uoff), live_count(following)
        n = jnp.where(t == NB - 1, jnp.minimum(n, 16.0), n)
        for p in range(1, LIVE // 8):
            state = lax.cond(
                n > 8.0 * p,
                lambda st, p=p: pivots(p, soff, st, spread_ref, rows_ref, side_ref),
                lambda st: st,
                state,
            )
        tiles, saved = state
        k = jnp.concatenate(tiles, 0)
        snext = coming - nn3(ut, at_rows(k, soff))
        linv_ref[t] = left(jnp.concatenate(saved, 0), 2 * LIVE)
        k_ref[t + 1] = left(k, uoff)
        return snext, coming_n

    @pl.when(upper | member)
    def _():
        k_ref[0] = jnp.zeros((LIVE, 128), F32)
        linv_ref[0] = jnp.zeros((LIVE, 128), F32)
        f_ref[0] = jnp.zeros((SLOTS, 128), F32)
        x_ref[0] = jnp.zeros((SLOTS, 128), F32)
        def pair(i, carry):
            carry = step(2 * i, False, *carry)
            return step(2 * i + 1, True, *carry)

        lax.fori_loop(0, NB // 2, pair, (pivot_block(0, 0), live_count(0)))
        double_row(NB - 3)
        solve_row(NB - 2)
        reduce_row(NB - 1)
        double_row(NB - 2)
        solve_row(NB - 1)
        double_row(NB - 1)
        for t in range(NB):
            put(x_ref[t], SLOTS * t, False)

    @pl.when(upper)
    def _():
        dead = jnp.where((row48 == lane48) & (row48 >= LIVE), 1.0, 0.0)
        place(out_ref, dead, SLOTS * s, before)

    @pl.when(member)
    def _():
        late = lane >= 16
        last = jnp.where(row < 16, links_ref[NB - 1], 0.0)
        own = jnp.where(late & (row < 16), pivot_block(NB - 1, 0), 0.0)
        over = jnp.where(late, left(links_ref[NB - 2], LIVE), 0.0)
        y = None
        for t in range(NB - 1, -1, -1):
            if y is None:
                y = g_ref[t]
                put(-nn3(y, pad_rows(left(last, 0), SLOTS)), SLOTS * NB, True)
                put(-nn3(y, pad_rows(own, SLOTS)), SLOTS * (NB - 1), True)
            else:
                y = g_ref[t] - nt3(y, pad_rows(k_ref[t + 1], 128))
            if t == NB - 2:
                put(-nn3(y, pad_rows(over, SLOTS)), SLOTS * (NB - 1), True)
            rising = pad_rows(left(links_ref[t], 2 * LIVE), 128)
            put(-nt3(y, rising), SLOTS * (t + NU), True)

    @pl.when(s >= 21)
    def _():
        targets = [s, s - NU, s + NU, s - 1, s + 1]
        valid = [True, g > 0, g < NG - 1, u > 0, u < NU - 1]
        for k in range(5):
            pos = SLOTS * jnp.clip(targets[k], 0, NG * NU - 1)
            place(out_ref, jnp.where(valid[k], blocks_ref[k], 0.0), pos, after)

    @pl.when(s == 21)
    def _():
        out_ref[0:16, DONE:] = jnp.zeros((16, NC - DONE), F32)


def factor(links, pivs, blocks):
    vmem = pl.BlockSpec(memory_space=pltpu.VMEM)
    return pl.pallas_call(
        factor_kernel,
        out_shape=jax.ShapeDtypeStruct((SLOTS, NC), F32),
        in_specs=[vmem, vmem, vmem],
        out_specs=vmem,
        scratch_shapes=[
            pltpu.VMEM((NB, LIVE, 128), F32),
            pltpu.VMEM((NB + 1, LIVE, 128), F32),
            pltpu.VMEM((NB, SLOTS, 128), F32),
            pltpu.VMEM((NB, SLOTS, 128), F32),
            pltpu.VMEM((NB, SLOTS, 128), F32),
            pltpu.VMEM((LIVE // 8, 8, 8, 128), F32),
            pltpu.VMEM((LIVE // 8, 8, 128), F32),
            pltpu.VMEM((LIVE // 8, 8, 8, 128), F32),
        ],
        compiler_params=pltpu.CompilerParams(vmem_limit_bytes=40 * 2**20),
        name="factor",
    )(links, pivs, blocks)


def per_device(modes, counts, kappa, react):
    kappa = pltpu.with_memory_space_constraint(kappa, pltpu.HBM)
    react = pltpu.with_memory_space_constraint(react, pltpu.HBM)
    blocks, links, pivs = assemble(counts, modes, kappa, react)
    return factor(links, pivs, blocks)


def solution(mesh):
    in_specs = (
        P(None, "grp", "sub", None),
        P(("grp", "sub")),
        P("grp", "sub", None),
        P("grp", "sub", None),
    )
    out_specs = P(("grp", "sub"), None)
    return jax.shard_map(
        per_device, mesh=mesh, in_specs=in_specs, out_specs=out_specs, check_vma=False
    )
```
